32 devices in a mesh: seq: 8 (over z, y), head: 4 (over x, core).
Axes of the slice: x: 2, y: 2, z: 4, core: 2. Of those that a mesh axis runs over, the one named last changes fastest.
Arguments:
- queries: bfloat16 [4096, 8192], P('seq', 'head'), may hold values from -4 to 4
- key_vecs: bfloat16 [4096, 8192], P('seq', 'head'), may hold values from -4 to 4
- value_vecs: bfloat16 [4096, 8192], P('seq', 'head'), may hold values from -6 to 6
- log_decay: float32 [4096, 64], P('seq', 'head'), may hold values from -3 to 0, as said below
- norm_gain: float32 [8192], P('head'), may hold values from 0.1 to 1.9
- cotangent: bfloat16 [4096, 8192], P('seq', 'head'), may hold values from -6 to 6
Outputs:
- attended: bfloat16 [4096, 8192], P('seq', 'head')
- grad_queries: bfloat16 [4096, 8192], P('seq', 'head')
- grad_keys: bfloat16 [4096, 8192], P('seq', 'head')
- grad_values: bfloat16 [4096, 8192], P('seq', 'head')
The draws below stay inside these ranges and needn't reach their ends.
Inputs may be any that keep to these rules, and one draw needn't show every extreme that they name: `log_decay`: every entry is negative.
All inputs are finite; a program needn't handle non-finite values.
Results may differ from the reference program's by a relative error of at most 0.0051.
Values sent between devices are 32-bit elements; how exact they have to be, the bound alone decides.
No kernel may reach another device: no remote copies, remote signals or barrier semaphores. Data moves between devices by JAX's collectives and lax.ppermute only.
A program may use at most 128 MiB of HBM per device.

```python
import math
import jax
import jax.numpy as jnp
from jax import lax

HEAD_TOTAL = 64
HEAD_DIM = 128
TOK_DEV = 512
BLOCK = 512
SEQUENCE_LENGTH = 4096


def draw_log_decay(key, part):
    every_key = jax.random.split(key, 7)
    fast_share = 0.5
    is_fast = jax.random.bernoulli(every_key[0], fast_share, (HEAD_TOTAL,))
    fast_rate = jnp.exp(jax.random.uniform(every_key[1], (HEAD_TOTAL,), jnp.float32, math.log(0.04), math.log(0.08)))
    slow_rate = jnp.exp(jax.random.uniform(every_key[2], (HEAD_TOTAL,), jnp.float32, math.log(0.1), math.log(0.5)))
    slow_rate = slow_rate * (math.log(10.0) / SEQUENCE_LENGTH)
    shard_count = SEQUENCE_LENGTH // TOK_DEV
    is_hard = jax.random.bernoulli(every_key[6], 1.0 / 3.0, (shard_count, HEAD_TOTAL))
    positions = jnp.arange(SEQUENCE_LENGTH)
    shard_of = positions // TOK_DEV
    within = positions % BLOCK
    rim_width = 3 * BLOCK // 16
    middle = (within >= rim_width) & (within < BLOCK - rim_width)
    hard_rows = is_hard[shard_of]
    fast_here = is_fast[None, :] & hard_rows & middle[:, None]
    baseline_rate = jnp.where(fast_here, fast_rate[None, :], slow_rate[None, :])
    jitter_level = jax.random.uniform(every_key[3], (SEQUENCE_LENGTH, HEAD_TOTAL), jnp.float32, 0.5, 1.5)
    spike_positions = jax.random.randint(every_key[4], (4,), 0, SEQUENCE_LENGTH)
    spike_depth = jax.random.uniform(every_key[5], (4, HEAD_TOTAL), jnp.float32, math.log(0.5), math.log(0.8))
    spike_flags = (positions[:, None] == spike_positions[None, :]).astype(jnp.float32)
    return -baseline_rate * jitter_level + spike_flags @ spike_depth


def level_of(stream_key, shape, pieces, low, largest):
    def one(dim, parts):
        steps = jax.random.uniform(jax.random.fold_in(jax.random.fold_in(stream_key, 6), dim), (parts,), jnp.float32, low / len(pieces), largest / len(pieces))
        return jnp.repeat(jnp.exp(steps), shape[dim] // parts).reshape((-1,) + (1,) * (len(shape) - dim - 1))

    gain = one(*pieces[0])
    for cut in pieces[1:]:
        gain = gain * one(*cut)
    return gain


def noise(rng, extent, scale, bound, cuts=(), held_as=jnp.bfloat16):
    level = level_of(rng, extent, cuts, -0.22, 0.18) if cuts else 1.0
    result = jax.random.normal(rng, extent, jnp.float32) * scale * level
    return jnp.minimum(jnp.maximum(result, -bound), bound).astype(held_as)


def setup_inputs(seed: int = 0) -> dict:
    splits = jax.random.split(jax.random.key(seed), 7)
    queries = noise(splits[0], (SEQUENCE_LENGTH, HEAD_TOTAL * HEAD_DIM), 0.3, 4.0, ((0, 8), (1, 4)))
    key_vecs = noise(splits[1], (SEQUENCE_LENGTH, HEAD_TOTAL * HEAD_DIM), 0.3, 4.0, ((0, 8), (1, 4)))
    value_vecs = noise(splits[2], (SEQUENCE_LENGTH, HEAD_TOTAL * HEAD_DIM), 1.0, 6.0, ((0, 8), (1, 4)))
    log_decay = draw_log_decay(jax.random.fold_in(splits[6], 71), 0)
    norm_gain = jnp.clip(1.0 + 0.18 * jax.random.normal(splits[4], (HEAD_TOTAL * HEAD_DIM,), jnp.float32), 0.1, 1.9)
    cotangent = noise(splits[5], (SEQUENCE_LENGTH, HEAD_TOTAL * HEAD_DIM), 1.0, 6.0, ((0, 8), (1, 4)))
    return {"queries": queries, "key_vecs": key_vecs, "value_vecs": value_vecs, "log_decay": log_decay, "norm_gain": norm_gain, "cotangent": cotangent}


highest = lax.Precision.HIGHEST
epsilon = 1e-06

def as_float(array):
    return array.astype(jnp.float32)

def block_decay(cumulative):
    transposed = cumulative.T
    spread_log = transposed[:, :, None] - transposed[:, None, :]
    length = cumulative.shape[0]
    causal = (jnp.arange(length)[:, None] >= jnp.arange(length)[None, :])[None]
    return jnp.where(causal, jnp.exp(jnp.where(causal, spread_log, 0.0)), 0.0)

def reference(queries, key_vecs, value_vecs, log_decay, norm_gain, cotangent):
    block_count = SEQUENCE_LENGTH // BLOCK
    feature_count = HEAD_TOTAL * HEAD_DIM

    def to_blocks(array):
        return array.reshape(block_count, BLOCK, HEAD_TOTAL, HEAD_DIM)
    query_blocks = to_blocks(queries)
    key_blocks = to_blocks(key_vecs)
    value_blocks = to_blocks(value_vecs)
    cumulative = jnp.cumsum(log_decay.reshape(block_count, BLOCK, HEAD_TOTAL), axis=1)
    totals = cumulative[:, -1, :]
    zero_state = jnp.zeros((HEAD_TOTAL, HEAD_DIM, HEAD_DIM), jnp.float32)

    def forward_step(running, inputs):
        query_block, key_block, value_block, block_cumul = inputs
        decays = block_decay(block_cumul)
        scores = jnp.einsum('thd,shd->hts', as_float(query_block), as_float(key_block))
        weights = (scores * decays).astype(jnp.bfloat16)
        inner_out = jnp.einsum('hts,shd->thd', as_float(weights), as_float(value_block))
        outer_out = jnp.exp(block_cumul)[:, :, None] * jnp.einsum('thd,hde->the', as_float(query_block), running, precision=highest)
        scaled_keys = as_float(key_block) * jnp.exp(block_cumul[-1][None] - block_cumul)[:, :, None]
        block_piece = jnp.einsum('shd,she->hde', scaled_keys, as_float(value_block), precision=highest)
        advanced = jnp.exp(block_cumul[-1])[:, None, None] * running + block_piece
        return (advanced, (inner_out + outer_out, running))
    final_state, (outputs, before) = lax.scan(forward_step, zero_state, (query_blocks, key_blocks, value_blocks, cumulative))
    flat_out = outputs.reshape(SEQUENCE_LENGTH, feature_count)
    inverse = lax.rsqrt(lax.optimization_barrier(jnp.sum(flat_out * flat_out, axis=1)) / feature_count + epsilon)
    normed = flat_out * inverse[:, None]
    attended = (normed * norm_gain[None]).astype(jnp.bfloat16)
    scaled_grad = as_float(cotangent) * norm_gain[None]
    mean_term = inverse * lax.optimization_barrier(jnp.sum(scaled_grad * flat_out, axis=1)) / feature_count
    grad_out = (inverse[:, None] * (scaled_grad - normed * mean_term[:, None])).astype(jnp.bfloat16)
    grad_blocks = to_blocks(grad_out)

    def backward_inner(inputs):
        query_block, key_block, value_block, block_cumul, grad_block = inputs
        decays = block_decay(block_cumul)
        scores = jnp.einsum('thd,shd->hts', as_float(query_block), as_float(key_block))
        weights = (scores * decays).astype(jnp.bfloat16)
        grad_scores = jnp.einsum('thd,shd->hts', as_float(grad_block), as_float(value_block))
        grad_weights = (grad_scores * decays).astype(jnp.bfloat16)
        inner_query = jnp.einsum('hts,shd->thd', as_float(grad_weights), as_float(key_block))
        inner_key = jnp.einsum('hts,thd->shd', as_float(grad_weights), as_float(query_block))
        inner_value = jnp.einsum('hts,thd->shd', as_float(weights), as_float(grad_block))
        lead_scale = jnp.exp(block_cumul)[:, :, None]
        grad_piece = jnp.einsum('thd,the->hde', as_float(query_block) * lead_scale, as_float(grad_block), precision=highest)
        return (inner_query, inner_key, inner_value, grad_piece)
    inner_query, inner_key, inner_value, grad_pieces = lax.map(backward_inner, (query_blocks, key_blocks, value_blocks, cumulative, grad_blocks))

    def backward_step(running, inputs):
        grad_piece, block_total = inputs
        return (grad_piece + jnp.exp(block_total)[:, None, None] * running, running)
    start_grad, after_grad = lax.scan(backward_step, zero_state, (grad_pieces, totals), reverse=True)
    lead_scale = jnp.exp(cumulative)[..., None]
    trail_scale = jnp.exp(totals[:, None, :] - cumulative)[..., None]
    grad_queries = inner_query + lead_scale * jnp.einsum('bthe,bhde->bthd', as_float(grad_blocks), before, precision=highest)
    grad_keys = inner_key + trail_scale * jnp.einsum('bshe,bhde->bshd', as_float(value_blocks), after_grad, precision=highest)
    grad_values = inner_value + trail_scale * jnp.einsum('bshd,bhde->bshe', as_float(key_blocks), after_grad, precision=highest)
    return (attended, grad_queries.reshape(SEQUENCE_LENGTH, feature_count).astype(jnp.bfloat16), grad_keys.reshape(SEQUENCE_LENGTH, feature_count).astype(jnp.bfloat16), grad_values.reshape(SEQUENCE_LENGTH, feature_count).astype(jnp.bfloat16))
```

```python
import functools

import jax
import jax.numpy as jnp
from jax import lax
from jax.experimental import pallas as pl
from jax.experimental.pallas import tpu as pltpu
from jax.sharding import PartitionSpec as P

HEAD_DIM = 128
BLOCK = 512
CHUNKS = 4
TILE = 256
epsilon = 1e-06
f32 = jnp.float32
bf16 = jnp.bfloat16

NN = (((1,), (0,)), ((), ()))
NT = (((1,), (1,)), ((), ()))
TN = (((0,), (0,)), ((), ()))


def dot(a, b, dims=NN):
    return lax.dot_general(a, b, dims, preferred_element_type=f32)


def halves(x):
    high = x.astype(bf16)
    return high, (x - high.astype(f32)).astype(bf16)


def column(row):
    return jnp.transpose(jnp.broadcast_to(row, (HEAD_DIM, row.shape[1])))


def wide(col, width):
    return jnp.concatenate([col] * (width // HEAD_DIM), axis=1)


def cumul_kernel(decay_ref, out_ref):
    decay = decay_ref[...]
    length = decay.shape[0]
    first = decay.astype(bf16)
    rest = decay - first.astype(f32)
    second = rest.astype(bf16)
    third = (rest - second.astype(f32)).astype(bf16)
    upto = lax.broadcasted_iota(jnp.int32, (length, length), 0) <= lax.broadcasted_iota(
        jnp.int32, (length, length), 1
    )
    upto = jnp.where(upto, 1.0, 0.0).astype(bf16)
    out_ref[...] = dot(first, upto, TN) + dot(second, upto, TN) + dot(third, upto, TN)


def head_row(cumul_ref, head):
    return cumul_ref[pl.ds(head, 1), :]


def trail_row(row):
    return jnp.exp(row[:, -1:] - row)


def outer_sum(left, scale_row, right):
    scaled = jnp.transpose(left.astype(f32)) * scale_row
    high, low = halves(scaled)
    return dot(high, right) + dot(low, right)


def cols(j):
    return slice(j * HEAD_DIM, (j + 1) * HEAD_DIM)


def pieces_kernel(chunk, half, y_ref, key_ref, value_ref, cumul_ref, send_ref, keep_ref):
    step = pl.program_id(0)
    group = jnp.where(step == 0, 1 - y_ref[0], y_ref[0])
    base = (2 * chunk + group) * half
    found = []
    for j in range(half):
        row = head_row(cumul_ref, base + j)
        found.append(outer_sum(key_ref[:, cols(j)], trail_row(row), value_ref[:, cols(j)]))

    @pl.when(step == 0)
    def _():
        for j in range(half):
            send_ref[j] = found[j]

    @pl.when(step == 1)
    def _():
        for j in range(half):
            keep_ref[j] = found[j]


def inner_kernel(chunk, half, query_ref, key_ref, value_ref, cumul_ref, out_ref):
    base = (2 * chunk + pl.program_id(0)) * half
    for j in range(half):
        row = head_row(cumul_ref, base + j)
        col = column(row)
        query, key, value = query_ref[:, cols(j)], key_ref[:, cols(j)], value_ref[:, cols(j)]
        for top in range(0, BLOCK, TILE):
            end = top + TILE
            scores = dot(query[top:end], key[:end], NT)
            spread = wide(col[top:end], end) - row[:, :end]
            causal = lax.broadcasted_iota(jnp.int32, (TILE, end), 0) + top >= (
                lax.broadcasted_iota(jnp.int32, (TILE, end), 1)
            )
            weights = (scores * jnp.exp(jnp.where(causal, spread, -1e30))).astype(bf16)
            out_ref[top:end, cols(j)] = dot(weights, value[:end])


def output_kernel(
    chunk, half, y_ref, inner_ref, query_ref, cot_ref, gain_ref, cumul_ref, mine_ref, theirs_ref,
    before_ref, out_ref, sums_ref, square_ref, product_ref,
):
    step = pl.program_id(0)
    group = jnp.where(step == 0, y_ref[0], 1 - y_ref[0])
    base = (2 * chunk + group) * half
    squares = jnp.zeros((BLOCK, HEAD_DIM), f32)
    products = jnp.zeros((BLOCK, HEAD_DIM), f32)
    for j in range(half):
        lead = jnp.exp(column(head_row(cumul_ref, base + j)))
        high, low = halves(jnp.where(step == 0, mine_ref[j], theirs_ref[j]))
        query = query_ref[:, cols(j)]
        out = inner_ref[:, cols(j)] + lead * (dot(query, high) + dot(query, low))
        out_ref[:, cols(j)] = out
        squares += out * out
        products += cot_ref[:, cols(j)].astype(f32) * gain_ref[:, cols(j)] * out

    @pl.when(step == 0)
    def _():
        square_ref[...] = squares
        product_ref[...] = products

    @pl.when(step == 1)
    def _():
        rows = lax.broadcasted_iota(jnp.int32, (8, HEAD_DIM), 0)
        total = before_ref[...]
        for place, part in ((0, square_ref[...] + squares), (1, product_ref[...] + products)):
            pick = jnp.where(rows == place, 1.0, 0.0).astype(bf16)
            high, low = halves(part)
            total += dot(pick, high, NT) + dot(pick, low, NT)
        sums_ref[...] = total


def grad_kernel(
    chunk, half, features, shares, y_ref, out_ref, cot_ref, gain_ref, query_ref, cumul_ref, *refs
):
    share_refs, refs = refs[:shares], refs[shares:]
    attended_ref, grad_ref, send_ref, keep_ref = refs[-4:]
    step = pl.program_id(0)
    group = jnp.where(step == 0, 1 - y_ref[0], y_ref[0])
    base = (2 * chunk + group) * half
    sums = share_refs[0][...]
    for share in share_refs[1:]:
        sums = sums + share[...]
    inverse = lax.rsqrt(sums[0:1] / features + epsilon)
    mean_term = inverse * sums[1:2] / features
    inverse_col, mean_col = column(inverse), column(mean_term)
    found = []
    for j in range(half):
        gain = gain_ref[:, cols(j)]
        normed = out_ref[:, cols(j)] * inverse_col
        attended_ref[:, cols(j)] = (normed * gain).astype(bf16)
        scaled_grad = cot_ref[:, cols(j)].astype(f32) * gain
        grad = (inverse_col * (scaled_grad - normed * mean_col)).astype(bf16)
        grad_ref[:, cols(j)] = grad
        row = head_row(cumul_ref, base + j)
        found.append(outer_sum(query_ref[:, cols(j)], jnp.exp(row), grad))

    @pl.when(step == 0)
    def _():
        for j in range(half):
            send_ref[j] = found[j]

    @pl.when(step == 1)
    def _():
        for j in range(half):
            keep_ref[j] = found[j]


def backward_kernel(
    chunk, half, y_ref, query_ref, key_ref, value_ref, grad_ref, cumul_ref, mine_ref, theirs_ref, *refs
):
    grad_query_ref, inner_key_ref, inner_value_ref = refs[-3:]
    step = pl.program_id(0)
    group = jnp.where(step == 0, y_ref[0], 1 - y_ref[0])
    base = (2 * chunk + group) * half
    for j in range(half):
        row = head_row(cumul_ref, base + j)
        col = column(row)
        query, key = query_ref[:, cols(j)], key_ref[:, cols(j)]
        value, grad = value_ref[:, cols(j)], grad_ref[:, cols(j)]
        high, low = halves(jnp.where(step == 0, mine_ref[j], theirs_ref[j]))
        outer = jnp.exp(col) * (dot(grad, high, NT) + dot(grad, low, NT))
        for top in range(0, BLOCK, TILE):
            end = top + TILE
            scores = dot(key[top:end], query[top:], NT)
            grad_scores = dot(value[top:end], grad[top:], NT)
            spread = row[:, top:] - wide(col[top:end], BLOCK - top)
            causal = lax.broadcasted_iota(jnp.int32, spread.shape, 0) <= (
                lax.broadcasted_iota(jnp.int32, spread.shape, 1)
            )
            decays = jnp.exp(jnp.where(causal, spread, -1e30))
            weights = (scores * decays).astype(bf16)
            grad_weights = (grad_scores * decays).astype(bf16)
            inner_value_ref[top:end, cols(j)] = dot(weights, grad[top:])
            inner_key_ref[top:end, cols(j)] = dot(grad_weights, query[top:])
            part = dot(grad_weights, key[top:end], TN)
            outer = part + outer if top == 0 else jnp.concatenate(
                [outer[:top], outer[top:] + part], axis=0
            )
        grad_query_ref[:, cols(j)] = outer.astype(bf16)


def final_kernel(
    chunk, half, y_ref, inner_key_ref, inner_value_ref, key_ref, value_ref, cumul_ref, mine_ref,
    theirs_ref, *refs,
):
    grad_key_ref, grad_value_ref = refs[-2:]
    step = pl.program_id(0)
    group = jnp.where(step == 0, y_ref[0], 1 - y_ref[0])
    base = (2 * chunk + group) * half
    for j in range(half):
        trail = column(trail_row(head_row(cumul_ref, base + j)))
        high, low = halves(jnp.where(step == 0, mine_ref[j], theirs_ref[j]))
        key, value = key_ref[:, cols(j)], value_ref[:, cols(j)]
        grad_key_ref[:, cols(j)] = (
            inner_key_ref[:, cols(j)] + trail * (dot(value, high, NT) + dot(value, low, NT))
        ).astype(bf16)
        grad_value_ref[:, cols(j)] = (
            inner_value_ref[:, cols(j)] + trail * (dot(key, high) + dot(key, low))
        ).astype(bf16)


def chain(sends, keeps, first, place, places, forward, first_decay, second_decay):
    count = len(sends)

    def device(where, member):
        return 2 * (where if forward else places - 1 - where) + member

    swap = [(2 * p + m, 2 * p + 1 - m) for p in range(places) for m in (0, 1)]
    received = [lax.ppermute(send, "seq", swap) for send in sends]
    firsts = [jnp.where(first, keep, got) for keep, got in zip(keeps, received)]
    pair_sums = [
        second_decay[c] * firsts[c] + jnp.where(first, received[c], keeps[c]) for c in range(count)
    ]
    pair_decay = first_decay * second_decay
    arrived = {}
    for step in range(2, count + places):
        senders = [p for p in range(places - 1) if 0 <= step - 2 - p < count]
        value = None
        for p in senders:
            c = step - 2 - p
            if p == 0:
                here = pair_sums[c]
            else:
                here = pair_decay[c] * arrived[step - 1] + pair_sums[c]
            value = here if value is None else jnp.where(place == p, here, value)
        pairs = [(device(p, m), device(p + 1, m)) for p in senders for m in (0, 1)]
        arrived[step] = lax.ppermute(value, "seq", pairs)
    mine, theirs = [], []
    for c in range(count):
        before = jnp.zeros_like(keeps[c])
        for p in range(1, places):
            before = jnp.where(place == p, arrived[c + 1 + p], before)
        after_first = first_decay[c] * before + firsts[c]
        mine.append(jnp.where(first, before, after_first))
        theirs.append(lax.ppermute(jnp.where(first, after_first, before), "seq", swap))
    return mine, theirs


def on_device(queries, key_vecs, value_vecs, log_decay, norm_gain, cotangent):
    tokens, width = queries.shape
    assert tokens == BLOCK
    heads = width // HEAD_DIM
    half = heads // (2 * CHUNKS)
    features = width * lax.axis_size("head")
    seq_count = lax.axis_size("seq")
    places = seq_count // 2
    my_index = lax.axis_index("seq")
    member = my_index % 2
    pair = my_index // 2
    member_ref = member.astype(jnp.int32).reshape(1)
    gain = norm_gain.reshape(1, width)

    group_width = half * HEAD_DIM
    state_shape = (half, HEAD_DIM, HEAD_DIM)
    state = jax.ShapeDtypeStruct(state_shape, f32)
    whole = jax.ShapeDtypeStruct((tokens, width), bf16)
    part = jax.ShapeDtypeStruct((tokens, 2 * group_width), f32)
    part_low = jax.ShapeDtypeStruct((tokens, 2 * group_width), bf16)
    sums_shape = jax.ShapeDtypeStruct((8, tokens), f32)
    any_spec = pl.BlockSpec(memory_space=pl.ANY)

    def fixed(shape):
        return pl.BlockSpec(shape, lambda i, y: (0,) * len(shape))

    def group_of(order, i, y):
        if order == "mine":
            return jnp.where(i == 0, y[0], 1 - y[0])
        if order == "theirs":
            return jnp.where(i == 0, 1 - y[0], y[0])
        return i

    def full(chunk, order, rows=tokens):
        return pl.BlockSpec((rows, group_width), lambda i, y: (0, 2 * chunk + group_of(order, i, y)))

    def local(order):
        return pl.BlockSpec((tokens, group_width), lambda i, y: (0, group_of(order, i, y)))

    def run(kernel, chunk, in_specs, out_specs, out_shape, args, scratch=(), aliases=None, cost=1.0):
        def body(y_ref, *refs):
            kernel(chunk, half, y_ref, *refs)

        return pl.pallas_call(
            body,
            out_shape=out_shape,
            grid_spec=pltpu.PrefetchScalarGridSpec(
                num_scalar_prefetch=1,
                grid=(2,),
                in_specs=in_specs,
                out_specs=out_specs,
                scratch_shapes=list(scratch),
            ),
            input_output_aliases=aliases or {},
            compiler_params=pltpu.CompilerParams(vmem_limit_bytes=32 * 1024 * 1024),
            cost_estimate=pl.CostEstimate(
                flops=int(cost * 1e9), bytes_accessed=int(cost * 2.5e6), transcendentals=0
            ),
        )(member_ref, *args)

    cumul = pl.pallas_call(
        cumul_kernel, out_shape=jax.ShapeDtypeStruct((heads, tokens), f32)
    )(log_decay)
    cumul_spec = fixed((heads, tokens))
    state_spec = fixed(state_shape)

    own_decay = jnp.exp(cumul[:, -1])
    swap = [(i, i ^ 1) for i in range(seq_count)]
    other_decay = jnp.exp(lax.ppermute(cumul[:, -1], "seq", swap))

    def kept(vector):
        grouped = vector.reshape(CHUNKS, 2, half)
        return jnp.where(member == 0, grouped[:, 0], grouped[:, 1])[:, :, None, None]

    low_decay = kept(jnp.where(member == 0, own_decay, other_decay))
    high_decay = kept(jnp.where(member == 0, other_decay, own_decay))

    sends, keeps = [], []
    for c in range(CHUNKS):
        send, keep = run(
            pieces_kernel, c, [full(c, "theirs"), full(c, "theirs"), cumul_spec],
            [state_spec] * 2, [state] * 2, (key_vecs, value_vecs, cumul), cost=1.5,
        )
        sends.append(send)
        keeps.append(keep)
    mine, theirs = chain(
        sends, keeps, member == 0, pair, places, True, low_decay, high_decay
    )
    inner = [
        run(
            lambda chunk, half, y_ref, *refs: inner_kernel(chunk, half, *refs), c,
            [full(c, "")] * 3 + [cumul_spec], local(""), part,
            (queries, key_vecs, value_vecs, cumul), cost=2.5,
        )
        for c in range(CHUNKS)
    ]

    sums = jnp.zeros(sums_shape.shape, f32)
    outs = []
    for c in range(CHUNKS):
        out, sums = run(
            output_kernel, c,
            [local("mine"), full(c, "mine"), full(c, "mine"), full(c, "mine", 1), cumul_spec,
             state_spec, state_spec, fixed(sums_shape.shape)],
            [local("mine"), fixed(sums_shape.shape)], [part, sums_shape],
            (inner[c], queries, cotangent, gain, cumul, mine[c], theirs[c], sums),
            scratch=[pltpu.VMEM((tokens, HEAD_DIM), f32)] * 2, cost=1.5,
        )
        outs.append(out)

    head_count = lax.axis_size("head")
    shares = [sums] + [
        lax.ppermute(sums, "head", [(i, (i + k) % head_count) for i in range(head_count)])
        for k in range(1, head_count)
    ]

    sends, keeps, grads = [], [], []
    attended = None
    for c in range(CHUNKS):
        before = [] if attended is None else [attended]
        attended, grad, send, keep = run(
            lambda chunk, half, *refs: grad_kernel(chunk, half, features, head_count, *refs), c,
            [local("theirs"), full(c, "theirs"), full(c, "theirs", 1), full(c, "theirs"), cumul_spec]
            + [fixed(sums_shape.shape)] * head_count + [any_spec] * len(before),
            [full(c, "theirs"), local("theirs"), state_spec, state_spec],
            [whole, part_low, state, state],
            (outs[c], cotangent, gain, queries, cumul, *shares, *before),
            aliases={6 + head_count: 0} if before else None, cost=1.5,
        )
        sends.append(send)
        keeps.append(keep)
        grads.append(grad)
    mine_after, theirs_after = chain(
        sends, keeps, member == 1, places - 1 - pair, places, False, high_decay, low_decay
    )

    grad_queries = None
    inner_grads = []
    for c in range(CHUNKS):
        before = [] if grad_queries is None else [grad_queries]
        grad_queries, inner_key, inner_value = run(
            backward_kernel, c,
            [full(c, "mine")] * 3 + [local("mine"), cumul_spec, state_spec, state_spec]
            + [any_spec] * len(before),
            [full(c, "mine"), local("mine"), local("mine")], [whole, part, part],
            (queries, key_vecs, value_vecs, grads[c], cumul, mine[c], theirs[c], *before),
            aliases={8: 0} if before else None, cost=4.0,
        )
        inner_grads.append((inner_key, inner_value))

    grad_keys = grad_values = None
    for c in range(CHUNKS):
        before = [] if grad_keys is None else [grad_keys, grad_values]
        grad_keys, grad_values = run(
            final_kernel, c,
            [local("mine")] * 2 + [full(c, "mine")] * 2 + [cumul_spec, state_spec, state_spec]
            + [any_spec] * len(before),
            [full(c, "mine")] * 2, [whole] * 2,
            (*inner_grads[c], key_vecs, value_vecs, cumul, mine_after[c], theirs_after[c], *before),
            aliases={8: 0, 9: 1} if before else None, cost=1.5,
        )
    return attended, grad_queries, grad_keys, grad_values


def solution(mesh):
    return jax.shard_map(
        on_device,
        mesh=mesh,
        in_specs=(
            P("seq", "head"),
            P("seq", "head"),
            P("seq", "head"),
            P("seq", "head"),
            P("head"),
            P("seq", "head"),
        ),
        out_specs=(P("seq", "head"), P("seq", "head"), P("seq", "head"), P("seq", "head")),
        check_vma=False,
    )
```

```python
import functools

import jax
import jax.numpy as jnp
from jax import lax
from jax.experimental import pallas as pl
from jax.experimental.pallas import tpu as pltpu
from jax.sharding import PartitionSpec as P

HEAD_DIM = 128
BLOCK = 512
CHUNKS = 2
TILE = 256
epsilon = 1e-06
f32 = jnp.float32
bf16 = jnp.bfloat16

NN = (((1,), (0,)), ((), ()))
NT = (((1,), (1,)), ((), ()))
TN = (((0,), (0,)), ((), ()))


def dot(a, b, dims=NN):
    return lax.dot_general(a, b, dims, preferred_element_type=f32)


def halves(x):
    high = x.astype(bf16)
    return high, (x - high.astype(f32)).astype(bf16)


def column(row):
    return jnp.transpose(jnp.broadcast_to(row, (HEAD_DIM, row.shape[1])))


def wide(col, width):
    return jnp.concatenate([col] * (width // HEAD_DIM), axis=1)


def cumul_kernel(decay_ref, out_ref):
    decay = decay_ref[...]
    length = decay.shape[1]
    first = decay.astype(bf16)
    rest = decay - first.astype(f32)
    second = rest.astype(bf16)
    third = (rest - second.astype(f32)).astype(bf16)
    upto = lax.broadcasted_iota(jnp.int32, (length, length), 0) <= lax.broadcasted_iota(
        jnp.int32, (length, length), 1
    )
    upto = jnp.where(upto, 1.0, 0.0).astype(bf16)
    out_ref[...] = dot(first, upto) + dot(second, upto) + dot(third, upto)


def trail_row(row):
    return jnp.exp(row[:, -1:] - row)


def outer_sum(left, scale_row, right):
    scaled = jnp.transpose(left.astype(f32)) * scale_row
    high, low = halves(scaled)
    return dot(high, right) + dot(low, right)


def cols(j):
    return slice(j * HEAD_DIM, (j + 1) * HEAD_DIM)


class Part:
    def __init__(self, chunk, slot, half):
        self.chunk, self.slot, self.half = chunk, slot, half
        self.steps = 2 if half % 2 == 0 else 1
        self.per_step = half // self.steps

    def group(self, info):
        return info[0] if self.slot == "mine" else 1 - info[0]

    def row(self, cumul_ref, info, j):
        head = (2 * self.chunk + self.group(info)) * self.half + pl.program_id(0) * self.per_step + j
        return cumul_ref[pl.ds(head, 1), :]

    def state_rows(self, j):
        start = (pl.program_id(0) * self.per_step + j) * HEAD_DIM
        return pl.ds(pl.multiple_of(start, HEAD_DIM), HEAD_DIM)


def store_decays(part, info, cumul_ref, out_ref):
    for j in range(part.per_step):
        row = part.row(cumul_ref, info, j)
        place = part.half * HEAD_DIM + pl.program_id(0) * part.per_step + j
        out_ref[pl.ds(place, 1), :] = jnp.broadcast_to(jnp.exp(row[:, -1:]), (1, HEAD_DIM))


def pieces_kernel(part, info, key_ref, value_ref, cumul_ref, out_ref):
    for j in range(part.per_step):
        row = part.row(cumul_ref, info, j)
        out_ref[part.state_rows(j), :] = outer_sum(
            key_ref[:, cols(j)], trail_row(row), value_ref[:, cols(j)]
        )
    store_decays(part, info, cumul_ref, out_ref)


def inner_kernel(part, info, query_ref, key_ref, value_ref, cumul_ref, out_ref):
    for j in range(part.per_step):
        row = part.row(cumul_ref, info, j)
        col = column(row)
        query, key, value = query_ref[:, cols(j)], key_ref[:, cols(j)], value_ref[:, cols(j)]
        for top in range(0, BLOCK, TILE):
            end = top + TILE
            scores = dot(query[top:end], key[:end], NT)
            spread = wide(col[top:end], end) - row[:, :end]
            causal = lax.broadcasted_iota(jnp.int32, (TILE, end), 0) + top >= (
                lax.broadcasted_iota(jnp.int32, (TILE, end), 1)
            )
            weights = (scores * jnp.exp(jnp.where(causal, spread, -1e30))).astype(bf16)
            out_ref[top:end, cols(j)] = dot(weights, value[:end])


def output_kernel(
    part, info, inner_ref, query_ref, cot_ref, gain_ref, cumul_ref, state_ref, before_ref,
    out_ref, sums_ref, square_ref, product_ref,
):
    step = pl.program_id(0)
    squares = jnp.zeros((BLOCK, HEAD_DIM), f32)
    products = jnp.zeros((BLOCK, HEAD_DIM), f32)
    for j in range(part.per_step):
        lead = jnp.exp(column(part.row(cumul_ref, info, j)))
        high, low = halves(state_ref[part.state_rows(j), :])
        query = query_ref[:, cols(j)]
        out = inner_ref[:, cols(j)] + lead * (dot(query, high) + dot(query, low))
        out_ref[:, cols(j)] = out
        squares += out * out
        products += cot_ref[:, cols(j)].astype(f32) * gain_ref[:, cols(j)] * out

    @pl.when(step == 0)
    def _():
        square_ref[...] = squares
        product_ref[...] = products

    @pl.when(step > 0)
    def _():
        square_ref[...] += squares
        product_ref[...] += products

    @pl.when(step == part.steps - 1)
    def _():
        rows = lax.broadcasted_iota(jnp.int32, (8, HEAD_DIM), 0)
        total = before_ref[...]
        for place, ref in ((0, square_ref), (1, product_ref)):
            pick = jnp.where(rows == place, 1.0, 0.0).astype(bf16)
            high, low = halves(ref[...])
            total += dot(pick, high, NT) + dot(pick, low, NT)
        sums_ref[...] = total


def grad_kernel(features, part, info, out_ref, cot_ref, gain_ref, query_ref, cumul_ref, *refs):
    shares, (attended_ref, grad_ref, piece_ref) = refs[:-3], refs[-3:]
    sums = shares[0][...]
    for share in shares[1:]:
        sums = sums + share[...]
    inverse = lax.rsqrt(sums[0:1] / features + epsilon)
    mean_term = inverse * sums[1:2] / features
    inverse_col, mean_col = column(inverse), column(mean_term)
    for j in range(part.per_step):
        gain = gain_ref[:, cols(j)]
        normed = out_ref[:, cols(j)] * inverse_col
        attended_ref[:, cols(j)] = (normed * gain).astype(bf16)
        scaled_grad = cot_ref[:, cols(j)].astype(f32) * gain
        grad = (inverse_col * (scaled_grad - normed * mean_col)).astype(bf16)
        grad_ref[:, cols(j)] = grad
        row = part.row(cumul_ref, info, j)
        piece_ref[part.state_rows(j), :] = outer_sum(query_ref[:, cols(j)], jnp.exp(row), grad)
    store_decays(part, info, cumul_ref, piece_ref)


def backward_kernel(
    part, info, query_ref, key_ref, value_ref, grad_ref, cumul_ref, state_ref,
    grad_query_ref, inner_key_ref, inner_value_ref,
):
    for j in range(part.per_step):
        row = part.row(cumul_ref, info, j)
        col = column(row)
        query, key = query_ref[:, cols(j)], key_ref[:, cols(j)]
        value, grad = value_ref[:, cols(j)], grad_ref[:, cols(j)]
        high, low = halves(state_ref[part.state_rows(j), :])
        outer = jnp.exp(col) * (dot(grad, high, NT) + dot(grad, low, NT))
        for top in range(0, BLOCK, TILE):
            end = top + TILE
            scores = dot(key[top:end], query[top:], NT)
            grad_scores = dot(value[top:end], grad[top:], NT)
            spread = row[:, top:] - wide(col[top:end], BLOCK - top)
            causal = lax.broadcasted_iota(jnp.int32, spread.shape, 0) <= (
                lax.broadcasted_iota(jnp.int32, spread.shape, 1)
            )
            decays = jnp.exp(jnp.where(causal, spread, -1e30))
            weights = (scores * decays).astype(bf16)
            grad_weights = (grad_scores * decays).astype(bf16)
            inner_value_ref[top:end, cols(j)] = dot(weights, grad[top:])
            inner_key_ref[top:end, cols(j)] = dot(grad_weights, query[top:])
            inner_query = dot(grad_weights, key[top:end], TN)
            outer = inner_query + outer if top == 0 else jnp.concatenate(
                [outer[:top], outer[top:] + inner_query], axis=0
            )
        grad_query_ref[:, cols(j)] = outer.astype(bf16)


def final_kernel(
    part, info, inner_key_ref, inner_value_ref, key_ref, value_ref, cumul_ref, state_ref,
    grad_key_ref, grad_value_ref,
):
    for j in range(part.per_step):
        trail = column(trail_row(part.row(cumul_ref, info, j)))
        high, low = halves(state_ref[part.state_rows(j), :])
        key, value = key_ref[:, cols(j)], value_ref[:, cols(j)]
        grad_key_ref[:, cols(j)] = (
            inner_key_ref[:, cols(j)] + trail * (dot(value, high, NT) + dot(value, low, NT))
        ).astype(bf16)
        grad_value_ref[:, cols(j)] = (
            inner_value_ref[:, cols(j)] + trail * (dot(key, high) + dot(key, low))
        ).astype(bf16)


def ordered(is_first, half, j, keep_ref, got_ref):
    rows = slice(j * HEAD_DIM, (j + 1) * HEAD_DIM)
    place = slice(half * HEAD_DIM + j, half * HEAD_DIM + j + 1)
    keep, got = keep_ref[rows, :], got_ref[rows, :]
    keep_decay, got_decay = keep_ref[place, :], got_ref[place, :]
    return (
        jnp.where(is_first, keep, got),
        jnp.where(is_first, got, keep),
        jnp.where(is_first, keep_decay, got_decay),
        jnp.where(is_first, got_decay, keep_decay),
    )


def hop_kernel(half, senders, info, *refs):
    out_ref, arrived_ref = refs[-1], refs[-2]
    for index, p in enumerate(senders):
        keep_ref, got_ref = refs[2 * index], refs[2 * index + 1]

        @pl.when(info[2] == p)
        def _():
            for j in range(half):
                first, second, first_decay, second_decay = ordered(
                    info[1] == 1, half, j, keep_ref, got_ref
                )
                value = second_decay * first + second
                if p > 0:
                    value += (first_decay * second_decay) * arrived_ref[cols(j), :]
                out_ref[cols(j), :] = value


def last_kernel(half, info, keep_ref, got_ref, *refs):
    arrived, (mine_ref, send_ref) = refs[:-2], refs[-2:]
    is_first = info[1] == 1
    for p in range(len(arrived) + 1):

        @pl.when(info[2] == p)
        def _():
            for j in range(half):
                first, _, first_decay, _ = ordered(is_first, half, j, keep_ref, got_ref)
                if p == 0:
                    before, after = jnp.zeros_like(first), first
                else:
                    before = arrived[p - 1][cols(j), :]
                    after = first_decay * before + first
                mine_ref[cols(j), :] = jnp.where(is_first, before, after)
                send_ref[cols(j), :] = jnp.where(is_first, after, before)


def on_device(queries, key_vecs, value_vecs, log_decay, norm_gain, cotangent):
    tokens, width = queries.shape
    assert tokens == BLOCK
    heads = width // HEAD_DIM
    half = heads // (2 * CHUNKS)
    head_count = lax.axis_size("head")
    features = width * head_count
    places = lax.axis_size("seq") // 2
    my_index = lax.axis_index("seq")
    member, pair = my_index % 2, my_index // 2
    gain = norm_gain.reshape(1, width)

    any_spec = pl.BlockSpec(memory_space=pl.ANY)
    wide_state = jax.ShapeDtypeStruct((half * HEAD_DIM + 8, HEAD_DIM), f32)
    state = jax.ShapeDtypeStruct((half * HEAD_DIM, HEAD_DIM), f32)
    whole = jax.ShapeDtypeStruct((tokens, width), bf16)
    local = jax.ShapeDtypeStruct((tokens, half * HEAD_DIM), f32)
    local_low = jax.ShapeDtypeStruct((tokens, half * HEAD_DIM), bf16)
    sums_shape = jax.ShapeDtypeStruct((8, tokens), f32)
    forward_info = jnp.stack([member, 1 - member, pair]).astype(jnp.int32)
    backward_info = jnp.stack([member, member, places - 1 - pair]).astype(jnp.int32)

    def run(kernel, info, grid, ins, outs, scratch=(), after=(), aliases=None, cost=1.0):
        used = len(ins)
        after = [x for i, x in enumerate(after) if not any(x is y for y in after[:i])]

        def body(info_ref, *refs):
            kernel(info_ref, *refs[:used], *refs[used + len(after):])

        return pl.pallas_call(
            body,
            out_shape=[shape for shape, _ in outs],
            grid_spec=pltpu.PrefetchScalarGridSpec(
                num_scalar_prefetch=1,
                grid=(grid,),
                in_specs=[spec for _, spec in ins] + [any_spec] * len(after),
                out_specs=[spec for _, spec in outs],
                scratch_shapes=list(scratch),
            ),
            input_output_aliases=aliases or {},
            compiler_params=pltpu.CompilerParams(vmem_limit_bytes=16 * 1024 * 1024),
            cost_estimate=pl.CostEstimate(
                flops=int(cost * 1e9), bytes_accessed=int(cost * 2.5e6), transcendentals=0
            ),
        )(info, *[array for array, _ in ins], *after)

    def fixed(shape):
        return pl.BlockSpec(shape, lambda i, info: (0,) * len(shape))

    def plain(array):
        return array, fixed(array.shape)

    def give(shape):
        return shape, fixed(shape.shape)

    class Views(Part):
        def full(self, array, rows=tokens):
            return array, self.full_spec(rows)

        def full_spec(self, rows=tokens):
            return pl.BlockSpec(
                (rows, self.per_step * HEAD_DIM),
                lambda i, info: (0, (2 * self.chunk + self.group(info)) * self.steps + i),
            )

        def local(self, array):
            return array, pl.BlockSpec((tokens, self.per_step * HEAD_DIM), lambda i, info: (0, i))

        def call(self, kernel, ins, outs, **options):
            return run(functools.partial(kernel, self), forward_info, self.steps, ins, outs, **options)

    mine_parts = [Views(c, "mine", half) for c in range(CHUNKS)]
    their_parts = [Views(c, "theirs", half) for c in range(CHUNKS)]

    cumul = pl.pallas_call(
        cumul_kernel, out_shape=jax.ShapeDtypeStruct((heads, tokens), f32)
    )(log_decay.T)

    swap = [(2 * p + m, 2 * p + 1 - m) for p in range(places) for m in (0, 1)]

    def chain(make_piece, info, forward, early, filler, on_mine):
        step = 1 if forward else -1
        ring = [
            (2 * p + m, 2 * ((p + step) % places) + m) for p in range(places) for m in (0, 1)
        ]
        received, last = [], ()
        for c in range(CHUNKS):
            sent = make_piece(their_parts[c], last)
            received.append(lax.ppermute(sent, "seq", swap))
            last = (sent,)
        keeps = []
        for c in range(CHUNKS):
            keeps.append(make_piece(mine_parts[c], last))
            last = (keeps[-1],)
        for work in early:
            last = (work(last),)
        arrived, mine, theirs = {}, [], []
        for r in range(2, CHUNKS + places + 1):
            if r < CHUNKS + places:
                senders = [p for p in range(places - 1) if 0 <= r - 2 - p < CHUNKS]
                ins = []
                for p in senders:
                    ins += [plain(keeps[r - 2 - p]), plain(received[r - 2 - p])]
                ins.append(plain(arrived[r - 1]) if r > 2 else plain(keeps[0]))
                value, = run(
                    functools.partial(hop_kernel, half, senders), info, 1, ins, [give(state)],
                    after=last, cost=0.3,
                )
                arrived[r] = lax.ppermute(value, "seq", ring)
                last = (value,)
            c = r - 1 - places
            if 0 <= c:
                ins = [plain(keeps[c]), plain(received[c])]
                ins += [plain(arrived[c + 1 + p]) for p in range(1, places)]
                own, send = run(
                    functools.partial(last_kernel, half), info, 1, ins, [give(state)] * 2,
                    after=last, cost=0.3,
                )
                theirs.append(lax.ppermute(send, "seq", swap))
                mine.append(own)
                last = (send,)
                filler.append(functools.partial(on_mine, c, own))
            if filler:
                last = (filler.pop(0)(last),)
        while filler:
            last = (filler.pop(0)(last),)
        return mine, theirs, last

    def forward_piece(part, after):
        return part.call(
            pieces_kernel, [part.full(key_vecs), part.full(value_vecs), plain(cumul)],
            [give(wide_state)], after=after, cost=1.0,
        )[0]

    inner, outs = {}, {}
    state_sums = [jnp.zeros(sums_shape.shape, f32)]

    def inner_work(part, after):
        inner[part], = part.call(
            inner_kernel,
            [part.full(queries), part.full(key_vecs), part.full(value_vecs), plain(cumul)],
            [part.local(local)], after=after, cost=2.2,
        )
        return inner[part]

    def output_work(part, before, after):
        outs[part], sums = part.call(
            output_kernel,
            [part.local(inner[part]), part.full(queries), part.full(cotangent), part.full(gain, 1),
             plain(cumul), plain(before), plain(state_sums[0])],
            [part.local(local), give(sums_shape)],
            scratch=[pltpu.VMEM((tokens, HEAD_DIM), f32)] * 2, after=after, cost=1.4,
        )
        state_sums[0] = sums
        return sums

    inner_order = [part for c in range(CHUNKS) for part in (mine_parts[c], their_parts[c])]
    works = [functools.partial(inner_work, part) for part in inner_order]
    mine, theirs, last = chain(
        forward_piece, forward_info, True, works[:1], works[1:],
        lambda c, own, after: output_work(mine_parts[c], own, after),
    )
    for c in range(CHUNKS):
        last = (output_work(their_parts[c], theirs[c], last),)

    sums = state_sums[0]
    shares = [sums] + [
        lax.ppermute(sums, "head", [(i, (i + k) % head_count) for i in range(head_count)])
        for k in range(1, head_count)
    ]

    attended, grad_queries, grad_keys, grad_values = [], [], [], []
    grads, inner_grads = {}, {}

    def target(held):
        return tuple(held[-1:])

    def backward_piece(part, after):
        before = target(attended)
        whole_out, grads[part], piece = part.call(
            functools.partial(grad_kernel, features),
            [part.local(outs[part]), part.full(cotangent), part.full(gain, 1), part.full(queries),
             plain(cumul)] + [plain(share) for share in shares],
            [(whole, part.full_spec()), part.local(local_low), give(wide_state)],
            after=before + tuple(after), aliases={6 + head_count: 0} if before else None, cost=2.0,
        )
        attended.append(whole_out)
        return piece

    def backward_work(part, before, after):
        held = target(grad_queries)
        whole_out, *inner_grads[part] = part.call(
            backward_kernel,
            [part.full(queries), part.full(key_vecs), part.full(value_vecs),
             part.local(grads[part]), plain(cumul), plain(before)],
            [(whole, part.full_spec()), part.local(local), part.local(local)],
            after=held + tuple(after), aliases={7: 0} if held else None, cost=4.3,
        )
        grad_queries.append(whole_out)
        return inner_grads[part][0]

    def final_work(part, before, after):
        held = target(grad_keys) + target(grad_values)
        whole_key, whole_value = part.call(
            final_kernel,
            [part.local(inner_grads[part][0]), part.local(inner_grads[part][1]),
             part.full(key_vecs), part.full(value_vecs), plain(cumul), plain(before)],
            [(whole, part.full_spec())] * 2,
            after=held + tuple(after), aliases={7: 0, 8: 1} if held else None, cost=2.0,
        )
        grad_keys.append(whole_key)
        grad_values.append(whole_value)
        return whole_key

    works = []
    for c in range(CHUNKS):
        works.append(functools.partial(backward_work, mine_parts[c], mine[c]))
        works.append(functools.partial(backward_work, their_parts[c], theirs[c]))
    mine_after, theirs_after, last = chain(
        backward_piece, backward_info, False, [], works,
        lambda c, own, after: final_work(mine_parts[c], own, after),
    )
    for c in range(CHUNKS):
        final_work(their_parts[c], theirs_after[c], last)
        last = ()
    return attended[-1], grad_queries[-1], grad_keys[-1], grad_values[-1]


def solution(mesh):
    return jax.shard_map(
        on_device,
        mesh=mesh,
        in_specs=(
            P("seq", "head"),
            P("seq", "head"),
            P("seq", "head"),
            P("seq", "head"),
            P("head"),
            P("seq", "head"),
        ),
        out_specs=(P("seq", "head"), P("seq", "head"), P("seq", "head"), P("seq", "head")),
        check_vma=False,
    )
```

```python
import functools

import jax
import jax.numpy as jnp
from jax import lax
from jax.experimental import pallas as pl
from jax.experimental.pallas import tpu as pltpu
from jax.sharding import PartitionSpec as P

HEAD_DIM = 128
BLOCK = 512
CHUNKS = 2
TILE = 256
epsilon = 1e-06
f32 = jnp.float32
bf16 = jnp.bfloat16

NN = (((1,), (0,)), ((), ()))
NT = (((1,), (1,)), ((), ()))
TN = (((0,), (0,)), ((), ()))


def dot(a, b, dims=NN):
    return lax.dot_general(a, b, dims, preferred_element_type=f32)


def halves(x):
    high = x.astype(bf16)
    return high, (x - high.astype(f32)).astype(bf16)


def column(row):
    return jnp.transpose(jnp.broadcast_to(row, (HEAD_DIM, row.shape[1])))


def wide(col, width):
    return jnp.concatenate([col] * (width // HEAD_DIM), axis=1)


def cumulative(decay):
    length = decay.shape[1]
    first = decay.astype(bf16)
    rest = decay - first.astype(f32)
    second = rest.astype(bf16)
    third = (rest - second.astype(f32)).astype(bf16)
    upto = lax.broadcasted_iota(jnp.int32, (length, length), 0) <= lax.broadcasted_iota(
        jnp.int32, (length, length), 1
    )
    upto = jnp.where(upto, 1.0, 0.0).astype(bf16)
    return dot(first, upto) + dot(second, upto) + dot(third, upto)


def trail_row(row):
    return jnp.exp(row[:, -1:] - row)


def outer_sum(left, scale_row, right):
    scaled = jnp.transpose(left.astype(f32)) * scale_row
    high, low = halves(scaled)
    return dot(high, right) + dot(low, right)


def cols(j):
    return slice(j * HEAD_DIM, (j + 1) * HEAD_DIM)


class Part:
    def __init__(self, chunk, slot, half):
        self.chunk, self.slot, self.half = chunk, slot, half
        self.steps = 2 if half % 2 == 0 else 1
        self.per_step = half // self.steps

    def group(self, info):
        return info[0][0] if self.slot == "mine" else 1 - info[0][0]

    def row(self, cumul_ref, info, j):
        head = (2 * self.chunk + self.group(info)) * self.half + pl.program_id(0) * self.per_step + j
        return cumul_ref[pl.ds(head, 1), :]

    def state_rows(self, j):
        start = (pl.program_id(0) * self.per_step + j) * HEAD_DIM
        return pl.ds(pl.multiple_of(start, HEAD_DIM), HEAD_DIM)


def store_decays(part, info, cumul_ref, out_ref):
    for j in range(part.per_step):
        row = part.row(cumul_ref, info, j)
        place = part.half * HEAD_DIM + pl.program_id(0) * part.per_step + j
        out_ref[pl.ds(place, 1), :] = jnp.broadcast_to(jnp.exp(row[:, -1:]), (1, HEAD_DIM))


def pieces_kernel(part, info, key_ref, value_ref, cumul_ref, out_ref):
    for j in range(part.per_step):
        row = part.row(cumul_ref, info, j)
        out_ref[part.state_rows(j), :] = outer_sum(
            key_ref[:, cols(j)], trail_row(row), value_ref[:, cols(j)]
        )
    store_decays(part, info, cumul_ref, out_ref)


def first_pieces_kernel(part, info, key_ref, value_ref, decay_ref, out_ref, cumul_ref):
    @pl.when(pl.program_id(0) == 0)
    def _():
        cumul_ref[...] = cumulative(decay_ref[...])

    pieces_kernel(part, info, key_ref, value_ref, cumul_ref, out_ref)


def inner_kernel(part, info, query_ref, key_ref, value_ref, cumul_ref, out_ref):
    for j in range(part.per_step):
        row = part.row(cumul_ref, info, j)
        col = column(row)
        query, key, value = query_ref[:, cols(j)], key_ref[:, cols(j)], value_ref[:, cols(j)]
        for top in range(0, BLOCK, TILE):
            end = top + TILE
            scores = dot(query[top:end], key[:end], NT)
            spread = wide(col[top:end], end) - row[:, :end]
            causal = lax.broadcasted_iota(jnp.int32, (TILE, end), 0) + top >= (
                lax.broadcasted_iota(jnp.int32, (TILE, end), 1)
            )
            weights = (scores * jnp.exp(jnp.where(causal, spread, -1e30))).astype(bf16)
            out_ref[top:end, cols(j)] = dot(weights, value[:end])


def output_kernel(
    part, info, inner_ref, query_ref, cot_ref, gain_ref, cumul_ref, state_ref, before_ref,
    out_ref, sums_ref, square_ref, product_ref,
):
    step = pl.program_id(0)
    squares = jnp.zeros((BLOCK, HEAD_DIM), f32)
    products = jnp.zeros((BLOCK, HEAD_DIM), f32)
    for j in range(part.per_step):
        lead = jnp.exp(column(part.row(cumul_ref, info, j)))
        high, low = halves(state_ref[part.state_rows(j), :])
        query = query_ref[:, cols(j)]
        out = inner_ref[:, cols(j)] + lead * (dot(query, high) + dot(query, low))
        out_ref[:, cols(j)] = out
        squares += out * out
        products += cot_ref[:, cols(j)].astype(f32) * gain_ref[:, cols(j)] * out

    @pl.when(step == 0)
    def _():
        square_ref[...] = squares
        product_ref[...] = products

    @pl.when(step > 0)
    def _():
        square_ref[...] += squares
        product_ref[...] += products

    @pl.when(step == part.steps - 1)
    def _():
        rows = lax.broadcasted_iota(jnp.int32, (8, HEAD_DIM), 0)
        total = before_ref[...]
        for place, ref in ((0, square_ref), (1, product_ref)):
            pick = jnp.where(rows == place, 1.0, 0.0).astype(bf16)
            high, low = halves(ref[...])
            total += dot(pick, high, NT) + dot(pick, low, NT)
        sums_ref[...] = total


def grad_kernel(features, part, info, out_ref, cot_ref, gain_ref, query_ref, cumul_ref, *refs):
    shares, (attended_ref, grad_ref, piece_ref) = refs[:-3], refs[-3:]
    sums = shares[0][...]
    for share in shares[1:]:
        sums = sums + share[...]
    inverse = lax.rsqrt(sums[0:1] / features + epsilon)
    mean_term = inverse * sums[1:2] / features
    inverse_col, mean_col = column(inverse), column(mean_term)
    for j in range(part.per_step):
        gain = gain_ref[:, cols(j)]
        normed = out_ref[:, cols(j)] * inverse_col
        attended_ref[:, cols(j)] = (normed * gain).astype(bf16)
        scaled_grad = cot_ref[:, cols(j)].astype(f32) * gain
        grad = (inverse_col * (scaled_grad - normed * mean_col)).astype(bf16)
        grad_ref[:, cols(j)] = grad
        row = part.row(cumul_ref, info, j)
        piece_ref[part.state_rows(j), :] = outer_sum(query_ref[:, cols(j)], jnp.exp(row), grad)
    store_decays(part, info, cumul_ref, piece_ref)


def backward_kernel(
    part, info, query_ref, key_ref, value_ref, grad_ref, cumul_ref, state_ref,
    grad_query_ref, inner_key_ref, inner_value_ref,
):
    for j in range(part.per_step):
        row = part.row(cumul_ref, info, j)
        col = column(row)
        query, key = query_ref[:, cols(j)], key_ref[:, cols(j)]
        value, grad = value_ref[:, cols(j)], grad_ref[:, cols(j)]
        high, low = halves(state_ref[part.state_rows(j), :])
        outer = jnp.exp(col) * (dot(grad, high, NT) + dot(grad, low, NT))
        for top in range(0, BLOCK, TILE):
            end = top + TILE
            scores = dot(key[top:end], query[top:], NT)
            grad_scores = dot(value[top:end], grad[top:], NT)
            spread = row[:, top:] - wide(col[top:end], BLOCK - top)
            causal = lax.broadcasted_iota(jnp.int32, spread.shape, 0) <= (
                lax.broadcasted_iota(jnp.int32, spread.shape, 1)
            )
            decays = jnp.exp(jnp.where(causal, spread, -1e30))
            weights = (scores * decays).astype(bf16)
            grad_weights = (grad_scores * decays).astype(bf16)
            inner_value_ref[top:end, cols(j)] = dot(weights, grad[top:])
            inner_key_ref[top:end, cols(j)] = dot(grad_weights, query[top:])
            inner_query = dot(grad_weights, key[top:end], TN)
            outer = inner_query + outer if top == 0 else jnp.concatenate(
                [outer[:top], outer[top:] + inner_query], axis=0
            )
        grad_query_ref[:, cols(j)] = outer.astype(bf16)


def final_kernel(
    part, info, inner_key_ref, inner_value_ref, key_ref, value_ref, cumul_ref, state_ref,
    grad_key_ref, grad_value_ref,
):
    for j in range(part.per_step):
        trail = column(trail_row(part.row(cumul_ref, info, j)))
        high, low = halves(state_ref[part.state_rows(j), :])
        key, value = key_ref[:, cols(j)], value_ref[:, cols(j)]
        grad_key_ref[:, cols(j)] = (
            inner_key_ref[:, cols(j)] + trail * (dot(value, high, NT) + dot(value, low, NT))
        ).astype(bf16)
        grad_value_ref[:, cols(j)] = (
            inner_value_ref[:, cols(j)] + trail * (dot(key, high) + dot(key, low))
        ).astype(bf16)


def ordered(is_first, half, j, keep_ref, got_ref):
    rows = slice(j * HEAD_DIM, (j + 1) * HEAD_DIM)
    place = slice(half * HEAD_DIM + j, half * HEAD_DIM + j + 1)
    keep, got = keep_ref[rows, :], got_ref[rows, :]
    keep_decay, got_decay = keep_ref[place, :], got_ref[place, :]
    return (
        jnp.where(is_first, keep, got),
        jnp.where(is_first, got, keep),
        jnp.where(is_first, keep_decay, got_decay),
        jnp.where(is_first, got_decay, keep_decay),
    )


def scan_position(places, forward, info):
    member, pair = info[0][0], info[1][0]
    if forward:
        return member == 0, pair
    return member == 1, places - 1 - pair


def hop_kernel(half, senders, position, info, *refs):
    is_first, place = position(info)
    out_ref, arrived_ref = refs[-1], refs[-2]
    for index, p in enumerate(senders):
        keep_ref, got_ref = refs[2 * index], refs[2 * index + 1]

        @pl.when(place == p)
        def _():
            for j in range(half):
                first, second, first_decay, second_decay = ordered(
                    is_first, half, j, keep_ref, got_ref
                )
                value = second_decay * first + second
                if p > 0:
                    value += (first_decay * second_decay) * arrived_ref[cols(j), :]
                out_ref[cols(j), :] = value


def last_kernel(half, position, info, keep_ref, got_ref, *refs):
    arrived, (mine_ref, send_ref) = refs[:-2], refs[-2:]
    is_first, place = position(info)
    for p in range(len(arrived) + 1):

        @pl.when(place == p)
        def _():
            for j in range(half):
                first, _, first_decay, _ = ordered(is_first, half, j, keep_ref, got_ref)
                if p == 0:
                    before, after = jnp.zeros_like(first), first
                else:
                    before = arrived[p - 1][cols(j), :]
                    after = first_decay * before + first
                mine_ref[cols(j), :] = jnp.where(is_first, before, after)
                send_ref[cols(j), :] = jnp.where(is_first, after, before)


def on_device(queries, key_vecs, value_vecs, log_decay, norm_gain, cotangent):
    tokens, width = queries.shape
    assert tokens == BLOCK
    heads = width // HEAD_DIM
    half = heads // (2 * CHUNKS)
    head_count = lax.axis_size("head")
    features = width * head_count
    places = lax.axis_size("seq") // 2
    my_index = lax.axis_index("seq")
    member, pair = my_index % 2, my_index // 2
    gain = norm_gain.reshape(1, width)

    any_spec = pl.BlockSpec(memory_space=pl.ANY)
    wide_state = jax.ShapeDtypeStruct((half * HEAD_DIM + 8, HEAD_DIM), f32)
    state = jax.ShapeDtypeStruct((half * HEAD_DIM, HEAD_DIM), f32)
    whole = jax.ShapeDtypeStruct((tokens, width), bf16)
    local = jax.ShapeDtypeStruct((tokens, half * HEAD_DIM), f32)
    local_low = jax.ShapeDtypeStruct((tokens, half * HEAD_DIM), bf16)
    sums_shape = jax.ShapeDtypeStruct((8, tokens), f32)
    info = (member.astype(jnp.int32).reshape(1), pair.astype(jnp.int32).reshape(1))

    def run(kernel, grid, ins, outs, scratch=(), after=(), aliases=None, cost=1.0):
        used = len(ins)
        after = [x for i, x in enumerate(after) if not any(x is y for y in after[:i])]

        def body(member_ref, pair_ref, *refs):
            kernel((member_ref, pair_ref), *refs[:used], *refs[used + len(after):])

        return pl.pallas_call(
            body,
            out_shape=[shape for shape, _ in outs],
            grid_spec=pltpu.PrefetchScalarGridSpec(
                num_scalar_prefetch=2,
                grid=(grid,),
                in_specs=[spec for _, spec in ins] + [any_spec] * len(after),
                out_specs=[spec for _, spec in outs],
                scratch_shapes=list(scratch),
            ),
            input_output_aliases=aliases or {},
            compiler_params=pltpu.CompilerParams(vmem_limit_bytes=60 * 1024 * 1024),
            cost_estimate=pl.CostEstimate(
                flops=int(cost * 1e9), bytes_accessed=int(cost * 2.5e6), transcendentals=0
            ),
        )(*info, *[array for array, _ in ins], *after)

    def fixed(shape):
        return pl.BlockSpec(shape, lambda i, *info: (0,) * len(shape))

    def plain(array):
        return array, fixed(array.shape)

    def give(shape):
        return shape, fixed(shape.shape)

    class Views(Part):
        def full(self, array, rows=tokens):
            return array, self.full_spec(rows)

        def full_spec(self, rows=tokens):
            return pl.BlockSpec(
                (rows, self.per_step * HEAD_DIM),
                lambda i, *info: (0, (2 * self.chunk + self.group(info)) * self.steps + i),
            )

        def local(self, array):
            return array, pl.BlockSpec((tokens, self.per_step * HEAD_DIM), lambda i, *info: (0, i))

        def call(self, kernel, ins, outs, **options):
            return run(functools.partial(kernel, self), self.steps, ins, outs, **options)

    mine_parts = [Views(c, "mine", half) for c in range(CHUNKS)]
    their_parts = [Views(c, "theirs", half) for c in range(CHUNKS)]

    swap = [(2 * p + m, 2 * p + 1 - m) for p in range(places) for m in (0, 1)]

    def chain(make_piece, forward, early, filler, on_mine):
        position = functools.partial(scan_position, places, forward)

        def device(place, m):
            return 2 * (place if forward else places - 1 - place) + m

        received, last = [], ()
        for c in range(CHUNKS):
            sent = make_piece(their_parts[c], last)
            received.append(lax.ppermute(sent, "seq", swap))
            last = (sent,)
        keeps = []
        for c in range(CHUNKS):
            keeps.append(make_piece(mine_parts[c], last))
            last = (keeps[-1],)
        for work in early:
            last = (work(last),)
        arrived, mine, theirs = {}, [], []
        for r in range(2, CHUNKS + places + 1):
            if r < CHUNKS + places:
                senders = [p for p in range(places - 1) if 0 <= r - 2 - p < CHUNKS]
                ins = []
                for p in senders:
                    ins += [plain(keeps[r - 2 - p]), plain(received[r - 2 - p])]
                ins.append(plain(arrived[r - 1]) if r > 2 else plain(keeps[0]))
                value, = run(
                    functools.partial(hop_kernel, half, senders, position), 1, ins, [give(state)],
                    after=last, cost=0.3,
                )
                pairs = [(device(p, m), device(p + 1, m)) for p in senders for m in (0, 1)]
                arrived[r] = lax.ppermute(value, "seq", pairs)
                last = (value,)
            c = r - 1 - places
            if 0 <= c:
                ins = [plain(keeps[c]), plain(received[c])]
                ins += [plain(arrived[c + 1 + p]) for p in range(1, places)]
                own, send = run(
                    functools.partial(last_kernel, half, position), 1, ins, [give(state)] * 2,
                    after=last, cost=0.3,
                )
                theirs.append(lax.ppermute(send, "seq", swap))
                mine.append(own)
                last = (send,)
                filler.append(functools.partial(on_mine, c, own))
            if filler:
                last = (filler.pop(0)(last),)
        while filler:
            last = (filler.pop(0)(last),)
        return mine, theirs, last

    held_cumul = []

    def forward_piece(part, after):
        if not held_cumul:
            piece, cumul = part.call(
                first_pieces_kernel,
                [part.full(key_vecs), part.full(value_vecs), plain(log_decay.T)],
                [give(wide_state), give(jax.ShapeDtypeStruct((heads, tokens), f32))], cost=1.0,
            )
            held_cumul.append(cumul)
            return piece
        cumul = held_cumul[0]
        return part.call(
            pieces_kernel, [part.full(key_vecs), part.full(value_vecs), plain(cumul)],
            [give(wide_state)], after=after, cost=1.0,
        )[0]

    inner, outs = {}, {}

    def cumul_in():
        return plain(held_cumul[0])

    state_sums = [jnp.zeros(sums_shape.shape, f32)]

    def inner_work(part, after):
        inner[part], = part.call(
            inner_kernel,
            [part.full(queries), part.full(key_vecs), part.full(value_vecs), cumul_in()],
            [part.local(local)], after=after, cost=2.2,
        )
        return inner[part]

    def output_work(part, before, after):
        outs[part], sums = part.call(
            output_kernel,
            [part.local(inner[part]), part.full(queries), part.full(cotangent), part.full(gain, 1),
             cumul_in(), plain(before), plain(state_sums[0])],
            [part.local(local), give(sums_shape)],
            scratch=[pltpu.VMEM((tokens, HEAD_DIM), f32)] * 2, after=after, cost=1.4,
        )
        state_sums[0] = sums
        return sums

    inner_order = [part for c in range(CHUNKS) for part in (mine_parts[c], their_parts[c])]
    works = [functools.partial(inner_work, part) for part in inner_order]
    mine, theirs, last = chain(
        forward_piece, True, works[:1], works[1:],
        lambda c, own, after: output_work(mine_parts[c], own, after),
    )
    for c in range(CHUNKS):
        last = (output_work(their_parts[c], theirs[c], last),)

    sums = state_sums[0]
    shares = [sums] + [
        lax.ppermute(sums, "head", [(i, (i + k) % head_count) for i in range(head_count)])
        for k in range(1, head_count)
    ]

    attended, grad_queries, grad_keys, grad_values = [], [], [], []
    grads, inner_grads = {}, {}

    def target(held):
        return tuple(held[-1:])

    def backward_piece(part, after):
        before = target(attended)
        whole_out, grads[part], piece = part.call(
            functools.partial(grad_kernel, features),
            [part.local(outs[part]), part.full(cotangent), part.full(gain, 1), part.full(queries),
             cumul_in()] + [plain(share) for share in shares],
            [(whole, part.full_spec()), part.local(local_low), give(wide_state)],
            after=before + tuple(after), aliases={7 + head_count: 0} if before else None, cost=2.0,
        )
        attended.append(whole_out)
        return piece

    def backward_work(part, before, after):
        held = target(grad_queries)
        whole_out, *inner_grads[part] = part.call(
            backward_kernel,
            [part.full(queries), part.full(key_vecs), part.full(value_vecs),
             part.local(grads[part]), cumul_in(), plain(before)],
            [(whole, part.full_spec()), part.local(local), part.local(local)],
            after=held + tuple(after), aliases={8: 0} if held else None, cost=4.3,
        )
        grad_queries.append(whole_out)
        return inner_grads[part][0]

    def final_work(part, before, after):
        held = target(grad_keys) + target(grad_values)
        whole_key, whole_value = part.call(
            final_kernel,
            [part.local(inner_grads[part][0]), part.local(inner_grads[part][1]),
             part.full(key_vecs), part.full(value_vecs), cumul_in(), plain(before)],
            [(whole, part.full_spec())] * 2,
            after=held + tuple(after), aliases={8: 0, 9: 1} if held else None, cost=2.0,
        )
        grad_keys.append(whole_key)
        grad_values.append(whole_value)
        return whole_key

    works = []
    for c in range(CHUNKS):
        works.append(functools.partial(backward_work, mine_parts[c], mine[c]))
        works.append(functools.partial(backward_work, their_parts[c], theirs[c]))
    mine_after, theirs_after, last = chain(
        backward_piece, False, [], works,
        lambda c, own, after: final_work(mine_parts[c], own, after),
    )
    for c in range(CHUNKS):
        final_work(their_parts[c], theirs_after[c], last)
        last = ()
    return attended[-1], grad_queries[-1], grad_keys[-1], grad_values[-1]


def solution(mesh):
    return jax.shard_map(
        on_device,
        mesh=mesh,
        in_specs=(
            P("seq", "head"),
            P("seq", "head"),
            P("seq", "head"),
            P("seq", "head"),
            P("head"),
            P("seq", "head"),
        ),
        out_specs=(P("seq", "head"), P("seq", "head"), P("seq", "head"), P("seq", "head")),
        check_vma=False,
    )
```

```python
import functools

import jax
import jax.numpy as jnp
from jax import lax
from jax.experimental import pallas as pl
from jax.experimental.pallas import tpu as pltpu
from jax.sharding import PartitionSpec as P

HEAD_DIM = 128
BLOCK = 512
CHUNKS = 2
TILE = 256
epsilon = 1e-06
f32 = jnp.float32
bf16 = jnp.bfloat16

NN = (((1,), (0,)), ((), ()))
NT = (((1,), (1,)), ((), ()))
TN = (((0,), (0,)), ((), ()))


def dot(a, b, dims=NN):
    return lax.dot_general(a, b, dims, preferred_element_type=f32)


def halves(x):
    high = x.astype(bf16)
    return high, (x - high.astype(f32)).astype(bf16)


def column(row):
    return jnp.transpose(jnp.broadcast_to(row, (HEAD_DIM, row.shape[1])))


def wide(col, width):
    return jnp.concatenate([col] * (width // HEAD_DIM), axis=1)


def cumulative(decay):
    length = decay.shape[1]
    first = decay.astype(bf16)
    rest = decay - first.astype(f32)
    second = rest.astype(bf16)
    third = (rest - second.astype(f32)).astype(bf16)
    upto = lax.broadcasted_iota(jnp.int32, (length, length), 0) <= lax.broadcasted_iota(
        jnp.int32, (length, length), 1
    )
    upto = jnp.where(upto, 1.0, 0.0).astype(bf16)
    return dot(first, upto) + dot(second, upto) + dot(third, upto)


def trail_row(row):
    return jnp.exp(row[:, -1:] - row)


def outer_sum(left, scale_row, right):
    scaled = jnp.transpose(left.astype(f32)) * scale_row
    high, low = halves(scaled)
    return dot(high, right) + dot(low, right)


def cols(j):
    return slice(j * HEAD_DIM, (j + 1) * HEAD_DIM)


class Part:
    def __init__(self, chunk, slot, half):
        self.chunk, self.slot, self.half = chunk, slot, half
        self.steps = 2 if half % 2 == 0 else 1
        self.per_step = half // self.steps

    def group(self, info):
        return info[0][0] if self.slot == "mine" else 1 - info[0][0]

    def row(self, cumul_ref, info, j):
        head = (2 * self.chunk + self.group(info)) * self.half + pl.program_id(0) * self.per_step + j
        return cumul_ref[pl.ds(head, 1), :]

    def state_rows(self, j):
        start = (pl.program_id(0) * self.per_step + j) * HEAD_DIM
        return pl.ds(pl.multiple_of(start, HEAD_DIM), HEAD_DIM)


def store_decays(part, info, cumul_ref, out_ref):
    for j in range(part.per_step):
        row = part.row(cumul_ref, info, j)
        place = part.half * HEAD_DIM + pl.program_id(0) * part.per_step + j
        out_ref[pl.ds(place, 1), :] = jnp.broadcast_to(jnp.exp(row[:, -1:]), (1, HEAD_DIM))


def pieces_kernel(part, info, key_ref, value_ref, cumul_ref, out_ref):
    for j in range(part.per_step):
        row = part.row(cumul_ref, info, j)
        out_ref[part.state_rows(j), :] = outer_sum(
            key_ref[:, cols(j)], trail_row(row), value_ref[:, cols(j)]
        )
    store_decays(part, info, cumul_ref, out_ref)


def first_pieces_kernel(part, info, key_ref, value_ref, decay_ref, out_ref, cumul_ref):
    @pl.when(pl.program_id(0) == 0)
    def _():
        cumul_ref[...] = cumulative(decay_ref[...])

    pieces_kernel(part, info, key_ref, value_ref, cumul_ref, out_ref)


def inner_kernel(part, info, query_ref, key_ref, value_ref, cumul_ref, out_ref):
    for j in range(part.per_step):
        row = part.row(cumul_ref, info, j)
        col = column(row)
        query, key, value = query_ref[:, cols(j)], key_ref[:, cols(j)], value_ref[:, cols(j)]
        for top in range(0, BLOCK, TILE):
            end = top + TILE
            scores = dot(query[top:end], key[:end], NT)
            spread = wide(col[top:end], end) - row[:, :end]
            causal = lax.broadcasted_iota(jnp.int32, (TILE, end), 0) + top >= (
                lax.broadcasted_iota(jnp.int32, (TILE, end), 1)
            )
            weights = (scores * jnp.exp(jnp.where(causal, spread, -1e30))).astype(bf16)
            out_ref[top:end, cols(j)] = dot(weights, value[:end])


def output_kernel(
    part, info, inner_ref, query_ref, cot_ref, gain_ref, cumul_ref, state_ref, before_ref,
    out_ref, sums_ref, square_ref, product_ref,
):
    step = pl.program_id(0)
    squares = jnp.zeros((BLOCK, HEAD_DIM), f32)
    products = jnp.zeros((BLOCK, HEAD_DIM), f32)
    for j in range(part.per_step):
        lead = jnp.exp(column(part.row(cumul_ref, info, j)))
        high, low = halves(state_ref[part.state_rows(j), :])
        query = query_ref[:, cols(j)]
        out = inner_ref[:, cols(j)] + lead * (dot(query, high) + dot(query, low))
        out_ref[:, cols(j)] = out
        squares += out * out
        products += cot_ref[:, cols(j)].astype(f32) * gain_ref[:, cols(j)] * out

    @pl.when(step == 0)
    def _():
        square_ref[...] = squares
        product_ref[...] = products

    @pl.when(step > 0)
    def _():
        square_ref[...] += squares
        product_ref[...] += products

    @pl.when(step == part.steps - 1)
    def _():
        rows = lax.broadcasted_iota(jnp.int32, (8, HEAD_DIM), 0)
        total = before_ref[...]
        for place, ref in ((0, square_ref), (1, product_ref)):
            pick = jnp.where(rows == place, 1.0, 0.0).astype(bf16)
            high, low = halves(ref[...])
            total += dot(pick, high, NT) + dot(pick, low, NT)
        sums_ref[...] = total


def grad_kernel(features, part, info, out_ref, cot_ref, gain_ref, query_ref, cumul_ref, *refs):
    shares, (attended_ref, grad_ref, piece_ref) = refs[:-3], refs[-3:]
    sums = shares[0][...]
    for share in shares[1:]:
        sums = sums + share[...]
    inverse = lax.rsqrt(sums[0:1] / features + epsilon)
    mean_term = inverse * sums[1:2] / features
    inverse_col, mean_col = column(inverse), column(mean_term)
    for j in range(part.per_step):
        gain = gain_ref[:, cols(j)]
        normed = out_ref[:, cols(j)] * inverse_col
        attended_ref[:, cols(j)] = (normed * gain).astype(bf16)
        scaled_grad = cot_ref[:, cols(j)].astype(f32) * gain
        grad = (inverse_col * (scaled_grad - normed * mean_col)).astype(bf16)
        grad_ref[:, cols(j)] = grad
        row = part.row(cumul_ref, info, j)
        piece_ref[part.state_rows(j), :] = outer_sum(query_ref[:, cols(j)], jnp.exp(row), grad)
    store_decays(part, info, cumul_ref, piece_ref)


def backward_kernel(
    part, info, query_ref, key_ref, value_ref, grad_ref, cumul_ref, state_ref,
    grad_query_ref, inner_key_ref, inner_value_ref,
):
    for j in range(part.per_step):
        row = part.row(cumul_ref, info, j)
        col = column(row)
        query, key = query_ref[:, cols(j)], key_ref[:, cols(j)]
        value, grad = value_ref[:, cols(j)], grad_ref[:, cols(j)]
        high, low = halves(state_ref[part.state_rows(j), :])
        outer = jnp.exp(col) * (dot(grad, high, NT) + dot(grad, low, NT))
        for top in range(0, BLOCK, TILE):
            end = top + TILE
            scores = dot(key[top:end], query[top:], NT)
            grad_scores = dot(value[top:end], grad[top:], NT)
            spread = row[:, top:] - wide(col[top:end], BLOCK - top)
            causal = lax.broadcasted_iota(jnp.int32, spread.shape, 0) <= (
                lax.broadcasted_iota(jnp.int32, spread.shape, 1)
            )
            decays = jnp.exp(jnp.where(causal, spread, -1e30))
            weights = (scores * decays).astype(bf16)
            grad_weights = (grad_scores * decays).astype(bf16)
            inner_value_ref[top:end, cols(j)] = dot(weights, grad[top:])
            inner_key_ref[top:end, cols(j)] = dot(grad_weights, query[top:])
            inner_query = dot(grad_weights, key[top:end], TN)
            outer = inner_query + outer if top == 0 else jnp.concatenate(
                [outer[:top], outer[top:] + inner_query], axis=0
            )
        grad_query_ref[:, cols(j)] = outer.astype(bf16)


def final_kernel(
    part, info, inner_key_ref, inner_value_ref, key_ref, value_ref, cumul_ref, state_ref,
    grad_key_ref, grad_value_ref,
):
    for j in range(part.per_step):
        trail = column(trail_row(part.row(cumul_ref, info, j)))
        high, low = halves(state_ref[part.state_rows(j), :])
        key, value = key_ref[:, cols(j)], value_ref[:, cols(j)]
        grad_key_ref[:, cols(j)] = (
            inner_key_ref[:, cols(j)] + trail * (dot(value, high, NT) + dot(value, low, NT))
        ).astype(bf16)
        grad_value_ref[:, cols(j)] = (
            inner_value_ref[:, cols(j)] + trail * (dot(key, high) + dot(key, low))
        ).astype(bf16)


def ordered(is_first, half, j, keep_ref, got_ref):
    rows = slice(j * HEAD_DIM, (j + 1) * HEAD_DIM)
    place = slice(half * HEAD_DIM + j, half * HEAD_DIM + j + 1)
    keep, got = keep_ref[rows, :], got_ref[rows, :]
    keep_decay, got_decay = keep_ref[place, :], got_ref[place, :]
    return (
        jnp.where(is_first, keep, got),
        jnp.where(is_first, got, keep),
        jnp.where(is_first, keep_decay, got_decay),
        jnp.where(is_first, got_decay, keep_decay),
    )


def scan_position(places, forward, info):
    member, pair = info[0][0], info[1][0]
    if forward:
        return member == 0, pair
    return member == 1, places - 1 - pair


def hop_kernel(half, senders, position, info, *refs):
    is_first, place = position(info)
    out_ref, arrived_ref = refs[-1], refs[-2]
    for index, p in enumerate(senders):
        keep_ref, got_ref = refs[2 * index], refs[2 * index + 1]

        @pl.when(place == p)
        def _():
            for j in range(half):
                first, second, first_decay, second_decay = ordered(
                    is_first, half, j, keep_ref, got_ref
                )
                value = second_decay * first + second
                if p > 0:
                    value += (first_decay * second_decay) * arrived_ref[cols(j), :]
                out_ref[cols(j), :] = value


def last_kernel(half, position, info, keep_ref, got_ref, *refs):
    arrived, (mine_ref, send_ref) = refs[:-2], refs[-2:]
    is_first, place = position(info)
    for p in range(len(arrived) + 1):

        @pl.when(place == p)
        def _():
            for j in range(half):
                first, _, first_decay, _ = ordered(is_first, half, j, keep_ref, got_ref)
                if p == 0:
                    before, after = jnp.zeros_like(first), first
                else:
                    before = arrived[p - 1][cols(j), :]
                    after = first_decay * before + first
                mine_ref[cols(j), :] = jnp.where(is_first, before, after)
                send_ref[cols(j), :] = jnp.where(is_first, after, before)


def on_device(queries, key_vecs, value_vecs, log_decay, norm_gain, cotangent):
    tokens, width = queries.shape
    assert tokens == BLOCK
    heads = width // HEAD_DIM
    half = heads // (2 * CHUNKS)
    head_count = lax.axis_size("head")
    features = width * head_count
    places = lax.axis_size("seq") // 2
    my_index = lax.axis_index("seq")
    member, pair = my_index % 2, my_index // 2
    gain = norm_gain.reshape(1, width)

    any_spec = pl.BlockSpec(memory_space=pl.ANY)
    wide_state = jax.ShapeDtypeStruct((half * HEAD_DIM + 8, HEAD_DIM), f32)
    state = jax.ShapeDtypeStruct((half * HEAD_DIM, HEAD_DIM), f32)
    whole = jax.ShapeDtypeStruct((tokens, width), bf16)
    local = jax.ShapeDtypeStruct((tokens, half * HEAD_DIM), f32)
    local_low = jax.ShapeDtypeStruct((tokens, half * HEAD_DIM), bf16)
    sums_shape = jax.ShapeDtypeStruct((8, tokens), f32)
    info = (member.astype(jnp.int32).reshape(1), pair.astype(jnp.int32).reshape(1))

    def run(kernel, grid, ins, outs, scratch=(), after=(), aliases=None, cost=1.0):
        used = len(ins)
        after = [x for i, x in enumerate(after) if not any(x is y for y in after[:i])]

        def body(member_ref, pair_ref, *refs):
            kernel((member_ref, pair_ref), *refs[:used], *refs[used + len(after):])

        return pl.pallas_call(
            body,
            out_shape=[shape for shape, _ in outs],
            grid_spec=pltpu.PrefetchScalarGridSpec(
                num_scalar_prefetch=2,
                grid=(grid,),
                in_specs=[spec for _, spec in ins] + [any_spec] * len(after),
                out_specs=[spec for _, spec in outs],
                scratch_shapes=list(scratch),
            ),
            input_output_aliases=aliases or {},
            compiler_params=pltpu.CompilerParams(vmem_limit_bytes=16 * 1024 * 1024),
            cost_estimate=pl.CostEstimate(
                flops=int(cost * 1e9), bytes_accessed=int(cost * 2.5e6), transcendentals=0
            ),
        )(*info, *[array for array, _ in ins], *after)

    def fixed(shape):
        return pl.BlockSpec(shape, lambda i, *info: (0,) * len(shape))

    def plain(array):
        return array, fixed(array.shape)

    def give(shape):
        return shape, fixed(shape.shape)

    class Views(Part):
        def full(self, array, rows=tokens):
            return array, self.full_spec(rows)

        def full_spec(self, rows=tokens):
            return pl.BlockSpec(
                (rows, self.per_step * HEAD_DIM),
                lambda i, *info: (0, (2 * self.chunk + self.group(info)) * self.steps + i),
            )

        def local(self, array):
            return array, pl.BlockSpec((tokens, self.per_step * HEAD_DIM), lambda i, *info: (0, i))

        def call(self, kernel, ins, outs, **options):
            return run(functools.partial(kernel, self), self.steps, ins, outs, **options)

    mine_parts = [Views(c, "mine", half) for c in range(CHUNKS)]
    their_parts = [Views(c, "theirs", half) for c in range(CHUNKS)]

    swap = [(2 * p + m, 2 * p + 1 - m) for p in range(places) for m in (0, 1)]

    def chain(make_piece, forward, early, filler, on_mine):
        position = functools.partial(scan_position, places, forward)

        def device(place, m):
            return 2 * (place if forward else places - 1 - place) + m

        received, last = [], ()
        for c in range(CHUNKS):
            sent = make_piece(their_parts[c], last)
            received.append(lax.ppermute(sent, "seq", swap))
            last = (sent,)
        keeps = []
        for c in range(CHUNKS):
            keeps.append(make_piece(mine_parts[c], last))
            last = (keeps[-1],)
        for work in early:
            last = (work(last),)
        arrived, mine, theirs = {}, [], []
        for r in range(2, CHUNKS + places + 1):
            if r < CHUNKS + places:
                senders = [p for p in range(places - 1) if 0 <= r - 2 - p < CHUNKS]
                ins = []
                for p in senders:
                    ins += [plain(keeps[r - 2 - p]), plain(received[r - 2 - p])]
                ins.append(plain(arrived[r - 1]) if r > 2 else plain(keeps[0]))
                value, = run(
                    functools.partial(hop_kernel, half, senders, position), 1, ins, [give(state)],
                    after=last, cost=0.3,
                )
                pairs = [(device(p, m), device(p + 1, m)) for p in senders for m in (0, 1)]
                arrived[r] = lax.ppermute(value, "seq", pairs)
                last = (value,)
            c = r - 1 - places
            if 0 <= c:
                ins = [plain(keeps[c]), plain(received[c])]
                ins += [plain(arrived[c + 1 + p]) for p in range(1, places)]
                own, send = run(
                    functools.partial(last_kernel, half, position), 1, ins, [give(state)] * 2,
                    after=last, cost=0.3,
                )
                theirs.append(lax.ppermute(send, "seq", swap))
                mine.append(own)
                last = (send,)
                filler.append(functools.partial(on_mine, c, own))
            if filler:
                last = (filler.pop(0)(last),)
        while filler:
            last = (filler.pop(0)(last),)
        return mine, theirs, last

    held_cumul = []

    def forward_piece(part, after):
        if not held_cumul:
            piece, cumul = part.call(
                first_pieces_kernel,
                [part.full(key_vecs), part.full(value_vecs), plain(log_decay.T)],
                [give(wide_state), give(jax.ShapeDtypeStruct((heads, tokens), f32))], cost=1.0,
            )
            held_cumul.append(cumul)
            return piece
        cumul = held_cumul[0]
        return part.call(
            pieces_kernel, [part.full(key_vecs), part.full(value_vecs), plain(cumul)],
            [give(wide_state)], after=after, cost=1.0,
        )[0]

    inner, outs = {}, {}

    def cumul_in():
        return plain(held_cumul[0])

    state_sums = [jnp.zeros(sums_shape.shape, f32)]

    def inner_work(part, after):
        inner[part], = part.call(
            inner_kernel,
            [part.full(queries), part.full(key_vecs), part.full(value_vecs), cumul_in()],
            [part.local(local)], after=after, cost=2.2,
        )
        return inner[part]

    def output_work(part, before, after):
        outs[part], sums = part.call(
            output_kernel,
            [part.local(inner[part]), part.full(queries), part.full(cotangent), part.full(gain, 1),
             cumul_in(), plain(before), plain(state_sums[0])],
            [part.local(local), give(sums_shape)],
            scratch=[pltpu.VMEM((tokens, HEAD_DIM), f32)] * 2, after=after, cost=1.4,
        )
        state_sums[0] = sums
        return sums

    inner_order = [part for c in range(CHUNKS) for part in (mine_parts[c], their_parts[c])]
    works = [functools.partial(inner_work, part) for part in inner_order]
    mine, theirs, last = chain(
        forward_piece, True, works[:1], works[1:],
        lambda c, own, after: output_work(mine_parts[c], own, after),
    )
    for c in range(CHUNKS):
        last = (output_work(their_parts[c], theirs[c], last),)

    sums = state_sums[0]
    shares = [sums] + [
        lax.ppermute(sums, "head", [(i, (i + k) % head_count) for i in range(head_count)])
        for k in range(1, head_count)
    ]

    attended, grad_queries, grad_keys, grad_values = [], [], [], []
    grads, inner_grads = {}, {}

    def target(held):
        return tuple(held[-1:])

    def backward_piece(part, after):
        before = target(attended)
        whole_out, grads[part], piece = part.call(
            functools.partial(grad_kernel, features),
            [part.local(outs[part]), part.full(cotangent), part.full(gain, 1), part.full(queries),
             cumul_in()] + [plain(share) for share in shares],
            [(whole, part.full_spec()), part.local(local_low), give(wide_state)],
            after=before + tuple(after), aliases={7 + head_count: 0} if before else None, cost=2.0,
        )
        attended.append(whole_out)
        return piece

    def backward_work(part, before, after):
        held = target(grad_queries)
        whole_out, *inner_grads[part] = part.call(
            backward_kernel,
            [part.full(queries), part.full(key_vecs), part.full(value_vecs),
             part.local(grads[part]), cumul_in(), plain(before)],
            [(whole, part.full_spec()), part.local(local), part.local(local)],
            after=held + tuple(after), aliases={8: 0} if held else None, cost=4.3,
        )
        grad_queries.append(whole_out)
        return inner_grads[part][0]

    def final_work(part, before, after):
        held = target(grad_keys) + target(grad_values)
        whole_key, whole_value = part.call(
            final_kernel,
            [part.local(inner_grads[part][0]), part.local(inner_grads[part][1]),
             part.full(key_vecs), part.full(value_vecs), cumul_in(), plain(before)],
            [(whole, part.full_spec())] * 2,
            after=held + tuple(after), aliases={8: 0, 9: 1} if held else None, cost=2.0,
        )
        grad_keys.append(whole_key)
        grad_values.append(whole_value)
        return whole_key

    works = []
    for c in range(CHUNKS):
        works.append(functools.partial(backward_work, mine_parts[c], mine[c]))
        works.append(functools.partial(backward_work, their_parts[c], theirs[c]))
    mine_after, theirs_after, last = chain(
        backward_piece, False, [], works,
        lambda c, own, after: final_work(mine_parts[c], own, after),
    )
    for c in range(CHUNKS):
        final_work(their_parts[c], theirs_after[c], last)
        last = ()
    return attended[-1], grad_queries[-1], grad_keys[-1], grad_values[-1]


def solution(mesh):
    return jax.shard_map(
        on_device,
        mesh=mesh,
        in_specs=(
            P("seq", "head"),
            P("seq", "head"),
            P("seq", "head"),
            P("seq", "head"),
            P("head"),
            P("seq", "head"),
        ),
        out_specs=(P("seq", "head"), P("seq", "head"), P("seq", "head"), P("seq", "head")),
        check_vma=False,
    )
```

```python
import functools

import jax
import jax.numpy as jnp
from jax import lax
from jax.experimental import pallas as pl
from jax.experimental.pallas import tpu as pltpu
from jax.sharding import PartitionSpec as P

HEAD_DIM = 128
BLOCK = 512
CHUNKS = 2
TILE = 256
epsilon = 1e-06
f32 = jnp.float32
bf16 = jnp.bfloat16

NN = (((1,), (0,)), ((), ()))
NT = (((1,), (1,)), ((), ()))
TN = (((0,), (0,)), ((), ()))


def dot(a, b, dims=NN):
    return lax.dot_general(a, b, dims, preferred_element_type=f32)


def halves(x):
    high = x.astype(bf16)
    return high, (x - high.astype(f32)).astype(bf16)


def column(row):
    return jnp.transpose(jnp.broadcast_to(row, (HEAD_DIM, row.shape[1])))


def wide(col, width):
    return jnp.concatenate([col] * (width // HEAD_DIM), axis=1)


def cumulative(decay):
    length = decay.shape[1]
    first = decay.astype(bf16)
    rest = decay - first.astype(f32)
    second = rest.astype(bf16)
    third = (rest - second.astype(f32)).astype(bf16)
    upto = lax.broadcasted_iota(jnp.int32, (length, length), 0) <= lax.broadcasted_iota(
        jnp.int32, (length, length), 1
    )
    upto = jnp.where(upto, 1.0, 0.0).astype(bf16)
    return dot(first, upto) + dot(second, upto) + dot(third, upto)


def trail_row(row):
    return jnp.exp(row[:, -1:] - row)


def outer_sum(left, scale_row, right):
    scaled = jnp.transpose(left.astype(f32)) * scale_row
    high, low = halves(scaled)
    return dot(high, right) + dot(low, right)


def cols(j):
    return slice(j * HEAD_DIM, (j + 1) * HEAD_DIM)


class Part:
    def __init__(self, chunk, slot, half):
        self.chunk, self.slot, self.half = chunk, slot, half
        self.steps = 2 if half % 2 == 0 else 1
        self.per_step = half // self.steps

    def group(self, info):
        return info[0][0] if self.slot == "mine" else 1 - info[0][0]

    def head(self, info, j):
        return (2 * self.chunk + self.group(info)) * self.half + pl.program_id(0) * self.per_step + j

    def row(self, cumul_ref, info, j):
        return cumul_ref[pl.ds(self.head(info, j), 1), :]

    def wide_cols(self, info, j):
        return pl.ds(pl.multiple_of(self.head(info, j) * HEAD_DIM, HEAD_DIM), HEAD_DIM)

    def state_rows(self, j):
        start = (pl.program_id(0) * self.per_step + j) * HEAD_DIM
        return pl.ds(pl.multiple_of(start, HEAD_DIM), HEAD_DIM)


def store_decays(part, info, cumul_ref, out_ref):
    for j in range(part.per_step):
        row = part.row(cumul_ref, info, j)
        place = part.half * HEAD_DIM + pl.program_id(0) * part.per_step + j
        out_ref[pl.ds(place, 1), :] = jnp.broadcast_to(jnp.exp(row[:, -1:]), (1, HEAD_DIM))


def pieces_kernel(part, info, key_ref, value_ref, cumul_ref, out_ref):
    for j in range(part.per_step):
        row = part.row(cumul_ref, info, j)
        at = part.wide_cols(info, j)
        out_ref[part.state_rows(j), :] = outer_sum(key_ref[:, at], trail_row(row), value_ref[:, at])
    store_decays(part, info, cumul_ref, out_ref)


def first_pieces_kernel(part, info, key_ref, value_ref, decay_ref, out_ref, cumul_ref):
    @pl.when(pl.program_id(0) == 0)
    def _():
        cumul_ref[...] = cumulative(decay_ref[...])

    pieces_kernel(part, info, key_ref, value_ref, cumul_ref, out_ref)


def inner_kernel(part, info, query_ref, key_ref, value_ref, cumul_ref, out_ref):
    for j in range(part.per_step):
        row = part.row(cumul_ref, info, j)
        col = column(row)
        at = part.wide_cols(info, j)
        query, key, value = query_ref[:, at], key_ref[:, at], value_ref[:, at]
        for top in range(0, BLOCK, TILE):
            end = top + TILE
            scores = dot(query[top:end], key[:end], NT)
            spread = wide(col[top:end], end) - row[:, :end]
            causal = lax.broadcasted_iota(jnp.int32, (TILE, end), 0) + top >= (
                lax.broadcasted_iota(jnp.int32, (TILE, end), 1)
            )
            weights = (scores * jnp.exp(jnp.where(causal, spread, -1e30))).astype(bf16)
            out_ref[top:end, part.state_rows(j)] = dot(weights, value[:end])


def output_kernel(
    part, info, inner_ref, query_ref, cot_ref, gain_ref, cumul_ref, state_ref, before_ref,
    out_ref, sums_ref, square_ref, product_ref,
):
    step = pl.program_id(0)
    squares = jnp.zeros((BLOCK, HEAD_DIM), f32)
    products = jnp.zeros((BLOCK, HEAD_DIM), f32)
    for j in range(part.per_step):
        lead = jnp.exp(column(part.row(cumul_ref, info, j)))
        high, low = halves(state_ref[part.state_rows(j), :])
        at, here = part.wide_cols(info, j), part.state_rows(j)
        query = query_ref[:, at]
        out = inner_ref[:, here] + lead * (dot(query, high) + dot(query, low))
        out_ref[:, here] = out
        squares += out * out
        products += cot_ref[:, at].astype(f32) * gain_ref[:, at] * out

    @pl.when(step == 0)
    def _():
        square_ref[...] = squares
        product_ref[...] = products

    @pl.when(step > 0)
    def _():
        square_ref[...] += squares
        product_ref[...] += products

    @pl.when(step == part.steps - 1)
    def _():
        rows = lax.broadcasted_iota(jnp.int32, (8, HEAD_DIM), 0)
        total = before_ref[...]
        for place, ref in ((0, square_ref), (1, product_ref)):
            pick = jnp.where(rows == place, 1.0, 0.0).astype(bf16)
            high, low = halves(ref[...])
            total += dot(pick, high, NT) + dot(pick, low, NT)
        sums_ref[...] = total


def grad_kernel(features, part, info, out_ref, cot_ref, gain_ref, query_ref, cumul_ref, *refs):
    shares, (attended_ref, grad_ref, piece_ref) = refs[:-3], refs[-3:]
    sums = shares[0][...]
    for share in shares[1:]:
        sums = sums + share[...]
    inverse = lax.rsqrt(sums[0:1] / features + epsilon)
    mean_term = inverse * sums[1:2] / features
    inverse_col, mean_col = column(inverse), column(mean_term)
    for j in range(part.per_step):
        at, here = part.wide_cols(info, j), part.state_rows(j)
        gain = gain_ref[:, at]
        normed = out_ref[:, here] * inverse_col
        attended_ref[:, cols(j)] = (normed * gain).astype(bf16)
        scaled_grad = cot_ref[:, at].astype(f32) * gain
        grad = (inverse_col * (scaled_grad - normed * mean_col)).astype(bf16)
        grad_ref[:, here] = grad
        row = part.row(cumul_ref, info, j)
        piece_ref[part.state_rows(j), :] = outer_sum(query_ref[:, at], jnp.exp(row), grad)
    store_decays(part, info, cumul_ref, piece_ref)


def backward_kernel(
    part, info, query_ref, key_ref, value_ref, grad_ref, cumul_ref, state_ref,
    grad_query_ref, inner_key_ref, inner_value_ref,
):
    for j in range(part.per_step):
        row = part.row(cumul_ref, info, j)
        col = column(row)
        at, here = part.wide_cols(info, j), part.state_rows(j)
        query, key = query_ref[:, at], key_ref[:, at]
        value, grad = value_ref[:, at], grad_ref[:, here]
        high, low = halves(state_ref[part.state_rows(j), :])
        outer = jnp.exp(col) * (dot(grad, high, NT) + dot(grad, low, NT))
        for top in range(0, BLOCK, TILE):
            end = top + TILE
            scores = dot(key[top:end], query[top:], NT)
            grad_scores = dot(value[top:end], grad[top:], NT)
            spread = row[:, top:] - wide(col[top:end], BLOCK - top)
            causal = lax.broadcasted_iota(jnp.int32, spread.shape, 0) <= (
                lax.broadcasted_iota(jnp.int32, spread.shape, 1)
            )
            decays = jnp.exp(jnp.where(causal, spread, -1e30))
            weights = (scores * decays).astype(bf16)
            grad_weights = (grad_scores * decays).astype(bf16)
            inner_value_ref[top:end, here] = dot(weights, grad[top:])
            inner_key_ref[top:end, here] = dot(grad_weights, query[top:])
            inner_query = dot(grad_weights, key[top:end], TN)
            outer = inner_query + outer if top == 0 else jnp.concatenate(
                [outer[:top], outer[top:] + inner_query], axis=0
            )
        grad_query_ref[:, cols(j)] = outer.astype(bf16)


def final_kernel(
    part, info, inner_key_ref, inner_value_ref, key_ref, value_ref, cumul_ref, state_ref,
    grad_key_ref, grad_value_ref,
):
    for j in range(part.per_step):
        trail = column(trail_row(part.row(cumul_ref, info, j)))
        high, low = halves(state_ref[part.state_rows(j), :])
        at, here = part.wide_cols(info, j), part.state_rows(j)
        key, value = key_ref[:, at], value_ref[:, at]
        grad_key_ref[:, cols(j)] = (
            inner_key_ref[:, here] + trail * (dot(value, high, NT) + dot(value, low, NT))
        ).astype(bf16)
        grad_value_ref[:, cols(j)] = (
            inner_value_ref[:, here] + trail * (dot(key, high) + dot(key, low))
        ).astype(bf16)


def ordered(is_first, half, j, keep_ref, got_ref):
    rows = slice(j * HEAD_DIM, (j + 1) * HEAD_DIM)
    place = slice(half * HEAD_DIM + j, half * HEAD_DIM + j + 1)
    keep, got = keep_ref[rows, :], got_ref[rows, :]
    keep_decay, got_decay = keep_ref[place, :], got_ref[place, :]
    return (
        jnp.where(is_first, keep, got),
        jnp.where(is_first, got, keep),
        jnp.where(is_first, keep_decay, got_decay),
        jnp.where(is_first, got_decay, keep_decay),
    )


def scan_position(places, forward, info):
    member, pair = info[0][0], info[1][0]
    if forward:
        return member == 0, pair
    return member == 1, places - 1 - pair


def hop_kernel(half, senders, position, info, *refs):
    is_first, place = position(info)
    out_ref, arrived_ref = refs[-1], refs[-2]
    for index, p in enumerate(senders):
        keep_ref, got_ref = refs[2 * index], refs[2 * index + 1]

        @pl.when(place == p)
        def _():
            for j in range(half):
                first, second, first_decay, second_decay = ordered(
                    is_first, half, j, keep_ref, got_ref
                )
                value = second_decay * first + second
                if p > 0:
                    value += (first_decay * second_decay) * arrived_ref[cols(j), :]
                out_ref[cols(j), :] = value


def last_kernel(half, position, info, keep_ref, got_ref, *refs):
    arrived, (mine_ref, send_ref) = refs[:-2], refs[-2:]
    is_first, place = position(info)
    for p in range(len(arrived) + 1):

        @pl.when(place == p)
        def _():
            for j in range(half):
                first, _, first_decay, _ = ordered(is_first, half, j, keep_ref, got_ref)
                if p == 0:
                    before, after = jnp.zeros_like(first), first
                else:
                    before = arrived[p - 1][cols(j), :]
                    after = first_decay * before + first
                mine_ref[cols(j), :] = jnp.where(is_first, before, after)
                send_ref[cols(j), :] = jnp.where(is_first, after, before)


def on_device(queries, key_vecs, value_vecs, log_decay, norm_gain, cotangent):
    tokens, width = queries.shape
    assert tokens == BLOCK
    heads = width // HEAD_DIM
    half = heads // (2 * CHUNKS)
    head_count = lax.axis_size("head")
    features = width * head_count
    places = lax.axis_size("seq") // 2
    my_index = lax.axis_index("seq")
    member, pair = my_index % 2, my_index // 2
    gain = norm_gain.reshape(1, width)

    any_spec = pl.BlockSpec(memory_space=pl.ANY)
    wide_state = jax.ShapeDtypeStruct((half * HEAD_DIM + 8, HEAD_DIM), f32)
    state = jax.ShapeDtypeStruct((half * HEAD_DIM, HEAD_DIM), f32)
    whole = jax.ShapeDtypeStruct((tokens, width), bf16)
    local = jax.ShapeDtypeStruct((tokens, half * HEAD_DIM), f32)
    local_low = jax.ShapeDtypeStruct((tokens, half * HEAD_DIM), bf16)
    sums_shape = jax.ShapeDtypeStruct((8, tokens), f32)
    info = (member.astype(jnp.int32).reshape(1), pair.astype(jnp.int32).reshape(1))

    def run(kernel, grid, ins, outs, scratch=(), after=(), aliases=None, cost=1.0):
        used = len(ins)
        after = [x for i, x in enumerate(after) if not any(x is y for y in after[:i])]

        def body(member_ref, pair_ref, *refs):
            kernel((member_ref, pair_ref), *refs[:used], *refs[used + len(after):])

        return pl.pallas_call(
            body,
            out_shape=[shape for shape, _ in outs],
            grid_spec=pltpu.PrefetchScalarGridSpec(
                num_scalar_prefetch=2,
                grid=(grid,),
                in_specs=[spec for _, spec in ins] + [any_spec] * len(after),
                out_specs=[spec for _, spec in outs],
                scratch_shapes=list(scratch),
            ),
            input_output_aliases=aliases or {},
            compiler_params=pltpu.CompilerParams(vmem_limit_bytes=24 * 1024 * 1024),
            cost_estimate=pl.CostEstimate(
                flops=int(cost * 1e9), bytes_accessed=int(cost * 2.5e6), transcendentals=0
            ),
        )(*info, *[array for array, _ in ins], *after)

    def fixed(shape):
        return pl.BlockSpec(shape, lambda i, *info: (0,) * len(shape))

    def plain(array):
        return array, fixed(array.shape)

    def give(shape):
        return shape, fixed(shape.shape)

    class Views(Part):
        def full_spec(self):
            return pl.BlockSpec(
                (tokens, self.per_step * HEAD_DIM),
                lambda i, *info: (0, (2 * self.chunk + self.group(info)) * self.steps + i),
            )

        def call(self, kernel, ins, outs, **options):
            return run(functools.partial(kernel, self), self.steps, ins, outs, **options)

    mine_parts = [Views(c, "mine", half) for c in range(CHUNKS)]
    their_parts = [Views(c, "theirs", half) for c in range(CHUNKS)]

    swap = [(2 * p + m, 2 * p + 1 - m) for p in range(places) for m in (0, 1)]

    def chain(make_piece, forward, early, filler, on_mine):
        position = functools.partial(scan_position, places, forward)

        def device(place, m):
            return 2 * (place if forward else places - 1 - place) + m

        received, last = [], ()
        for c in range(CHUNKS):
            sent = make_piece(their_parts[c], last)
            received.append(lax.ppermute(sent, "seq", swap))
            last = (sent,)
        keeps = []
        for c in range(CHUNKS):
            keeps.append(make_piece(mine_parts[c], last))
            last = (keeps[-1],)
        for work in early:
            last = (work(last),)
        arrived, mine, theirs = {}, [], []
        for r in range(2, CHUNKS + places + 1):
            if r < CHUNKS + places:
                senders = [p for p in range(places - 1) if 0 <= r - 2 - p < CHUNKS]
                ins = []
                for p in senders:
                    ins += [plain(keeps[r - 2 - p]), plain(received[r - 2 - p])]
                ins.append(plain(arrived[r - 1]) if r > 2 else plain(keeps[0]))
                value, = run(
                    functools.partial(hop_kernel, half, senders, position), 1, ins, [give(state)],
                    after=last, cost=0.3,
                )
                pairs = [(device(p, m), device(p + 1, m)) for p in senders for m in (0, 1)]
                arrived[r] = lax.ppermute(value, "seq", pairs)
                last = (value,)
            c = r - 1 - places
            if 0 <= c:
                ins = [plain(keeps[c]), plain(received[c])]
                ins += [plain(arrived[c + 1 + p]) for p in range(1, places)]
                own, send = run(
                    functools.partial(last_kernel, half, position), 1, ins, [give(state)] * 2,
                    after=last, cost=0.3,
                )
                theirs.append(lax.ppermute(send, "seq", swap))
                mine.append(own)
                last = (send,)
                filler.append(functools.partial(on_mine, c, own))
            if filler:
                last = (filler.pop(0)(last),)
        while filler:
            last = (filler.pop(0)(last),)
        return mine, theirs, last

    held_cumul = []

    def forward_piece(part, after):
        if not held_cumul:
            piece, cumul = part.call(
                first_pieces_kernel,
                [plain(key_vecs), plain(value_vecs), plain(log_decay.T)],
                [give(wide_state), give(jax.ShapeDtypeStruct((heads, tokens), f32))], cost=1.0,
            )
            held_cumul.append(cumul)
            return piece
        cumul = held_cumul[0]
        return part.call(
            pieces_kernel, [plain(key_vecs), plain(value_vecs), plain(cumul)],
            [give(wide_state)], after=after, cost=1.0,
        )[0]

    inner, outs = {}, {}

    def cumul_in():
        return plain(held_cumul[0])

    state_sums = [jnp.zeros(sums_shape.shape, f32)]

    def inner_work(part, after):
        inner[part], = part.call(
            inner_kernel,
            [plain(queries), plain(key_vecs), plain(value_vecs), cumul_in()],
            [give(local)], after=after, cost=2.2,
        )
        return inner[part]

    def output_work(part, before, after):
        outs[part], sums = part.call(
            output_kernel,
            [plain(inner[part]), plain(queries), plain(cotangent), plain(gain),
             cumul_in(), plain(before), plain(state_sums[0])],
            [give(local), give(sums_shape)],
            scratch=[pltpu.VMEM((tokens, HEAD_DIM), f32)] * 2, after=after, cost=1.4,
        )
        state_sums[0] = sums
        return sums

    inner_order = [part for c in range(CHUNKS) for part in (mine_parts[c], their_parts[c])]
    works = [functools.partial(inner_work, part) for part in inner_order]
    mine, theirs, last = chain(
        forward_piece, True, works[:1], works[1:],
        lambda c, own, after: output_work(mine_parts[c], own, after),
    )
    for c in range(CHUNKS):
        last = (output_work(their_parts[c], theirs[c], last),)

    sums = state_sums[0]
    shares = [sums] + [
        lax.ppermute(sums, "head", [(i, (i + k) % head_count) for i in range(head_count)])
        for k in range(1, head_count)
    ]

    attended, grad_queries, grad_keys, grad_values = [], [], [], []
    grads, inner_grads = {}, {}

    def target(held):
        return tuple(held[-1:])

    def backward_piece(part, after):
        before = target(attended)
        whole_out, grads[part], piece = part.call(
            functools.partial(grad_kernel, features),
            [plain(outs[part]), plain(cotangent), plain(gain), plain(queries),
             cumul_in()] + [plain(share) for share in shares],
            [(whole, part.full_spec()), give(local_low), give(wide_state)],
            after=before + tuple(after), aliases={7 + head_count: 0} if before else None, cost=2.0,
        )
        attended.append(whole_out)
        return piece

    def backward_work(part, before, after):
        held = target(grad_queries)
        whole_out, *inner_grads[part] = part.call(
            backward_kernel,
            [plain(queries), plain(key_vecs), plain(value_vecs),
             plain(grads[part]), cumul_in(), plain(before)],
            [(whole, part.full_spec()), give(local), give(local)],
            after=held + tuple(after), aliases={8: 0} if held else None, cost=4.3,
        )
        grad_queries.append(whole_out)
        return inner_grads[part][0]

    def final_work(part, before, after):
        held = target(grad_keys) + target(grad_values)
        whole_key, whole_value = part.call(
            final_kernel,
            [plain(inner_grads[part][0]), plain(inner_grads[part][1]),
             plain(key_vecs), plain(value_vecs), cumul_in(), plain(before)],
            [(whole, part.full_spec())] * 2,
            after=held + tuple(after), aliases={8: 0, 9: 1} if held else None, cost=2.0,
        )
        grad_keys.append(whole_key)
        grad_values.append(whole_value)
        return whole_key

    works = []
    for c in range(CHUNKS):
        works.append(functools.partial(backward_work, mine_parts[c], mine[c]))
        works.append(functools.partial(backward_work, their_parts[c], theirs[c]))
    mine_after, theirs_after, last = chain(
        backward_piece, False, [], works,
        lambda c, own, after: final_work(mine_parts[c], own, after),
    )
    for c in range(CHUNKS):
        final_work(their_parts[c], theirs_after[c], last)
        last = ()
    return attended[-1], grad_queries[-1], grad_keys[-1], grad_values[-1]


def solution(mesh):
    return jax.shard_map(
        on_device,
        mesh=mesh,
        in_specs=(
            P("seq", "head"),
            P("seq", "head"),
            P("seq", "head"),
            P("seq", "head"),
            P("head"),
            P("seq", "head"),
        ),
        out_specs=(P("seq", "head"), P("seq", "head"), P("seq", "head"), P("seq", "head")),
        check_vma=False,
    )
```

```python
import functools

import jax
import jax.numpy as jnp
from jax import lax
from jax.experimental import pallas as pl
from jax.experimental.pallas import tpu as pltpu
from jax.sharding import PartitionSpec as P

HEAD_DIM = 128
BLOCK = 512
CHUNKS = 4
TILE = 256
epsilon = 1e-06
f32 = jnp.float32
bf16 = jnp.bfloat16

NN = (((1,), (0,)), ((), ()))
NT = (((1,), (1,)), ((), ()))
TN = (((0,), (0,)), ((), ()))


def dot(a, b, dims=NN):
    return lax.dot_general(a, b, dims, preferred_element_type=f32)


def halves(x):
    high = x.astype(bf16)
    return high, (x - high.astype(f32)).astype(bf16)


def column(row):
    return jnp.transpose(jnp.broadcast_to(row, (HEAD_DIM, row.shape[1])))


def wide(col, width):
    return jnp.concatenate([col] * (width // HEAD_DIM), axis=1)


def cumulative(decay):
    length = decay.shape[1]
    first = decay.astype(bf16)
    rest = decay - first.astype(f32)
    second = rest.astype(bf16)
    third = (rest - second.astype(f32)).astype(bf16)
    upto = lax.broadcasted_iota(jnp.int32, (length, length), 0) <= lax.broadcasted_iota(
        jnp.int32, (length, length), 1
    )
    upto = jnp.where(upto, 1.0, 0.0).astype(bf16)
    return dot(first, upto) + dot(second, upto) + dot(third, upto)


def trail_row(row):
    return jnp.exp(row[:, -1:] - row)


def outer_sum(left, scale_row, right):
    scaled = jnp.transpose(left.astype(f32)) * scale_row
    high, low = halves(scaled)
    return dot(high, right) + dot(low, right)


def cols(j):
    return slice(j * HEAD_DIM, (j + 1) * HEAD_DIM)


class Part:
    def __init__(self, chunk, slot, half):
        self.chunk, self.slot, self.half = chunk, slot, half
        self.steps = 2 if half % 4 == 0 else 1
        self.per_step = half // self.steps

    def group(self, info):
        return info[0][0] if self.slot == "mine" else 1 - info[0][0]

    def head(self, info, j):
        return (2 * self.chunk + self.group(info)) * self.half + pl.program_id(0) * self.per_step + j

    def row(self, cumul_ref, info, j):
        return cumul_ref[pl.ds(self.head(info, j), 1), :]

    def wide_cols(self, info, j):
        return pl.ds(pl.multiple_of(self.head(info, j) * HEAD_DIM, HEAD_DIM), HEAD_DIM)

    def state_rows(self, j):
        start = (pl.program_id(0) * self.per_step + j) * HEAD_DIM
        return pl.ds(pl.multiple_of(start, HEAD_DIM), HEAD_DIM)


def store_decays(part, info, cumul_ref, out_ref):
    for j in range(part.per_step):
        row = part.row(cumul_ref, info, j)
        place = part.half * HEAD_DIM + pl.program_id(0) * part.per_step + j
        out_ref[pl.ds(place, 1), :] = jnp.broadcast_to(jnp.exp(row[:, -1:]), (1, HEAD_DIM))


def pieces_kernel(part, info, key_ref, value_ref, cumul_ref, out_ref):
    for j in range(part.per_step):
        row = part.row(cumul_ref, info, j)
        at = part.wide_cols(info, j)
        out_ref[part.state_rows(j), :] = outer_sum(key_ref[:, at], trail_row(row), value_ref[:, at])
    store_decays(part, info, cumul_ref, out_ref)


def first_pieces_kernel(part, info, key_ref, value_ref, decay_ref, out_ref, cumul_ref):
    @pl.when(pl.program_id(0) == 0)
    def _():
        cumul_ref[...] = cumulative(decay_ref[...])

    pieces_kernel(part, info, key_ref, value_ref, cumul_ref, out_ref)


def inner_kernel(part, info, query_ref, key_ref, value_ref, cumul_ref, out_ref):
    for j in range(part.per_step):
        row = part.row(cumul_ref, info, j)
        col = column(row)
        at = part.wide_cols(info, j)
        query, key, value = query_ref[:, at], key_ref[:, at], value_ref[:, at]
        for top in range(0, BLOCK, TILE):
            end = top + TILE
            scores = dot(query[top:end], key[:end], NT)
            spread = wide(col[top:end], end) - row[:, :end]
            causal = lax.broadcasted_iota(jnp.int32, (TILE, end), 0) + top >= (
                lax.broadcasted_iota(jnp.int32, (TILE, end), 1)
            )
            weights = (scores * jnp.exp(jnp.where(causal, spread, -1e30))).astype(bf16)
            out_ref[top:end, part.state_rows(j)] = dot(weights, value[:end])


def output_kernel(
    part, info, inner_ref, query_ref, cot_ref, gain_ref, cumul_ref, state_ref, before_ref,
    out_ref, sums_ref, square_ref, product_ref,
):
    step = pl.program_id(0)
    squares = jnp.zeros((BLOCK, HEAD_DIM), f32)
    products = jnp.zeros((BLOCK, HEAD_DIM), f32)
    for j in range(part.per_step):
        lead = jnp.exp(column(part.row(cumul_ref, info, j)))
        high, low = halves(state_ref[part.state_rows(j), :])
        at, here = part.wide_cols(info, j), part.state_rows(j)
        query = query_ref[:, at]
        out = inner_ref[:, here] + lead * (dot(query, high) + dot(query, low))
        out_ref[:, here] = out
        squares += out * out
        products += cot_ref[:, at].astype(f32) * gain_ref[:, at] * out

    @pl.when(step == 0)
    def _():
        square_ref[...] = squares
        product_ref[...] = products

    @pl.when(step > 0)
    def _():
        square_ref[...] += squares
        product_ref[...] += products

    @pl.when(step == part.steps - 1)
    def _():
        rows = lax.broadcasted_iota(jnp.int32, (8, HEAD_DIM), 0)
        total = before_ref[...]
        for place, ref in ((0, square_ref), (1, product_ref)):
            pick = jnp.where(rows == place, 1.0, 0.0).astype(bf16)
            high, low = halves(ref[...])
            total += dot(pick, high, NT) + dot(pick, low, NT)
        sums_ref[...] = total


def grad_kernel(features, part, info, out_ref, cot_ref, gain_ref, query_ref, cumul_ref, *refs):
    shares, (attended_ref, grad_ref, piece_ref) = refs[:-3], refs[-3:]
    sums = shares[0][...]
    for share in shares[1:]:
        sums = sums + share[...]
    inverse = lax.rsqrt(sums[0:1] / features + epsilon)
    mean_term = inverse * sums[1:2] / features
    inverse_col, mean_col = column(inverse), column(mean_term)
    for j in range(part.per_step):
        at, here = part.wide_cols(info, j), part.state_rows(j)
        gain = gain_ref[:, at]
        normed = out_ref[:, here] * inverse_col
        attended_ref[:, cols(j)] = (normed * gain).astype(bf16)
        scaled_grad = cot_ref[:, at].astype(f32) * gain
        grad = (inverse_col * (scaled_grad - normed * mean_col)).astype(bf16)
        grad_ref[:, here] = grad
        row = part.row(cumul_ref, info, j)
        piece_ref[part.state_rows(j), :] = outer_sum(query_ref[:, at], jnp.exp(row), grad)
    store_decays(part, info, cumul_ref, piece_ref)


def backward_kernel(
    part, info, query_ref, key_ref, value_ref, grad_ref, cumul_ref, state_ref,
    grad_query_ref, inner_key_ref, inner_value_ref,
):
    for j in range(part.per_step):
        row = part.row(cumul_ref, info, j)
        col = column(row)
        at, here = part.wide_cols(info, j), part.state_rows(j)
        query, key = query_ref[:, at], key_ref[:, at]
        value, grad = value_ref[:, at], grad_ref[:, here]
        high, low = halves(state_ref[part.state_rows(j), :])
        outer = jnp.exp(col) * (dot(grad, high, NT) + dot(grad, low, NT))
        for top in range(0, BLOCK, TILE):
            end = top + TILE
            scores = dot(key[top:end], query[top:], NT)
            grad_scores = dot(value[top:end], grad[top:], NT)
            spread = row[:, top:] - wide(col[top:end], BLOCK - top)
            causal = lax.broadcasted_iota(jnp.int32, spread.shape, 0) <= (
                lax.broadcasted_iota(jnp.int32, spread.shape, 1)
            )
            decays = jnp.exp(jnp.where(causal, spread, -1e30))
            weights = (scores * decays).astype(bf16)
            grad_weights = (grad_scores * decays).astype(bf16)
            inner_value_ref[top:end, here] = dot(weights, grad[top:])
            inner_key_ref[top:end, here] = dot(grad_weights, query[top:])
            inner_query = dot(grad_weights, key[top:end], TN)
            outer = inner_query + outer if top == 0 else jnp.concatenate(
                [outer[:top], outer[top:] + inner_query], axis=0
            )
        grad_query_ref[:, cols(j)] = outer.astype(bf16)


def final_kernel(
    part, info, inner_key_ref, inner_value_ref, key_ref, value_ref, cumul_ref, state_ref,
    grad_key_ref, grad_value_ref,
):
    for j in range(part.per_step):
        trail = column(trail_row(part.row(cumul_ref, info, j)))
        high, low = halves(state_ref[part.state_rows(j), :])
        at, here = part.wide_cols(info, j), part.state_rows(j)
        key, value = key_ref[:, at], value_ref[:, at]
        grad_key_ref[:, cols(j)] = (
            inner_key_ref[:, here] + trail * (dot(value, high, NT) + dot(value, low, NT))
        ).astype(bf16)
        grad_value_ref[:, cols(j)] = (
            inner_value_ref[:, here] + trail * (dot(key, high) + dot(key, low))
        ).astype(bf16)


def ordered(is_first, half, j, keep_ref, got_ref):
    rows = slice(j * HEAD_DIM, (j + 1) * HEAD_DIM)
    place = slice(half * HEAD_DIM + j, half * HEAD_DIM + j + 1)
    keep, got = keep_ref[rows, :], got_ref[rows, :]
    keep_decay, got_decay = keep_ref[place, :], got_ref[place, :]
    return (
        jnp.where(is_first, keep, got),
        jnp.where(is_first, got, keep),
        jnp.where(is_first, keep_decay, got_decay),
        jnp.where(is_first, got_decay, keep_decay),
    )


def scan_position(places, forward, info):
    member, pair = info[0][0], info[1][0]
    if forward:
        return member == 0, pair
    return member == 1, places - 1 - pair


def hop_kernel(half, senders, position, info, *refs):
    is_first, place = position(info)
    out_ref, arrived_ref = refs[-1], refs[-2]
    for index, p in enumerate(senders):
        keep_ref, got_ref = refs[2 * index], refs[2 * index + 1]

        @pl.when(place == p)
        def _():
            for j in range(half):
                first, second, first_decay, second_decay = ordered(
                    is_first, half, j, keep_ref, got_ref
                )
                value = second_decay * first + second
                if p > 0:
                    value += (first_decay * second_decay) * arrived_ref[cols(j), :]
                out_ref[cols(j), :] = value


def last_kernel(half, position, info, keep_ref, got_ref, *refs):
    arrived, (mine_ref, send_ref) = refs[:-2], refs[-2:]
    is_first, place = position(info)
    for p in range(len(arrived) + 1):

        @pl.when(place == p)
        def _():
            for j in range(half):
                first, _, first_decay, _ = ordered(is_first, half, j, keep_ref, got_ref)
                if p == 0:
                    before, after = jnp.zeros_like(first), first
                else:
                    before = arrived[p - 1][cols(j), :]
                    after = first_decay * before + first
                mine_ref[cols(j), :] = jnp.where(is_first, before, after)
                send_ref[cols(j), :] = jnp.where(is_first, after, before)


def on_device(queries, key_vecs, value_vecs, log_decay, norm_gain, cotangent):
    tokens, width = queries.shape
    assert tokens == BLOCK
    heads = width // HEAD_DIM
    half = heads // (2 * CHUNKS)
    head_count = lax.axis_size("head")
    features = width * head_count
    places = lax.axis_size("seq") // 2
    my_index = lax.axis_index("seq")
    member, pair = my_index % 2, my_index // 2
    gain = norm_gain.reshape(1, width)

    any_spec = pl.BlockSpec(memory_space=pl.ANY)
    wide_state = jax.ShapeDtypeStruct((half * HEAD_DIM + 8, HEAD_DIM), f32)
    state = jax.ShapeDtypeStruct((half * HEAD_DIM, HEAD_DIM), f32)
    whole = jax.ShapeDtypeStruct((tokens, width), bf16)
    local = jax.ShapeDtypeStruct((tokens, half * HEAD_DIM), f32)
    local_low = jax.ShapeDtypeStruct((tokens, half * HEAD_DIM), bf16)
    sums_shape = jax.ShapeDtypeStruct((8, tokens), f32)
    info = (member.astype(jnp.int32).reshape(1), pair.astype(jnp.int32).reshape(1))

    def run(kernel, grid, ins, outs, scratch=(), after=(), aliases=None, cost=1.0):
        used = len(ins)
        after = [x for i, x in enumerate(after) if not any(x is y for y in after[:i])]

        def body(member_ref, pair_ref, *refs):
            kernel((member_ref, pair_ref), *refs[:used], *refs[used + len(after):])

        return pl.pallas_call(
            body,
            out_shape=[shape for shape, _ in outs],
            grid_spec=pltpu.PrefetchScalarGridSpec(
                num_scalar_prefetch=2,
                grid=(grid,),
                in_specs=[spec for _, spec in ins] + [any_spec] * len(after),
                out_specs=[spec for _, spec in outs],
                scratch_shapes=list(scratch),
            ),
            input_output_aliases=aliases or {},
            compiler_params=pltpu.CompilerParams(vmem_limit_bytes=24 * 1024 * 1024),
            cost_estimate=pl.CostEstimate(
                flops=int(cost * 1e9), bytes_accessed=int(cost * 2.5e6), transcendentals=0
            ),
        )(*info, *[array for array, _ in ins], *after)

    def fixed(shape):
        return pl.BlockSpec(shape, lambda i, *info: (0,) * len(shape))

    def plain(array):
        return array, fixed(array.shape)

    def give(shape):
        return shape, fixed(shape.shape)

    class Views(Part):
        def full_spec(self):
            return pl.BlockSpec(
                (tokens, self.per_step * HEAD_DIM),
                lambda i, *info: (0, (2 * self.chunk + self.group(info)) * self.steps + i),
            )

        def call(self, kernel, ins, outs, **options):
            return run(functools.partial(kernel, self), self.steps, ins, outs, **options)

    mine_parts = [Views(c, "mine", half) for c in range(CHUNKS)]
    their_parts = [Views(c, "theirs", half) for c in range(CHUNKS)]

    swap = [(2 * p + m, 2 * p + 1 - m) for p in range(places) for m in (0, 1)]

    def chain(make_piece, forward, early, filler, on_mine):
        position = functools.partial(scan_position, places, forward)

        def device(place, m):
            return 2 * (place if forward else places - 1 - place) + m

        received, last = [], ()
        for c in range(CHUNKS):
            sent = make_piece(their_parts[c], last)
            received.append(lax.ppermute(sent, "seq", swap))
            last = (sent,)
        keeps = []
        for c in range(CHUNKS):
            keeps.append(make_piece(mine_parts[c], last))
            last = (keeps[-1],)
        for work in early:
            last = (work(last),)
        arrived, mine, theirs = {}, [], []
        for r in range(2, CHUNKS + places + 1):
            if r < CHUNKS + places:
                senders = [p for p in range(places - 1) if 0 <= r - 2 - p < CHUNKS]
                ins = []
                for p in senders:
                    ins += [plain(keeps[r - 2 - p]), plain(received[r - 2 - p])]
                ins.append(plain(arrived[r - 1]) if r > 2 else plain(keeps[0]))
                value, = run(
                    functools.partial(hop_kernel, half, senders, position), 1, ins, [give(state)],
                    after=last, cost=0.3,
                )
                pairs = [(device(p, m), device(p + 1, m)) for p in senders for m in (0, 1)]
                arrived[r] = lax.ppermute(value, "seq", pairs)
                last = (value,)
            c = r - 1 - places
            if 0 <= c:
                ins = [plain(keeps[c]), plain(received[c])]
                ins += [plain(arrived[c + 1 + p]) for p in range(1, places)]
                own, send = run(
                    functools.partial(last_kernel, half, position), 1, ins, [give(state)] * 2,
                    after=last, cost=0.3,
                )
                theirs.append(lax.ppermute(send, "seq", swap))
                mine.append(own)
                last = (send,)
                filler.append(functools.partial(on_mine, c, own))
            if filler:
                last = (filler.pop(0)(last),)
        while filler:
            last = (filler.pop(0)(last),)
        return mine, theirs, last

    held_cumul = []

    def forward_piece(part, after):
        if not held_cumul:
            piece, cumul = part.call(
                first_pieces_kernel,
                [plain(key_vecs), plain(value_vecs), plain(log_decay.T)],
                [give(wide_state), give(jax.ShapeDtypeStruct((heads, tokens), f32))], cost=1.0,
            )
            held_cumul.append(cumul)
            return piece
        cumul = held_cumul[0]
        return part.call(
            pieces_kernel, [plain(key_vecs), plain(value_vecs), plain(cumul)],
            [give(wide_state)], after=after, cost=1.0,
        )[0]

    inner, outs = {}, {}

    def cumul_in():
        return plain(held_cumul[0])

    state_sums = [jnp.zeros(sums_shape.shape, f32)]

    def inner_work(part, after):
        inner[part], = part.call(
            inner_kernel,
            [plain(queries), plain(key_vecs), plain(value_vecs), cumul_in()],
            [give(local)], after=after, cost=2.2,
        )
        return inner[part]

    def output_work(part, before, after):
        outs[part], sums = part.call(
            output_kernel,
            [plain(inner[part]), plain(queries), plain(cotangent), plain(gain),
             cumul_in(), plain(before), plain(state_sums[0])],
            [give(local), give(sums_shape)],
            scratch=[pltpu.VMEM((tokens, HEAD_DIM), f32)] * 2, after=after, cost=1.4,
        )
        state_sums[0] = sums
        return sums

    inner_order = [part for c in range(CHUNKS) for part in (mine_parts[c], their_parts[c])]
    works = [functools.partial(inner_work, part) for part in inner_order]
    mine, theirs, last = chain(
        forward_piece, True, works[:1], works[1:],
        lambda c, own, after: output_work(mine_parts[c], own, after),
    )
    for c in range(CHUNKS):
        last = (output_work(their_parts[c], theirs[c], last),)

    sums = state_sums[0]
    shares = [sums] + [
        lax.ppermute(sums, "head", [(i, (i + k) % head_count) for i in range(head_count)])
        for k in range(1, head_count)
    ]

    attended, grad_queries, grad_keys, grad_values = [], [], [], []
    grads, inner_grads = {}, {}

    def target(held):
        return tuple(held[-1:])

    def backward_piece(part, after):
        before = target(attended)
        whole_out, grads[part], piece = part.call(
            functools.partial(grad_kernel, features),
            [plain(outs[part]), plain(cotangent), plain(gain), plain(queries),
             cumul_in()] + [plain(share) for share in shares],
            [(whole, part.full_spec()), give(local_low), give(wide_state)],
            after=before + tuple(after), aliases={7 + head_count: 0} if before else None, cost=2.0,
        )
        attended.append(whole_out)
        return piece

    def backward_work(part, before, after):
        held = target(grad_queries)
        whole_out, *inner_grads[part] = part.call(
            backward_kernel,
            [plain(queries), plain(key_vecs), plain(value_vecs),
             plain(grads[part]), cumul_in(), plain(before)],
            [(whole, part.full_spec()), give(local), give(local)],
            after=held + tuple(after), aliases={8: 0} if held else None, cost=4.3,
        )
        grad_queries.append(whole_out)
        return inner_grads[part][0]

    def final_work(part, before, after):
        held = target(grad_keys) + target(grad_values)
        whole_key, whole_value = part.call(
            final_kernel,
            [plain(inner_grads[part][0]), plain(inner_grads[part][1]),
             plain(key_vecs), plain(value_vecs), cumul_in(), plain(before)],
            [(whole, part.full_spec())] * 2,
            after=held + tuple(after), aliases={8: 0, 9: 1} if held else None, cost=2.0,
        )
        grad_keys.append(whole_key)
        grad_values.append(whole_value)
        return whole_key

    works = []
    for c in range(CHUNKS):
        works.append(functools.partial(backward_work, mine_parts[c], mine[c]))
        works.append(functools.partial(backward_work, their_parts[c], theirs[c]))
    mine_after, theirs_after, last = chain(
        backward_piece, False, [], works,
        lambda c, own, after: final_work(mine_parts[c], own, after),
    )
    for c in range(CHUNKS):
        final_work(their_parts[c], theirs_after[c], last)
        last = ()
    return attended[-1], grad_queries[-1], grad_keys[-1], grad_values[-1]


def solution(mesh):
    return jax.shard_map(
        on_device,
        mesh=mesh,
        in_specs=(
            P("seq", "head"),
            P("seq", "head"),
            P("seq", "head"),
            P("seq", "head"),
            P("head"),
            P("seq", "head"),
        ),
        out_specs=(P("seq", "head"), P("seq", "head"), P("seq", "head"), P("seq", "head")),
        check_vma=False,
    )
```

```python
import functools

import jax
import jax.numpy as jnp
from jax import lax
from jax.experimental import pallas as pl
from jax.experimental.pallas import tpu as pltpu
from jax.sharding import PartitionSpec as P

HEAD_DIM = 128
BLOCK = 512
CHUNKS = 2
TILE = 256
epsilon = 1e-06
f32 = jnp.float32
bf16 = jnp.bfloat16

NN = (((1,), (0,)), ((), ()))
NT = (((1,), (1,)), ((), ()))
TN = (((0,), (0,)), ((), ()))


def dot(a, b, dims=NN):
    return lax.dot_general(a, b, dims, preferred_element_type=f32)


def halves(x):
    high = x.astype(bf16)
    return high, (x - high.astype(f32)).astype(bf16)


def column(row):
    return jnp.transpose(jnp.broadcast_to(row, (HEAD_DIM, row.shape[1])))


def wide(col, width):
    return jnp.concatenate([col] * (width // HEAD_DIM), axis=1)


def cumulative(decay):
    length = decay.shape[1]
    first = decay.astype(bf16)
    rest = decay - first.astype(f32)
    second = rest.astype(bf16)
    third = (rest - second.astype(f32)).astype(bf16)
    upto = lax.broadcasted_iota(jnp.int32, (length, length), 0) <= lax.broadcasted_iota(
        jnp.int32, (length, length), 1
    )
    upto = jnp.where(upto, 1.0, 0.0).astype(bf16)
    return dot(first, upto) + dot(second, upto) + dot(third, upto)


def trail_row(row):
    return jnp.exp(row[:, -1:] - row)


def outer_sum(left, scale_row, right):
    scaled = jnp.transpose(left.astype(f32)) * scale_row
    high, low = halves(scaled)
    return dot(high, right) + dot(low, right)


def cols(j):
    return slice(j * HEAD_DIM, (j + 1) * HEAD_DIM)


class Part:
    def __init__(self, chunk, slot, half):
        self.chunk, self.slot, self.half = chunk, slot, half
        self.steps = 2 if half % 4 == 0 else 1
        self.per_step = half // self.steps

    def group(self, info):
        return info[0][0] if self.slot == "mine" else 1 - info[0][0]

    def head(self, info, j):
        return (2 * self.chunk + self.group(info)) * self.half + pl.program_id(0) * self.per_step + j

    def row(self, cumul_ref, info, j):
        return cumul_ref[pl.ds(self.head(info, j), 1), :]

    def wide_cols(self, info, j):
        return pl.ds(pl.multiple_of(self.head(info, j) * HEAD_DIM, HEAD_DIM), HEAD_DIM)

    def state_rows(self, j):
        start = (pl.program_id(0) * self.per_step + j) * HEAD_DIM
        return pl.ds(pl.multiple_of(start, HEAD_DIM), HEAD_DIM)


def store_decays(part, info, cumul_ref, out_ref):
    for j in range(part.per_step):
        row = part.row(cumul_ref, info, j)
        place = part.half * HEAD_DIM + pl.program_id(0) * part.per_step + j
        out_ref[pl.ds(place, 1), :] = jnp.broadcast_to(jnp.exp(row[:, -1:]), (1, HEAD_DIM))


def pieces_kernel(part, info, key_ref, value_ref, cumul_ref, out_ref):
    for j in range(part.per_step):
        row = part.row(cumul_ref, info, j)
        at = part.wide_cols(info, j)
        out_ref[part.state_rows(j), :] = outer_sum(key_ref[:, at], trail_row(row), value_ref[:, at])
    store_decays(part, info, cumul_ref, out_ref)


def first_pieces_kernel(part, info, key_ref, value_ref, decay_ref, out_ref, cumul_ref):
    @pl.when(pl.program_id(0) == 0)
    def _():
        cumul_ref[...] = cumulative(decay_ref[...])

    pieces_kernel(part, info, key_ref, value_ref, cumul_ref, out_ref)


def inner_kernel(part, info, query_ref, key_ref, value_ref, cumul_ref, out_ref):
    for j in range(part.per_step):
        row = part.row(cumul_ref, info, j)
        col = column(row)
        at = part.wide_cols(info, j)
        query, key, value = query_ref[:, at], key_ref[:, at], value_ref[:, at]
        for top in range(0, BLOCK, TILE):
            end = top + TILE
            scores = dot(query[top:end], key[:end], NT)
            spread = wide(col[top:end], end) - row[:, :end]
            causal = lax.broadcasted_iota(jnp.int32, (TILE, end), 0) + top >= (
                lax.broadcasted_iota(jnp.int32, (TILE, end), 1)
            )
            weights = (scores * jnp.exp(jnp.where(causal, spread, -1e30))).astype(bf16)
            out_ref[top:end, part.state_rows(j)] = dot(weights, value[:end])


def output_kernel(
    part, info, inner_ref, query_ref, cot_ref, gain_ref, cumul_ref, state_ref, before_ref,
    out_ref, sums_ref, square_ref, product_ref,
):
    step = pl.program_id(0)
    squares = jnp.zeros((BLOCK, HEAD_DIM), f32)
    products = jnp.zeros((BLOCK, HEAD_DIM), f32)
    for j in range(part.per_step):
        lead = jnp.exp(column(part.row(cumul_ref, info, j)))
        high, low = halves(state_ref[part.state_rows(j), :])
        at, here = part.wide_cols(info, j), part.state_rows(j)
        query = query_ref[:, at]
        out = inner_ref[:, here] + lead * (dot(query, high) + dot(query, low))
        out_ref[:, here] = out
        squares += out * out
        products += cot_ref[:, at].astype(f32) * gain_ref[:, at] * out

    @pl.when(step == 0)
    def _():
        square_ref[...] = squares
        product_ref[...] = products

    @pl.when(step > 0)
    def _():
        square_ref[...] += squares
        product_ref[...] += products

    @pl.when(step == part.steps - 1)
    def _():
        rows = lax.broadcasted_iota(jnp.int32, (8, HEAD_DIM), 0)
        total = before_ref[...]
        for place, ref in ((0, square_ref), (1, product_ref)):
            pick = jnp.where(rows == place, 1.0, 0.0).astype(bf16)
            high, low = halves(ref[...])
            total += dot(pick, high, NT) + dot(pick, low, NT)
        sums_ref[...] = total


def grad_kernel(features, part, info, out_ref, cot_ref, gain_ref, query_ref, cumul_ref, *refs):
    shares, (attended_ref, grad_ref, piece_ref) = refs[:-3], refs[-3:]
    sums = shares[0][...]
    for share in shares[1:]:
        sums = sums + share[...]
    inverse = lax.rsqrt(sums[0:1] / features + epsilon)
    mean_term = inverse * sums[1:2] / features
    inverse_col, mean_col = column(inverse), column(mean_term)
    for j in range(part.per_step):
        at, here = part.wide_cols(info, j), part.state_rows(j)
        gain = gain_ref[:, at]
        normed = out_ref[:, here] * inverse_col
        attended_ref[:, cols(j)] = (normed * gain).astype(bf16)
        scaled_grad = cot_ref[:, at].astype(f32) * gain
        grad = (inverse_col * (scaled_grad - normed * mean_col)).astype(bf16)
        grad_ref[:, here] = grad
        row = part.row(cumul_ref, info, j)
        piece_ref[part.state_rows(j), :] = outer_sum(query_ref[:, at], jnp.exp(row), grad)
    store_decays(part, info, cumul_ref, piece_ref)


def backward_kernel(
    part, info, query_ref, key_ref, value_ref, grad_ref, cumul_ref, state_ref,
    grad_query_ref, inner_key_ref, inner_value_ref,
):
    for j in range(part.per_step):
        row = part.row(cumul_ref, info, j)
        col = column(row)
        at, here = part.wide_cols(info, j), part.state_rows(j)
        query, key = query_ref[:, at], key_ref[:, at]
        value, grad = value_ref[:, at], grad_ref[:, here]
        high, low = halves(state_ref[part.state_rows(j), :])
        outer = jnp.exp(col) * (dot(grad, high, NT) + dot(grad, low, NT))
        for top in range(0, BLOCK, TILE):
            end = top + TILE
            scores = dot(key[top:end], query[top:], NT)
            grad_scores = dot(value[top:end], grad[top:], NT)
            spread = row[:, top:] - wide(col[top:end], BLOCK - top)
            causal = lax.broadcasted_iota(jnp.int32, spread.shape, 0) <= (
                lax.broadcasted_iota(jnp.int32, spread.shape, 1)
            )
            decays = jnp.exp(jnp.where(causal, spread, -1e30))
            weights = (scores * decays).astype(bf16)
            grad_weights = (grad_scores * decays).astype(bf16)
            inner_value_ref[top:end, here] = dot(weights, grad[top:])
            inner_key_ref[top:end, here] = dot(grad_weights, query[top:])
            inner_query = dot(grad_weights, key[top:end], TN)
            outer = inner_query + outer if top == 0 else jnp.concatenate(
                [outer[:top], outer[top:] + inner_query], axis=0
            )
        grad_query_ref[:, cols(j)] = outer.astype(bf16)


def final_kernel(
    part, info, inner_key_ref, inner_value_ref, key_ref, value_ref, cumul_ref, state_ref,
    grad_key_ref, grad_value_ref,
):
    for j in range(part.per_step):
        trail = column(trail_row(part.row(cumul_ref, info, j)))
        high, low = halves(state_ref[part.state_rows(j), :])
        at, here = part.wide_cols(info, j), part.state_rows(j)
        key, value = key_ref[:, at], value_ref[:, at]
        grad_key_ref[:, cols(j)] = (
            inner_key_ref[:, here] + trail * (dot(value, high, NT) + dot(value, low, NT))
        ).astype(bf16)
        grad_value_ref[:, cols(j)] = (
            inner_value_ref[:, here] + trail * (dot(key, high) + dot(key, low))
        ).astype(bf16)


def ordered(is_first, half, j, keep_ref, got_ref):
    rows = slice(j * HEAD_DIM, (j + 1) * HEAD_DIM)
    place = slice(half * HEAD_DIM + j, half * HEAD_DIM + j + 1)
    keep, got = keep_ref[rows, :], got_ref[rows, :]
    keep_decay, got_decay = keep_ref[place, :], got_ref[place, :]
    return (
        jnp.where(is_first, keep, got),
        jnp.where(is_first, got, keep),
        jnp.where(is_first, keep_decay, got_decay),
        jnp.where(is_first, got_decay, keep_decay),
    )


def scan_position(places, forward, info):
    member, pair = info[0][0], info[1][0]
    if forward:
        return member == 0, pair
    return member == 1, places - 1 - pair


def hop_kernel(half, p, position, info, keep_ref, got_ref, *refs):
    arrived, out_ref = refs[:-1], refs[-1]
    is_first, place = position(info)

    @pl.when(place == p)
    def _():
        for j in range(half):
            first, second, first_decay, second_decay = ordered(is_first, half, j, keep_ref, got_ref)
            value = second_decay * first + second
            for arrived_ref in arrived:
                value += (first_decay * second_decay) * arrived_ref[cols(j), :]
            out_ref[cols(j), :] = value


def last_kernel(half, position, info, keep_ref, got_ref, *refs):
    arrived, (mine_ref, send_ref) = refs[:-2], refs[-2:]
    is_first, place = position(info)
    for p in range(len(arrived) + 1):

        @pl.when(place == p)
        def _():
            for j in range(half):
                first, _, first_decay, _ = ordered(is_first, half, j, keep_ref, got_ref)
                if p == 0:
                    before, after = jnp.zeros_like(first), first
                else:
                    before = arrived[p - 1][cols(j), :]
                    after = first_decay * before + first
                mine_ref[cols(j), :] = jnp.where(is_first, before, after)
                send_ref[cols(j), :] = jnp.where(is_first, after, before)


def on_device(queries, key_vecs, value_vecs, log_decay, norm_gain, cotangent):
    tokens, width = queries.shape
    assert tokens == BLOCK
    heads = width // HEAD_DIM
    half = heads // (2 * CHUNKS)
    head_count = lax.axis_size("head")
    features = width * head_count
    places = lax.axis_size("seq") // 2
    my_index = lax.axis_index("seq")
    member, pair = my_index % 2, my_index // 2
    gain = norm_gain.reshape(1, width)

    any_spec = pl.BlockSpec(memory_space=pl.ANY)
    wide_state = jax.ShapeDtypeStruct((half * HEAD_DIM + 8, HEAD_DIM), f32)
    state = jax.ShapeDtypeStruct((half * HEAD_DIM, HEAD_DIM), f32)
    whole = jax.ShapeDtypeStruct((tokens, width), bf16)
    local = jax.ShapeDtypeStruct((tokens, half * HEAD_DIM), f32)
    local_low = jax.ShapeDtypeStruct((tokens, half * HEAD_DIM), bf16)
    sums_shape = jax.ShapeDtypeStruct((8, tokens), f32)
    info = (member.astype(jnp.int32).reshape(1), pair.astype(jnp.int32).reshape(1))

    def run(kernel, grid, ins, outs, scratch=(), after=(), aliases=None, cost=1.0):
        used = len(ins)
        after = [x for i, x in enumerate(after) if not any(x is y for y in after[:i])]

        def body(member_ref, pair_ref, *refs):
            kernel((member_ref, pair_ref), *refs[:used], *refs[used + len(after):])

        return pl.pallas_call(
            body,
            out_shape=[shape for shape, _ in outs],
            grid_spec=pltpu.PrefetchScalarGridSpec(
                num_scalar_prefetch=2,
                grid=(grid,),
                in_specs=[spec for _, spec in ins] + [any_spec] * len(after),
                out_specs=[spec for _, spec in outs],
                scratch_shapes=list(scratch),
            ),
            input_output_aliases=aliases or {},
            compiler_params=pltpu.CompilerParams(vmem_limit_bytes=24 * 1024 * 1024),
            cost_estimate=pl.CostEstimate(
                flops=int(cost * 1e9), bytes_accessed=int(cost * 2.5e6), transcendentals=0
            ),
        )(*info, *[array for array, _ in ins], *after)

    def fixed(shape):
        return pl.BlockSpec(shape, lambda i, *info: (0,) * len(shape))

    def plain(array):
        return array, fixed(array.shape)

    def give(shape):
        return shape, fixed(shape.shape)

    class Views(Part):
        def full_spec(self):
            return pl.BlockSpec(
                (tokens, self.per_step * HEAD_DIM),
                lambda i, *info: (0, (2 * self.chunk + self.group(info)) * self.steps + i),
            )

        def call(self, kernel, ins, outs, **options):
            return run(functools.partial(kernel, self), self.steps, ins, outs, **options)

    mine_parts = [Views(c, "mine", half) for c in range(CHUNKS)]
    their_parts = [Views(c, "theirs", half) for c in range(CHUNKS)]

    swap = [(2 * p + m, 2 * p + 1 - m) for p in range(places) for m in (0, 1)]

    def chain(make_piece, forward, early, filler, on_mine):
        position = functools.partial(scan_position, places, forward)

        def device(place, m):
            return 2 * (place if forward else places - 1 - place) + m

        received, last = [], ()
        for c in range(CHUNKS):
            sent = make_piece(their_parts[c], last)
            received.append(lax.ppermute(sent, "seq", swap))
            last = (sent,)
        keeps = []
        for c in range(CHUNKS):
            keeps.append(make_piece(mine_parts[c], last))
            last = (keeps[-1],)
        for work in early:
            last = (work(last),)
        arrived, mine, theirs = {}, [], []
        for p in range(places - 1):
            pairs = [(device(p, m), device(p + 1, m)) for m in (0, 1)]
            for c in range(CHUNKS):
                ins = [plain(keeps[c]), plain(received[c])]
                if p > 0:
                    ins.append(plain(arrived[c, p]))
                value, = run(
                    functools.partial(hop_kernel, half, p, position), 1, ins, [give(state)],
                    after=last, cost=0.3,
                )
                arrived[c, p + 1] = lax.ppermute(value, "seq", pairs)
                last = (value,)
            if filler:
                last = (filler.pop(0)(last),)
        for c in range(CHUNKS):
            ins = [plain(keeps[c]), plain(received[c])]
            ins += [plain(arrived[c, p]) for p in range(1, places)]
            own, send = run(
                functools.partial(last_kernel, half, position), 1, ins, [give(state)] * 2,
                after=last, cost=0.3,
            )
            theirs.append(lax.ppermute(send, "seq", swap))
            mine.append(own)
            last = (send,)
            filler.append(functools.partial(on_mine, c, own))
            last = (filler.pop(0)(last),)
        while filler:
            last = (filler.pop(0)(last),)
        return mine, theirs, last

    held_cumul = []

    def forward_piece(part, after):
        if not held_cumul:
            piece, cumul = part.call(
                first_pieces_kernel,
                [plain(key_vecs), plain(value_vecs), plain(log_decay.T)],
                [give(wide_state), give(jax.ShapeDtypeStruct((heads, tokens), f32))], cost=1.0,
            )
            held_cumul.append(cumul)
            return piece
        cumul = held_cumul[0]
        return part.call(
            pieces_kernel, [plain(key_vecs), plain(value_vecs), plain(cumul)],
            [give(wide_state)], after=after, cost=1.0,
        )[0]

    inner, outs = {}, {}

    def cumul_in():
        return plain(held_cumul[0])

    state_sums = [jnp.zeros(sums_shape.shape, f32)]

    def inner_work(part, after):
        inner[part], = part.call(
            inner_kernel,
            [plain(queries), plain(key_vecs), plain(value_vecs), cumul_in()],
            [give(local)], after=after, cost=2.2,
        )
        return inner[part]

    def output_work(part, before, after):
        outs[part], sums = part.call(
            output_kernel,
            [plain(inner[part]), plain(queries), plain(cotangent), plain(gain),
             cumul_in(), plain(before), plain(state_sums[0])],
            [give(local), give(sums_shape)],
            scratch=[pltpu.VMEM((tokens, HEAD_DIM), f32)] * 2, after=after, cost=1.4,
        )
        state_sums[0] = sums
        return sums

    inner_order = [part for c in range(CHUNKS) for part in (mine_parts[c], their_parts[c])]
    works = [functools.partial(inner_work, part) for part in inner_order]
    mine, theirs, last = chain(
        forward_piece, True, works[:1], works[1:],
        lambda c, own, after: output_work(mine_parts[c], own, after),
    )
    for c in range(CHUNKS):
        last = (output_work(their_parts[c], theirs[c], last),)

    sums = state_sums[0]
    shares = [sums] + [
        lax.ppermute(sums, "head", [(i, (i + k) % head_count) for i in range(head_count)])
        for k in range(1, head_count)
    ]

    attended, grad_queries, grad_keys, grad_values = [], [], [], []
    grads, inner_grads = {}, {}

    def target(held):
        return tuple(held[-1:])

    def backward_piece(part, after):
        before = target(attended)
        whole_out, grads[part], piece = part.call(
            functools.partial(grad_kernel, features),
            [plain(outs[part]), plain(cotangent), plain(gain), plain(queries),
             cumul_in()] + [plain(share) for share in shares],
            [(whole, part.full_spec()), give(local_low), give(wide_state)],
            after=before + tuple(after), aliases={7 + head_count: 0} if before else None, cost=2.0,
        )
        attended.append(whole_out)
        return piece

    def backward_work(part, before, after):
        held = target(grad_queries)
        whole_out, *inner_grads[part] = part.call(
            backward_kernel,
            [plain(queries), plain(key_vecs), plain(value_vecs),
             plain(grads[part]), cumul_in(), plain(before)],
            [(whole, part.full_spec()), give(local), give(local)],
            after=held + tuple(after), aliases={8: 0} if held else None, cost=4.3,
        )
        grad_queries.append(whole_out)
        return inner_grads[part][0]

    def final_work(part, before, after):
        held = target(grad_keys) + target(grad_values)
        whole_key, whole_value = part.call(
            final_kernel,
            [plain(inner_grads[part][0]), plain(inner_grads[part][1]),
             plain(key_vecs), plain(value_vecs), cumul_in(), plain(before)],
            [(whole, part.full_spec())] * 2,
            after=held + tuple(after), aliases={8: 0, 9: 1} if held else None, cost=2.0,
        )
        grad_keys.append(whole_key)
        grad_values.append(whole_value)
        return whole_key

    works = []
    for c in range(CHUNKS):
        works.append(functools.partial(backward_work, mine_parts[c], mine[c]))
        works.append(functools.partial(backward_work, their_parts[c], theirs[c]))
    mine_after, theirs_after, last = chain(
        backward_piece, False, [], works,
        lambda c, own, after: final_work(mine_parts[c], own, after),
    )
    for c in range(CHUNKS):
        final_work(their_parts[c], theirs_after[c], last)
        last = ()
    return attended[-1], grad_queries[-1], grad_keys[-1], grad_values[-1]


def solution(mesh):
    return jax.shard_map(
        on_device,
        mesh=mesh,
        in_specs=(
            P("seq", "head"),
            P("seq", "head"),
            P("seq", "head"),
            P("seq", "head"),
            P("head"),
            P("seq", "head"),
        ),
        out_specs=(P("seq", "head"), P("seq", "head"), P("seq", "head"), P("seq", "head")),
        check_vma=False,
    )
```

```python
import functools

import jax
import jax.numpy as jnp
from jax import lax
from jax.experimental import pallas as pl
from jax.experimental.pallas import tpu as pltpu
from jax.sharding import PartitionSpec as P

HEAD_DIM = 128
BLOCK = 512
CHUNKS = 2
TILE = 256
epsilon = 1e-06
f32 = jnp.float32
bf16 = jnp.bfloat16

NN = (((1,), (0,)), ((), ()))
NT = (((1,), (1,)), ((), ()))
TN = (((0,), (0,)), ((), ()))


def dot(a, b, dims=NN):
    return lax.dot_general(a, b, dims, preferred_element_type=f32)


def halves(x):
    high = x.astype(bf16)
    return high, (x - high.astype(f32)).astype(bf16)


def column(row):
    return jnp.transpose(jnp.broadcast_to(row, (HEAD_DIM, row.shape[1])))


def wide(col, width):
    return jnp.concatenate([col] * (width // HEAD_DIM), axis=1)


def cumulative(decay):
    length = decay.shape[1]
    first = decay.astype(bf16)
    rest = decay - first.astype(f32)
    second = rest.astype(bf16)
    third = (rest - second.astype(f32)).astype(bf16)
    upto = lax.broadcasted_iota(jnp.int32, (length, length), 0) <= lax.broadcasted_iota(
        jnp.int32, (length, length), 1
    )
    upto = jnp.where(upto, 1.0, 0.0).astype(bf16)
    return dot(first, upto) + dot(second, upto) + dot(third, upto)


def trail_row(row):
    return jnp.exp(row[:, -1:] - row)


def outer_sum(left, scale_row, right):
    scaled = jnp.transpose(left.astype(f32)) * scale_row
    high, low = halves(scaled)
    return dot(high, right) + dot(low, right)


def cols(j):
    return slice(j * HEAD_DIM, (j + 1) * HEAD_DIM)


class Part:
    def __init__(self, chunk, slot, half):
        self.chunk, self.slot, self.half = chunk, slot, half
        self.steps = 2 if half % 4 == 0 else 1
        self.per_step = half // self.steps

    def group(self, info):
        return info[0][0] if self.slot == "mine" else 1 - info[0][0]

    def head(self, info, j):
        return (2 * self.chunk + self.group(info)) * self.half + pl.program_id(0) * self.per_step + j

    def row(self, cumul_ref, info, j):
        return cumul_ref[pl.ds(self.head(info, j), 1), :]

    def wide_cols(self, info, j):
        return pl.ds(pl.multiple_of(self.head(info, j) * HEAD_DIM, HEAD_DIM), HEAD_DIM)

    def state_rows(self, j):
        start = (pl.program_id(0) * self.per_step + j) * HEAD_DIM
        return pl.ds(pl.multiple_of(start, HEAD_DIM), HEAD_DIM)


def store_decays(part, info, cumul_ref, out_ref):
    for j in range(part.per_step):
        row = part.row(cumul_ref, info, j)
        place = part.half * HEAD_DIM + pl.program_id(0) * part.per_step + j
        out_ref[pl.ds(place, 1), :] = jnp.broadcast_to(jnp.exp(row[:, -1:]), (1, HEAD_DIM))


def pieces_kernel(part, info, key_ref, value_ref, cumul_ref, out_ref):
    for j in range(part.per_step):
        row = part.row(cumul_ref, info, j)
        at = part.wide_cols(info, j)
        out_ref[part.state_rows(j), :] = outer_sum(key_ref[:, at], trail_row(row), value_ref[:, at])
    store_decays(part, info, cumul_ref, out_ref)


def first_pieces_kernel(part, info, key_ref, value_ref, decay_ref, out_ref, cumul_ref):
    @pl.when(pl.program_id(0) == 0)
    def _():
        cumul_ref[...] = cumulative(decay_ref[...])

    for j in range(part.per_step):
        row = part.row(cumul_ref, info, j)
        out_ref[part.state_rows(j), :] = outer_sum(
            key_ref[:, cols(j)], trail_row(row), value_ref[:, cols(j)]
        )
    store_decays(part, info, cumul_ref, out_ref)


def inner_kernel(part, info, query_ref, key_ref, value_ref, cumul_ref, out_ref):
    for j in range(part.per_step):
        row = part.row(cumul_ref, info, j)
        col = column(row)
        at = part.wide_cols(info, j)
        query, key, value = query_ref[:, at], key_ref[:, at], value_ref[:, at]
        for top in range(0, BLOCK, TILE):
            end = top + TILE
            scores = dot(query[top:end], key[:end], NT)
            spread = wide(col[top:end], end) - row[:, :end]
            causal = lax.broadcasted_iota(jnp.int32, (TILE, end), 0) + top >= (
                lax.broadcasted_iota(jnp.int32, (TILE, end), 1)
            )
            weights = (scores * jnp.exp(jnp.where(causal, spread, -1e30))).astype(bf16)
            out_ref[top:end, part.state_rows(j)] = dot(weights, value[:end])


def output_kernel(
    part, info, inner_ref, query_ref, cot_ref, gain_ref, cumul_ref, state_ref, before_ref,
    out_ref, sums_ref, square_ref, product_ref,
):
    step = pl.program_id(0)
    squares = jnp.zeros((BLOCK, HEAD_DIM), f32)
    products = jnp.zeros((BLOCK, HEAD_DIM), f32)
    for j in range(part.per_step):
        lead = jnp.exp(column(part.row(cumul_ref, info, j)))
        high, low = halves(state_ref[part.state_rows(j), :])
        at, here = part.wide_cols(info, j), part.state_rows(j)
        query = query_ref[:, at]
        out = inner_ref[:, here] + lead * (dot(query, high) + dot(query, low))
        out_ref[:, here] = out
        squares += out * out
        products += cot_ref[:, at].astype(f32) * gain_ref[:, at] * out

    @pl.when(step == 0)
    def _():
        square_ref[...] = squares
        product_ref[...] = products

    @pl.when(step > 0)
    def _():
        square_ref[...] += squares
        product_ref[...] += products

    @pl.when(step == part.steps - 1)
    def _():
        rows = lax.broadcasted_iota(jnp.int32, (8, HEAD_DIM), 0)
        total = before_ref[...]
        for place, ref in ((0, square_ref), (1, product_ref)):
            pick = jnp.where(rows == place, 1.0, 0.0).astype(bf16)
            high, low = halves(ref[...])
            total += dot(pick, high, NT) + dot(pick, low, NT)
        sums_ref[...] = total


def grad_kernel(features, part, info, out_ref, cot_ref, gain_ref, query_ref, cumul_ref, *refs):
    shares, (attended_ref, grad_ref, piece_ref) = refs[:-3], refs[-3:]
    sums = shares[0][...]
    for share in shares[1:]:
        sums = sums + share[...]
    inverse = lax.rsqrt(sums[0:1] / features + epsilon)
    mean_term = inverse * sums[1:2] / features
    inverse_col, mean_col = column(inverse), column(mean_term)
    for j in range(part.per_step):
        at, here = part.wide_cols(info, j), part.state_rows(j)
        gain = gain_ref[:, at]
        normed = out_ref[:, here] * inverse_col
        attended_ref[:, cols(j)] = (normed * gain).astype(bf16)
        scaled_grad = cot_ref[:, at].astype(f32) * gain
        grad = (inverse_col * (scaled_grad - normed * mean_col)).astype(bf16)
        grad_ref[:, here] = grad
        row = part.row(cumul_ref, info, j)
        piece_ref[part.state_rows(j), :] = outer_sum(query_ref[:, at], jnp.exp(row), grad)
    store_decays(part, info, cumul_ref, piece_ref)


def backward_kernel(
    part, info, query_ref, key_ref, value_ref, grad_ref, cumul_ref, state_ref,
    grad_query_ref, inner_key_ref, inner_value_ref,
):
    for j in range(part.per_step):
        row = part.row(cumul_ref, info, j)
        col = column(row)
        at, here = part.wide_cols(info, j), part.state_rows(j)
        query, key = query_ref[:, at], key_ref[:, at]
        value, grad = value_ref[:, at], grad_ref[:, here]
        high, low = halves(state_ref[part.state_rows(j), :])
        outer = jnp.exp(col) * (dot(grad, high, NT) + dot(grad, low, NT))
        for top in range(0, BLOCK, TILE):
            end = top + TILE
            scores = dot(key[top:end], query[top:], NT)
            grad_scores = dot(value[top:end], grad[top:], NT)
            spread = row[:, top:] - wide(col[top:end], BLOCK - top)
            causal = lax.broadcasted_iota(jnp.int32, spread.shape, 0) <= (
                lax.broadcasted_iota(jnp.int32, spread.shape, 1)
            )
            decays = jnp.exp(jnp.where(causal, spread, -1e30))
            weights = (scores * decays).astype(bf16)
            grad_weights = (grad_scores * decays).astype(bf16)
            inner_value_ref[top:end, here] = dot(weights, grad[top:])
            inner_key_ref[top:end, here] = dot(grad_weights, query[top:])
            inner_query = dot(grad_weights, key[top:end], TN)
            outer = inner_query + outer if top == 0 else jnp.concatenate(
                [outer[:top], outer[top:] + inner_query], axis=0
            )
        grad_query_ref[:, cols(j)] = outer.astype(bf16)


def final_kernel(
    part, info, inner_key_ref, inner_value_ref, key_ref, value_ref, cumul_ref, state_ref,
    grad_key_ref, grad_value_ref,
):
    for j in range(part.per_step):
        trail = column(trail_row(part.row(cumul_ref, info, j)))
        high, low = halves(state_ref[part.state_rows(j), :])
        at, here = part.wide_cols(info, j), part.state_rows(j)
        key, value = key_ref[:, at], value_ref[:, at]
        grad_key_ref[:, cols(j)] = (
            inner_key_ref[:, here] + trail * (dot(value, high, NT) + dot(value, low, NT))
        ).astype(bf16)
        grad_value_ref[:, cols(j)] = (
            inner_value_ref[:, here] + trail * (dot(key, high) + dot(key, low))
        ).astype(bf16)


def ordered(is_first, half, j, keep_ref, got_ref):
    rows = slice(j * HEAD_DIM, (j + 1) * HEAD_DIM)
    place = slice(half * HEAD_DIM + j, half * HEAD_DIM + j + 1)
    keep, got = keep_ref[rows, :], got_ref[rows, :]
    keep_decay, got_decay = keep_ref[place, :], got_ref[place, :]
    return (
        jnp.where(is_first, keep, got),
        jnp.where(is_first, got, keep),
        jnp.where(is_first, keep_decay, got_decay),
        jnp.where(is_first, got_decay, keep_decay),
    )


def scan_position(places, forward, info):
    member, pair = info[0][0], info[1][0]
    if forward:
        return member == 0, pair
    return member == 1, places - 1 - pair


def copy_kernel(info, in_ref, out_ref):
    out_ref[...] = in_ref[...]


def hop_kernel(half, p, position, info, keep_ref, got_ref, *refs):
    arrived, out_ref = refs[:-1], refs[-1]
    is_first, place = position(info)

    @pl.when(place == p)
    def _():
        for j in range(half):
            first, second, first_decay, second_decay = ordered(is_first, half, j, keep_ref, got_ref)
            value = second_decay * first + second
            for arrived_ref in arrived:
                value += (first_decay * second_decay) * arrived_ref[cols(j), :]
            out_ref[cols(j), :] = value


def last_kernel(half, position, info, keep_ref, got_ref, *refs):
    arrived, (mine_ref, send_ref) = refs[:-2], refs[-2:]
    is_first, place = position(info)
    for p in range(len(arrived) + 1):

        @pl.when(place == p)
        def _():
            for j in range(half):
                first, _, first_decay, _ = ordered(is_first, half, j, keep_ref, got_ref)
                if p == 0:
                    before, after = jnp.zeros_like(first), first
                else:
                    before = arrived[p - 1][cols(j), :]
                    after = first_decay * before + first
                mine_ref[cols(j), :] = jnp.where(is_first, before, after)
                send_ref[cols(j), :] = jnp.where(is_first, after, before)


def on_device(queries, key_vecs, value_vecs, log_decay, norm_gain, cotangent):
    tokens, width = queries.shape
    assert tokens == BLOCK
    heads = width // HEAD_DIM
    half = heads // (2 * CHUNKS)
    head_count = lax.axis_size("head")
    features = width * head_count
    places = lax.axis_size("seq") // 2
    my_index = lax.axis_index("seq")
    member, pair = my_index % 2, my_index // 2
    gain = norm_gain.reshape(1, width)

    any_spec = pl.BlockSpec(memory_space=pl.ANY)
    wide_state = jax.ShapeDtypeStruct((half * HEAD_DIM + 8, HEAD_DIM), f32)
    state = jax.ShapeDtypeStruct((half * HEAD_DIM, HEAD_DIM), f32)
    whole = jax.ShapeDtypeStruct((tokens, width), bf16)
    local = jax.ShapeDtypeStruct((tokens, half * HEAD_DIM), f32)
    local_low = jax.ShapeDtypeStruct((tokens, half * HEAD_DIM), bf16)
    sums_shape = jax.ShapeDtypeStruct((8, tokens), f32)
    info = (member.astype(jnp.int32).reshape(1), pair.astype(jnp.int32).reshape(1))

    def run(kernel, grid, ins, outs, scratch=(), after=(), aliases=None, cost=1.0, limit=24):
        used = len(ins)
        after = [x for i, x in enumerate(after) if not any(x is y for y in after[:i])]

        def body(member_ref, pair_ref, *refs):
            kernel((member_ref, pair_ref), *refs[:used], *refs[used + len(after):])

        return pl.pallas_call(
            body,
            out_shape=[shape for shape, _ in outs],
            grid_spec=pltpu.PrefetchScalarGridSpec(
                num_scalar_prefetch=2,
                grid=(grid,),
                in_specs=[spec for _, spec in ins] + [any_spec] * len(after),
                out_specs=[spec for _, spec in outs],
                scratch_shapes=list(scratch),
            ),
            input_output_aliases=aliases or {},
            compiler_params=pltpu.CompilerParams(vmem_limit_bytes=limit * 1024 * 1024),
            cost_estimate=pl.CostEstimate(
                flops=int(cost * 1e9), bytes_accessed=int(cost * 2.5e6), transcendentals=0
            ),
        )(*info, *[array for array, _ in ins], *after)

    def fixed(shape):
        return pl.BlockSpec(shape, lambda i, *info: (0,) * len(shape))

    def plain(array):
        return array, fixed(array.shape)

    def give(shape):
        return shape, fixed(shape.shape)

    class Views(Part):
        def full_spec(self):
            return pl.BlockSpec(
                (tokens, self.per_step * HEAD_DIM),
                lambda i, *info: (0, (2 * self.chunk + self.group(info)) * self.steps + i),
            )

        def call(self, kernel, ins, outs, **options):
            return run(functools.partial(kernel, self), self.steps, ins, outs, **options)

    mine_parts = [Views(c, "mine", half) for c in range(CHUNKS)]
    their_parts = [Views(c, "theirs", half) for c in range(CHUNKS)]

    swap = [(2 * p + m, 2 * p + 1 - m) for p in range(places) for m in (0, 1)]

    def chain(make_piece, forward, early, filler, on_mine):
        position = functools.partial(scan_position, places, forward)

        def device(place, m):
            return 2 * (place if forward else places - 1 - place) + m

        sends, keeps, last = [], [], ()
        for part in their_parts + mine_parts:
            piece = make_piece(part, last)
            (sends if part.slot == "theirs" else keeps).append(piece)
            last = () if forward and len(sends) == 1 else (piece,)
        for work in early:
            last = (work(last),)
        received = [lax.ppermute(sends[0], "seq", swap)]
        for c in range(1, CHUNKS):
            sent, = run(copy_kernel, 1, [plain(sends[c])], [give(wide_state)], after=last, cost=0.2)
            received.append(lax.ppermute(sent, "seq", swap))
            last = (sent,)
        arrived, mine, theirs, done = {}, [], [], []
        for p in range(places - 1):
            pairs = [(device(p, m), device(p + 1, m)) for m in (0, 1)]
            for c in range(CHUNKS):
                ins = [plain(keeps[c]), plain(received[c])]
                if p > 0:
                    ins.append(plain(arrived[c, p]))
                value, = run(
                    functools.partial(hop_kernel, half, p, position), 1, ins, [give(state)],
                    after=last, cost=0.3,
                )
                arrived[c, p + 1] = lax.ppermute(value, "seq", pairs)
                last = (value,)
            for _ in range(-(-len(filler) // (places - 1 - p)) if p else 1):
                if filler:
                    last = (filler.pop(0)(last),)
        for c in range(CHUNKS):
            ins = [plain(keeps[c]), plain(received[c])]
            ins += [plain(arrived[c, p]) for p in range(1, places)]
            own, send = run(
                functools.partial(last_kernel, half, position), 1, ins, [give(state)] * 2,
                after=last, cost=0.3,
            )
            theirs.append(lax.ppermute(send, "seq", swap))
            mine.append(own)
            last = (send,)
            if c < CHUNKS - 1 and not forward:
                continue
            filler += [functools.partial(on_mine, i, mine[i]) for i in range(len(mine)) if i not in done]
            done += range(len(mine))
            last = (filler.pop(0)(last),)
        while filler:
            last = (filler.pop(0)(last),)
        return mine, theirs, last

    held_cumul = []

    def forward_piece(part, after):
        if not held_cumul:
            piece, cumul = part.call(
                first_pieces_kernel,
                [(key_vecs, part.full_spec()), (value_vecs, part.full_spec()), plain(log_decay.T)],
                [give(wide_state), give(jax.ShapeDtypeStruct((heads, tokens), f32))], cost=1.0,
                limit=60,
            )
            held_cumul.append(cumul)
            return piece
        cumul = held_cumul[0]
        return part.call(
            pieces_kernel, [plain(key_vecs), plain(value_vecs), plain(cumul)],
            [give(wide_state)], after=after, cost=1.0,
        )[0]

    inner, outs = {}, {}

    def cumul_in():
        return plain(held_cumul[0])

    state_sums = [jnp.zeros(sums_shape.shape, f32)]

    def inner_work(part, after):
        inner[part], = part.call(
            inner_kernel,
            [plain(queries), plain(key_vecs), plain(value_vecs), cumul_in()],
            [give(local)], after=after, cost=2.2,
        )
        return inner[part]

    def output_work(part, before, after):
        outs[part], sums = part.call(
            output_kernel,
            [plain(inner[part]), plain(queries), plain(cotangent), plain(gain),
             cumul_in(), plain(before), plain(state_sums[0])],
            [give(local), give(sums_shape)],
            scratch=[pltpu.VMEM((tokens, HEAD_DIM), f32)] * 2, after=after, cost=1.4,
        )
        state_sums[0] = sums
        return sums

    inner_order = [part for c in range(CHUNKS) for part in (mine_parts[c], their_parts[c])]
    works = [functools.partial(inner_work, part) for part in inner_order]
    mine, theirs, last = chain(
        forward_piece, True, works[:1], works[1:],
        lambda c, own, after: output_work(mine_parts[c], own, after),
    )
    for c in range(CHUNKS):
        last = (output_work(their_parts[c], theirs[c], last),)

    sums = state_sums[0]
    shares = [sums] + [
        lax.ppermute(sums, "head", [(i, (i + k) % head_count) for i in range(head_count)])
        for k in range(1, head_count)
    ]

    attended, grad_queries, grad_keys, grad_values = [], [], [], []
    grads, inner_grads = {}, {}

    def target(held):
        return tuple(held[-1:])

    def backward_piece(part, after):
        before = target(attended)
        whole_out, grads[part], piece = part.call(
            functools.partial(grad_kernel, features),
            [plain(outs[part]), plain(cotangent), plain(gain), plain(queries),
             cumul_in()] + [plain(share) for share in shares],
            [(whole, part.full_spec()), give(local_low), give(wide_state)],
            after=before + tuple(after), aliases={7 + head_count: 0} if before else None, cost=2.0,
        )
        attended.append(whole_out)
        return piece

    def backward_work(part, before, after):
        held = target(grad_queries)
        whole_out, *inner_grads[part] = part.call(
            backward_kernel,
            [plain(queries), plain(key_vecs), plain(value_vecs),
             plain(grads[part]), cumul_in(), plain(before)],
            [(whole, part.full_spec()), give(local), give(local)],
            after=held + tuple(after), aliases={8: 0} if held else None, cost=4.3,
        )
        grad_queries.append(whole_out)
        return inner_grads[part][0]

    def final_work(part, before, after):
        held = target(grad_keys) + target(grad_values)
        whole_key, whole_value = part.call(
            final_kernel,
            [plain(inner_grads[part][0]), plain(inner_grads[part][1]),
             plain(key_vecs), plain(value_vecs), cumul_in(), plain(before)],
            [(whole, part.full_spec())] * 2,
            after=held + tuple(after), aliases={8: 0, 9: 1} if held else None, cost=2.0,
        )
        grad_keys.append(whole_key)
        grad_values.append(whole_value)
        return whole_key

    works = []
    for c in range(CHUNKS):
        works.append(functools.partial(backward_work, mine_parts[c], mine[c]))
        works.append(functools.partial(backward_work, their_parts[c], theirs[c]))
    mine_after, theirs_after, last = chain(
        backward_piece, False, [], works,
        lambda c, own, after: final_work(mine_parts[c], own, after),
    )
    for c in range(CHUNKS):
        final_work(their_parts[c], theirs_after[c], last)
        last = ()
    return attended[-1], grad_queries[-1], grad_keys[-1], grad_values[-1]


def solution(mesh):
    return jax.shard_map(
        on_device,
        mesh=mesh,
        in_specs=(
            P("seq", "head"),
            P("seq", "head"),
            P("seq", "head"),
            P("seq", "head"),
            P("head"),
            P("seq", "head"),
        ),
        out_specs=(P("seq", "head"), P("seq", "head"), P("seq", "head"), P("seq", "head")),
        check_vma=False,
    )
```

```python
import functools

import jax
import jax.numpy as jnp
from jax import lax
from jax.experimental import pallas as pl
from jax.experimental.pallas import tpu as pltpu
from jax.sharding import PartitionSpec as P

HEAD_DIM = 128
BLOCK = 512
FORWARD_CHUNKS = 4
BACKWARD_CHUNKS = 2
TILE = 256
epsilon = 1e-06
f32 = jnp.float32
bf16 = jnp.bfloat16

NN = (((1,), (0,)), ((), ()))
NT = (((1,), (1,)), ((), ()))
TN = (((0,), (0,)), ((), ()))


def dot(a, b, dims=NN):
    return lax.dot_general(a, b, dims, preferred_element_type=f32)


def halves(x):
    high = x.astype(bf16)
    return high, (x - high.astype(f32)).astype(bf16)


def column(row):
    return jnp.transpose(jnp.broadcast_to(row, (HEAD_DIM, row.shape[1])))


def wide(col, width):
    return jnp.concatenate([col] * (width // HEAD_DIM), axis=1)


def cumulative(decay):
    length = decay.shape[1]
    first = decay.astype(bf16)
    rest = decay - first.astype(f32)
    second = rest.astype(bf16)
    third = (rest - second.astype(f32)).astype(bf16)
    upto = lax.broadcasted_iota(jnp.int32, (length, length), 0) <= lax.broadcasted_iota(
        jnp.int32, (length, length), 1
    )
    upto = jnp.where(upto, 1.0, 0.0).astype(bf16)
    return dot(first, upto) + dot(second, upto) + dot(third, upto)


def trail_row(row):
    return jnp.exp(row[:, -1:] - row)


def outer_sum(left, scale_row, right):
    scaled = jnp.transpose(left.astype(f32)) * scale_row
    high, low = halves(scaled)
    return dot(high, right) + dot(low, right)


def cols(j):
    return slice(j * HEAD_DIM, (j + 1) * HEAD_DIM)


class Part:
    def __init__(self, first, count, slot, group_heads):
        self.first, self.count, self.slot, self.group_heads = first, count, slot, group_heads
        self.steps = 2 if count % 4 == 0 else 1
        self.per_step = count // self.steps

    def group(self, info):
        return info[0][0] if self.slot == "mine" else 1 - info[0][0]

    def head(self, info, o):
        return self.group(info) * self.group_heads + self.first + o

    def row(self, cumul_ref, info, o):
        return cumul_ref[pl.ds(self.head(info, o), 1), :]

    def wide_cols(self, info, o):
        return pl.ds(pl.multiple_of(self.head(info, o) * HEAD_DIM, HEAD_DIM), HEAD_DIM)

    def each(self, body):
        for step in range(self.steps):

            @pl.when(pl.program_id(0) == step)
            def _():
                for j in range(self.per_step):
                    body(step * self.per_step + j, j)


def rows_of(refs, o):
    size = refs[0].shape[0] // HEAD_DIM
    return refs[o // size][cols(o % size), :]


def cols_of(refs, o):
    size = refs[0].shape[1] // HEAD_DIM
    return refs[o // size][:, cols(o % size)]


def store_decay(part, info, cumul_ref, o, out_ref):
    row = part.row(cumul_ref, info, o)
    place = part.count * HEAD_DIM + o
    out_ref[place:place + 1, :] = jnp.broadcast_to(jnp.exp(row[:, -1:]), (1, HEAD_DIM))


def pieces_kernel(part, info, key_ref, value_ref, cumul_ref, out_ref):
    def head(o, j):
        at = part.wide_cols(info, o)
        out_ref[cols(o), :] = outer_sum(
            key_ref[:, at], trail_row(part.row(cumul_ref, info, o)), value_ref[:, at]
        )
        store_decay(part, info, cumul_ref, o, out_ref)

    part.each(head)


def first_pieces_kernel(part, info, key_ref, value_ref, decay_ref, out_ref, cumul_ref):
    @pl.when(pl.program_id(0) == 0)
    def _():
        cumul_ref[...] = cumulative(decay_ref[...])

    def head(o, j):
        out_ref[cols(o), :] = outer_sum(
            key_ref[:, cols(j)], trail_row(part.row(cumul_ref, info, o)), value_ref[:, cols(j)]
        )
        store_decay(part, info, cumul_ref, o, out_ref)

    part.each(head)


def inner_kernel(part, info, query_ref, key_ref, value_ref, cumul_ref, out_ref):
    def head(o, j):
        row = part.row(cumul_ref, info, o)
        col = column(row)
        at = part.wide_cols(info, o)
        query, key, value = query_ref[:, at], key_ref[:, at], value_ref[:, at]
        for top in range(0, BLOCK, TILE):
            end = top + TILE
            scores = dot(query[top:end], key[:end], NT)
            spread = wide(col[top:end], end) - row[:, :end]
            causal = lax.broadcasted_iota(jnp.int32, (TILE, end), 0) + top >= (
                lax.broadcasted_iota(jnp.int32, (TILE, end), 1)
            )
            weights = (scores * jnp.exp(jnp.where(causal, spread, -1e30))).astype(bf16)
            out_ref[top:end, cols(o)] = dot(weights, value[:end])

    part.each(head)


def output_kernel(
    part, offset, info, inner_ref, query_ref, cot_ref, gain_ref, cumul_ref, state_ref, before_ref,
    out_ref, sums_ref, square_ref, product_ref,
):
    def head(o, j):
        lead = jnp.exp(column(part.row(cumul_ref, info, o)))
        high, low = halves(state_ref[cols(o), :])
        at = part.wide_cols(info, o)
        query = query_ref[:, at]
        out = inner_ref[:, cols(offset + o)] + lead * (dot(query, high) + dot(query, low))
        out_ref[:, cols(o)] = out
        squares = out * out
        products = cot_ref[:, at].astype(f32) * gain_ref[:, at] * out
        if o == 0:
            square_ref[...] = squares
            product_ref[...] = products
        else:
            square_ref[...] += squares
            product_ref[...] += products

    part.each(head)

    @pl.when(pl.program_id(0) == part.steps - 1)
    def _():
        rows = lax.broadcasted_iota(jnp.int32, (8, HEAD_DIM), 0)
        total = before_ref[...]
        for place, ref in ((0, square_ref), (1, product_ref)):
            pick = jnp.where(rows == place, 1.0, 0.0).astype(bf16)
            high, low = halves(ref[...])
            total += dot(pick, high, NT) + dot(pick, low, NT)
        sums_ref[...] = total


def grad_kernel(features, part, held, info, *refs):
    outs, (cot_ref, gain_ref, query_ref, cumul_ref, *refs) = refs[:held], refs[held:]
    shares, (attended_ref, grad_ref, piece_ref) = refs[:-3], refs[-3:]
    sums = shares[0][...]
    for share in shares[1:]:
        sums = sums + share[...]
    inverse = lax.rsqrt(sums[0:1] / features + epsilon)
    mean_term = inverse * sums[1:2] / features
    inverse_col, mean_col = column(inverse), column(mean_term)

    def head(o, j):
        at = part.wide_cols(info, o)
        gain = gain_ref[:, at]
        normed = cols_of(outs, o) * inverse_col
        attended_ref[:, cols(j)] = (normed * gain).astype(bf16)
        scaled_grad = cot_ref[:, at].astype(f32) * gain
        grad = (inverse_col * (scaled_grad - normed * mean_col)).astype(bf16)
        grad_ref[:, cols(o)] = grad
        lead = jnp.exp(part.row(cumul_ref, info, o))
        piece_ref[cols(o), :] = outer_sum(query_ref[:, at], lead, grad)
        store_decay(part, info, cumul_ref, o, piece_ref)

    part.each(head)


def backward_kernel(part, info, query_ref, key_ref, value_ref, grad_ref, cumul_ref, *refs):
    states, (grad_query_ref, inner_key_ref, inner_value_ref) = refs[:-3], refs[-3:]

    def head(o, j):
        row = part.row(cumul_ref, info, o)
        col = column(row)
        at = part.wide_cols(info, o)
        query, key = query_ref[:, at], key_ref[:, at]
        value, grad = value_ref[:, at], grad_ref[:, cols(o)]
        high, low = halves(rows_of(states, o))
        outer = jnp.exp(col) * (dot(grad, high, NT) + dot(grad, low, NT))
        for top in range(0, BLOCK, TILE):
            end = top + TILE
            scores = dot(key[top:end], query[top:], NT)
            grad_scores = dot(value[top:end], grad[top:], NT)
            spread = row[:, top:] - wide(col[top:end], BLOCK - top)
            causal = lax.broadcasted_iota(jnp.int32, spread.shape, 0) <= (
                lax.broadcasted_iota(jnp.int32, spread.shape, 1)
            )
            decays = jnp.exp(jnp.where(causal, spread, -1e30))
            weights = (scores * decays).astype(bf16)
            grad_weights = (grad_scores * decays).astype(bf16)
            inner_value_ref[top:end, cols(o)] = dot(weights, grad[top:])
            inner_key_ref[top:end, cols(o)] = dot(grad_weights, query[top:])
            inner_query = dot(grad_weights, key[top:end], TN)
            outer = inner_query + outer if top == 0 else jnp.concatenate(
                [outer[:top], outer[top:] + inner_query], axis=0
            )
        grad_query_ref[:, cols(j)] = outer.astype(bf16)

    part.each(head)


def final_kernel(
    part, info, inner_key_ref, inner_value_ref, key_ref, value_ref, cumul_ref, state_ref,
    grad_key_ref, grad_value_ref,
):
    def head(o, j):
        trail = column(trail_row(part.row(cumul_ref, info, o)))
        high, low = halves(state_ref[cols(o), :])
        at = part.wide_cols(info, o)
        key, value = key_ref[:, at], value_ref[:, at]
        grad_key_ref[:, cols(j)] = (
            inner_key_ref[:, cols(o)] + trail * (dot(value, high, NT) + dot(value, low, NT))
        ).astype(bf16)
        grad_value_ref[:, cols(j)] = (
            inner_value_ref[:, cols(o)] + trail * (dot(key, high) + dot(key, low))
        ).astype(bf16)

    part.each(head)


def ordered(is_first, half, j, keep_ref, got_ref):
    rows = slice(j * HEAD_DIM, (j + 1) * HEAD_DIM)
    place = slice(half * HEAD_DIM + j, half * HEAD_DIM + j + 1)
    keep, got = keep_ref[rows, :], got_ref[rows, :]
    keep_decay, got_decay = keep_ref[place, :], got_ref[place, :]
    return (
        jnp.where(is_first, keep, got),
        jnp.where(is_first, got, keep),
        jnp.where(is_first, keep_decay, got_decay),
        jnp.where(is_first, got_decay, keep_decay),
    )


def scan_position(places, forward, info):
    member, pair = info[0][0], info[1][0]
    if forward:
        return member == 0, pair
    return member == 1, places - 1 - pair


def copy_kernel(info, in_ref, out_ref):
    out_ref[...] = in_ref[...]


def hop_kernel(half, p, position, info, keep_ref, got_ref, *refs):
    arrived, out_ref = refs[:-1], refs[-1]
    is_first, place = position(info)

    @pl.when(place == p)
    def _():
        for j in range(half):
            first, second, first_decay, second_decay = ordered(is_first, half, j, keep_ref, got_ref)
            value = second_decay * first + second
            for arrived_ref in arrived:
                value += (first_decay * second_decay) * arrived_ref[cols(j), :]
            out_ref[cols(j), :] = value


def last_kernel(half, position, info, keep_ref, got_ref, *refs):
    arrived, (mine_ref, send_ref) = refs[:-2], refs[-2:]
    is_first, place = position(info)
    for p in range(len(arrived) + 1):

        @pl.when(place == p)
        def _():
            for j in range(half):
                first, _, first_decay, _ = ordered(is_first, half, j, keep_ref, got_ref)
                if p == 0:
                    before, after = jnp.zeros_like(first), first
                else:
                    before = arrived[p - 1][cols(j), :]
                    after = first_decay * before + first
                mine_ref[cols(j), :] = jnp.where(is_first, before, after)
                send_ref[cols(j), :] = jnp.where(is_first, after, before)


def on_device(queries, key_vecs, value_vecs, log_decay, norm_gain, cotangent):
    tokens, width = queries.shape
    assert tokens == BLOCK
    heads = width // HEAD_DIM
    group_heads = heads // 2
    head_count = lax.axis_size("head")
    features = width * head_count
    places = lax.axis_size("seq") // 2
    my_index = lax.axis_index("seq")
    member, pair = my_index % 2, my_index // 2
    gain = norm_gain.reshape(1, width)
    info = (member.astype(jnp.int32).reshape(1), pair.astype(jnp.int32).reshape(1))

    any_spec = pl.BlockSpec(memory_space=pl.ANY)
    whole = jax.ShapeDtypeStruct((tokens, width), bf16)
    sums_shape = jax.ShapeDtypeStruct((8, tokens), f32)

    def states_of(count, extra=0):
        return jax.ShapeDtypeStruct((count * HEAD_DIM + extra, HEAD_DIM), f32)

    def local_of(count, dtype=f32):
        return jax.ShapeDtypeStruct((tokens, count * HEAD_DIM), dtype)

    def run(kernel, grid, ins, outs, scratch=(), after=(), aliases=None, cost=1.0, limit=24):
        used = len(ins)
        after = [x for i, x in enumerate(after) if not any(x is y for y in after[:i])]

        def body(member_ref, pair_ref, *refs):
            kernel((member_ref, pair_ref), *refs[:used], *refs[used + len(after):])

        return pl.pallas_call(
            body,
            out_shape=[shape for shape, _ in outs],
            grid_spec=pltpu.PrefetchScalarGridSpec(
                num_scalar_prefetch=2,
                grid=(grid,),
                in_specs=[spec for _, spec in ins] + [any_spec] * len(after),
                out_specs=[spec for _, spec in outs],
                scratch_shapes=list(scratch),
            ),
            input_output_aliases=aliases or {},
            compiler_params=pltpu.CompilerParams(vmem_limit_bytes=limit * 1024 * 1024),
            cost_estimate=pl.CostEstimate(
                flops=int(cost * 1e9), bytes_accessed=int(cost * 2.5e6), transcendentals=0
            ),
        )(*info, *[array for array, _ in ins], *after)

    def fixed(shape):
        return pl.BlockSpec(shape, lambda i, *info: (0,) * len(shape))

    def plain(array):
        return array, fixed(array.shape)

    def give(shape):
        return shape, fixed(shape.shape)

    class Calls(Part):
        def full_spec(self):
            width = self.per_step
            return pl.BlockSpec(
                (tokens, width * HEAD_DIM),
                lambda i, *info: (
                    0, (self.group(info) * self.group_heads + self.first) // width + i
                ),
            )

        def call(self, kernel, ins, outs, **options):
            return run(functools.partial(kernel, self), self.steps, ins, outs, **options)

    def parts_of(chunks, slot):
        count = group_heads // chunks
        return [Calls(c * count, count, slot, group_heads) for c in range(chunks)]

    swap = [(2 * p + m, 2 * p + 1 - m) for p in range(places) for m in (0, 1)]

    def chain(chunks, make_piece, forward, filler, on_mine, on_theirs):
        position = functools.partial(scan_position, places, forward)
        my_parts, their_parts = parts_of(chunks, "mine"), parts_of(chunks, "theirs")
        count = group_heads // chunks
        state, wide_state = states_of(count), states_of(count, 8)

        def device(place, m):
            return 2 * (place if forward else places - 1 - place) + m

        sends, keeps, received, last = [], [], [], ()

        def exchange(last):
            c = len(received)
            if c == 0 or c >= chunks:
                if c == 0:
                    received.append(lax.ppermute(sends[0], "seq", swap))
                return last
            sent, = run(copy_kernel, 1, [plain(sends[c])], [give(wide_state)], after=last, cost=0.02)
            received.append(lax.ppermute(sent, "seq", swap))
            return (sent,)

        for part in their_parts:
            sends.append(make_piece(part, last))
            last = () if forward and len(sends) == 1 else (sends[-1],)
        last = exchange(last)
        if forward:
            last = exchange(last)
        rest = [functools.partial(make_piece, part) for part in my_parts]
        for make in rest[:1] if forward else rest:
            keeps.append(make(last))
            last = (keeps[-1],)
        if not forward:
            last = exchange(last)
        arrived, mine, theirs, late = {}, [], [], []
        for step in range(chunks + places - 1):
            for p in range(places - 1):
                c = step - p
                if not 0 <= c < chunks:
                    continue
                ins = [plain(keeps[c]), plain(received[c])]
                if p > 0:
                    ins.append(plain(arrived[c, p]))
                value, = run(
                    functools.partial(hop_kernel, count, p, position), 1, ins, [give(state)],
                    after=last, cost=0.3,
                )
                pairs = [(device(p, m), device(p + 1, m)) for m in (0, 1)]
                arrived[c, p + 1] = lax.ppermute(value, "seq", pairs)
                last = (value,)
            last = exchange(last)
            while len(keeps) < chunks:
                keeps.append(rest[len(keeps)](last))
                last = (keeps[-1],)
            c = step + 1 - places
            if c >= 0:
                ins = [plain(keeps[c]), plain(received[c])]
                ins += [plain(arrived[c, p]) for p in range(1, places)]
                own, send = run(
                    functools.partial(last_kernel, count, position), 1, ins, [give(state)] * 2,
                    after=last, cost=0.3,
                )
                theirs.append(lax.ppermute(send, "seq", swap))
                mine.append(own)
                last = (send,)
                filler.append(functools.partial(on_mine, c, own))
                late.append(functools.partial(on_theirs, c, theirs[c]))
                if c >= 2:
                    filler.append(late.pop(0))
                if forward and c >= chunks - 2 and filler:
                    last = (filler.pop(0)(last),)
            if filler:
                last = (filler.pop(0)(last),)
        for work in filler + late:
            last = (work(last),)
        return mine, theirs

    inner, outs = {}, {}
    held_cumul, held_sums = [], [jnp.zeros(sums_shape.shape, f32)]
    back_count = group_heads // BACKWARD_CHUNKS
    front_count = group_heads // FORWARD_CHUNKS
    per_back = back_count // front_count
    back_parts = {slot: parts_of(BACKWARD_CHUNKS, slot) for slot in ("mine", "theirs")}
    front_parts = {slot: parts_of(FORWARD_CHUNKS, slot) for slot in ("mine", "theirs")}

    def cumul_in():
        return plain(held_cumul[0])

    def forward_piece(part, after):
        if not held_cumul:
            piece, cumul = part.call(
                first_pieces_kernel,
                [(key_vecs, part.full_spec()), (value_vecs, part.full_spec()), plain(log_decay.T)],
                [give(states_of(part.count, 8)), give(jax.ShapeDtypeStruct((heads, tokens), f32))],
                cost=0.05, limit=60,
            )
            held_cumul.append(cumul)
            return piece
        return part.call(
            pieces_kernel, [plain(key_vecs), plain(value_vecs), cumul_in()],
            [give(states_of(part.count, 8))], after=after, cost=0.05,
        )[0]

    def inner_work(slot, c, after):
        part = back_parts[slot][c]
        inner[slot, c], = part.call(
            inner_kernel, [plain(queries), plain(key_vecs), plain(value_vecs), cumul_in()],
            [give(local_of(part.count))], after=after, cost=2.2 if inner else 0.1,
        )
        return inner[slot, c]

    def output_work(slot, c, before, after):
        part = front_parts[slot][c]
        outs[slot, c], held_sums[0] = run(
            functools.partial(output_kernel, part, c % per_back * front_count), part.steps,
            [plain(inner[slot, c // per_back]), plain(queries), plain(cotangent), plain(gain),
             cumul_in(), plain(before), plain(held_sums[0])],
            [give(local_of(part.count)), give(sums_shape)],
            scratch=[pltpu.VMEM((tokens, HEAD_DIM), f32)] * 2, after=after, cost=0.8,
        )
        return held_sums[0]

    works = [
        functools.partial(inner_work, slot, c)
        for c in range(BACKWARD_CHUNKS) for slot in ("mine", "theirs")
    ]
    mine, theirs = chain(
        FORWARD_CHUNKS, forward_piece, True, works,
        functools.partial(output_work, "mine"), functools.partial(output_work, "theirs"),
    )
    states = {"mine": mine, "theirs": theirs}

    sums = held_sums[0]
    shares = [sums] + [
        lax.ppermute(sums, "head", [(i, (i + k) % head_count) for i in range(head_count)])
        for k in range(1, head_count)
    ]

    attended, grad_queries, grad_keys, grad_values = [], [], [], []
    grads, inner_grads = {}, {}

    def target(held):
        return tuple(held[-1:])

    def covered(c):
        return range(c * per_back, (c + 1) * per_back)

    def backward_piece(part, after):
        before = target(attended)
        c = part.first // part.count
        ins = [plain(outs[part.slot, i]) for i in covered(c)]
        ins += [plain(cotangent), plain(gain), plain(queries), cumul_in()]
        ins += [plain(share) for share in shares]
        whole_out, grads[part.slot, c], piece = run(
            functools.partial(grad_kernel, features, part, per_back), part.steps, ins,
            [(whole, part.full_spec()), give(local_of(part.count, bf16)),
             give(states_of(part.count, 8))],
            after=before + tuple(after), aliases={2 + len(ins): 0} if before else None, cost=2.0,
        )
        attended.append(whole_out)
        return piece

    def backward_work(slot, c, after):
        part, held = back_parts[slot][c], target(grad_queries)
        ins = [plain(queries), plain(key_vecs), plain(value_vecs), plain(grads[slot, c]), cumul_in()]
        ins += [plain(states[slot][i]) for i in covered(c)]
        whole_out, *inner_grads[slot, c] = part.call(
            backward_kernel, ins,
            [(whole, part.full_spec()), give(local_of(part.count)), give(local_of(part.count))],
            after=held + tuple(after), aliases={2 + len(ins): 0} if held else None, cost=4.3,
        )
        grad_queries.append(whole_out)
        return inner_grads[slot, c][0]

    def final_work(slot, c, before, after):
        part, held = back_parts[slot][c], target(grad_keys) + target(grad_values)
        ins = [plain(array) for array in (*inner_grads[slot, c], key_vecs, value_vecs)]
        ins += [cumul_in(), plain(before)]
        whole_key, whole_value = part.call(
            final_kernel, ins, [(whole, part.full_spec())] * 2, after=held + tuple(after),
            aliases={2 + len(ins): 0, 3 + len(ins): 1} if held else None, cost=2.0,
        )
        grad_keys.append(whole_key)
        grad_values.append(whole_value)
        return whole_key

    works = [
        functools.partial(backward_work, slot, c)
        for c in range(BACKWARD_CHUNKS) for slot in ("mine", "theirs")
    ]
    chain(
        BACKWARD_CHUNKS, backward_piece, False, works,
        functools.partial(final_work, "mine"), functools.partial(final_work, "theirs"),
    )
    return attended[-1], grad_queries[-1], grad_keys[-1], grad_values[-1]


def solution(mesh):
    return jax.shard_map(
        on_device,
        mesh=mesh,
        in_specs=(
            P("seq", "head"),
            P("seq", "head"),
            P("seq", "head"),
            P("seq", "head"),
            P("head"),
            P("seq", "head"),
        ),
        out_specs=(P("seq", "head"), P("seq", "head"), P("seq", "head"), P("seq", "head")),
        check_vma=False,
    )
```

```python
import functools

import jax
import jax.numpy as jnp
from jax import lax
from jax.experimental import pallas as pl
from jax.experimental.pallas import tpu as pltpu
from jax.sharding import PartitionSpec as P

HEAD_DIM = 128
BLOCK = 512
FORWARD_CHUNKS = 2
BACKWARD_CHUNKS = 2
TILE = 256
epsilon = 1e-06
f32 = jnp.float32
bf16 = jnp.bfloat16

NN = (((1,), (0,)), ((), ()))
NT = (((1,), (1,)), ((), ()))
TN = (((0,), (0,)), ((), ()))


def dot(a, b, dims=NN):
    return lax.dot_general(a, b, dims, preferred_element_type=f32)


def halves(x):
    high = x.astype(bf16)
    return high, (x - high.astype(f32)).astype(bf16)


def column(row):
    return jnp.transpose(jnp.broadcast_to(row, (HEAD_DIM, row.shape[1])))


def wide(col, width):
    return jnp.concatenate([col] * (width // HEAD_DIM), axis=1)


def cumulative(decay):
    length = decay.shape[1]
    first = decay.astype(bf16)
    rest = decay - first.astype(f32)
    second = rest.astype(bf16)
    third = (rest - second.astype(f32)).astype(bf16)
    upto = lax.broadcasted_iota(jnp.int32, (length, length), 0) <= lax.broadcasted_iota(
        jnp.int32, (length, length), 1
    )
    upto = jnp.where(upto, 1.0, 0.0).astype(bf16)
    return dot(first, upto) + dot(second, upto) + dot(third, upto)


def trail_row(row):
    return jnp.exp(row[:, -1:] - row)


def outer_sum(left, scale_row, right):
    scaled = jnp.transpose(left.astype(f32)) * scale_row
    high, low = halves(scaled)
    return dot(high, right) + dot(low, right)


def cols(j):
    return slice(j * HEAD_DIM, (j + 1) * HEAD_DIM)


class Part:
    def __init__(self, first, count, slot, group_heads):
        self.first, self.count, self.slot, self.group_heads = first, count, slot, group_heads
        self.steps = 2 if count % 4 == 0 else 1
        self.per_step = count // self.steps

    def group(self, info):
        return info[0][0] if self.slot == "mine" else 1 - info[0][0]

    def head(self, info, o):
        return self.group(info) * self.group_heads + self.first + o

    def row(self, cumul_ref, info, o):
        return cumul_ref[pl.ds(self.head(info, o), 1), :]

    def wide_cols(self, info, o):
        return pl.ds(pl.multiple_of(self.head(info, o) * HEAD_DIM, HEAD_DIM), HEAD_DIM)

    def each(self, body):
        for j in range(self.per_step):
            body(pl.program_id(0) * self.per_step + j if self.steps > 1 else j, j)


def at_head(o):
    if isinstance(o, int):
        return cols(o)
    return pl.ds(pl.multiple_of(o * HEAD_DIM, HEAD_DIM), HEAD_DIM)


def chosen(part, values, o, j):
    read, refs = values
    if len(refs) == 1:
        return read(refs[0], at_head(o))
    found = read(refs[0], cols(j))
    for step in range(1, part.steps):
        found = jnp.where(pl.program_id(0) == step, read(refs[step], cols(j)), found)
    return found


def store_decay(part, info, cumul_ref, o, out_ref):
    row = part.row(cumul_ref, info, o)
    out_ref[pl.ds(part.count * HEAD_DIM + o, 1), :] = jnp.broadcast_to(
        jnp.exp(row[:, -1:]), (1, HEAD_DIM)
    )


def pieces_kernel(part, info, key_ref, value_ref, cumul_ref, out_ref):
    def head(o, j):
        at = part.wide_cols(info, o)
        out_ref[at_head(o), :] = outer_sum(
            key_ref[:, at], trail_row(part.row(cumul_ref, info, o)), value_ref[:, at]
        )
        store_decay(part, info, cumul_ref, o, out_ref)

    part.each(head)


def first_pieces_kernel(part, info, key_ref, value_ref, decay_ref, out_ref, cumul_ref):
    @pl.when(pl.program_id(0) == 0)
    def _():
        cumul_ref[...] = cumulative(decay_ref[...])

    def head(o, j):
        out_ref[at_head(o), :] = outer_sum(
            key_ref[:, cols(j)], trail_row(part.row(cumul_ref, info, o)), value_ref[:, cols(j)]
        )
        store_decay(part, info, cumul_ref, o, out_ref)

    part.each(head)


def inner_kernel(part, info, query_ref, key_ref, value_ref, cumul_ref, out_ref):
    def head(o, j):
        row = part.row(cumul_ref, info, o)
        col = column(row)
        at = part.wide_cols(info, o)
        query, key, value = query_ref[:, at], key_ref[:, at], value_ref[:, at]
        for top in range(0, BLOCK, TILE):
            end = top + TILE
            scores = dot(query[top:end], key[:end], NT)
            spread = wide(col[top:end], end) - row[:, :end]
            causal = lax.broadcasted_iota(jnp.int32, (TILE, end), 0) + top >= (
                lax.broadcasted_iota(jnp.int32, (TILE, end), 1)
            )
            weights = (scores * jnp.exp(jnp.where(causal, spread, -1e30))).astype(bf16)
            out_ref[top:end, at_head(o)] = dot(weights, value[:end])

    part.each(head)


def output_kernel(
    part, offset, info, inner_ref, query_ref, cot_ref, gain_ref, cumul_ref, state_ref, before_ref,
    out_ref, sums_ref, square_ref, product_ref,
):
    @pl.when(pl.program_id(0) == 0)
    def _():
        square_ref[...] = jnp.zeros_like(square_ref)
        product_ref[...] = jnp.zeros_like(product_ref)

    def head(o, j):
        lead = jnp.exp(column(part.row(cumul_ref, info, o)))
        high, low = halves(state_ref[at_head(o), :])
        at = part.wide_cols(info, o)
        query = query_ref[:, at]
        out = inner_ref[:, at_head(offset + o)] + lead * (dot(query, high) + dot(query, low))
        out_ref[:, at_head(o)] = out
        square_ref[...] += out * out
        product_ref[...] += cot_ref[:, at].astype(f32) * gain_ref[:, at] * out

    part.each(head)

    @pl.when(pl.program_id(0) == part.steps - 1)
    def _():
        rows = lax.broadcasted_iota(jnp.int32, (8, HEAD_DIM), 0)
        total = before_ref[...]
        for place, ref in ((0, square_ref), (1, product_ref)):
            pick = jnp.where(rows == place, 1.0, 0.0).astype(bf16)
            high, low = halves(ref[...])
            total += dot(pick, high, NT) + dot(pick, low, NT)
        sums_ref[...] = total


def grad_kernel(features, part, held, info, *refs):
    outs, (cot_ref, gain_ref, query_ref, cumul_ref, *refs) = refs[:held], refs[held:]
    shares, (attended_ref, grad_ref, piece_ref) = refs[:-3], refs[-3:]
    sums = shares[0][...]
    for share in shares[1:]:
        sums = sums + share[...]
    inverse = lax.rsqrt(sums[0:1] / features + epsilon)
    mean_term = inverse * sums[1:2] / features
    inverse_col, mean_col = column(inverse), column(mean_term)

    def head(o, j):
        at = part.wide_cols(info, o)
        gain = gain_ref[:, at]
        normed = chosen(part, (lambda ref, at: ref[:, at], outs), o, j) * inverse_col
        attended_ref[:, cols(j)] = (normed * gain).astype(bf16)
        scaled_grad = cot_ref[:, at].astype(f32) * gain
        grad = (inverse_col * (scaled_grad - normed * mean_col)).astype(bf16)
        grad_ref[:, at_head(o)] = grad
        lead = jnp.exp(part.row(cumul_ref, info, o))
        piece_ref[at_head(o), :] = outer_sum(query_ref[:, at], lead, grad)
        store_decay(part, info, cumul_ref, o, piece_ref)

    part.each(head)


def backward_kernel(part, info, query_ref, key_ref, value_ref, grad_ref, cumul_ref, *refs):
    states, (grad_query_ref, inner_key_ref, inner_value_ref) = refs[:-3], refs[-3:]

    def head(o, j):
        row = part.row(cumul_ref, info, o)
        col = column(row)
        at = part.wide_cols(info, o)
        query, key = query_ref[:, at], key_ref[:, at]
        value, grad = value_ref[:, at], grad_ref[:, at_head(o)]
        high, low = halves(chosen(part, (lambda ref, at: ref[at, :], states), o, j))
        outer = jnp.exp(col) * (dot(grad, high, NT) + dot(grad, low, NT))
        for top in range(0, BLOCK, TILE):
            end = top + TILE
            scores = dot(key[top:end], query[top:], NT)
            grad_scores = dot(value[top:end], grad[top:], NT)
            spread = row[:, top:] - wide(col[top:end], BLOCK - top)
            causal = lax.broadcasted_iota(jnp.int32, spread.shape, 0) <= (
                lax.broadcasted_iota(jnp.int32, spread.shape, 1)
            )
            decays = jnp.exp(jnp.where(causal, spread, -1e30))
            weights = (scores * decays).astype(bf16)
            grad_weights = (grad_scores * decays).astype(bf16)
            inner_value_ref[top:end, at_head(o)] = dot(weights, grad[top:])
            inner_key_ref[top:end, at_head(o)] = dot(grad_weights, query[top:])
            inner_query = dot(grad_weights, key[top:end], TN)
            outer = inner_query + outer if top == 0 else jnp.concatenate(
                [outer[:top], outer[top:] + inner_query], axis=0
            )
        grad_query_ref[:, cols(j)] = outer.astype(bf16)

    part.each(head)


def final_kernel(
    part, info, inner_key_ref, inner_value_ref, key_ref, value_ref, cumul_ref, state_ref,
    grad_key_ref, grad_value_ref,
):
    def head(o, j):
        trail = column(trail_row(part.row(cumul_ref, info, o)))
        high, low = halves(state_ref[at_head(o), :])
        at = part.wide_cols(info, o)
        key, value = key_ref[:, at], value_ref[:, at]
        grad_key_ref[:, cols(j)] = (
            inner_key_ref[:, at_head(o)] + trail * (dot(value, high, NT) + dot(value, low, NT))
        ).astype(bf16)
        grad_value_ref[:, cols(j)] = (
            inner_value_ref[:, at_head(o)] + trail * (dot(key, high) + dot(key, low))
        ).astype(bf16)

    part.each(head)


def ordered(is_first, half, j, keep_ref, got_ref):
    rows = slice(j * HEAD_DIM, (j + 1) * HEAD_DIM)
    place = slice(half * HEAD_DIM + j, half * HEAD_DIM + j + 1)
    keep, got = keep_ref[rows, :], got_ref[rows, :]
    keep_decay, got_decay = keep_ref[place, :], got_ref[place, :]
    return (
        jnp.where(is_first, keep, got),
        jnp.where(is_first, got, keep),
        jnp.where(is_first, keep_decay, got_decay),
        jnp.where(is_first, got_decay, keep_decay),
    )


def scan_position(places, forward, info):
    member, pair = info[0][0], info[1][0]
    if forward:
        return member == 0, pair
    return member == 1, places - 1 - pair


def copy_kernel(info, in_ref, out_ref):
    out_ref[...] = in_ref[...]


def hop_kernel(half, p, position, info, keep_ref, got_ref, *refs):
    arrived, out_ref = refs[:-1], refs[-1]
    is_first, place = position(info)

    @pl.when(place == p)
    def _():
        for j in range(half):
            first, second, first_decay, second_decay = ordered(is_first, half, j, keep_ref, got_ref)
            value = second_decay * first + second
            for arrived_ref in arrived:
                value += (first_decay * second_decay) * arrived_ref[cols(j), :]
            out_ref[cols(j), :] = value


def last_kernel(half, position, info, keep_ref, got_ref, *refs):
    arrived, (mine_ref, send_ref) = refs[:-2], refs[-2:]
    is_first, place = position(info)
    for p in range(len(arrived) + 1):

        @pl.when(place == p)
        def _():
            for j in range(half):
                first, _, first_decay, _ = ordered(is_first, half, j, keep_ref, got_ref)
                if p == 0:
                    before, after = jnp.zeros_like(first), first
                else:
                    before = arrived[p - 1][cols(j), :]
                    after = first_decay * before + first
                mine_ref[cols(j), :] = jnp.where(is_first, before, after)
                send_ref[cols(j), :] = jnp.where(is_first, after, before)


def on_device(queries, key_vecs, value_vecs, log_decay, norm_gain, cotangent):
    tokens, width = queries.shape
    assert tokens == BLOCK
    heads = width // HEAD_DIM
    group_heads = heads // 2
    head_count = lax.axis_size("head")
    features = width * head_count
    places = lax.axis_size("seq") // 2
    my_index = lax.axis_index("seq")
    member, pair = my_index % 2, my_index // 2
    gain = norm_gain.reshape(1, width)
    info = (member.astype(jnp.int32).reshape(1), pair.astype(jnp.int32).reshape(1))

    any_spec = pl.BlockSpec(memory_space=pl.ANY)
    whole = jax.ShapeDtypeStruct((tokens, width), bf16)
    sums_shape = jax.ShapeDtypeStruct((8, tokens), f32)

    def states_of(count, extra=0):
        return jax.ShapeDtypeStruct((count * HEAD_DIM + extra, HEAD_DIM), f32)

    def local_of(count, dtype=f32):
        return jax.ShapeDtypeStruct((tokens, count * HEAD_DIM), dtype)

    def run(kernel, grid, ins, outs, scratch=(), after=(), aliases=None, cost=1.0, limit=24):
        used = len(ins)
        after = [x for i, x in enumerate(after) if not any(x is y for y in after[:i])]

        def body(member_ref, pair_ref, *refs):
            kernel((member_ref, pair_ref), *refs[:used], *refs[used + len(after):])

        return pl.pallas_call(
            body,
            out_shape=[shape for shape, _ in outs],
            grid_spec=pltpu.PrefetchScalarGridSpec(
                num_scalar_prefetch=2,
                grid=(grid,),
                in_specs=[spec for _, spec in ins] + [any_spec] * len(after),
                out_specs=[spec for _, spec in outs],
                scratch_shapes=list(scratch),
            ),
            input_output_aliases=aliases or {},
            compiler_params=pltpu.CompilerParams(vmem_limit_bytes=limit * 1024 * 1024),
            cost_estimate=pl.CostEstimate(
                flops=int(cost * 1e9), bytes_accessed=int(cost * 2.5e6), transcendentals=0
            ),
        )(*info, *[array for array, _ in ins], *after)

    def fixed(shape):
        return pl.BlockSpec(shape, lambda i, *info: (0,) * len(shape))

    def plain(array):
        return array, fixed(array.shape)

    def give(shape):
        return shape, fixed(shape.shape)

    class Calls(Part):
        def full_spec(self):
            width = self.per_step
            return pl.BlockSpec(
                (tokens, width * HEAD_DIM),
                lambda i, *info: (
                    0, (self.group(info) * self.group_heads + self.first) // width + i
                ),
            )

        def call(self, kernel, ins, outs, **options):
            return run(functools.partial(kernel, self), self.steps, ins, outs, **options)

    def parts_of(chunks, slot):
        count = group_heads // chunks
        return [Calls(c * count, count, slot, group_heads) for c in range(chunks)]

    swap = [(2 * p + m, 2 * p + 1 - m) for p in range(places) for m in (0, 1)]

    def chain(chunks, make_piece, forward, filler, on_mine, on_theirs):
        position = functools.partial(scan_position, places, forward)
        my_parts, their_parts = parts_of(chunks, "mine"), parts_of(chunks, "theirs")
        count = group_heads // chunks
        state, wide_state = states_of(count), states_of(count, 8)

        def device(place, m):
            return 2 * (place if forward else places - 1 - place) + m

        sends, keeps, received, last = [], [], [], ()

        def exchange(last):
            c = len(received)
            if c == 0 or c >= chunks:
                if c == 0:
                    received.append(lax.ppermute(sends[0], "seq", swap))
                return last
            sent, = run(copy_kernel, 1, [plain(sends[c])], [give(wide_state)], after=last, cost=0.02)
            received.append(lax.ppermute(sent, "seq", swap))
            return (sent,)

        for part in their_parts:
            sends.append(make_piece(part, last))
            last = () if forward and len(sends) == 1 else (sends[-1],)
        last = exchange(last)
        if forward:
            last = exchange(last)
        rest = [functools.partial(make_piece, part) for part in my_parts]
        for make in rest[:1] if forward else rest:
            keeps.append(make(last))
            last = (keeps[-1],)
        if not forward:
            last = exchange(last)
        arrived, mine, theirs, late = {}, [], [], []
        for step in range(chunks + places - 1):
            for p in range(places - 1):
                c = step - p
                if not 0 <= c < chunks:
                    continue
                ins = [plain(keeps[c]), plain(received[c])]
                if p > 0:
                    ins.append(plain(arrived[c, p]))
                value, = run(
                    functools.partial(hop_kernel, count, p, position), 1, ins, [give(state)],
                    after=last, cost=0.3,
                )
                pairs = [(device(p, m), device(p + 1, m)) for m in (0, 1)]
                arrived[c, p + 1] = lax.ppermute(value, "seq", pairs)
                last = (value,)
            last = exchange(last)
            while len(keeps) < chunks:
                keeps.append(rest[len(keeps)](last))
                last = (keeps[-1],)
            c = step + 1 - places
            if c >= 0:
                ins = [plain(keeps[c]), plain(received[c])]
                ins += [plain(arrived[c, p]) for p in range(1, places)]
                own, send = run(
                    functools.partial(last_kernel, count, position), 1, ins, [give(state)] * 2,
                    after=last, cost=0.3,
                )
                theirs.append(lax.ppermute(send, "seq", swap))
                mine.append(own)
                last = (send,)
                filler.append(functools.partial(on_mine, c, own))
                late.append(functools.partial(on_theirs, c, theirs[c]))
                if c >= 2:
                    filler.append(late.pop(0))
                if forward and c >= chunks - 2 and filler:
                    last = (filler.pop(0)(last),)
            if filler:
                last = (filler.pop(0)(last),)
        for work in filler + late:
            last = (work(last),)
        return mine, theirs

    inner, outs = {}, {}
    held_cumul, held_sums = [], [jnp.zeros(sums_shape.shape, f32)]
    back_count = group_heads // BACKWARD_CHUNKS
    front_count = group_heads // FORWARD_CHUNKS
    per_back = back_count // front_count
    back_parts = {slot: parts_of(BACKWARD_CHUNKS, slot) for slot in ("mine", "theirs")}
    front_parts = {slot: parts_of(FORWARD_CHUNKS, slot) for slot in ("mine", "theirs")}

    def cumul_in():
        return plain(held_cumul[0])

    def forward_piece(part, after):
        if not held_cumul:
            piece, cumul = part.call(
                first_pieces_kernel,
                [(key_vecs, part.full_spec()), (value_vecs, part.full_spec()), plain(log_decay.T)],
                [give(states_of(part.count, 8)), give(jax.ShapeDtypeStruct((heads, tokens), f32))],
                cost=0.05, limit=60,
            )
            held_cumul.append(cumul)
            return piece
        return part.call(
            pieces_kernel, [plain(key_vecs), plain(value_vecs), cumul_in()],
            [give(states_of(part.count, 8))], after=after, cost=0.05,
        )[0]

    def inner_work(slot, c, after):
        part = back_parts[slot][c]
        inner[slot, c], = part.call(
            inner_kernel, [plain(queries), plain(key_vecs), plain(value_vecs), cumul_in()],
            [give(local_of(part.count))], after=after, cost=2.2 if inner else 0.1,
        )
        return inner[slot, c]

    def output_work(slot, c, before, after):
        part = front_parts[slot][c]
        outs[slot, c], held_sums[0] = run(
            functools.partial(output_kernel, part, c % per_back * front_count), part.steps,
            [plain(inner[slot, c // per_back]), plain(queries), plain(cotangent), plain(gain),
             cumul_in(), plain(before), plain(held_sums[0])],
            [give(local_of(part.count)), give(sums_shape)],
            scratch=[pltpu.VMEM((tokens, HEAD_DIM), f32)] * 2, after=after, cost=0.8,
        )
        return held_sums[0]

    works = [
        functools.partial(inner_work, slot, c)
        for c in range(BACKWARD_CHUNKS) for slot in ("mine", "theirs")
    ]
    mine, theirs = chain(
        FORWARD_CHUNKS, forward_piece, True, works,
        functools.partial(output_work, "mine"), functools.partial(output_work, "theirs"),
    )
    states = {"mine": mine, "theirs": theirs}

    sums = held_sums[0]
    shares = [sums] + [
        lax.ppermute(sums, "head", [(i, (i + k) % head_count) for i in range(head_count)])
        for k in range(1, head_count)
    ]

    attended, grad_queries, grad_keys, grad_values = [], [], [], []
    grads, inner_grads = {}, {}

    def target(held):
        return tuple(held[-1:])

    def covered(c):
        return range(c * per_back, (c + 1) * per_back)

    def backward_piece(part, after):
        before = target(attended)
        c = part.first // part.count
        ins = [plain(outs[part.slot, i]) for i in covered(c)]
        ins += [plain(cotangent), plain(gain), plain(queries), cumul_in()]
        ins += [plain(share) for share in shares]
        whole_out, grads[part.slot, c], piece = run(
            functools.partial(grad_kernel, features, part, per_back), part.steps, ins,
            [(whole, part.full_spec()), give(local_of(part.count, bf16)),
             give(states_of(part.count, 8))],
            after=before + tuple(after), aliases={2 + len(ins): 0} if before else None, cost=2.0,
        )
        attended.append(whole_out)
        return piece

    def backward_work(slot, c, after):
        part, held = back_parts[slot][c], target(grad_queries)
        ins = [plain(queries), plain(key_vecs), plain(value_vecs), plain(grads[slot, c]), cumul_in()]
        ins += [plain(states[slot][i]) for i in covered(c)]
        whole_out, *inner_grads[slot, c] = part.call(
            backward_kernel, ins,
            [(whole, part.full_spec()), give(local_of(part.count)), give(local_of(part.count))],
            after=held + tuple(after), aliases={2 + len(ins): 0} if held else None, cost=4.3,
        )
        grad_queries.append(whole_out)
        return inner_grads[slot, c][0]

    def final_work(slot, c, before, after):
        part, held = back_parts[slot][c], target(grad_keys) + target(grad_values)
        ins = [plain(array) for array in (*inner_grads[slot, c], key_vecs, value_vecs)]
        ins += [cumul_in(), plain(before)]
        whole_key, whole_value = part.call(
            final_kernel, ins, [(whole, part.full_spec())] * 2, after=held + tuple(after),
            aliases={2 + len(ins): 0, 3 + len(ins): 1} if held else None, cost=2.0,
        )
        grad_keys.append(whole_key)
        grad_values.append(whole_value)
        return whole_key

    works = [
        functools.partial(backward_work, slot, c)
        for c in range(BACKWARD_CHUNKS) for slot in ("mine", "theirs")
    ]
    chain(
        BACKWARD_CHUNKS, backward_piece, False, works,
        functools.partial(final_work, "mine"), functools.partial(final_work, "theirs"),
    )
    return attended[-1], grad_queries[-1], grad_keys[-1], grad_values[-1]


def solution(mesh):
    return jax.shard_map(
        on_device,
        mesh=mesh,
        in_specs=(
            P("seq", "head"),
            P("seq", "head"),
            P("seq", "head"),
            P("seq", "head"),
            P("head"),
            P("seq", "head"),
        ),
        out_specs=(P("seq", "head"), P("seq", "head"), P("seq", "head"), P("seq", "head")),
        check_vma=False,
    )
```

```python
import functools

import jax
import jax.numpy as jnp
from jax import lax
from jax.experimental import pallas as pl
from jax.experimental.pallas import tpu as pltpu
from jax.sharding import PartitionSpec as P

HEAD_DIM = 128
BLOCK = 512
FORWARD_CHUNKS = 2
BACKWARD_CHUNKS = 2
TILE = 256
epsilon = 1e-06
f32 = jnp.float32
bf16 = jnp.bfloat16

NN = (((1,), (0,)), ((), ()))
NT = (((1,), (1,)), ((), ()))
TN = (((0,), (0,)), ((), ()))


def dot(a, b, dims=NN):
    return lax.dot_general(a, b, dims, preferred_element_type=f32)


def halves(x):
    high = x.astype(bf16)
    return high, (x - high.astype(f32)).astype(bf16)


def column(row):
    return jnp.transpose(jnp.broadcast_to(row, (HEAD_DIM, row.shape[1])))


def wide(col, width):
    return jnp.concatenate([col] * (width // HEAD_DIM), axis=1)


def cumulative(decay):
    length = decay.shape[1]
    first = decay.astype(bf16)
    rest = decay - first.astype(f32)
    second = rest.astype(bf16)
    third = (rest - second.astype(f32)).astype(bf16)
    upto = lax.broadcasted_iota(jnp.int32, (length, length), 0) <= lax.broadcasted_iota(
        jnp.int32, (length, length), 1
    )
    upto = jnp.where(upto, 1.0, 0.0).astype(bf16)
    return dot(first, upto) + dot(second, upto) + dot(third, upto)


def trail_row(row):
    return jnp.exp(row[:, -1:] - row)


def outer_sum(left, scale_row, right):
    scaled = jnp.transpose(left).astype(f32) * scale_row
    return dot(scaled.astype(bf16), right)


def cols(j):
    return slice(j * HEAD_DIM, (j + 1) * HEAD_DIM)


class Part:
    def __init__(self, first, count, slot, group_heads, per_step=2):
        self.first, self.count, self.slot, self.group_heads = first, count, slot, group_heads
        self.per_step = per_step if count % per_step == 0 else 1
        self.steps = count // self.per_step

    def group(self, info):
        return info[0][0] if self.slot == "mine" else 1 - info[0][0]

    def head(self, info, o):
        return self.group(info) * self.group_heads + self.first + o

    def row(self, cumul_ref, info, o):
        return cumul_ref[pl.ds(self.head(info, o), 1), :]

    def wide_cols(self, info, o):
        return pl.ds(pl.multiple_of(self.head(info, o) * HEAD_DIM, HEAD_DIM), HEAD_DIM)

    def each(self, body):
        for j in range(self.per_step):
            body(pl.program_id(0) * self.per_step + j if self.steps > 1 else j, j)


def at_head(o):
    if isinstance(o, int):
        return cols(o)
    return pl.ds(pl.multiple_of(o * HEAD_DIM, HEAD_DIM), HEAD_DIM)


def chosen(part, values, o, j):
    read, refs = values
    if len(refs) == 1:
        return read(refs[0], at_head(o))
    size = part.count // len(refs)
    found = None
    for step in range(part.steps):
        index = step * part.per_step + j
        here = read(refs[index // size], cols(index % size))
        found = here if found is None else jnp.where(pl.program_id(0) == step, here, found)
    return found


def store_decay(part, info, cumul_ref, o, out_ref):
    row = part.row(cumul_ref, info, o)
    out_ref[pl.ds(part.count * HEAD_DIM + o, 1), :] = jnp.broadcast_to(
        jnp.exp(row[:, -1:]), (1, HEAD_DIM)
    )


def pieces_kernel(part, info, key_ref, value_ref, cumul_ref, out_ref):
    def head(o, j):
        at = part.wide_cols(info, o)
        out_ref[at_head(o), :] = outer_sum(
            key_ref[:, at], trail_row(part.row(cumul_ref, info, o)), value_ref[:, at]
        )
        store_decay(part, info, cumul_ref, o, out_ref)

    part.each(head)


def first_pieces_kernel(part, info, key_ref, value_ref, decay_ref, out_ref, cumul_ref):
    @pl.when(pl.program_id(0) == 0)
    def _():
        cumul_ref[...] = cumulative(decay_ref[...])

    def head(o, j):
        out_ref[at_head(o), :] = outer_sum(
            key_ref[:, cols(j)], trail_row(part.row(cumul_ref, info, o)), value_ref[:, cols(j)]
        )
        store_decay(part, info, cumul_ref, o, out_ref)

    part.each(head)


def inner_kernel(part, info, query_ref, key_ref, value_ref, cumul_ref, out_ref):
    def head(o, j):
        row = part.row(cumul_ref, info, o)
        col = column(row)
        at = part.wide_cols(info, o)
        query, key, value = query_ref[:, at], key_ref[:, at], value_ref[:, at]
        for top in range(0, BLOCK, TILE):
            end = top + TILE
            scores = dot(query[top:end], key[:end], NT)
            spread = wide(col[top:end], end) - row[:, :end]
            causal = lax.broadcasted_iota(jnp.int32, (TILE, end), 0) + top >= (
                lax.broadcasted_iota(jnp.int32, (TILE, end), 1)
            )
            weights = (scores * jnp.exp(jnp.where(causal, spread, -1e30))).astype(bf16)
            out_ref[top:end, at_head(o)] = dot(weights, value[:end])

    part.each(head)


def output_kernel(
    part, offset, info, inner_ref, query_ref, cot_ref, gain_ref, cumul_ref, state_ref, before_ref,
    out_ref, sums_ref, square_ref, product_ref,
):
    @pl.when(pl.program_id(0) == 0)
    def _():
        square_ref[...] = jnp.zeros_like(square_ref)
        product_ref[...] = jnp.zeros_like(product_ref)

    def head(o, j):
        lead = jnp.exp(column(part.row(cumul_ref, info, o)))
        at = part.wide_cols(info, o)
        state = state_ref[at_head(o), :].astype(bf16)
        out = inner_ref[:, at_head(offset + o)] + lead * dot(query_ref[:, at], state)
        out_ref[:, at_head(o)] = out
        square_ref[...] += out * out
        product_ref[...] += cot_ref[:, at].astype(f32) * gain_ref[:, at] * out

    part.each(head)

    @pl.when(pl.program_id(0) == part.steps - 1)
    def _():
        rows = lax.broadcasted_iota(jnp.int32, (8, HEAD_DIM), 0)
        total = before_ref[...]
        for place, ref in ((0, square_ref), (1, product_ref)):
            pick = jnp.where(rows == place, 1.0, 0.0).astype(bf16)
            high, low = halves(ref[...])
            total += dot(pick, high, NT) + dot(pick, low, NT)
        sums_ref[...] = total


def grad_kernel(features, part, held, info, *refs):
    outs, (cot_ref, gain_ref, query_ref, cumul_ref, *refs) = refs[:held], refs[held:]
    shares, (attended_ref, grad_ref, piece_ref) = refs[:-3], refs[-3:]
    sums = shares[0][...]
    for share in shares[1:]:
        sums = sums + share[...]
    inverse = lax.rsqrt(sums[0:1] / features + epsilon)
    mean_term = inverse * sums[1:2] / features
    inverse_col, mean_col = column(inverse), column(mean_term)

    def head(o, j):
        at = part.wide_cols(info, o)
        gain = gain_ref[:, at]
        normed = chosen(part, (lambda ref, at: ref[:, at], outs), o, j) * inverse_col
        attended_ref[:, cols(j)] = (normed * gain).astype(bf16)
        scaled_grad = cot_ref[:, at].astype(f32) * gain
        grad = (inverse_col * (scaled_grad - normed * mean_col)).astype(bf16)
        grad_ref[:, at_head(o)] = grad
        lead = jnp.exp(part.row(cumul_ref, info, o))
        piece_ref[at_head(o), :] = outer_sum(query_ref[:, at], lead, grad)
        store_decay(part, info, cumul_ref, o, piece_ref)

    part.each(head)


def backward_kernel(
    part, offset, state_offset, info, query_ref, key_ref, value_ref, grad_ref, cumul_ref, state_ref,
    grad_query_ref, inner_key_ref, inner_value_ref,
):
    def head(o, j):
        row = part.row(cumul_ref, info, o)
        col = column(row)
        at = part.wide_cols(info, o)
        query, key = query_ref[:, at], key_ref[:, at]
        value, grad = value_ref[:, at], grad_ref[:, at_head(offset + o)]
        state = state_ref[at_head(state_offset + o), :].astype(bf16)
        outer = jnp.exp(col) * dot(grad, state, NT)
        for top in range(0, BLOCK, TILE):
            end = top + TILE
            scores = dot(key[top:end], query[top:], NT)
            grad_scores = dot(value[top:end], grad[top:], NT)
            spread = row[:, top:] - wide(col[top:end], BLOCK - top)
            causal = lax.broadcasted_iota(jnp.int32, spread.shape, 0) <= (
                lax.broadcasted_iota(jnp.int32, spread.shape, 1)
            )
            decays = jnp.exp(jnp.where(causal, spread, -1e30))
            weights = (scores * decays).astype(bf16)
            grad_weights = (grad_scores * decays).astype(bf16)
            inner_value_ref[top:end, at_head(o)] = dot(weights, grad[top:]).astype(bf16)
            inner_key_ref[top:end, at_head(o)] = dot(grad_weights, query[top:]).astype(bf16)
            inner_query = dot(grad_weights, key[top:end], TN)
            outer = inner_query + outer if top == 0 else jnp.concatenate(
                [outer[:top], outer[top:] + inner_query], axis=0
            )
        grad_query_ref[:, cols(j)] = outer.astype(bf16)

    part.each(head)


def final_kernel(part, held, info, *refs):
    inner_keys, inner_values, refs = refs[:held], refs[held:2 * held], refs[2 * held:]
    key_ref, value_ref, cumul_ref, state_ref, grad_key_ref, grad_value_ref = refs

    def head(o, j):
        trail = column(trail_row(part.row(cumul_ref, info, o)))
        state = state_ref[at_head(o), :].astype(bf16)
        at = part.wide_cols(info, o)
        inner_key = chosen(part, (lambda ref, at: ref[:, at], inner_keys), o, j).astype(f32)
        inner_value = chosen(part, (lambda ref, at: ref[:, at], inner_values), o, j).astype(f32)
        grad_key_ref[:, cols(j)] = (
            inner_key + trail * dot(value_ref[:, at], state, NT)
        ).astype(bf16)
        grad_value_ref[:, cols(j)] = (inner_value + trail * dot(key_ref[:, at], state)).astype(bf16)

    part.each(head)


def ordered(is_first, half, j, keep_ref, got_ref):
    rows = slice(j * HEAD_DIM, (j + 1) * HEAD_DIM)
    place = slice(half * HEAD_DIM + j, half * HEAD_DIM + j + 1)
    keep, got = keep_ref[rows, :], got_ref[rows, :]
    keep_decay, got_decay = keep_ref[place, :], got_ref[place, :]
    return (
        jnp.where(is_first, keep, got),
        jnp.where(is_first, got, keep),
        jnp.where(is_first, keep_decay, got_decay),
        jnp.where(is_first, got_decay, keep_decay),
    )


def scan_position(places, forward, info):
    member, pair = info[0][0], info[1][0]
    if forward:
        return member == 0, pair
    return member == 1, places - 1 - pair


def copy_kernel(info, in_ref, out_ref):
    out_ref[...] = in_ref[...]


def hop_kernel(half, p, position, info, keep_ref, got_ref, *refs):
    arrived, out_ref = refs[:-1], refs[-1]
    is_first, place = position(info)

    @pl.when(place == p)
    def _():
        for j in range(half):
            first, second, first_decay, second_decay = ordered(is_first, half, j, keep_ref, got_ref)
            value = second_decay * first + second
            for arrived_ref in arrived:
                value += (first_decay * second_decay) * arrived_ref[cols(j), :]
            out_ref[cols(j), :] = value


def last_kernel(half, position, info, keep_ref, got_ref, *refs):
    arrived, (mine_ref, send_ref) = refs[:-2], refs[-2:]
    is_first, place = position(info)
    for p in range(len(arrived) + 1):

        @pl.when(place == p)
        def _():
            for j in range(half):
                first, _, first_decay, _ = ordered(is_first, half, j, keep_ref, got_ref)
                if p == 0:
                    before, after = jnp.zeros_like(first), first
                else:
                    before = arrived[p - 1][cols(j), :]
                    after = first_decay * before + first
                mine_ref[cols(j), :] = jnp.where(is_first, before, after)
                send_ref[cols(j), :] = jnp.where(is_first, after, before)


def on_device(queries, key_vecs, value_vecs, log_decay, norm_gain, cotangent):
    tokens, width = queries.shape
    assert tokens == BLOCK
    heads = width // HEAD_DIM
    group_heads = heads // 2
    head_count = lax.axis_size("head")
    features = width * head_count
    places = lax.axis_size("seq") // 2
    my_index = lax.axis_index("seq")
    member, pair = my_index % 2, my_index // 2
    gain = norm_gain.reshape(1, width)
    info = (member.astype(jnp.int32).reshape(1), pair.astype(jnp.int32).reshape(1))

    any_spec = pl.BlockSpec(memory_space=pl.ANY)
    whole = jax.ShapeDtypeStruct((tokens, width), bf16)
    sums_shape = jax.ShapeDtypeStruct((8, tokens), f32)

    def states_of(count, extra=0):
        return jax.ShapeDtypeStruct((count * HEAD_DIM + extra, HEAD_DIM), f32)

    def local_of(count, dtype=f32):
        return jax.ShapeDtypeStruct((tokens, count * HEAD_DIM), dtype)

    def run(kernel, grid, ins, outs, scratch=(), after=(), aliases=None, cost=1.0, limit=24):
        used = len(ins)
        after = [x for i, x in enumerate(after) if not any(x is y for y in after[:i])]

        def body(member_ref, pair_ref, *refs):
            kernel((member_ref, pair_ref), *refs[:used], *refs[used + len(after):])

        return pl.pallas_call(
            body,
            out_shape=[shape for shape, _ in outs],
            grid_spec=pltpu.PrefetchScalarGridSpec(
                num_scalar_prefetch=2,
                grid=(grid,),
                in_specs=[spec for _, spec in ins] + [any_spec] * len(after),
                out_specs=[spec for _, spec in outs],
                scratch_shapes=list(scratch),
            ),
            input_output_aliases=aliases or {},
            compiler_params=pltpu.CompilerParams(vmem_limit_bytes=limit * 1024 * 1024),
            cost_estimate=pl.CostEstimate(
                flops=int(cost * 1e9), bytes_accessed=int(cost * 2.5e6), transcendentals=0
            ),
        )(*info, *[array for array, _ in ins], *after)

    def fixed(shape):
        return pl.BlockSpec(shape, lambda i, *info: (0,) * len(shape))

    def plain(array):
        return array, fixed(array.shape)

    def give(shape):
        return shape, fixed(shape.shape)

    class Calls(Part):
        def full_spec(self):
            width = self.per_step
            return pl.BlockSpec(
                (tokens, width * HEAD_DIM),
                lambda i, *info: (
                    0, (self.group(info) * self.group_heads + self.first) // width + i
                ),
            )

        def call(self, kernel, ins, outs, **options):
            return run(functools.partial(kernel, self), self.steps, ins, outs, **options)

    def parts_of(chunks, slot, per_step=2):
        count = group_heads // chunks
        return [Calls(c * count, count, slot, group_heads, per_step) for c in range(chunks)]

    swap = [(2 * p + m, 2 * p + 1 - m) for p in range(places) for m in (0, 1)]

    def chain(chunks, make_piece, forward, filler, plan, on_mine, on_theirs):
        position = functools.partial(scan_position, places, forward)
        my_parts, their_parts = parts_of(chunks, "mine"), parts_of(chunks, "theirs")
        count = group_heads // chunks
        state, wide_state = states_of(count), states_of(count, 8)

        def device(place, m):
            return 2 * (place if forward else places - 1 - place) + m

        sends, keeps, received, last = [], [], [], ()

        def exchange(last):
            c = len(received)
            if c == 0 or c >= chunks:
                if c == 0:
                    received.append(lax.ppermute(sends[0], "seq", swap))
                return last
            sent, = run(copy_kernel, 1, [plain(sends[c])], [give(wide_state)], after=last, cost=0.02)
            received.append(lax.ppermute(sent, "seq", swap))
            return (sent,)

        for part in their_parts:
            sends.append(make_piece(part, last))
            last = () if forward and len(sends) == 1 else (sends[-1],)
        last = exchange(last)
        for part in my_parts:
            keeps.append(make_piece(part, last))
            last = (keeps[-1],)
        last = exchange(last)

        def fill(slot, last):
            for _ in range(plan[slot] if slot < len(plan) else 1):
                if filler:
                    last = (filler.pop(0)(last),)
            return last

        last = fill(0, last)
        arrived, mine, theirs, late = {}, [], [], []
        for step in range(chunks + places - 1):
            for p in range(places - 1):
                c = step - p
                if not 0 <= c < chunks:
                    continue
                ins = [plain(keeps[c]), plain(received[c])]
                if p > 0:
                    ins.append(plain(arrived[c, p]))
                value, = run(
                    functools.partial(hop_kernel, count, p, position), 1, ins, [give(state)],
                    after=last, cost=0.3,
                )
                pairs = [(device(p, m), device(p + 1, m)) for m in (0, 1)]
                arrived[c, p + 1] = lax.ppermute(value, "seq", pairs)
                last = (value,)
            last = exchange(last)
            c = step + 1 - places
            if c >= 0:
                ins = [plain(keeps[c]), plain(received[c])]
                ins += [plain(arrived[c, p]) for p in range(1, places)]
                own, send = run(
                    functools.partial(last_kernel, count, position), 1, ins, [give(state)] * 2,
                    after=last, cost=0.3,
                )
                theirs.append(lax.ppermute(send, "seq", swap))
                mine.append(own)
                last = (send,)
                filler.append(functools.partial(on_mine, c, own))
                late.append(functools.partial(on_theirs, c, theirs[c]))
                if c >= 2:
                    filler.append(late.pop(0))
            last = fill(step + 1, last)
        for work in filler + late:
            last = (work(last),)
        return mine, theirs

    inner, outs = {}, {}
    held_cumul, held_sums = [], [jnp.zeros(sums_shape.shape, f32)]
    back_count = group_heads // BACKWARD_CHUNKS
    front_count = group_heads // FORWARD_CHUNKS
    per_back = back_count // front_count
    back_parts = {slot: parts_of(BACKWARD_CHUNKS, slot) for slot in ("mine", "theirs")}
    thin = min(2 * BACKWARD_CHUNKS, group_heads)
    per_thin = thin // BACKWARD_CHUNKS
    thin_parts = {slot: parts_of(thin, slot, 1) for slot in ("mine", "theirs")}
    front_parts = {slot: parts_of(FORWARD_CHUNKS, slot) for slot in ("mine", "theirs")}

    def cumul_in():
        return plain(held_cumul[0])

    def forward_piece(part, after):
        if not held_cumul:
            piece, cumul = part.call(
                first_pieces_kernel,
                [(key_vecs, part.full_spec()), (value_vecs, part.full_spec()), plain(log_decay.T)],
                [give(states_of(part.count, 8)), give(jax.ShapeDtypeStruct((heads, tokens), f32))],
                cost=0.05, limit=60,
            )
            held_cumul.append(cumul)
            return piece
        return part.call(
            pieces_kernel, [plain(key_vecs), plain(value_vecs), cumul_in()],
            [give(states_of(part.count, 8))], after=after, cost=0.05,
        )[0]

    def inner_work(slot, c, after):
        part = back_parts[slot][c]
        inner[slot, c], = part.call(
            inner_kernel, [plain(queries), plain(key_vecs), plain(value_vecs), cumul_in()],
            [give(local_of(part.count))], after=after, cost=2.2 if inner else 0.1,
        )
        return inner[slot, c]

    def output_work(slot, c, before, after):
        part = front_parts[slot][c]
        outs[slot, c], held_sums[0] = run(
            functools.partial(output_kernel, part, c % per_back * front_count), part.steps,
            [plain(inner[slot, c // per_back]), plain(queries), plain(cotangent), plain(gain),
             cumul_in(), plain(before), plain(held_sums[0])],
            [give(local_of(part.count)), give(sums_shape)],
            scratch=[pltpu.VMEM((tokens, HEAD_DIM), f32)] * 2, after=after, cost=0.8,
        )
        return held_sums[0]

    works = [
        functools.partial(inner_work, slot, c)
        for c in range(BACKWARD_CHUNKS) for slot in ("mine", "theirs")
    ]
    mine, theirs = chain(
        FORWARD_CHUNKS, forward_piece, True, works, (1, 0, 1, 1, 2),
        functools.partial(output_work, "mine"), functools.partial(output_work, "theirs"),
    )
    states = {"mine": mine, "theirs": theirs}

    sums = held_sums[0]
    shares = [sums] + [
        lax.ppermute(sums, "head", [(i, (i + k) % head_count) for i in range(head_count)])
        for k in range(1, head_count)
    ]

    attended, grad_queries, grad_keys, grad_values = [], [], [], []
    grads, inner_grads = {}, {}

    def target(held):
        return tuple(held[-1:])

    def covered(c):
        return range(c * per_back, (c + 1) * per_back)

    def backward_piece(part, after):
        before = target(attended)
        c = part.first // part.count
        ins = [plain(outs[part.slot, i]) for i in covered(c)]
        ins += [plain(cotangent), plain(gain), plain(queries), cumul_in()]
        ins += [plain(share) for share in shares]
        whole_out, grads[part.slot, c], piece = run(
            functools.partial(grad_kernel, features, part, per_back), part.steps, ins,
            [(whole, part.full_spec()), give(local_of(part.count, bf16)),
             give(states_of(part.count, 8))],
            after=before + tuple(after), aliases={2 + len(ins): 0} if before else None, cost=2.0,
        )
        attended.append(whole_out)
        return piece

    def backward_work(slot, c, after):
        part, held = thin_parts[slot][c], target(grad_queries)
        chunk, offset = c // per_thin, part.first % back_count
        ins = [plain(queries), plain(key_vecs), plain(value_vecs), plain(grads[slot, chunk])]
        ins += [cumul_in(), plain(states[slot][part.first // front_count])]
        whole_out, *inner_grads[slot, c] = run(
            functools.partial(backward_kernel, part, offset, part.first % front_count), part.steps, ins,
            [(whole, part.full_spec())] + [give(local_of(part.count, bf16))] * 2,
            after=held + tuple(after), aliases={2 + len(ins): 0} if held else None, cost=2.2,
        )
        grad_queries.append(whole_out)
        return inner_grads[slot, c][0]

    def final_work(slot, c, before, after):
        part, held = back_parts[slot][c], target(grad_keys) + target(grad_values)
        thins = [inner_grads[slot, i] for i in range(c * per_thin, (c + 1) * per_thin)]
        ins = [plain(pair[0]) for pair in thins] + [plain(pair[1]) for pair in thins]
        ins += [plain(key_vecs), plain(value_vecs), cumul_in(), plain(before)]
        whole_key, whole_value = run(
            functools.partial(final_kernel, part, per_thin), part.steps, ins,
            [(whole, part.full_spec())] * 2, after=held + tuple(after),
            aliases={2 + len(ins): 0, 3 + len(ins): 1} if held else None, cost=2.0,
        )
        grad_keys.append(whole_key)
        grad_values.append(whole_value)
        return whole_key

    works = [
        functools.partial(backward_work, slot, c)
        for c in range(thin) for slot in ("mine", "theirs")
    ]
    chain(
        BACKWARD_CHUNKS, backward_piece, False, works, (1, 1, 2, 2, 1, 9),
        functools.partial(final_work, "mine"), functools.partial(final_work, "theirs"),
    )
    return attended[-1], grad_queries[-1], grad_keys[-1], grad_values[-1]


def solution(mesh):
    return jax.shard_map(
        on_device,
        mesh=mesh,
        in_specs=(
            P("seq", "head"),
            P("seq", "head"),
            P("seq", "head"),
            P("seq", "head"),
            P("head"),
            P("seq", "head"),
        ),
        out_specs=(P("seq", "head"), P("seq", "head"), P("seq", "head"), P("seq", "head")),
        check_vma=False,
    )
```

```python
import functools

import jax
import jax.numpy as jnp
from jax import lax
from jax.experimental import pallas as pl
from jax.experimental.pallas import tpu as pltpu
from jax.sharding import PartitionSpec as P

HEAD_DIM = 128
BLOCK = 512
FORWARD_CHUNKS = 2
BACKWARD_CHUNKS = 2
TILE = 256
epsilon = 1e-06
f32 = jnp.float32
bf16 = jnp.bfloat16

NN = (((1,), (0,)), ((), ()))
NT = (((1,), (1,)), ((), ()))
TN = (((0,), (0,)), ((), ()))


def dot(a, b, dims=NN):
    return lax.dot_general(a, b, dims, preferred_element_type=f32)


def halves(x):
    high = x.astype(bf16)
    return high, (x - high.astype(f32)).astype(bf16)


def column(row):
    return jnp.transpose(jnp.broadcast_to(row, (HEAD_DIM, row.shape[1])))


def wide(col, width):
    return jnp.concatenate([col] * (width // HEAD_DIM), axis=1)


def cumulative(decay):
    length = decay.shape[1]
    first = decay.astype(bf16)
    rest = decay - first.astype(f32)
    second = rest.astype(bf16)
    third = (rest - second.astype(f32)).astype(bf16)
    upto = lax.broadcasted_iota(jnp.int32, (length, length), 0) <= lax.broadcasted_iota(
        jnp.int32, (length, length), 1
    )
    upto = jnp.where(upto, 1.0, 0.0).astype(bf16)
    return dot(first, upto) + dot(second, upto) + dot(third, upto)


def trail_row(row):
    return jnp.exp(row[:, -1:] - row)


def outer_sum(left, scale_row, right):
    scaled = jnp.transpose(left.astype(f32)) * scale_row
    high, low = halves(scaled)
    return dot(high, right) + dot(low, right)


def cols(j):
    return slice(j * HEAD_DIM, (j + 1) * HEAD_DIM)


class Part:
    def __init__(self, first, count, slot, group_heads):
        self.first, self.count, self.slot, self.group_heads = first, count, slot, group_heads
        self.steps = 2 if count % 4 == 0 else 1
        self.per_step = count // self.steps

    def group(self, info):
        return info[0][0] if self.slot == "mine" else 1 - info[0][0]

    def head(self, info, o):
        return self.group(info) * self.group_heads + self.first + o

    def row(self, cumul_ref, info, o):
        return cumul_ref[pl.ds(self.head(info, o), 1), :]

    def wide_cols(self, info, o):
        return pl.ds(pl.multiple_of(self.head(info, o) * HEAD_DIM, HEAD_DIM), HEAD_DIM)

    def each(self, body):
        for j in range(self.per_step):
            body(pl.program_id(0) * self.per_step + j if self.steps > 1 else j, j)


def at_head(o):
    if isinstance(o, int):
        return cols(o)
    return pl.ds(pl.multiple_of(o * HEAD_DIM, HEAD_DIM), HEAD_DIM)


def chosen(part, values, o, j):
    read, refs = values
    if len(refs) == 1:
        return read(refs[0], at_head(o))
    found = read(refs[0], cols(j))
    for step in range(1, part.steps):
        found = jnp.where(pl.program_id(0) == step, read(refs[step], cols(j)), found)
    return found


def store_decay(part, info, cumul_ref, o, out_ref):
    row = part.row(cumul_ref, info, o)
    out_ref[pl.ds(part.count * HEAD_DIM + o, 1), :] = jnp.broadcast_to(
        jnp.exp(row[:, -1:]), (1, HEAD_DIM)
    )


def pieces_kernel(part, info, key_ref, value_ref, cumul_ref, out_ref):
    def head(o, j):
        at = part.wide_cols(info, o)
        out_ref[at_head(o), :] = outer_sum(
            key_ref[:, at], trail_row(part.row(cumul_ref, info, o)), value_ref[:, at]
        )
        store_decay(part, info, cumul_ref, o, out_ref)

    part.each(head)


def first_pieces_kernel(part, info, key_ref, value_ref, decay_ref, out_ref, cumul_ref):
    @pl.when(pl.program_id(0) == 0)
    def _():
        cumul_ref[...] = cumulative(decay_ref[...])

    def head(o, j):
        out_ref[at_head(o), :] = outer_sum(
            key_ref[:, cols(j)], trail_row(part.row(cumul_ref, info, o)), value_ref[:, cols(j)]
        )
        store_decay(part, info, cumul_ref, o, out_ref)

    part.each(head)


def inner_kernel(part, info, query_ref, key_ref, value_ref, cumul_ref, out_ref):
    def head(o, j):
        row = part.row(cumul_ref, info, o)
        col = column(row)
        at = part.wide_cols(info, o)
        query, key, value = query_ref[:, at], key_ref[:, at], value_ref[:, at]
        for top in range(0, BLOCK, TILE):
            end = top + TILE
            scores = dot(query[top:end], key[:end], NT)
            spread = wide(col[top:end], end) - row[:, :end]
            causal = lax.broadcasted_iota(jnp.int32, (TILE, end), 0) + top >= (
                lax.broadcasted_iota(jnp.int32, (TILE, end), 1)
            )
            weights = (scores * jnp.exp(jnp.where(causal, spread, -1e30))).astype(bf16)
            out_ref[top:end, at_head(o)] = dot(weights, value[:end])

    part.each(head)


def output_kernel(
    part, offset, info, inner_ref, query_ref, cot_ref, gain_ref, cumul_ref, state_ref, before_ref,
    out_ref, sums_ref, square_ref, product_ref,
):
    @pl.when(pl.program_id(0) == 0)
    def _():
        square_ref[...] = jnp.zeros_like(square_ref)
        product_ref[...] = jnp.zeros_like(product_ref)

    def head(o, j):
        lead = jnp.exp(column(part.row(cumul_ref, info, o)))
        high, low = halves(state_ref[at_head(o), :])
        at = part.wide_cols(info, o)
        query = query_ref[:, at]
        out = inner_ref[:, at_head(offset + o)] + lead * (dot(query, high) + dot(query, low))
        out_ref[:, at_head(o)] = out
        square_ref[...] += out * out
        product_ref[...] += cot_ref[:, at].astype(f32) * gain_ref[:, at] * out

    part.each(head)

    @pl.when(pl.program_id(0) == part.steps - 1)
    def _():
        rows = lax.broadcasted_iota(jnp.int32, (8, HEAD_DIM), 0)
        total = before_ref[...]
        for place, ref in ((0, square_ref), (1, product_ref)):
            pick = jnp.where(rows == place, 1.0, 0.0).astype(bf16)
            high, low = halves(ref[...])
            total += dot(pick, high, NT) + dot(pick, low, NT)
        sums_ref[...] = total


def grad_kernel(features, part, held, info, *refs):
    outs, (cot_ref, gain_ref, query_ref, cumul_ref, *refs) = refs[:held], refs[held:]
    shares, (attended_ref, grad_ref, piece_ref) = refs[:-3], refs[-3:]
    sums = shares[0][...]
    for share in shares[1:]:
        sums = sums + share[...]
    inverse = lax.rsqrt(sums[0:1] / features + epsilon)
    mean_term = inverse * sums[1:2] / features
    inverse_col, mean_col = column(inverse), column(mean_term)

    def head(o, j):
        at = part.wide_cols(info, o)
        gain = gain_ref[:, at]
        normed = chosen(part, (lambda ref, at: ref[:, at], outs), o, j) * inverse_col
        attended_ref[:, cols(j)] = (normed * gain).astype(bf16)
        scaled_grad = cot_ref[:, at].astype(f32) * gain
        grad = (inverse_col * (scaled_grad - normed * mean_col)).astype(bf16)
        grad_ref[:, at_head(o)] = grad
        lead = jnp.exp(part.row(cumul_ref, info, o))
        piece_ref[at_head(o), :] = outer_sum(query_ref[:, at], lead, grad)
        store_decay(part, info, cumul_ref, o, piece_ref)

    part.each(head)


def backward_kernel(part, info, query_ref, key_ref, value_ref, grad_ref, cumul_ref, *refs):
    states, (grad_query_ref, inner_key_ref, inner_value_ref) = refs[:-3], refs[-3:]

    def head(o, j):
        row = part.row(cumul_ref, info, o)
        col = column(row)
        at = part.wide_cols(info, o)
        query, key = query_ref[:, at], key_ref[:, at]
        value, grad = value_ref[:, at], grad_ref[:, at_head(o)]
        high, low = halves(chosen(part, (lambda ref, at: ref[at, :], states), o, j))
        outer = jnp.exp(col) * (dot(grad, high, NT) + dot(grad, low, NT))
        for top in range(0, BLOCK, TILE):
            end = top + TILE
            scores = dot(key[top:end], query[top:], NT)
            grad_scores = dot(value[top:end], grad[top:], NT)
            spread = row[:, top:] - wide(col[top:end], BLOCK - top)
            causal = lax.broadcasted_iota(jnp.int32, spread.shape, 0) <= (
                lax.broadcasted_iota(jnp.int32, spread.shape, 1)
            )
            decays = jnp.exp(jnp.where(causal, spread, -1e30))
            weights = (scores * decays).astype(bf16)
            grad_weights = (grad_scores * decays).astype(bf16)
            inner_value_ref[top:end, at_head(o)] = dot(weights, grad[top:])
            inner_key_ref[top:end, at_head(o)] = dot(grad_weights, query[top:])
            inner_query = dot(grad_weights, key[top:end], TN)
            outer = inner_query + outer if top == 0 else jnp.concatenate(
                [outer[:top], outer[top:] + inner_query], axis=0
            )
        grad_query_ref[:, cols(j)] = outer.astype(bf16)

    part.each(head)


def final_kernel(
    part, info, inner_key_ref, inner_value_ref, key_ref, value_ref, cumul_ref, state_ref,
    grad_key_ref, grad_value_ref, token_ref,
):
    token_ref[...] = jnp.zeros_like(token_ref)

    def head(o, j):
        trail = column(trail_row(part.row(cumul_ref, info, o)))
        high, low = halves(state_ref[at_head(o), :])
        at = part.wide_cols(info, o)
        key, value = key_ref[:, at], value_ref[:, at]
        grad_key_ref[:, cols(j)] = (
            inner_key_ref[:, at_head(o)] + trail * (dot(value, high, NT) + dot(value, low, NT))
        ).astype(bf16)
        grad_value_ref[:, cols(j)] = (
            inner_value_ref[:, at_head(o)] + trail * (dot(key, high) + dot(key, low))
        ).astype(bf16)

    part.each(head)


def ordered(is_first, half, j, keep_ref, got_ref):
    rows = slice(j * HEAD_DIM, (j + 1) * HEAD_DIM)
    place = slice(half * HEAD_DIM + j, half * HEAD_DIM + j + 1)
    keep, got = keep_ref[rows, :], got_ref[rows, :]
    keep_decay, got_decay = keep_ref[place, :], got_ref[place, :]
    return (
        jnp.where(is_first, keep, got),
        jnp.where(is_first, got, keep),
        jnp.where(is_first, keep_decay, got_decay),
        jnp.where(is_first, got_decay, keep_decay),
    )


def scan_position(places, forward, info):
    member, pair = info[0][0], info[1][0]
    if forward:
        return member == 0, pair
    return member == 1, places - 1 - pair


def copy_kernel(info, in_ref, out_ref):
    out_ref[...] = in_ref[...]


def hop_kernel(half, p, position, info, keep_ref, got_ref, *refs):
    arrived, out_ref = refs[:-1], refs[-1]
    is_first, place = position(info)

    @pl.when(place == p)
    def _():
        for j in range(half):
            first, second, first_decay, second_decay = ordered(is_first, half, j, keep_ref, got_ref)
            value = second_decay * first + second
            for arrived_ref in arrived:
                value += (first_decay * second_decay) * arrived_ref[cols(j), :]
            out_ref[cols(j), :] = value


def last_kernel(half, position, info, keep_ref, got_ref, *refs):
    arrived, (mine_ref, send_ref) = refs[:-2], refs[-2:]
    is_first, place = position(info)
    for p in range(len(arrived) + 1):

        @pl.when(place == p)
        def _():
            for j in range(half):
                first, _, first_decay, _ = ordered(is_first, half, j, keep_ref, got_ref)
                if p == 0:
                    before, after = jnp.zeros_like(first), first
                else:
                    before = arrived[p - 1][cols(j), :]
                    after = first_decay * before + first
                mine_ref[cols(j), :] = jnp.where(is_first, before, after)
                send_ref[cols(j), :] = jnp.where(is_first, after, before)


def on_device(queries, key_vecs, value_vecs, log_decay, norm_gain, cotangent):
    tokens, width = queries.shape
    assert tokens == BLOCK
    heads = width // HEAD_DIM
    group_heads = heads // 2
    head_count = lax.axis_size("head")
    features = width * head_count
    places = lax.axis_size("seq") // 2
    my_index = lax.axis_index("seq")
    member, pair = my_index % 2, my_index // 2
    gain = norm_gain.reshape(1, width)
    info = (member.astype(jnp.int32).reshape(1), pair.astype(jnp.int32).reshape(1))

    any_spec = pl.BlockSpec(memory_space=pl.ANY)
    whole = jax.ShapeDtypeStruct((tokens, width), bf16)
    sums_shape = jax.ShapeDtypeStruct((8, tokens), f32)

    def states_of(count, extra=0):
        return jax.ShapeDtypeStruct((count * HEAD_DIM + extra, HEAD_DIM), f32)

    def local_of(count, dtype=f32):
        return jax.ShapeDtypeStruct((tokens, count * HEAD_DIM), dtype)

    def run(kernel, grid, ins, outs, scratch=(), after=(), aliases=None, cost=1.0, limit=24):
        used = len(ins)
        after = [x for i, x in enumerate(after) if not any(x is y for y in after[:i])]

        def body(member_ref, pair_ref, *refs):
            kernel((member_ref, pair_ref), *refs[:used], *refs[used + len(after):])

        return pl.pallas_call(
            body,
            out_shape=[shape for shape, _ in outs],
            grid_spec=pltpu.PrefetchScalarGridSpec(
                num_scalar_prefetch=2,
                grid=(grid,),
                in_specs=[spec for _, spec in ins] + [any_spec] * len(after),
                out_specs=[spec for _, spec in outs],
                scratch_shapes=list(scratch),
            ),
            input_output_aliases=aliases or {},
            compiler_params=pltpu.CompilerParams(vmem_limit_bytes=limit * 1024 * 1024),
            cost_estimate=pl.CostEstimate(
                flops=int(cost * 1e9), bytes_accessed=int(cost * 2.5e6), transcendentals=0
            ),
        )(*info, *[array for array, _ in ins], *after)

    def fixed(shape):
        return pl.BlockSpec(shape, lambda i, *info: (0,) * len(shape))

    def plain(array):
        return array, fixed(array.shape)

    def give(shape):
        return shape, fixed(shape.shape)

    class Calls(Part):
        def full_spec(self):
            width = self.per_step
            return pl.BlockSpec(
                (tokens, width * HEAD_DIM),
                lambda i, *info: (
                    0, (self.group(info) * self.group_heads + self.first) // width + i
                ),
            )

        def call(self, kernel, ins, outs, **options):
            return run(functools.partial(kernel, self), self.steps, ins, outs, **options)

    def parts_of(chunks, slot):
        count = group_heads // chunks
        return [Calls(c * count, count, slot, group_heads) for c in range(chunks)]

    swap = [(2 * p + m, 2 * p + 1 - m) for p in range(places) for m in (0, 1)]

    def chain(chunks, make_piece, forward, filler, on_mine, on_theirs):
        position = functools.partial(scan_position, places, forward)
        my_parts, their_parts = parts_of(chunks, "mine"), parts_of(chunks, "theirs")
        count = group_heads // chunks
        state, wide_state = states_of(count), states_of(count, 8)

        def device(place, m):
            return 2 * (place if forward else places - 1 - place) + m

        sends, keeps, received, last = [], [], [], ()

        def exchange(last):
            c = len(received)
            if c == 0 or c >= chunks:
                if c == 0:
                    received.append(lax.ppermute(sends[0], "seq", swap))
                return last
            sent, = run(copy_kernel, 1, [plain(sends[c])], [give(wide_state)], after=last, cost=0.02)
            received.append(lax.ppermute(sent, "seq", swap))
            return (sent,)

        for part in their_parts:
            sends.append(make_piece(part, last))
            last = () if forward and len(sends) == 1 else (sends[-1],)
        last = exchange(last)
        for part in my_parts:
            keeps.append(make_piece(part, last))
            last = (keeps[-1],)
        last = exchange(last + (received[0],) if forward else last)
        arrived, mine, theirs, late = {}, [], [], []
        for step in range(chunks + places - 1):
            for p in range(places - 1):
                c = step - p
                if not 0 <= c < chunks:
                    continue
                ins = [plain(keeps[c]), plain(received[c])]
                if p > 0:
                    ins.append(plain(arrived[c, p]))
                value, = run(
                    functools.partial(hop_kernel, count, p, position), 1, ins, [give(state)],
                    after=last, cost=0.3,
                )
                pairs = [(device(p, m), device(p + 1, m)) for m in (0, 1)]
                arrived[c, p + 1] = lax.ppermute(value, "seq", pairs)
                last = (value,)
            last = exchange(last)
            if filler:
                last = (filler.pop(0)(last),)
            c = step + 1 - places
            if c >= 0:
                ins = [plain(keeps[c]), plain(received[c])]
                ins += [plain(arrived[c, p]) for p in range(1, places)]
                own, send = run(
                    functools.partial(last_kernel, count, position), 1, ins, [give(state)] * 2,
                    after=last, cost=0.3,
                )
                theirs.append(lax.ppermute(send, "seq", swap))
                mine.append(own)
                last = (send,)
                filler.append(functools.partial(on_mine, c, own))
                late.append(functools.partial(on_theirs, c, theirs[c]))
                if c >= 2:
                    filler.append(late.pop(0))
                last = (filler.pop(0)(last),)
        for work in filler + late:
            last = (work(last),)
        return mine, theirs

    inner, outs = {}, {}
    held_cumul, held_sums = [], [jnp.zeros(sums_shape.shape, f32)]
    back_count = group_heads // BACKWARD_CHUNKS
    front_count = group_heads // FORWARD_CHUNKS
    per_back = back_count // front_count
    back_parts = {slot: parts_of(BACKWARD_CHUNKS, slot) for slot in ("mine", "theirs")}
    front_parts = {slot: parts_of(FORWARD_CHUNKS, slot) for slot in ("mine", "theirs")}

    def cumul_in():
        return plain(held_cumul[0])

    def forward_piece(part, after):
        if not held_cumul:
            piece, cumul = part.call(
                first_pieces_kernel,
                [(key_vecs, part.full_spec()), (value_vecs, part.full_spec()), plain(log_decay.T)],
                [give(states_of(part.count, 8)), give(jax.ShapeDtypeStruct((heads, tokens), f32))],
                cost=0.05, limit=60,
            )
            held_cumul.append(cumul)
            return piece
        return part.call(
            pieces_kernel, [plain(key_vecs), plain(value_vecs), cumul_in()],
            [give(states_of(part.count, 8))], after=after, cost=0.05,
        )[0]

    def inner_work(slot, c, after):
        part = back_parts[slot][c]
        inner[slot, c], = part.call(
            inner_kernel, [plain(queries), plain(key_vecs), plain(value_vecs), cumul_in()],
            [give(local_of(part.count))], after=after, cost=2.2 if inner else 0.1,
        )
        return inner[slot, c]

    def output_work(slot, c, before, after):
        part = front_parts[slot][c]
        outs[slot, c], held_sums[0] = run(
            functools.partial(output_kernel, part, c % per_back * front_count), part.steps,
            [plain(inner[slot, c // per_back]), plain(queries), plain(cotangent), plain(gain),
             cumul_in(), plain(before), plain(held_sums[0])],
            [give(local_of(part.count)), give(sums_shape)],
            scratch=[pltpu.VMEM((tokens, HEAD_DIM), f32)] * 2, after=after, cost=0.8,
        )
        return held_sums[0]

    works = [
        functools.partial(inner_work, slot, c)
        for c in range(BACKWARD_CHUNKS) for slot in ("mine", "theirs")
    ]
    mine, theirs = chain(
        FORWARD_CHUNKS, forward_piece, True, works,
        functools.partial(output_work, "mine"), functools.partial(output_work, "theirs"),
    )
    states = {"mine": mine, "theirs": theirs}

    sums = held_sums[0]
    shares = [sums] + [
        lax.ppermute(sums, "head", [(i, (i + k) % head_count) for i in range(head_count)])
        for k in range(1, head_count)
    ]

    attended, grad_queries, grad_keys, grad_values = [], [], [], []
    grads, inner_grads = {}, {}

    def target(held):
        return tuple(held[-1:])

    def covered(c):
        return range(c * per_back, (c + 1) * per_back)

    def backward_piece(part, after):
        before = target(attended)
        c = part.first // part.count
        ins = [plain(outs[part.slot, i]) for i in covered(c)]
        ins += [plain(cotangent), plain(gain), plain(queries), cumul_in()]
        ins += [plain(share) for share in shares]
        whole_out, grads[part.slot, c], piece = run(
            functools.partial(grad_kernel, features, part, per_back), part.steps, ins,
            [(whole, part.full_spec()), give(local_of(part.count, bf16)),
             give(states_of(part.count, 8))],
            after=before + tuple(after), aliases={2 + len(ins): 0} if before else None, cost=2.0,
        )
        attended.append(whole_out)
        return piece

    def backward_work(slot, c, after):
        part, held = back_parts[slot][c], target(grad_queries)
        ins = [plain(queries), plain(key_vecs), plain(value_vecs), plain(grads[slot, c]), cumul_in()]
        ins += [plain(states[slot][i]) for i in covered(c)]
        whole_out, *inner_grads[slot, c] = part.call(
            backward_kernel, ins,
            [(whole, part.full_spec()), give(local_of(part.count)), give(local_of(part.count))],
            after=held + tuple(after), aliases={2 + len(ins): 0} if held else None, cost=4.3,
        )
        grad_queries.append(whole_out)
        return inner_grads[slot, c][0]

    def final_work(slot, c, before, after):
        part, held = back_parts[slot][c], target(grad_keys) + target(grad_values)
        ins = [plain(array) for array in (*inner_grads[slot, c], key_vecs, value_vecs)]
        ins += [cumul_in(), plain(before)]
        whole_key, whole_value, token = part.call(
            final_kernel, ins,
            [(whole, part.full_spec())] * 2 + [give(jax.ShapeDtypeStruct((8, HEAD_DIM), f32))],
            after=held + tuple(after),
            aliases={2 + len(ins): 0, 3 + len(ins): 1} if held else None, cost=2.0,
        )
        grad_keys.append(whole_key)
        grad_values.append(whole_value)
        return token

    works = [
        functools.partial(backward_work, slot, c)
        for c in range(BACKWARD_CHUNKS) for slot in ("mine", "theirs")
    ]
    chain(
        BACKWARD_CHUNKS, backward_piece, False, works,
        functools.partial(final_work, "mine"), functools.partial(final_work, "theirs"),
    )
    return attended[-1], grad_queries[-1], grad_keys[-1], grad_values[-1]


def solution(mesh):
    return jax.shard_map(
        on_device,
        mesh=mesh,
        in_specs=(
            P("seq", "head"),
            P("seq", "head"),
            P("seq", "head"),
            P("seq", "head"),
            P("head"),
            P("seq", "head"),
        ),
        out_specs=(P("seq", "head"), P("seq", "head"), P("seq", "head"), P("seq", "head")),
        check_vma=False,
    )
```

```python
import functools

import jax
import jax.numpy as jnp
from jax import lax
from jax.experimental import pallas as pl
from jax.experimental.pallas import tpu as pltpu
from jax.sharding import PartitionSpec as P

HEAD_DIM = 128
BLOCK = 512
FORWARD_CHUNKS = 2
BACKWARD_CHUNKS = 2
TILE = 256
epsilon = 1e-06
f32 = jnp.float32
bf16 = jnp.bfloat16

NN = (((1,), (0,)), ((), ()))
NT = (((1,), (1,)), ((), ()))
TN = (((0,), (0,)), ((), ()))


def dot(a, b, dims=NN):
    return lax.dot_general(a, b, dims, preferred_element_type=f32)


def halves(x):
    high = x.astype(bf16)
    return high, (x - high.astype(f32)).astype(bf16)


def column(row):
    return jnp.transpose(jnp.broadcast_to(row, (HEAD_DIM, row.shape[1])))


def wide(col, width):
    return jnp.concatenate([col] * (width // HEAD_DIM), axis=1)


def cumulative(decay):
    length = decay.shape[1]
    first = decay.astype(bf16)
    rest = decay - first.astype(f32)
    second = rest.astype(bf16)
    third = (rest - second.astype(f32)).astype(bf16)
    upto = lax.broadcasted_iota(jnp.int32, (length, length), 0) <= lax.broadcasted_iota(
        jnp.int32, (length, length), 1
    )
    upto = jnp.where(upto, 1.0, 0.0).astype(bf16)
    return dot(first, upto) + dot(second, upto) + dot(third, upto)


def trail_row(row):
    return jnp.exp(row[:, -1:] - row)


def outer_sum(left, scale_row, right):
    scaled = jnp.transpose(left.astype(f32)) * scale_row
    high, low = halves(scaled)
    return dot(high, right) + dot(low, right)


def cols(j):
    return slice(j * HEAD_DIM, (j + 1) * HEAD_DIM)


class Part:
    def __init__(self, first, count, slot, group_heads):
        self.first, self.count, self.slot, self.group_heads = first, count, slot, group_heads
        self.steps = 2 if count % 4 == 0 else 1
        self.per_step = count // self.steps

    def group(self, info):
        return info[0][0] if self.slot == "mine" else 1 - info[0][0]

    def head(self, info, o):
        return self.group(info) * self.group_heads + self.first + o

    def row(self, cumul_ref, info, o):
        return cumul_ref[pl.ds(self.head(info, o), 1), :]

    def wide_cols(self, info, o):
        return pl.ds(pl.multiple_of(self.head(info, o) * HEAD_DIM, HEAD_DIM), HEAD_DIM)

    def each(self, body):
        for j in range(self.per_step):
            body(pl.program_id(0) * self.per_step + j if self.steps > 1 else j, j)


def at_head(o):
    if isinstance(o, int):
        return cols(o)
    return pl.ds(pl.multiple_of(o * HEAD_DIM, HEAD_DIM), HEAD_DIM)


def chosen(part, values, o, j):
    read, refs = values
    if len(refs) == 1:
        return read(refs[0], at_head(o))
    found = read(refs[0], cols(j))
    for step in range(1, part.steps):
        found = jnp.where(pl.program_id(0) == step, read(refs[step], cols(j)), found)
    return found


def store_decay(part, info, cumul_ref, o, out_ref):
    row = part.row(cumul_ref, info, o)
    out_ref[pl.ds(part.count * HEAD_DIM + o, 1), :] = jnp.broadcast_to(
        jnp.exp(row[:, -1:]), (1, HEAD_DIM)
    )


def pieces_kernel(part, info, key_ref, value_ref, cumul_ref, out_ref):
    def head(o, j):
        at = part.wide_cols(info, o)
        out_ref[at_head(o), :] = outer_sum(
            key_ref[:, at], trail_row(part.row(cumul_ref, info, o)), value_ref[:, at]
        )
        store_decay(part, info, cumul_ref, o, out_ref)

    part.each(head)


def first_pieces_kernel(part, info, key_ref, value_ref, decay_ref, out_ref, cumul_ref):
    @pl.when(pl.program_id(0) == 0)
    def _():
        cumul_ref[...] = cumulative(decay_ref[...])

    def head(o, j):
        out_ref[at_head(o), :] = outer_sum(
            key_ref[:, cols(j)], trail_row(part.row(cumul_ref, info, o)), value_ref[:, cols(j)]
        )
        store_decay(part, info, cumul_ref, o, out_ref)

    part.each(head)


def inner_kernel(part, info, query_ref, key_ref, value_ref, cumul_ref, out_ref):
    def head(o, j):
        row = part.row(cumul_ref, info, o)
        col = column(row)
        at = part.wide_cols(info, o)
        query, key, value = query_ref[:, at], key_ref[:, at], value_ref[:, at]
        for top in range(0, BLOCK, TILE):
            end = top + TILE
            scores = dot(query[top:end], key[:end], NT)
            spread = wide(col[top:end], end) - row[:, :end]
            causal = lax.broadcasted_iota(jnp.int32, (TILE, end), 0) + top >= (
                lax.broadcasted_iota(jnp.int32, (TILE, end), 1)
            )
            weights = (scores * jnp.exp(jnp.where(causal, spread, -1e30))).astype(bf16)
            out_ref[top:end, at_head(o)] = dot(weights, value[:end])

    part.each(head)


def output_kernel(
    part, offset, info, inner_ref, query_ref, cot_ref, gain_ref, cumul_ref, state_ref, before_ref,
    out_ref, sums_ref, square_ref, product_ref,
):
    @pl.when(pl.program_id(0) == 0)
    def _():
        square_ref[...] = jnp.zeros_like(square_ref)
        product_ref[...] = jnp.zeros_like(product_ref)

    def head(o, j):
        lead = jnp.exp(column(part.row(cumul_ref, info, o)))
        high, low = halves(state_ref[at_head(o), :])
        at = part.wide_cols(info, o)
        query = query_ref[:, at]
        out = inner_ref[:, at_head(offset + o)] + lead * (dot(query, high) + dot(query, low))
        out_ref[:, at_head(o)] = out
        square_ref[...] += out * out
        product_ref[...] += cot_ref[:, at].astype(f32) * gain_ref[:, at] * out

    part.each(head)

    @pl.when(pl.program_id(0) == part.steps - 1)
    def _():
        rows = lax.broadcasted_iota(jnp.int32, (8, HEAD_DIM), 0)
        total = before_ref[...]
        for place, ref in ((0, square_ref), (1, product_ref)):
            pick = jnp.where(rows == place, 1.0, 0.0).astype(bf16)
            high, low = halves(ref[...])
            total += dot(pick, high, NT) + dot(pick, low, NT)
        sums_ref[...] = total


def grad_kernel(features, part, held, info, *refs):
    outs, (cot_ref, gain_ref, query_ref, cumul_ref, *refs) = refs[:held], refs[held:]
    shares, (attended_ref, grad_ref, piece_ref) = refs[:-3], refs[-3:]
    sums = shares[0][...]
    for share in shares[1:]:
        sums = sums + share[...]
    inverse = lax.rsqrt(sums[0:1] / features + epsilon)
    mean_term = inverse * sums[1:2] / features
    inverse_col, mean_col = column(inverse), column(mean_term)

    def head(o, j):
        at = part.wide_cols(info, o)
        gain = gain_ref[:, at]
        normed = chosen(part, (lambda ref, at: ref[:, at], outs), o, j) * inverse_col
        attended_ref[:, cols(j)] = (normed * gain).astype(bf16)
        scaled_grad = cot_ref[:, at].astype(f32) * gain
        grad = (inverse_col * (scaled_grad - normed * mean_col)).astype(bf16)
        grad_ref[:, at_head(o)] = grad
        lead = jnp.exp(part.row(cumul_ref, info, o))
        piece_ref[at_head(o), :] = outer_sum(query_ref[:, at], lead, grad)
        store_decay(part, info, cumul_ref, o, piece_ref)

    part.each(head)


def backward_kernel(part, info, query_ref, key_ref, value_ref, grad_ref, cumul_ref, *refs):
    states, (grad_query_ref, inner_key_ref, inner_value_ref) = refs[:-3], refs[-3:]

    def head(o, j):
        row = part.row(cumul_ref, info, o)
        col = column(row)
        at = part.wide_cols(info, o)
        query, key = query_ref[:, at], key_ref[:, at]
        value, grad = value_ref[:, at], grad_ref[:, at_head(o)]
        high, low = halves(chosen(part, (lambda ref, at: ref[at, :], states), o, j))
        outer = jnp.exp(col) * (dot(grad, high, NT) + dot(grad, low, NT))
        for top in range(0, BLOCK, TILE):
            end = top + TILE
            scores = dot(key[top:end], query[top:], NT)
            grad_scores = dot(value[top:end], grad[top:], NT)
            spread = row[:, top:] - wide(col[top:end], BLOCK - top)
            causal = lax.broadcasted_iota(jnp.int32, spread.shape, 0) <= (
                lax.broadcasted_iota(jnp.int32, spread.shape, 1)
            )
            decays = jnp.exp(jnp.where(causal, spread, -1e30))
            weights = (scores * decays).astype(bf16)
            grad_weights = (grad_scores * decays).astype(bf16)
            inner_value_ref[top:end, at_head(o)] = dot(weights, grad[top:])
            inner_key_ref[top:end, at_head(o)] = dot(grad_weights, query[top:])
            inner_query = dot(grad_weights, key[top:end], TN)
            outer = inner_query + outer if top == 0 else jnp.concatenate(
                [outer[:top], outer[top:] + inner_query], axis=0
            )
        grad_query_ref[:, cols(j)] = outer.astype(bf16)

    part.each(head)


def final_kernel(
    part, info, inner_key_ref, inner_value_ref, key_ref, value_ref, cumul_ref, state_ref,
    grad_key_ref, grad_value_ref, token_ref,
):
    token_ref[...] = jnp.zeros_like(token_ref)

    def head(o, j):
        trail = column(trail_row(part.row(cumul_ref, info, o)))
        high, low = halves(state_ref[at_head(o), :])
        at = part.wide_cols(info, o)
        key, value = key_ref[:, at], value_ref[:, at]
        grad_key_ref[:, cols(j)] = (
            inner_key_ref[:, at_head(o)] + trail * (dot(value, high, NT) + dot(value, low, NT))
        ).astype(bf16)
        grad_value_ref[:, cols(j)] = (
            inner_value_ref[:, at_head(o)] + trail * (dot(key, high) + dot(key, low))
        ).astype(bf16)

    part.each(head)


def ordered(is_first, half, j, keep_ref, got_ref):
    rows = slice(j * HEAD_DIM, (j + 1) * HEAD_DIM)
    place = slice(half * HEAD_DIM + j, half * HEAD_DIM + j + 1)
    keep, got = keep_ref[rows, :], got_ref[rows, :]
    keep_decay, got_decay = keep_ref[place, :], got_ref[place, :]
    return (
        jnp.where(is_first, keep, got),
        jnp.where(is_first, got, keep),
        jnp.where(is_first, keep_decay, got_decay),
        jnp.where(is_first, got_decay, keep_decay),
    )


def scan_position(places, forward, info):
    member, pair = info[0][0], info[1][0]
    if forward:
        return member == 0, pair
    return member == 1, places - 1 - pair


def copy_kernel(info, in_ref, out_ref):
    out_ref[...] = in_ref[...]


def hop_kernel(half, p, position, info, keep_ref, got_ref, *refs):
    arrived, out_ref = refs[:-1], refs[-1]
    is_first, place = position(info)

    @pl.when(place == p)
    def _():
        for j in range(half):
            first, second, first_decay, second_decay = ordered(is_first, half, j, keep_ref, got_ref)
            value = second_decay * first + second
            for arrived_ref in arrived:
                value += (first_decay * second_decay) * arrived_ref[cols(j), :]
            out_ref[cols(j), :] = value


def last_kernel(half, position, info, keep_ref, front_ref, other_ref, *refs):
    arrived, (mine_ref, send_ref) = refs[:-2], refs[-2:]
    is_first, place = position(info)
    for p in range(len(arrived) + 1):

        @pl.when(place == p)
        def _():
            for j in range(half):
                first, _, first_decay, _ = ordered(
                    is_first, half, j, keep_ref, front_ref if p == 0 else other_ref
                )
                if p == 0:
                    before, after = jnp.zeros_like(first), first
                else:
                    before = arrived[p - 1][cols(j), :]
                    after = first_decay * before + first
                mine_ref[cols(j), :] = jnp.where(is_first, before, after)
                send_ref[cols(j), :] = jnp.where(is_first, after, before)


def on_device(queries, key_vecs, value_vecs, log_decay, norm_gain, cotangent):
    tokens, width = queries.shape
    assert tokens == BLOCK
    heads = width // HEAD_DIM
    group_heads = heads // 2
    head_count = lax.axis_size("head")
    features = width * head_count
    places = lax.axis_size("seq") // 2
    my_index = lax.axis_index("seq")
    member, pair = my_index % 2, my_index // 2
    gain = norm_gain.reshape(1, width)
    info = (member.astype(jnp.int32).reshape(1), pair.astype(jnp.int32).reshape(1))

    any_spec = pl.BlockSpec(memory_space=pl.ANY)
    whole = jax.ShapeDtypeStruct((tokens, width), bf16)
    sums_shape = jax.ShapeDtypeStruct((8, tokens), f32)

    def states_of(count, extra=0):
        return jax.ShapeDtypeStruct((count * HEAD_DIM + extra, HEAD_DIM), f32)

    def local_of(count, dtype=f32):
        return jax.ShapeDtypeStruct((tokens, count * HEAD_DIM), dtype)

    def run(kernel, grid, ins, outs, scratch=(), after=(), aliases=None, cost=1.0, limit=24):
        used = len(ins)
        after = [x for i, x in enumerate(after) if not any(x is y for y in after[:i])]

        def body(member_ref, pair_ref, *refs):
            kernel((member_ref, pair_ref), *refs[:used], *refs[used + len(after):])

        return pl.pallas_call(
            body,
            out_shape=[shape for shape, _ in outs],
            grid_spec=pltpu.PrefetchScalarGridSpec(
                num_scalar_prefetch=2,
                grid=(grid,),
                in_specs=[spec for _, spec in ins] + [any_spec] * len(after),
                out_specs=[spec for _, spec in outs],
                scratch_shapes=list(scratch),
            ),
            input_output_aliases=aliases or {},
            compiler_params=pltpu.CompilerParams(vmem_limit_bytes=limit * 1024 * 1024),
            cost_estimate=pl.CostEstimate(
                flops=int(cost * 1e9), bytes_accessed=int(cost * 2.5e6), transcendentals=0
            ),
        )(*info, *[array for array, _ in ins], *after)

    def fixed(shape):
        return pl.BlockSpec(shape, lambda i, *info: (0,) * len(shape))

    def plain(array):
        return array, fixed(array.shape)

    def give(shape):
        return shape, fixed(shape.shape)

    class Calls(Part):
        def full_spec(self):
            width = self.per_step
            return pl.BlockSpec(
                (tokens, width * HEAD_DIM),
                lambda i, *info: (
                    0, (self.group(info) * self.group_heads + self.first) // width + i
                ),
            )

        def call(self, kernel, ins, outs, **options):
            return run(functools.partial(kernel, self), self.steps, ins, outs, **options)

    def parts_of(chunks, slot):
        count = group_heads // chunks
        return [Calls(c * count, count, slot, group_heads) for c in range(chunks)]

    swap = [(2 * p + m, 2 * p + 1 - m) for p in range(places) for m in (0, 1)]

    def chain(chunks, make_piece, forward, filler, on_mine, on_theirs):
        position = functools.partial(scan_position, places, forward)
        my_parts, their_parts = parts_of(chunks, "mine"), parts_of(chunks, "theirs")
        count = group_heads // chunks
        state, wide_state = states_of(count), states_of(count, 8)

        def device(place, m):
            return 2 * (place if forward else places - 1 - place) + m

        sends, keeps, received, last = [], [], [], ()

        def exchange(last):
            c = len(received)
            if c == 0 or c >= chunks:
                if c == 0:
                    received.append([
                        lax.ppermute(sends[0], "seq", [(device(p, m), device(p, 1 - m)) for p in ps for m in (0, 1)])
                        for ps in ((0,), range(1, places))
                    ])
                return last
            sent, = run(copy_kernel, 1, [plain(sends[c])], [give(wide_state)], after=last, cost=0.02)
            received.append([lax.ppermute(sent, "seq", swap)])
            return (sent,)

        for part in their_parts:
            sends.append(make_piece(part, last))
            last = () if forward and len(sends) == 1 else (sends[-1],)
        last = exchange(last)
        if forward:
            last = exchange(last)
        rest = [functools.partial(make_piece, part) for part in my_parts]
        for make in rest[:1] if forward else rest:
            keeps.append(make(last))
            last = (keeps[-1],)
        if not forward:
            last = exchange(last)
        arrived, mine, theirs, late = {}, [], [], []
        for step in range(chunks + places - 1):
            for p in range(places - 1):
                c = step - p
                if not 0 <= c < chunks:
                    continue
                ins = [plain(keeps[c]), plain(received[c][0 if p == 0 else -1])]
                if p > 0:
                    ins.append(plain(arrived[c, p]))
                value, = run(
                    functools.partial(hop_kernel, count, p, position), 1, ins, [give(state)],
                    after=last, cost=0.3,
                )
                pairs = [(device(p, m), device(p + 1, m)) for m in (0, 1)]
                arrived[c, p + 1] = lax.ppermute(value, "seq", pairs)
                last = (value,)
            last = exchange(last)
            while len(keeps) < chunks:
                keeps.append(rest[len(keeps)](last))
                last = (keeps[-1],)
            if step == 0:
                last += (received[0][-1],)
            if filler:
                last = (filler.pop(0)(last),)
            c = step + 1 - places
            if c >= 0:
                ins = [plain(keeps[c]), plain(received[c][0]), plain(received[c][-1])]
                ins += [plain(arrived[c, p]) for p in range(1, places)]
                own, send = run(
                    functools.partial(last_kernel, count, position), 1, ins, [give(state)] * 2,
                    after=last, cost=0.3,
                )
                theirs.append(lax.ppermute(send, "seq", swap))
                mine.append(own)
                last = (send,)
                filler.append(functools.partial(on_mine, c, own))
                late.append(functools.partial(on_theirs, c, theirs[c]))
                if c >= 2:
                    filler.append(late.pop(0))
                last = (filler.pop(0)(last),)
        for work in filler + late:
            last = (work(last),)
        return mine, theirs

    inner, outs = {}, {}
    held_cumul, held_sums = [], [jnp.zeros(sums_shape.shape, f32)]
    back_count = group_heads // BACKWARD_CHUNKS
    front_count = group_heads // FORWARD_CHUNKS
    per_back = back_count // front_count
    back_parts = {slot: parts_of(BACKWARD_CHUNKS, slot) for slot in ("mine", "theirs")}
    front_parts = {slot: parts_of(FORWARD_CHUNKS, slot) for slot in ("mine", "theirs")}

    def cumul_in():
        return plain(held_cumul[0])

    def forward_piece(part, after):
        if not held_cumul:
            piece, cumul = part.call(
                first_pieces_kernel,
                [(key_vecs, part.full_spec()), (value_vecs, part.full_spec()), plain(log_decay.T)],
                [give(states_of(part.count, 8)), give(jax.ShapeDtypeStruct((heads, tokens), f32))],
                cost=0.05, limit=60,
            )
            held_cumul.append(cumul)
            return piece
        return part.call(
            pieces_kernel, [plain(key_vecs), plain(value_vecs), cumul_in()],
            [give(states_of(part.count, 8))], after=after, cost=0.05,
        )[0]

    def inner_work(slot, c, after):
        part = back_parts[slot][c]
        inner[slot, c], = part.call(
            inner_kernel, [plain(queries), plain(key_vecs), plain(value_vecs), cumul_in()],
            [give(local_of(part.count))], after=after, cost=2.2 if inner else 0.1,
        )
        return inner[slot, c]

    def output_work(slot, c, before, after):
        part = front_parts[slot][c]
        outs[slot, c], held_sums[0] = run(
            functools.partial(output_kernel, part, c % per_back * front_count), part.steps,
            [plain(inner[slot, c // per_back]), plain(queries), plain(cotangent), plain(gain),
             cumul_in(), plain(before), plain(held_sums[0])],
            [give(local_of(part.count)), give(sums_shape)],
            scratch=[pltpu.VMEM((tokens, HEAD_DIM), f32)] * 2, after=after, cost=0.8,
        )
        return held_sums[0]

    works = [
        functools.partial(inner_work, slot, c)
        for c in range(BACKWARD_CHUNKS) for slot in ("mine", "theirs")
    ]
    mine, theirs = chain(
        FORWARD_CHUNKS, forward_piece, True, works,
        functools.partial(output_work, "mine"), functools.partial(output_work, "theirs"),
    )
    states = {"mine": mine, "theirs": theirs}

    sums = held_sums[0]
    shares = [sums] + [
        lax.ppermute(sums, "head", [(i, (i + k) % head_count) for i in range(head_count)])
        for k in range(1, head_count)
    ]

    attended, grad_queries, grad_keys, grad_values = [], [], [], []
    grads, inner_grads = {}, {}

    def target(held):
        return tuple(held[-1:])

    def covered(c):
        return range(c * per_back, (c + 1) * per_back)

    def backward_piece(part, after):
        before = target(attended)
        c = part.first // part.count
        ins = [plain(outs[part.slot, i]) for i in covered(c)]
        ins += [plain(cotangent), plain(gain), plain(queries), cumul_in()]
        ins += [plain(share) for share in shares]
        whole_out, grads[part.slot, c], piece = run(
            functools.partial(grad_kernel, features, part, per_back), part.steps, ins,
            [(whole, part.full_spec()), give(local_of(part.count, bf16)),
             give(states_of(part.count, 8))],
            after=before + tuple(after), aliases={2 + len(ins): 0} if before else None, cost=2.0,
        )
        attended.append(whole_out)
        return piece

    def backward_work(slot, c, after):
        part, held = back_parts[slot][c], target(grad_queries)
        ins = [plain(queries), plain(key_vecs), plain(value_vecs), plain(grads[slot, c]), cumul_in()]
        ins += [plain(states[slot][i]) for i in covered(c)]
        whole_out, *inner_grads[slot, c] = part.call(
            backward_kernel, ins,
            [(whole, part.full_spec()), give(local_of(part.count)), give(local_of(part.count))],
            after=held + tuple(after), aliases={2 + len(ins): 0} if held else None, cost=4.3,
        )
        grad_queries.append(whole_out)
        return inner_grads[slot, c][0]

    def final_work(slot, c, before, after):
        part, held = back_parts[slot][c], target(grad_keys) + target(grad_values)
        ins = [plain(array) for array in (*inner_grads[slot, c], key_vecs, value_vecs)]
        ins += [cumul_in(), plain(before)]
        whole_key, whole_value, token = part.call(
            final_kernel, ins,
            [(whole, part.full_spec())] * 2 + [give(jax.ShapeDtypeStruct((8, HEAD_DIM), f32))],
            after=held + tuple(after),
            aliases={2 + len(ins): 0, 3 + len(ins): 1} if held else None, cost=2.0,
        )
        grad_keys.append(whole_key)
        grad_values.append(whole_value)
        return token

    works = [
        functools.partial(backward_work, slot, c)
        for c in range(BACKWARD_CHUNKS) for slot in ("mine", "theirs")
    ]
    chain(
        BACKWARD_CHUNKS, backward_piece, False, works,
        functools.partial(final_work, "mine"), functools.partial(final_work, "theirs"),
    )
    return attended[-1], grad_queries[-1], grad_keys[-1], grad_values[-1]


def solution(mesh):
    return jax.shard_map(
        on_device,
        mesh=mesh,
        in_specs=(
            P("seq", "head"),
            P("seq", "head"),
            P("seq", "head"),
            P("seq", "head"),
            P("head"),
            P("seq", "head"),
        ),
        out_specs=(P("seq", "head"), P("seq", "head"), P("seq", "head"), P("seq", "head")),
        check_vma=False,
    )
```

```python
import functools

import jax
import jax.numpy as jnp
from jax import lax
from jax.experimental import pallas as pl
from jax.experimental.pallas import tpu as pltpu
from jax.sharding import PartitionSpec as P

HEAD_DIM = 128
BLOCK = 512
FORWARD_CHUNKS = 2
BACKWARD_CHUNKS = 2
TILE = 256
epsilon = 1e-06
f32 = jnp.float32
bf16 = jnp.bfloat16

NN = (((1,), (0,)), ((), ()))
NT = (((1,), (1,)), ((), ()))
TN = (((0,), (0,)), ((), ()))


def dot(a, b, dims=NN):
    return lax.dot_general(a, b, dims, preferred_element_type=f32)


def halves(x):
    high = x.astype(bf16)
    return high, (x - high.astype(f32)).astype(bf16)


def column(row):
    return jnp.transpose(jnp.broadcast_to(row, (HEAD_DIM, row.shape[1])))


def wide(col, width):
    return jnp.concatenate([col] * (width // HEAD_DIM), axis=1)


def cumulative(decay):
    length = decay.shape[1]
    first = decay.astype(bf16)
    rest = decay - first.astype(f32)
    second = rest.astype(bf16)
    third = (rest - second.astype(f32)).astype(bf16)
    upto = lax.broadcasted_iota(jnp.int32, (length, length), 0) <= lax.broadcasted_iota(
        jnp.int32, (length, length), 1
    )
    upto = jnp.where(upto, 1.0, 0.0).astype(bf16)
    return dot(first, upto) + dot(second, upto) + dot(third, upto)


def trail_row(row):
    return jnp.exp(row[:, -1:] - row)


def outer_sum(left, scale_row, right):
    scaled = jnp.transpose(left.astype(f32)) * scale_row
    high, low = halves(scaled)
    return dot(high, right) + dot(low, right)


def cols(j):
    return slice(j * HEAD_DIM, (j + 1) * HEAD_DIM)


class Part:
    def __init__(self, first, count, slot, group_heads):
        self.first, self.count, self.slot, self.group_heads = first, count, slot, group_heads
        self.steps = 2 if count % 4 == 0 else 1
        self.per_step = count // self.steps

    def group(self, info):
        return info[0][0] if self.slot == "mine" else 1 - info[0][0]

    def head(self, info, o):
        return self.group(info) * self.group_heads + self.first + o

    def row(self, cumul_ref, info, o):
        return cumul_ref[pl.ds(self.head(info, o), 1), :]

    def wide_cols(self, info, o):
        return pl.ds(pl.multiple_of(self.head(info, o) * HEAD_DIM, HEAD_DIM), HEAD_DIM)

    def each(self, body):
        for j in range(self.per_step):
            body(pl.program_id(0) * self.per_step + j if self.steps > 1 else j, j)


def at_head(o):
    if isinstance(o, int):
        return cols(o)
    return pl.ds(pl.multiple_of(o * HEAD_DIM, HEAD_DIM), HEAD_DIM)


def chosen(part, values, o, j):
    read, refs = values
    if len(refs) == 1:
        return read(refs[0], at_head(o))
    found = read(refs[0], cols(j))
    for step in range(1, part.steps):
        found = jnp.where(pl.program_id(0) == step, read(refs[step], cols(j)), found)
    return found


def store_decay(part, info, cumul_ref, o, out_ref):
    row = part.row(cumul_ref, info, o)
    out_ref[pl.ds(part.count * HEAD_DIM + o, 1), :] = jnp.broadcast_to(
        jnp.exp(row[:, -1:]), (1, HEAD_DIM)
    )


def pieces_kernel(part, info, key_ref, value_ref, cumul_ref, out_ref):
    def head(o, j):
        at = part.wide_cols(info, o)
        out_ref[at_head(o), :] = outer_sum(
            key_ref[:, at], trail_row(part.row(cumul_ref, info, o)), value_ref[:, at]
        )
        store_decay(part, info, cumul_ref, o, out_ref)

    part.each(head)


def first_pieces_kernel(part, info, key_ref, value_ref, decay_ref, out_ref, cumul_ref):
    @pl.when(pl.program_id(0) == 0)
    def _():
        cumul_ref[...] = cumulative(decay_ref[...])

    def head(o, j):
        out_ref[at_head(o), :] = outer_sum(
            key_ref[:, cols(j)], trail_row(part.row(cumul_ref, info, o)), value_ref[:, cols(j)]
        )
        store_decay(part, info, cumul_ref, o, out_ref)

    part.each(head)


def inner_kernel(part, info, query_ref, key_ref, value_ref, cumul_ref, out_ref):
    def head(o, j):
        row = part.row(cumul_ref, info, o)
        col = column(row)
        at = part.wide_cols(info, o)
        query, key, value = query_ref[:, at], key_ref[:, at], value_ref[:, at]
        for top in range(0, BLOCK, TILE):
            end = top + TILE
            scores = dot(query[top:end], key[:end], NT)
            spread = wide(col[top:end], end) - row[:, :end]
            causal = lax.broadcasted_iota(jnp.int32, (TILE, end), 0) + top >= (
                lax.broadcasted_iota(jnp.int32, (TILE, end), 1)
            )
            weights = (scores * jnp.exp(jnp.where(causal, spread, -1e30))).astype(bf16)
            out_ref[top:end, at_head(o)] = dot(weights, value[:end])

    part.each(head)


def output_kernel(
    part, offset, info, inner_ref, query_ref, cot_ref, gain_ref, cumul_ref, state_ref, before_ref,
    out_ref, sums_ref, square_ref, product_ref,
):
    @pl.when(pl.program_id(0) == 0)
    def _():
        square_ref[...] = jnp.zeros_like(square_ref)
        product_ref[...] = jnp.zeros_like(product_ref)

    def head(o, j):
        lead = jnp.exp(column(part.row(cumul_ref, info, o)))
        high, low = halves(state_ref[at_head(o), :])
        at = part.wide_cols(info, o)
        query = query_ref[:, at]
        out = inner_ref[:, at_head(offset + o)] + lead * (dot(query, high) + dot(query, low))
        out_ref[:, at_head(o)] = out
        square_ref[...] += out * out
        product_ref[...] += cot_ref[:, at].astype(f32) * gain_ref[:, at] * out

    part.each(head)

    @pl.when(pl.program_id(0) == part.steps - 1)
    def _():
        rows = lax.broadcasted_iota(jnp.int32, (8, HEAD_DIM), 0)
        total = before_ref[...]
        for place, ref in ((0, square_ref), (1, product_ref)):
            pick = jnp.where(rows == place, 1.0, 0.0).astype(bf16)
            high, low = halves(ref[...])
            total += dot(pick, high, NT) + dot(pick, low, NT)
        sums_ref[...] = total


def grad_kernel(features, part, held, info, *refs):
    outs, (cot_ref, gain_ref, query_ref, cumul_ref, *refs) = refs[:held], refs[held:]
    shares, (attended_ref, grad_ref, piece_ref) = refs[:-3], refs[-3:]
    sums = shares[0][...]
    for share in shares[1:]:
        sums = sums + share[...]
    inverse = lax.rsqrt(sums[0:1] / features + epsilon)
    mean_term = inverse * sums[1:2] / features
    inverse_col, mean_col = column(inverse), column(mean_term)

    def head(o, j):
        at = part.wide_cols(info, o)
        gain = gain_ref[:, at]
        normed = chosen(part, (lambda ref, at: ref[:, at], outs), o, j) * inverse_col
        attended_ref[:, cols(j)] = (normed * gain).astype(bf16)
        scaled_grad = cot_ref[:, at].astype(f32) * gain
        grad = (inverse_col * (scaled_grad - normed * mean_col)).astype(bf16)
        grad_ref[:, at_head(o)] = grad
        lead = jnp.exp(part.row(cumul_ref, info, o))
        piece_ref[at_head(o), :] = outer_sum(query_ref[:, at], lead, grad)
        store_decay(part, info, cumul_ref, o, piece_ref)

    part.each(head)


def backward_kernel(part, info, query_ref, key_ref, value_ref, grad_ref, cumul_ref, *refs):
    states, (grad_query_ref, inner_key_ref, inner_value_ref) = refs[:-3], refs[-3:]

    def head(o, j):
        row = part.row(cumul_ref, info, o)
        col = column(row)
        at = part.wide_cols(info, o)
        query, key = query_ref[:, at], key_ref[:, at]
        value, grad = value_ref[:, at], grad_ref[:, at_head(o)]
        high, low = halves(chosen(part, (lambda ref, at: ref[at, :], states), o, j))
        outer = jnp.exp(col) * (dot(grad, high, NT) + dot(grad, low, NT))
        for top in range(0, BLOCK, TILE):
            end = top + TILE
            scores = dot(key[top:end], query[top:], NT)
            grad_scores = dot(value[top:end], grad[top:], NT)
            spread = row[:, top:] - wide(col[top:end], BLOCK - top)
            causal = lax.broadcasted_iota(jnp.int32, spread.shape, 0) <= (
                lax.broadcasted_iota(jnp.int32, spread.shape, 1)
            )
            decays = jnp.exp(jnp.where(causal, spread, -1e30))
            weights = (scores * decays).astype(bf16)
            grad_weights = (grad_scores * decays).astype(bf16)
            inner_value_ref[top:end, at_head(o)] = dot(weights, grad[top:])
            inner_key_ref[top:end, at_head(o)] = dot(grad_weights, query[top:])
            inner_query = dot(grad_weights, key[top:end], TN)
            outer = inner_query + outer if top == 0 else jnp.concatenate(
                [outer[:top], outer[top:] + inner_query], axis=0
            )
        grad_query_ref[:, cols(j)] = outer.astype(bf16)

    part.each(head)


def final_kernel(
    part, info, inner_key_ref, inner_value_ref, key_ref, value_ref, cumul_ref, state_ref,
    grad_key_ref, grad_value_ref, token_ref,
):
    token_ref[...] = jnp.zeros_like(token_ref)

    def head(o, j):
        trail = column(trail_row(part.row(cumul_ref, info, o)))
        high, low = halves(state_ref[at_head(o), :])
        at = part.wide_cols(info, o)
        key, value = key_ref[:, at], value_ref[:, at]
        grad_key_ref[:, cols(j)] = (
            inner_key_ref[:, at_head(o)] + trail * (dot(value, high, NT) + dot(value, low, NT))
        ).astype(bf16)
        grad_value_ref[:, cols(j)] = (
            inner_value_ref[:, at_head(o)] + trail * (dot(key, high) + dot(key, low))
        ).astype(bf16)

    part.each(head)


def ordered(is_first, half, j, keep_ref, got_ref):
    rows = slice(j * HEAD_DIM, (j + 1) * HEAD_DIM)
    place = slice(half * HEAD_DIM + j, half * HEAD_DIM + j + 1)
    keep, got = keep_ref[rows, :], got_ref[rows, :]
    keep_decay, got_decay = keep_ref[place, :], got_ref[place, :]
    return (
        jnp.where(is_first, keep, got),
        jnp.where(is_first, got, keep),
        jnp.where(is_first, keep_decay, got_decay),
        jnp.where(is_first, got_decay, keep_decay),
    )


def scan_position(places, forward, info):
    member, pair = info[0][0], info[1][0]
    if forward:
        return member == 0, pair
    return member == 1, places - 1 - pair


def copy_kernel(info, in_ref, out_ref):
    out_ref[...] = in_ref[...]


def hop_kernel(half, p, position, info, keep_ref, got_ref, *refs):
    arrived, out_ref = refs[:-1], refs[-1]
    is_first, place = position(info)

    @pl.when(place == p)
    def _():
        for j in range(half):
            first, second, first_decay, second_decay = ordered(is_first, half, j, keep_ref, got_ref)
            value = second_decay * first + second
            for arrived_ref in arrived:
                value += (first_decay * second_decay) * arrived_ref[cols(j), :]
            out_ref[cols(j), :] = value


def last_kernel(half, position, info, keep_ref, got_ref, *refs):
    arrived, (mine_ref, send_ref) = refs[:-2], refs[-2:]
    is_first, place = position(info)
    for p in range(len(arrived) + 1):

        @pl.when(place == p)
        def _():
            for j in range(half):
                first, _, first_decay, _ = ordered(is_first, half, j, keep_ref, got_ref)
                if p == 0:
                    before, after = jnp.zeros_like(first), first
                else:
                    before = arrived[p - 1][cols(j), :]
                    after = first_decay * before + first
                mine_ref[cols(j), :] = jnp.where(is_first, before, after)
                send_ref[cols(j), :] = jnp.where(is_first, after, before)


def on_device(queries, key_vecs, value_vecs, log_decay, norm_gain, cotangent):
    tokens, width = queries.shape
    assert tokens == BLOCK
    heads = width // HEAD_DIM
    group_heads = heads // 2
    head_count = lax.axis_size("head")
    features = width * head_count
    places = lax.axis_size("seq") // 2
    my_index = lax.axis_index("seq")
    member, pair = my_index % 2, my_index // 2
    gain = norm_gain.reshape(1, width)
    info = (member.astype(jnp.int32).reshape(1), pair.astype(jnp.int32).reshape(1))

    any_spec = pl.BlockSpec(memory_space=pl.ANY)
    whole = jax.ShapeDtypeStruct((tokens, width), bf16)
    sums_shape = jax.ShapeDtypeStruct((8, tokens), f32)

    def states_of(count, extra=0):
        return jax.ShapeDtypeStruct((count * HEAD_DIM + extra, HEAD_DIM), f32)

    def local_of(count, dtype=f32):
        return jax.ShapeDtypeStruct((tokens, count * HEAD_DIM), dtype)

    def run(kernel, grid, ins, outs, scratch=(), after=(), aliases=None, cost=1.0, limit=24):
        used = len(ins)
        after = [x for i, x in enumerate(after) if not any(x is y for y in after[:i])]

        def body(member_ref, pair_ref, *refs):
            kernel((member_ref, pair_ref), *refs[:used], *refs[used + len(after):])

        return pl.pallas_call(
            body,
            out_shape=[shape for shape, _ in outs],
            grid_spec=pltpu.PrefetchScalarGridSpec(
                num_scalar_prefetch=2,
                grid=(grid,),
                in_specs=[spec for _, spec in ins] + [any_spec] * len(after),
                out_specs=[spec for _, spec in outs],
                scratch_shapes=list(scratch),
            ),
            input_output_aliases=aliases or {},
            compiler_params=pltpu.CompilerParams(vmem_limit_bytes=limit * 1024 * 1024),
            cost_estimate=pl.CostEstimate(
                flops=int(cost * 1e9), bytes_accessed=int(cost * 2.5e6), transcendentals=0
            ),
        )(*info, *[array for array, _ in ins], *after)

    def fixed(shape):
        return pl.BlockSpec(shape, lambda i, *info: (0,) * len(shape))

    def plain(array):
        return array, fixed(array.shape)

    def give(shape):
        return shape, fixed(shape.shape)

    class Calls(Part):
        def full_spec(self):
            width = self.per_step
            return pl.BlockSpec(
                (tokens, width * HEAD_DIM),
                lambda i, *info: (
                    0, (self.group(info) * self.group_heads + self.first) // width + i
                ),
            )

        def call(self, kernel, ins, outs, **options):
            return run(functools.partial(kernel, self), self.steps, ins, outs, **options)

    def parts_of(chunks, slot):
        count = group_heads // chunks
        return [Calls(c * count, count, slot, group_heads) for c in range(chunks)]

    swap = [(2 * p + m, 2 * p + 1 - m) for p in range(places) for m in (0, 1)]

    def chain(chunks, make_piece, forward, filler, on_mine, on_theirs):
        position = functools.partial(scan_position, places, forward)
        my_parts, their_parts = parts_of(chunks, "mine"), parts_of(chunks, "theirs")
        count = group_heads // chunks
        state, wide_state = states_of(count), states_of(count, 8)

        def device(place, m):
            return 2 * (place if forward else places - 1 - place) + m

        sends, keeps, received, last = [], [], [], ()

        def exchange(last):
            c = len(received)
            if c == 0 or c >= chunks:
                if c == 0:
                    received.append(lax.ppermute(sends[0], "seq", swap))
                return last
            sent, = run(copy_kernel, 1, [plain(sends[c])], [give(wide_state)], after=last, cost=0.02)
            received.append(lax.ppermute(sent, "seq", swap))
            return (sent,)

        for part in their_parts:
            sends.append(make_piece(part, last))
            last = () if forward and len(sends) == 1 else (sends[-1],)
        last = exchange(last)
        if forward:
            last = exchange(last)
        rest = [functools.partial(make_piece, part) for part in my_parts]
        for make in rest[:1] if forward else rest:
            keeps.append(make(last))
            last = (keeps[-1],)
        if not forward:
            last = exchange(last)
        arrived, mine, theirs, late = {}, [], [], []
        for step in range(chunks + places - 1):
            for p in range(places - 1):
                c = step - p
                if not 0 <= c < chunks:
                    continue
                ins = [plain(keeps[c]), plain(received[c])]
                if p > 0:
                    ins.append(plain(arrived[c, p]))
                value, = run(
                    functools.partial(hop_kernel, count, p, position), 1, ins, [give(state)],
                    after=last, cost=0.3,
                )
                other = {p: p + 1, p + 1: p}
                pairs = [
                    (device(q, m), device(other.get(q, q), m)) for q in range(places) for m in (0, 1)
                ]
                arrived[c, p + 1] = lax.ppermute(value, "seq", pairs)
                last = (value,)
            last = exchange(last)
            while len(keeps) < chunks:
                keeps.append(rest[len(keeps)](last))
                last = (keeps[-1],)
            if filler:
                last = (filler.pop(0)(last),)
            c = step + 1 - places
            if c >= 0:
                ins = [plain(keeps[c]), plain(received[c])]
                ins += [plain(arrived[c, p]) for p in range(1, places)]
                own, send = run(
                    functools.partial(last_kernel, count, position), 1, ins, [give(state)] * 2,
                    after=last, cost=0.3,
                )
                theirs.append(lax.ppermute(send, "seq", swap))
                mine.append(own)
                last = (send,)
                filler.append(functools.partial(on_mine, c, own))
                late.append(functools.partial(on_theirs, c, theirs[c]))
                if c >= 2:
                    filler.append(late.pop(0))
                last = (filler.pop(0)(last),)
        for work in filler + late:
            last = (work(last),)
        return mine, theirs

    inner, outs = {}, {}
    held_cumul, held_sums = [], [jnp.zeros(sums_shape.shape, f32)]
    back_count = group_heads // BACKWARD_CHUNKS
    front_count = group_heads // FORWARD_CHUNKS
    per_back = back_count // front_count
    back_parts = {slot: parts_of(BACKWARD_CHUNKS, slot) for slot in ("mine", "theirs")}
    front_parts = {slot: parts_of(FORWARD_CHUNKS, slot) for slot in ("mine", "theirs")}

    def cumul_in():
        return plain(held_cumul[0])

    def forward_piece(part, after):
        if not held_cumul:
            piece, cumul = part.call(
                first_pieces_kernel,
                [(key_vecs, part.full_spec()), (value_vecs, part.full_spec()), plain(log_decay.T)],
                [give(states_of(part.count, 8)), give(jax.ShapeDtypeStruct((heads, tokens), f32))],
                cost=0.05, limit=60,
            )
            held_cumul.append(cumul)
            return piece
        return part.call(
            pieces_kernel, [plain(key_vecs), plain(value_vecs), cumul_in()],
            [give(states_of(part.count, 8))], after=after, cost=0.05,
        )[0]

    def inner_work(slot, c, after):
        part = back_parts[slot][c]
        inner[slot, c], = part.call(
            inner_kernel, [plain(queries), plain(key_vecs), plain(value_vecs), cumul_in()],
            [give(local_of(part.count))], after=after, cost=2.2 if inner else 0.1,
        )
        return inner[slot, c]

    def output_work(slot, c, before, after):
        part = front_parts[slot][c]
        outs[slot, c], held_sums[0] = run(
            functools.partial(output_kernel, part, c % per_back * front_count), part.steps,
            [plain(inner[slot, c // per_back]), plain(queries), plain(cotangent), plain(gain),
             cumul_in(), plain(before), plain(held_sums[0])],
            [give(local_of(part.count)), give(sums_shape)],
            scratch=[pltpu.VMEM((tokens, HEAD_DIM), f32)] * 2, after=after, cost=0.8,
        )
        return held_sums[0]

    works = [
        functools.partial(inner_work, slot, c)
        for c in range(BACKWARD_CHUNKS) for slot in ("mine", "theirs")
    ]
    mine, theirs = chain(
        FORWARD_CHUNKS, forward_piece, True, works,
        functools.partial(output_work, "mine"), functools.partial(output_work, "theirs"),
    )
    states = {"mine": mine, "theirs": theirs}

    sums = held_sums[0]
    shares = [sums] + [
        lax.ppermute(sums, "head", [(i, (i + k) % head_count) for i in range(head_count)])
        for k in range(1, head_count)
    ]

    attended, grad_queries, grad_keys, grad_values = [], [], [], []
    grads, inner_grads = {}, {}

    def target(held):
        return tuple(held[-1:])

    def covered(c):
        return range(c * per_back, (c + 1) * per_back)

    def backward_piece(part, after):
        before = target(attended)
        c = part.first // part.count
        ins = [plain(outs[part.slot, i]) for i in covered(c)]
        ins += [plain(cotangent), plain(gain), plain(queries), cumul_in()]
        ins += [plain(share) for share in shares]
        whole_out, grads[part.slot, c], piece = run(
            functools.partial(grad_kernel, features, part, per_back), part.steps, ins,
            [(whole, part.full_spec()), give(local_of(part.count, bf16)),
             give(states_of(part.count, 8))],
            after=before + tuple(after), aliases={2 + len(ins): 0} if before else None, cost=2.0,
        )
        attended.append(whole_out)
        return piece

    def backward_work(slot, c, after):
        part, held = back_parts[slot][c], target(grad_queries)
        ins = [plain(queries), plain(key_vecs), plain(value_vecs), plain(grads[slot, c]), cumul_in()]
        ins += [plain(states[slot][i]) for i in covered(c)]
        whole_out, *inner_grads[slot, c] = part.call(
            backward_kernel, ins,
            [(whole, part.full_spec()), give(local_of(part.count)), give(local_of(part.count))],
            after=held + tuple(after), aliases={2 + len(ins): 0} if held else None, cost=4.3,
        )
        grad_queries.append(whole_out)
        return inner_grads[slot, c][0]

    def final_work(slot, c, before, after):
        part, held = back_parts[slot][c], target(grad_keys) + target(grad_values)
        ins = [plain(array) for array in (*inner_grads[slot, c], key_vecs, value_vecs)]
        ins += [cumul_in(), plain(before)]
        whole_key, whole_value, token = part.call(
            final_kernel, ins,
            [(whole, part.full_spec())] * 2 + [give(jax.ShapeDtypeStruct((8, HEAD_DIM), f32))],
            after=held + tuple(after),
            aliases={2 + len(ins): 0, 3 + len(ins): 1} if held else None, cost=2.0,
        )
        grad_keys.append(whole_key)
        grad_values.append(whole_value)
        return token

    works = [
        functools.partial(backward_work, slot, c)
        for c in range(BACKWARD_CHUNKS) for slot in ("mine", "theirs")
    ]
    chain(
        BACKWARD_CHUNKS, backward_piece, False, works,
        functools.partial(final_work, "mine"), functools.partial(final_work, "theirs"),
    )
    return attended[-1], grad_queries[-1], grad_keys[-1], grad_values[-1]


def solution(mesh):
    return jax.shard_map(
        on_device,
        mesh=mesh,
        in_specs=(
            P("seq", "head"),
            P("seq", "head"),
            P("seq", "head"),
            P("seq", "head"),
            P("head"),
            P("seq", "head"),
        ),
        out_specs=(P("seq", "head"), P("seq", "head"), P("seq", "head"), P("seq", "head")),
        check_vma=False,
    )
```

```python
import functools

import jax
import jax.numpy as jnp
from jax import lax
from jax.experimental import pallas as pl
from jax.experimental.pallas import tpu as pltpu
from jax.sharding import PartitionSpec as P

HEAD_DIM = 128
BLOCK = 512
FORWARD_CHUNKS = 2
BACKWARD_CHUNKS = 2
TILE = 256
epsilon = 1e-06
f32 = jnp.float32
bf16 = jnp.bfloat16

NN = (((1,), (0,)), ((), ()))
NT = (((1,), (1,)), ((), ()))
TN = (((0,), (0,)), ((), ()))


def dot(a, b, dims=NN):
    return lax.dot_general(a, b, dims, preferred_element_type=f32)


def halves(x):
    high = x.astype(bf16)
    return high, (x - high.astype(f32)).astype(bf16)


def column(row):
    return jnp.transpose(jnp.broadcast_to(row, (HEAD_DIM, row.shape[1])))


def wide(col, width):
    return jnp.concatenate([col] * (width // HEAD_DIM), axis=1)


def cumulative(decay):
    length = decay.shape[1]
    first = decay.astype(bf16)
    rest = decay - first.astype(f32)
    second = rest.astype(bf16)
    third = (rest - second.astype(f32)).astype(bf16)
    upto = lax.broadcasted_iota(jnp.int32, (length, length), 0) <= lax.broadcasted_iota(
        jnp.int32, (length, length), 1
    )
    upto = jnp.where(upto, 1.0, 0.0).astype(bf16)
    return dot(first, upto) + dot(second, upto) + dot(third, upto)


def trail_row(row):
    return jnp.exp(row[:, -1:] - row)


def outer_sum(left, scale_row, right):
    scaled = jnp.transpose(left).astype(f32) * scale_row
    high, low = halves(scaled)
    return dot(high, right) + dot(low, right)


def cols(j):
    return slice(j * HEAD_DIM, (j + 1) * HEAD_DIM)


class Part:
    def __init__(self, first, count, slot, group_heads):
        self.first, self.count, self.slot, self.group_heads = first, count, slot, group_heads
        self.steps = 2 if count % 4 == 0 else 1
        self.per_step = count // self.steps

    def group(self, info):
        return info[0][0] if self.slot == "mine" else 1 - info[0][0]

    def head(self, info, o):
        return self.group(info) * self.group_heads + self.first + o

    def row(self, cumul_ref, info, o):
        return cumul_ref[pl.ds(self.head(info, o), 1), :]

    def wide_cols(self, info, o):
        return pl.ds(pl.multiple_of(self.head(info, o) * HEAD_DIM, HEAD_DIM), HEAD_DIM)

    def each(self, body):
        for j in range(self.per_step):
            body(pl.program_id(0) * self.per_step + j if self.steps > 1 else j, j)


def at_head(o):
    if isinstance(o, int):
        return cols(o)
    return pl.ds(pl.multiple_of(o * HEAD_DIM, HEAD_DIM), HEAD_DIM)


def chosen(part, values, o, j):
    read, refs = values
    if len(refs) == 1:
        return read(refs[0], at_head(o))
    found = read(refs[0], cols(j))
    for step in range(1, part.steps):
        found = jnp.where(pl.program_id(0) == step, read(refs[step], cols(j)), found)
    return found


def store_decay(part, info, cumul_ref, o, out_ref):
    row = part.row(cumul_ref, info, o)
    out_ref[pl.ds(part.count * HEAD_DIM + o, 1), :] = jnp.broadcast_to(
        jnp.exp(row[:, -1:]), (1, HEAD_DIM)
    )


def pieces_kernel(part, info, key_ref, value_ref, cumul_ref, out_ref):
    def head(o, j):
        at = part.wide_cols(info, o)
        out_ref[at_head(o), :] = outer_sum(
            key_ref[:, at], trail_row(part.row(cumul_ref, info, o)), value_ref[:, at]
        )
        store_decay(part, info, cumul_ref, o, out_ref)

    part.each(head)


def first_pieces_kernel(part, info, key_ref, value_ref, decay_ref, out_ref, cumul_ref):
    @pl.when(pl.program_id(0) == 0)
    def _():
        cumul_ref[...] = cumulative(decay_ref[...])

    def head(o, j):
        out_ref[at_head(o), :] = outer_sum(
            key_ref[:, cols(j)], trail_row(part.row(cumul_ref, info, o)), value_ref[:, cols(j)]
        )
        store_decay(part, info, cumul_ref, o, out_ref)

    part.each(head)


def inner_kernel(part, info, query_ref, key_ref, value_ref, cumul_ref, out_ref):
    def head(o, j):
        row = part.row(cumul_ref, info, o)
        col = column(row)
        at = part.wide_cols(info, o)
        query, key, value = query_ref[:, at], key_ref[:, at], value_ref[:, at]
        for top in range(0, BLOCK, TILE):
            end = top + TILE
            scores = dot(query[top:end], key[:end], NT)
            spread = wide(col[top:end], end) - row[:, :end]
            causal = lax.broadcasted_iota(jnp.int32, (TILE, end), 0) + top >= (
                lax.broadcasted_iota(jnp.int32, (TILE, end), 1)
            )
            weights = (scores * jnp.exp(jnp.where(causal, spread, -1e30))).astype(bf16)
            out_ref[top:end, at_head(o)] = dot(weights, value[:end])

    part.each(head)


def output_kernel(
    part, offset, info, inner_ref, query_ref, cot_ref, gain_ref, cumul_ref, state_ref, before_ref,
    out_ref, sums_ref, square_ref, product_ref,
):
    @pl.when(pl.program_id(0) == 0)
    def _():
        square_ref[...] = jnp.zeros_like(square_ref)
        product_ref[...] = jnp.zeros_like(product_ref)

    def head(o, j):
        lead = jnp.exp(column(part.row(cumul_ref, info, o)))
        high, low = halves(state_ref[at_head(o), :])
        at = part.wide_cols(info, o)
        query = query_ref[:, at]
        out = inner_ref[:, at_head(offset + o)] + lead * (dot(query, high) + dot(query, low))
        out_ref[:, at_head(o)] = out
        square_ref[...] += out * out
        product_ref[...] += cot_ref[:, at].astype(f32) * gain_ref[:, at] * out

    part.each(head)

    @pl.when(pl.program_id(0) == part.steps - 1)
    def _():
        rows = lax.broadcasted_iota(jnp.int32, (8, HEAD_DIM), 0)
        total = before_ref[...]
        for place, ref in ((0, square_ref), (1, product_ref)):
            pick = jnp.where(rows == place, 1.0, 0.0).astype(bf16)
            high, low = halves(ref[...])
            total += dot(pick, high, NT) + dot(pick, low, NT)
        sums_ref[...] = total


def grad_kernel(features, part, held, info, *refs):
    outs, (cot_ref, gain_ref, query_ref, cumul_ref, *refs) = refs[:held], refs[held:]
    shares, (attended_ref, grad_ref, piece_ref) = refs[:-3], refs[-3:]
    sums = shares[0][...]
    for share in shares[1:]:
        sums = sums + share[...]
    inverse = lax.rsqrt(sums[0:1] / features + epsilon)
    mean_term = inverse * sums[1:2] / features
    inverse_col, mean_col = column(inverse), column(mean_term)

    def head(o, j):
        at = part.wide_cols(info, o)
        gain = gain_ref[:, at]
        normed = chosen(part, (lambda ref, at: ref[:, at], outs), o, j) * inverse_col
        attended_ref[:, cols(j)] = (normed * gain).astype(bf16)
        scaled_grad = cot_ref[:, at].astype(f32) * gain
        grad = (inverse_col * (scaled_grad - normed * mean_col)).astype(bf16)
        grad_ref[:, at_head(o)] = grad
        lead = jnp.exp(part.row(cumul_ref, info, o))
        piece_ref[at_head(o), :] = outer_sum(query_ref[:, at], lead, grad)
        store_decay(part, info, cumul_ref, o, piece_ref)

    part.each(head)


def backward_kernel(part, info, query_ref, key_ref, value_ref, grad_ref, cumul_ref, *refs):
    states, (grad_query_ref, inner_key_ref, inner_value_ref) = refs[:-3], refs[-3:]

    def head(o, j):
        row = part.row(cumul_ref, info, o)
        col = column(row)
        at = part.wide_cols(info, o)
        query, key = query_ref[:, at], key_ref[:, at]
        value, grad = value_ref[:, at], grad_ref[:, at_head(o)]
        high, low = halves(chosen(part, (lambda ref, at: ref[at, :], states), o, j))
        outer = jnp.exp(col) * (dot(grad, high, NT) + dot(grad, low, NT))
        for top in range(0, BLOCK, TILE):
            end = top + TILE
            scores = dot(key[top:end], query[top:], NT)
            grad_scores = dot(value[top:end], grad[top:], NT)
            spread = row[:, top:] - wide(col[top:end], BLOCK - top)
            causal = lax.broadcasted_iota(jnp.int32, spread.shape, 0) <= (
                lax.broadcasted_iota(jnp.int32, spread.shape, 1)
            )
            decays = jnp.exp(jnp.where(causal, spread, -1e30))
            weights = (scores * decays).astype(bf16)
            grad_weights = (grad_scores * decays).astype(bf16)
            inner_value_ref[top:end, at_head(o)] = dot(weights, grad[top:])
            inner_key_ref[top:end, at_head(o)] = dot(grad_weights, query[top:])
            inner_query = dot(grad_weights, key[top:end], TN)
            outer = inner_query + outer if top == 0 else jnp.concatenate(
                [outer[:top], outer[top:] + inner_query], axis=0
            )
        grad_query_ref[:, cols(j)] = outer.astype(bf16)

    part.each(head)


def final_kernel(
    part, info, inner_key_ref, inner_value_ref, key_ref, value_ref, cumul_ref, state_ref,
    grad_key_ref, grad_value_ref, token_ref,
):
    token_ref[...] = jnp.zeros_like(token_ref)

    def head(o, j):
        trail = column(trail_row(part.row(cumul_ref, info, o)))
        high, low = halves(state_ref[at_head(o), :])
        at = part.wide_cols(info, o)
        key, value = key_ref[:, at], value_ref[:, at]
        grad_key_ref[:, cols(j)] = (
            inner_key_ref[:, at_head(o)] + trail * (dot(value, high, NT) + dot(value, low, NT))
        ).astype(bf16)
        grad_value_ref[:, cols(j)] = (
            inner_value_ref[:, at_head(o)] + trail * (dot(key, high) + dot(key, low))
        ).astype(bf16)

    part.each(head)


def ordered(is_first, half, j, keep_ref, got_ref):
    rows = slice(j * HEAD_DIM, (j + 1) * HEAD_DIM)
    place = slice(half * HEAD_DIM + j, half * HEAD_DIM + j + 1)
    keep, got = keep_ref[rows, :], got_ref[rows, :]
    keep_decay, got_decay = keep_ref[place, :], got_ref[place, :]
    return (
        jnp.where(is_first, keep, got),
        jnp.where(is_first, got, keep),
        jnp.where(is_first, keep_decay, got_decay),
        jnp.where(is_first, got_decay, keep_decay),
    )


def scan_position(places, forward, info):
    member, pair = info[0][0], info[1][0]
    if forward:
        return member == 0, pair
    return member == 1, places - 1 - pair


def copy_kernel(info, in_ref, out_ref):
    out_ref[...] = in_ref[...]


def hop_kernel(half, p, position, info, keep_ref, got_ref, *refs):
    arrived, out_ref = refs[:-1], refs[-1]
    is_first, place = position(info)

    @pl.when(place == p)
    def _():
        for j in range(half):
            first, second, first_decay, second_decay = ordered(is_first, half, j, keep_ref, got_ref)
            value = second_decay * first + second
            for arrived_ref in arrived:
                value += (first_decay * second_decay) * arrived_ref[cols(j), :]
            out_ref[cols(j), :] = value


def last_kernel(half, position, info, keep_ref, got_ref, *refs):
    arrived, (mine_ref, send_ref) = refs[:-2], refs[-2:]
    is_first, place = position(info)
    for p in range(len(arrived) + 1):

        @pl.when(place == p)
        def _():
            for j in range(half):
                first, _, first_decay, _ = ordered(is_first, half, j, keep_ref, got_ref)
                if p == 0:
                    before, after = jnp.zeros_like(first), first
                else:
                    before = arrived[p - 1][cols(j), :]
                    after = first_decay * before + first
                mine_ref[cols(j), :] = jnp.where(is_first, before, after)
                send_ref[cols(j), :] = jnp.where(is_first, after, before)


def on_device(queries, key_vecs, value_vecs, log_decay, norm_gain, cotangent):
    tokens, width = queries.shape
    assert tokens == BLOCK
    heads = width // HEAD_DIM
    group_heads = heads // 2
    head_count = lax.axis_size("head")
    features = width * head_count
    places = lax.axis_size("seq") // 2
    my_index = lax.axis_index("seq")
    member, pair = my_index % 2, my_index // 2
    gain = norm_gain.reshape(1, width)
    info = (member.astype(jnp.int32).reshape(1), pair.astype(jnp.int32).reshape(1))

    any_spec = pl.BlockSpec(memory_space=pl.ANY)
    whole = jax.ShapeDtypeStruct((tokens, width), bf16)
    sums_shape = jax.ShapeDtypeStruct((8, tokens), f32)

    def states_of(count, extra=0):
        return jax.ShapeDtypeStruct((count * HEAD_DIM + extra, HEAD_DIM), f32)

    def local_of(count, dtype=f32):
        return jax.ShapeDtypeStruct((tokens, count * HEAD_DIM), dtype)

    def run(kernel, grid, ins, outs, scratch=(), after=(), aliases=None, cost=1.0, limit=24):
        used = len(ins)
        after = [x for i, x in enumerate(after) if not any(x is y for y in after[:i])]

        def body(member_ref, pair_ref, *refs):
            kernel((member_ref, pair_ref), *refs[:used], *refs[used + len(after):])

        return pl.pallas_call(
            body,
            out_shape=[shape for shape, _ in outs],
            grid_spec=pltpu.PrefetchScalarGridSpec(
                num_scalar_prefetch=2,
                grid=(grid,),
                in_specs=[spec for _, spec in ins] + [any_spec] * len(after),
                out_specs=[spec for _, spec in outs],
                scratch_shapes=list(scratch),
            ),
            input_output_aliases=aliases or {},
            compiler_params=pltpu.CompilerParams(vmem_limit_bytes=limit * 1024 * 1024),
            cost_estimate=pl.CostEstimate(
                flops=int(cost * 1e9), bytes_accessed=int(cost * 2.5e6), transcendentals=0
            ),
        )(*info, *[array for array, _ in ins], *after)

    def fixed(shape):
        return pl.BlockSpec(shape, lambda i, *info: (0,) * len(shape))

    def plain(array):
        return array, fixed(array.shape)

    def give(shape):
        return shape, fixed(shape.shape)

    class Calls(Part):
        def full_spec(self):
            width = self.per_step
            return pl.BlockSpec(
                (tokens, width * HEAD_DIM),
                lambda i, *info: (
                    0, (self.group(info) * self.group_heads + self.first) // width + i
                ),
            )

        def call(self, kernel, ins, outs, **options):
            return run(functools.partial(kernel, self), self.steps, ins, outs, **options)

    def parts_of(chunks, slot):
        count = group_heads // chunks
        return [Calls(c * count, count, slot, group_heads) for c in range(chunks)]

    swap = [(2 * p + m, 2 * p + 1 - m) for p in range(places) for m in (0, 1)]

    def chain(chunks, make_piece, forward, filler, on_mine, on_theirs):
        position = functools.partial(scan_position, places, forward)
        my_parts, their_parts = parts_of(chunks, "mine"), parts_of(chunks, "theirs")
        count = group_heads // chunks
        state, wide_state = states_of(count), states_of(count, 8)

        def device(place, m):
            return 2 * (place if forward else places - 1 - place) + m

        sends, keeps, received, last = [], [], [], ()

        def exchange(last):
            c = len(received)
            if c == 0 or c >= chunks:
                if c == 0:
                    received.append(lax.ppermute(sends[0], "seq", swap))
                return last
            sent, = run(copy_kernel, 1, [plain(sends[c])], [give(wide_state)], after=last, cost=0.02)
            received.append(lax.ppermute(sent, "seq", swap))
            return (sent,)

        for part in their_parts:
            sends.append(make_piece(part, last))
            last = () if forward and len(sends) == 1 else (sends[-1],)
        last = exchange(last)
        if forward:
            last = exchange(last)
        rest = [functools.partial(make_piece, part) for part in my_parts]
        for make in rest[:1] if forward else rest:
            keeps.append(make(last))
            last = (keeps[-1],)
        if not forward:
            last = exchange(last)
        arrived, mine, theirs, late = {}, [], [], []
        for step in range(chunks + places - 1):
            for p in range(places - 1):
                c = step - p
                if not 0 <= c < chunks:
                    continue
                ins = [plain(keeps[c]), plain(received[c])]
                if p > 0:
                    ins.append(plain(arrived[c, p]))
                value, = run(
                    functools.partial(hop_kernel, count, p, position), 1, ins, [give(state)],
                    after=last, cost=0.3,
                )
                pairs = [(device(p, m), device(p + 1, m)) for m in (0, 1)]
                arrived[c, p + 1] = lax.ppermute(value, "seq", pairs)
                last = (value,)
            last = exchange(last)
            while len(keeps) < chunks:
                keeps.append(rest[len(keeps)](last))
                last = (keeps[-1],)
            if filler:
                last = (filler.pop(0)(last),)
            c = step + 1 - places
            if c >= 0:
                ins = [plain(keeps[c]), plain(received[c])]
                ins += [plain(arrived[c, p]) for p in range(1, places)]
                own, send = run(
                    functools.partial(last_kernel, count, position), 1, ins, [give(state)] * 2,
                    after=last, cost=0.3,
                )
                theirs.append(lax.ppermute(send, "seq", swap))
                mine.append(own)
                last = (send,)
                filler.append(functools.partial(on_mine, c, own))
                late.append(functools.partial(on_theirs, c, theirs[c]))
                if c >= 2:
                    filler.append(late.pop(0))
                last = (filler.pop(0)(last),)
        for work in filler + late:
            last = (work(last),)
        return mine, theirs

    inner, outs = {}, {}
    held_cumul, held_sums = [], [jnp.zeros(sums_shape.shape, f32)]
    back_count = group_heads // BACKWARD_CHUNKS
    front_count = group_heads // FORWARD_CHUNKS
    per_back = back_count // front_count
    back_parts = {slot: parts_of(BACKWARD_CHUNKS, slot) for slot in ("mine", "theirs")}
    front_parts = {slot: parts_of(FORWARD_CHUNKS, slot) for slot in ("mine", "theirs")}

    def cumul_in():
        return plain(held_cumul[0])

    def forward_piece(part, after):
        if not held_cumul:
            piece, cumul = part.call(
                first_pieces_kernel,
                [(key_vecs, part.full_spec()), (value_vecs, part.full_spec()), plain(log_decay.T)],
                [give(states_of(part.count, 8)), give(jax.ShapeDtypeStruct((heads, tokens), f32))],
                cost=0.05, limit=60,
            )
            held_cumul.append(cumul)
            return piece
        return part.call(
            pieces_kernel, [plain(key_vecs), plain(value_vecs), cumul_in()],
            [give(states_of(part.count, 8))], after=after, cost=0.05,
        )[0]

    def inner_work(slot, c, after):
        part = back_parts[slot][c]
        inner[slot, c], = part.call(
            inner_kernel, [plain(queries), plain(key_vecs), plain(value_vecs), cumul_in()],
            [give(local_of(part.count))], after=after, cost=2.2 if inner else 0.1,
        )
        return inner[slot, c]

    def output_work(slot, c, before, after):
        part = front_parts[slot][c]
        outs[slot, c], held_sums[0] = run(
            functools.partial(output_kernel, part, c % per_back * front_count), part.steps,
            [plain(inner[slot, c // per_back]), plain(queries), plain(cotangent), plain(gain),
             cumul_in(), plain(before), plain(held_sums[0])],
            [give(local_of(part.count)), give(sums_shape)],
            scratch=[pltpu.VMEM((tokens, HEAD_DIM), f32)] * 2, after=after, cost=0.8,
        )
        return held_sums[0]

    works = [
        functools.partial(inner_work, slot, c)
        for c in range(BACKWARD_CHUNKS) for slot in ("mine", "theirs")
    ]
    mine, theirs = chain(
        FORWARD_CHUNKS, forward_piece, True, works,
        functools.partial(output_work, "mine"), functools.partial(output_work, "theirs"),
    )
    states = {"mine": mine, "theirs": theirs}

    sums = held_sums[0]
    shares = [sums] + [
        lax.ppermute(sums, "head", [(i, (i + k) % head_count) for i in range(head_count)])
        for k in range(1, head_count)
    ]

    attended, grad_queries, grad_keys, grad_values = [], [], [], []
    grads, inner_grads = {}, {}

    def target(held):
        return tuple(held[-1:])

    def covered(c):
        return range(c * per_back, (c + 1) * per_back)

    def backward_piece(part, after):
        before = target(attended)
        c = part.first // part.count
        ins = [plain(outs[part.slot, i]) for i in covered(c)]
        ins += [plain(cotangent), plain(gain), plain(queries), cumul_in()]
        ins += [plain(share) for share in shares]
        whole_out, grads[part.slot, c], piece = run(
            functools.partial(grad_kernel, features, part, per_back), part.steps, ins,
            [(whole, part.full_spec()), give(local_of(part.count, bf16)),
             give(states_of(part.count, 8))],
            after=before + tuple(after), aliases={2 + len(ins): 0} if before else None, cost=2.0,
        )
        attended.append(whole_out)
        return piece

    def backward_work(slot, c, after):
        part, held = back_parts[slot][c], target(grad_queries)
        ins = [plain(queries), plain(key_vecs), plain(value_vecs), plain(grads[slot, c]), cumul_in()]
        ins += [plain(states[slot][i]) for i in covered(c)]
        whole_out, *inner_grads[slot, c] = part.call(
            backward_kernel, ins,
            [(whole, part.full_spec()), give(local_of(part.count)), give(local_of(part.count))],
            after=held + tuple(after), aliases={2 + len(ins): 0} if held else None, cost=4.3,
        )
        grad_queries.append(whole_out)
        return inner_grads[slot, c][0]

    def final_work(slot, c, before, after):
        part, held = back_parts[slot][c], target(grad_keys) + target(grad_values)
        ins = [plain(array) for array in (*inner_grads[slot, c], key_vecs, value_vecs)]
        ins += [cumul_in(), plain(before)]
        whole_key, whole_value, token = part.call(
            final_kernel, ins,
            [(whole, part.full_spec())] * 2 + [give(jax.ShapeDtypeStruct((8, HEAD_DIM), f32))],
            after=held + tuple(after),
            aliases={2 + len(ins): 0, 3 + len(ins): 1} if held else None, cost=2.0,
        )
        grad_keys.append(whole_key)
        grad_values.append(whole_value)
        return token

    works = [
        functools.partial(backward_work, slot, c)
        for c in range(BACKWARD_CHUNKS) for slot in ("mine", "theirs")
    ]
    chain(
        BACKWARD_CHUNKS, backward_piece, False, works,
        functools.partial(final_work, "mine"), functools.partial(final_work, "theirs"),
    )
    return attended[-1], grad_queries[-1], grad_keys[-1], grad_values[-1]


def solution(mesh):
    return jax.shard_map(
        on_device,
        mesh=mesh,
        in_specs=(
            P("seq", "head"),
            P("seq", "head"),
            P("seq", "head"),
            P("seq", "head"),
            P("head"),
            P("seq", "head"),
        ),
        out_specs=(P("seq", "head"), P("seq", "head"), P("seq", "head"), P("seq", "head")),
        check_vma=False,
    )
```

```python
import functools

import jax
import jax.numpy as jnp
from jax import lax
from jax.experimental import pallas as pl
from jax.experimental.pallas import tpu as pltpu
from jax.sharding import PartitionSpec as P

HEAD_DIM = 128
BLOCK = 512
FORWARD_CHUNKS = 2
BACKWARD_CHUNKS = 2
TILE = 256
epsilon = 1e-06
f32 = jnp.float32
bf16 = jnp.bfloat16

NN = (((1,), (0,)), ((), ()))
NT = (((1,), (1,)), ((), ()))
TN = (((0,), (0,)), ((), ()))


def dot(a, b, dims=NN):
    return lax.dot_general(a, b, dims, preferred_element_type=f32)


def halves(x):
    high = x.astype(bf16)
    return high, (x - high.astype(f32)).astype(bf16)


def column(row):
    return jnp.transpose(jnp.broadcast_to(row, (HEAD_DIM, row.shape[1])))


def wide(col, width):
    return jnp.concatenate([col] * (width // HEAD_DIM), axis=1)


def cumulative(decay):
    length = decay.shape[1]
    first = decay.astype(bf16)
    rest = decay - first.astype(f32)
    second = rest.astype(bf16)
    third = (rest - second.astype(f32)).astype(bf16)
    upto = lax.broadcasted_iota(jnp.int32, (length, length), 0) <= lax.broadcasted_iota(
        jnp.int32, (length, length), 1
    )
    upto = jnp.where(upto, 1.0, 0.0).astype(bf16)
    return dot(first, upto) + dot(second, upto) + dot(third, upto)


def trail_row(row):
    return jnp.exp(row[:, -1:] - row)


def outer_sum(left, scale_row, right):
    scaled = jnp.transpose(left.astype(f32)) * scale_row
    high, low = halves(scaled)
    return dot(high, right) + dot(low, right)


def cols(j):
    return slice(j * HEAD_DIM, (j + 1) * HEAD_DIM)


class Part:
    def __init__(self, first, count, slot, group_heads):
        self.first, self.count, self.slot, self.group_heads = first, count, slot, group_heads
        self.steps = 2 if count % 4 == 0 else 1
        self.per_step = count // self.steps

    def group(self, info):
        return info[0][0] if self.slot == "mine" else 1 - info[0][0]

    def head(self, info, o):
        return self.group(info) * self.group_heads + self.first + o

    def row(self, cumul_ref, info, o):
        return cumul_ref[pl.ds(self.head(info, o), 1), :]

    def wide_cols(self, info, o):
        return pl.ds(pl.multiple_of(self.head(info, o) * HEAD_DIM, HEAD_DIM), HEAD_DIM)

    def each(self, body):
        for j in range(self.per_step):
            body(pl.program_id(0) * self.per_step + j if self.steps > 1 else j, j)


def at_head(o):
    if isinstance(o, int):
        return cols(o)
    return pl.ds(pl.multiple_of(o * HEAD_DIM, HEAD_DIM), HEAD_DIM)


def chosen(part, values, o, j):
    read, refs = values
    if len(refs) == 1:
        return read(refs[0], at_head(o))
    found = read(refs[0], cols(j))
    for step in range(1, part.steps):
        found = jnp.where(pl.program_id(0) == step, read(refs[step], cols(j)), found)
    return found


def store_decay(part, info, cumul_ref, o, out_ref):
    row = part.row(cumul_ref, info, o)
    out_ref[pl.ds(part.count * HEAD_DIM + o, 1), :] = jnp.broadcast_to(
        jnp.exp(row[:, -1:]), (1, HEAD_DIM)
    )


def pieces_kernel(part, info, key_ref, value_ref, cumul_ref, out_ref):
    def head(o, j):
        at = part.wide_cols(info, o)
        out_ref[at_head(o), :] = outer_sum(
            key_ref[:, at], trail_row(part.row(cumul_ref, info, o)), value_ref[:, at]
        )
        store_decay(part, info, cumul_ref, o, out_ref)

    part.each(head)


def first_pieces_kernel(part, info, key_ref, value_ref, decay_ref, out_ref, cumul_ref):
    @pl.when(pl.program_id(0) == 0)
    def _():
        cumul_ref[...] = cumulative(decay_ref[...])

    def head(o, j):
        out_ref[at_head(o), :] = outer_sum(
            key_ref[:, cols(j)], trail_row(part.row(cumul_ref, info, o)), value_ref[:, cols(j)]
        )
        store_decay(part, info, cumul_ref, o, out_ref)

    part.each(head)


def inner_kernel(part, info, query_ref, key_ref, value_ref, cumul_ref, out_ref):
    def head(o, j):
        row = part.row(cumul_ref, info, o)
        col = column(row)
        at = part.wide_cols(info, o)
        query, key, value = query_ref[:, at], key_ref[:, at], value_ref[:, at]
        for top in range(0, BLOCK, TILE):
            end = top + TILE
            scores = dot(query[top:end], key[:end], NT)
            spread = wide(col[top:end], end) - row[:, :end]
            causal = lax.broadcasted_iota(jnp.int32, (TILE, end), 0) + top >= (
                lax.broadcasted_iota(jnp.int32, (TILE, end), 1)
            )
            weights = (scores * jnp.exp(jnp.where(causal, spread, -1e30))).astype(bf16)
            out_ref[top:end, at_head(o)] = dot(weights, value[:end])

    part.each(head)


def output_kernel(
    part, offset, info, inner_ref, query_ref, cot_ref, gain_ref, cumul_ref, state_ref, before_ref,
    out_ref, sums_ref, square_ref, product_ref,
):
    @pl.when(pl.program_id(0) == 0)
    def _():
        square_ref[...] = jnp.zeros_like(square_ref)
        product_ref[...] = jnp.zeros_like(product_ref)

    def head(o, j):
        lead = jnp.exp(column(part.row(cumul_ref, info, o)))
        high, low = halves(state_ref[at_head(o), :])
        at = part.wide_cols(info, o)
        query = query_ref[:, at]
        out = inner_ref[:, at_head(offset + o)] + lead * (dot(query, high) + dot(query, low))
        out_ref[:, at_head(o)] = out
        square_ref[...] += out * out
        product_ref[...] += cot_ref[:, at].astype(f32) * gain_ref[:, at] * out

    part.each(head)

    @pl.when(pl.program_id(0) == part.steps - 1)
    def _():
        rows = lax.broadcasted_iota(jnp.int32, (8, HEAD_DIM), 0)
        total = before_ref[...]
        for place, ref in ((0, square_ref), (1, product_ref)):
            pick = jnp.where(rows == place, 1.0, 0.0).astype(bf16)
            high, low = halves(ref[...])
            total += dot(pick, high, NT) + dot(pick, low, NT)
        sums_ref[...] = total


def grad_kernel(features, part, held, info, *refs):
    outs, (cot_ref, gain_ref, query_ref, cumul_ref, *refs) = refs[:held], refs[held:]
    shares, (attended_ref, grad_ref, piece_ref) = refs[:-3], refs[-3:]
    sums = shares[0][...]
    for share in shares[1:]:
        sums = sums + share[...]
    inverse = lax.rsqrt(sums[0:1] / features + epsilon)
    mean_term = inverse * sums[1:2] / features
    inverse_col, mean_col = column(inverse), column(mean_term)

    def head(o, j):
        at = part.wide_cols(info, o)
        gain = gain_ref[:, at]
        normed = chosen(part, (lambda ref, at: ref[:, at], outs), o, j) * inverse_col
        attended_ref[:, cols(j)] = (normed * gain).astype(bf16)
        scaled_grad = cot_ref[:, at].astype(f32) * gain
        grad = (inverse_col * (scaled_grad - normed * mean_col)).astype(bf16)
        grad_ref[:, at_head(o)] = grad
        lead = jnp.exp(part.row(cumul_ref, info, o))
        piece_ref[at_head(o), :] = outer_sum(query_ref[:, at], lead, grad)
        store_decay(part, info, cumul_ref, o, piece_ref)

    part.each(head)


def backward_kernel(part, info, query_ref, key_ref, value_ref, grad_ref, cumul_ref, *refs):
    states, (grad_query_ref, inner_key_ref, inner_value_ref) = refs[:-3], refs[-3:]

    def head(o, j):
        row = part.row(cumul_ref, info, o)
        col = column(row)
        at = part.wide_cols(info, o)
        query, key = query_ref[:, at], key_ref[:, at]
        value, grad = value_ref[:, at], grad_ref[:, at_head(o)]
        high, low = halves(chosen(part, (lambda ref, at: ref[at, :], states), o, j))
        outer = jnp.exp(col) * (dot(grad, high, NT) + dot(grad, low, NT))
        for top in range(0, BLOCK, TILE):
            end = top + TILE
            scores = dot(key[top:end], query[top:], NT)
            grad_scores = dot(value[top:end], grad[top:], NT)
            spread = row[:, top:] - wide(col[top:end], BLOCK - top)
            causal = lax.broadcasted_iota(jnp.int32, spread.shape, 0) <= (
                lax.broadcasted_iota(jnp.int32, spread.shape, 1)
            )
            decays = jnp.exp(jnp.where(causal, spread, -1e30))
            weights = (scores * decays).astype(bf16)
            grad_weights = (grad_scores * decays).astype(bf16)
            inner_value_ref[top:end, at_head(o)] = dot(weights, grad[top:])
            inner_key_ref[top:end, at_head(o)] = dot(grad_weights, query[top:])
            inner_query = dot(grad_weights, key[top:end], TN)
            outer = inner_query + outer if top == 0 else jnp.concatenate(
                [outer[:top], outer[top:] + inner_query], axis=0
            )
        grad_query_ref[:, cols(j)] = outer.astype(bf16)

    part.each(head)


def final_kernel(
    part, info, inner_key_ref, inner_value_ref, key_ref, value_ref, cumul_ref, state_ref,
    grad_key_ref, grad_value_ref,
):
    def head(o, j):
        trail = column(trail_row(part.row(cumul_ref, info, o)))
        high, low = halves(state_ref[at_head(o), :])
        at = part.wide_cols(info, o)
        key, value = key_ref[:, at], value_ref[:, at]
        grad_key_ref[:, cols(j)] = (
            inner_key_ref[:, at_head(o)] + trail * (dot(value, high, NT) + dot(value, low, NT))
        ).astype(bf16)
        grad_value_ref[:, cols(j)] = (
            inner_value_ref[:, at_head(o)] + trail * (dot(key, high) + dot(key, low))
        ).astype(bf16)

    part.each(head)


def ordered(is_first, half, j, keep_ref, got_ref):
    rows = slice(j * HEAD_DIM, (j + 1) * HEAD_DIM)
    place = slice(half * HEAD_DIM + j, half * HEAD_DIM + j + 1)
    keep, got = keep_ref[rows, :], got_ref[rows, :]
    keep_decay, got_decay = keep_ref[place, :], got_ref[place, :]
    return (
        jnp.where(is_first, keep, got),
        jnp.where(is_first, got, keep),
        jnp.where(is_first, keep_decay, got_decay),
        jnp.where(is_first, got_decay, keep_decay),
    )


def scan_position(places, forward, info):
    member, pair = info[0][0], info[1][0]
    if forward:
        return member == 0, pair
    return member == 1, places - 1 - pair


def copy_kernel(info, in_ref, out_ref):
    out_ref[...] = in_ref[...]


def hop_kernel(half, p, position, info, keep_ref, got_ref, *refs):
    arrived, out_ref = refs[:-1], refs[-1]
    is_first, place = position(info)

    @pl.when(place == p)
    def _():
        for j in range(half):
            first, second, first_decay, second_decay = ordered(is_first, half, j, keep_ref, got_ref)
            value = second_decay * first + second
            for arrived_ref in arrived:
                value += (first_decay * second_decay) * arrived_ref[cols(j), :]
            out_ref[cols(j), :] = value


def last_kernel(half, position, info, keep_ref, got_ref, *refs):
    arrived, (mine_ref, send_ref) = refs[:-2], refs[-2:]
    is_first, place = position(info)
    for p in range(len(arrived) + 1):

        @pl.when(place == p)
        def _():
            for j in range(half):
                first, _, first_decay, _ = ordered(is_first, half, j, keep_ref, got_ref)
                if p == 0:
                    before, after = jnp.zeros_like(first), first
                else:
                    before = arrived[p - 1][cols(j), :]
                    after = first_decay * before + first
                mine_ref[cols(j), :] = jnp.where(is_first, before, after)
                send_ref[cols(j), :] = jnp.where(is_first, after, before)


def on_device(queries, key_vecs, value_vecs, log_decay, norm_gain, cotangent):
    tokens, width = queries.shape
    assert tokens == BLOCK
    heads = width // HEAD_DIM
    group_heads = heads // 2
    head_count = lax.axis_size("head")
    features = width * head_count
    places = lax.axis_size("seq") // 2
    my_index = lax.axis_index("seq")
    member, pair = my_index % 2, my_index // 2
    gain = norm_gain.reshape(1, width)
    info = (member.astype(jnp.int32).reshape(1), pair.astype(jnp.int32).reshape(1))

    any_spec = pl.BlockSpec(memory_space=pl.ANY)
    whole = jax.ShapeDtypeStruct((tokens, width), bf16)
    sums_shape = jax.ShapeDtypeStruct((8, tokens), f32)

    def states_of(count, extra=0):
        return jax.ShapeDtypeStruct((count * HEAD_DIM + extra, HEAD_DIM), f32)

    def local_of(count, dtype=f32):
        return jax.ShapeDtypeStruct((tokens, count * HEAD_DIM), dtype)

    def run(kernel, grid, ins, outs, scratch=(), after=(), aliases=None, cost=1.0, limit=24):
        used = len(ins)
        after = [x for i, x in enumerate(after) if not any(x is y for y in after[:i])]

        def body(member_ref, pair_ref, *refs):
            kernel((member_ref, pair_ref), *refs[:used], *refs[used + len(after):])

        return pl.pallas_call(
            body,
            out_shape=[shape for shape, _ in outs],
            grid_spec=pltpu.PrefetchScalarGridSpec(
                num_scalar_prefetch=2,
                grid=(grid,),
                in_specs=[spec for _, spec in ins] + [any_spec] * len(after),
                out_specs=[spec for _, spec in outs],
                scratch_shapes=list(scratch),
            ),
            input_output_aliases=aliases or {},
            compiler_params=pltpu.CompilerParams(vmem_limit_bytes=limit * 1024 * 1024),
            cost_estimate=pl.CostEstimate(
                flops=int(cost * 1e9), bytes_accessed=int(cost * 2.5e6), transcendentals=0
            ),
        )(*info, *[array for array, _ in ins], *after)

    def fixed(shape):
        return pl.BlockSpec(shape, lambda i, *info: (0,) * len(shape))

    def plain(array):
        return array, fixed(array.shape)

    def give(shape):
        return shape, fixed(shape.shape)

    class Calls(Part):
        def full_spec(self):
            width = self.per_step
            return pl.BlockSpec(
                (tokens, width * HEAD_DIM),
                lambda i, *info: (
                    0, (self.group(info) * self.group_heads + self.first) // width + i
                ),
            )

        def call(self, kernel, ins, outs, **options):
            return run(functools.partial(kernel, self), self.steps, ins, outs, **options)

    def parts_of(chunks, slot):
        count = group_heads // chunks
        return [Calls(c * count, count, slot, group_heads) for c in range(chunks)]

    swap = [(2 * p + m, 2 * p + 1 - m) for p in range(places) for m in (0, 1)]

    def chain(chunks, make_piece, forward, filler, on_mine, on_theirs):
        position = functools.partial(scan_position, places, forward)
        my_parts, their_parts = parts_of(chunks, "mine"), parts_of(chunks, "theirs")
        count = group_heads // chunks
        state, wide_state = states_of(count), states_of(count, 8)

        def device(place, m):
            return 2 * (place if forward else places - 1 - place) + m

        sends, keeps, received, last = [], [], [], ()

        def exchange(last):
            c = len(received)
            if c == 0 or c >= chunks:
                if c == 0:
                    received.append(lax.ppermute(sends[0], "seq", swap))
                return last
            sent, = run(copy_kernel, 1, [plain(sends[c])], [give(wide_state)], after=last, cost=0.02)
            received.append(lax.ppermute(sent, "seq", swap))
            return (sent,)

        for part in their_parts:
            sends.append(make_piece(part, last))
            last = () if forward and len(sends) == 1 else (sends[-1],)
        last = exchange(last)
        for part in my_parts:
            keeps.append(make_piece(part, last))
            last = (keeps[-1],)
        last = exchange(last)
        arrived, mine, theirs, late = {}, [], [], []
        for step in range(chunks + places - 1):
            for p in range(places - 1):
                c = step - p
                if not 0 <= c < chunks:
                    continue
                ins = [plain(keeps[c]), plain(received[c])]
                if p > 0:
                    ins.append(plain(arrived[c, p]))
                value, = run(
                    functools.partial(hop_kernel, count, p, position), 1, ins, [give(state)],
                    after=last, cost=0.3,
                )
                pairs = [(device(p, m), device(p + 1, m)) for m in (0, 1)]
                arrived[c, p + 1] = lax.ppermute(value, "seq", pairs)
                last = (value,)
            last = exchange(last)
            c = step + 1 - places
            if c >= 0:
                ins = [plain(keeps[c]), plain(received[c])]
                ins += [plain(arrived[c, p]) for p in range(1, places)]
                own, send = run(
                    functools.partial(last_kernel, count, position), 1, ins, [give(state)] * 2,
                    after=last, cost=0.3,
                )
                theirs.append(lax.ppermute(send, "seq", swap))
                mine.append(own)
                last = (send,)
                filler.append(functools.partial(on_mine, c, own))
                late.append(functools.partial(on_theirs, c, theirs[c]))
                if c >= 2:
                    filler.append(late.pop(0))
                if forward and c >= chunks - 2 and filler:
                    last = (filler.pop(0)(last),)
            if filler:
                last = (filler.pop(0)(last),)
        for work in filler + late:
            last = (work(last),)
        return mine, theirs

    inner, outs = {}, {}
    held_cumul, held_sums = [], [jnp.zeros(sums_shape.shape, f32)]
    back_count = group_heads // BACKWARD_CHUNKS
    front_count = group_heads // FORWARD_CHUNKS
    per_back = back_count // front_count
    back_parts = {slot: parts_of(BACKWARD_CHUNKS, slot) for slot in ("mine", "theirs")}
    front_parts = {slot: parts_of(FORWARD_CHUNKS, slot) for slot in ("mine", "theirs")}

    def cumul_in():
        return plain(held_cumul[0])

    def forward_piece(part, after):
        if not held_cumul:
            piece, cumul = part.call(
                first_pieces_kernel,
                [(key_vecs, part.full_spec()), (value_vecs, part.full_spec()), plain(log_decay.T)],
                [give(states_of(part.count, 8)), give(jax.ShapeDtypeStruct((heads, tokens), f32))],
                cost=0.05, limit=60,
            )
            held_cumul.append(cumul)
            return piece
        return part.call(
            pieces_kernel, [plain(key_vecs), plain(value_vecs), cumul_in()],
            [give(states_of(part.count, 8))], after=after, cost=0.05,
        )[0]

    def inner_work(slot, c, after):
        part = back_parts[slot][c]
        inner[slot, c], = part.call(
            inner_kernel, [plain(queries), plain(key_vecs), plain(value_vecs), cumul_in()],
            [give(local_of(part.count))], after=after, cost=2.2 if inner else 0.1,
        )
        return inner[slot, c]

    def output_work(slot, c, before, after):
        part = front_parts[slot][c]
        outs[slot, c], held_sums[0] = run(
            functools.partial(output_kernel, part, c % per_back * front_count), part.steps,
            [plain(inner[slot, c // per_back]), plain(queries), plain(cotangent), plain(gain),
             cumul_in(), plain(before), plain(held_sums[0])],
            [give(local_of(part.count)), give(sums_shape)],
            scratch=[pltpu.VMEM((tokens, HEAD_DIM), f32)] * 2, after=after, cost=0.8,
        )
        return held_sums[0]

    works = [
        functools.partial(inner_work, slot, c)
        for c in range(BACKWARD_CHUNKS) for slot in ("mine", "theirs")
    ]
    mine, theirs = chain(
        FORWARD_CHUNKS, forward_piece, True, works,
        functools.partial(output_work, "mine"), functools.partial(output_work, "theirs"),
    )
    states = {"mine": mine, "theirs": theirs}

    sums = held_sums[0]
    shares = [sums] + [
        lax.ppermute(sums, "head", [(i, (i + k) % head_count) for i in range(head_count)])
        for k in range(1, head_count)
    ]

    attended, grad_queries, grad_keys, grad_values = [], [], [], []
    grads, inner_grads = {}, {}

    def target(held):
        return tuple(held[-1:])

    def covered(c):
        return range(c * per_back, (c + 1) * per_back)

    def backward_piece(part, after):
        before = target(attended)
        c = part.first // part.count
        ins = [plain(outs[part.slot, i]) for i in covered(c)]
        ins += [plain(cotangent), plain(gain), plain(queries), cumul_in()]
        ins += [plain(share) for share in shares]
        whole_out, grads[part.slot, c], piece = run(
            functools.partial(grad_kernel, features, part, per_back), part.steps, ins,
            [(whole, part.full_spec()), give(local_of(part.count, bf16)),
             give(states_of(part.count, 8))],
            after=before + tuple(after), aliases={2 + len(ins): 0} if before else None, cost=2.0,
        )
        attended.append(whole_out)
        return piece

    def backward_work(slot, c, after):
        part, held = back_parts[slot][c], target(grad_queries)
        ins = [plain(queries), plain(key_vecs), plain(value_vecs), plain(grads[slot, c]), cumul_in()]
        ins += [plain(states[slot][i]) for i in covered(c)]
        whole_out, *inner_grads[slot, c] = part.call(
            backward_kernel, ins,
            [(whole, part.full_spec()), give(local_of(part.count)), give(local_of(part.count))],
            after=held + tuple(after), aliases={2 + len(ins): 0} if held else None, cost=4.3,
        )
        grad_queries.append(whole_out)
        return inner_grads[slot, c][0]

    def final_work(slot, c, before, after):
        part, held = back_parts[slot][c], target(grad_keys) + target(grad_values)
        ins = [plain(array) for array in (*inner_grads[slot, c], key_vecs, value_vecs)]
        ins += [cumul_in(), plain(before)]
        whole_key, whole_value = part.call(
            final_kernel, ins, [(whole, part.full_spec())] * 2, after=held + tuple(after),
            aliases={2 + len(ins): 0, 3 + len(ins): 1} if held else None, cost=2.0,
        )
        grad_keys.append(whole_key)
        grad_values.append(whole_value)
        return whole_key

    works = [
        functools.partial(backward_work, slot, c)
        for c in range(BACKWARD_CHUNKS) for slot in ("mine", "theirs")
    ]
    chain(
        BACKWARD_CHUNKS, backward_piece, False, works,
        functools.partial(final_work, "mine"), functools.partial(final_work, "theirs"),
    )
    return attended[-1], grad_queries[-1], grad_keys[-1], grad_values[-1]


def solution(mesh):
    return jax.shard_map(
        on_device,
        mesh=mesh,
        in_specs=(
            P("seq", "head"),
            P("seq", "head"),
            P("seq", "head"),
            P("seq", "head"),
            P("head"),
            P("seq", "head"),
        ),
        out_specs=(P("seq", "head"), P("seq", "head"), P("seq", "head"), P("seq", "head")),
        check_vma=False,
    )
```

```python
import functools

import jax
import jax.numpy as jnp
from jax import lax
from jax.experimental import pallas as pl
from jax.experimental.pallas import tpu as pltpu
from jax.sharding import PartitionSpec as P

HEAD_DIM = 128
BLOCK = 512
FORWARD_CHUNKS = 2
BACKWARD_CHUNKS = 2
TILE = 256
epsilon = 1e-06
f32 = jnp.float32
bf16 = jnp.bfloat16

NN = (((1,), (0,)), ((), ()))
NT = (((1,), (1,)), ((), ()))
TN = (((0,), (0,)), ((), ()))


def dot(a, b, dims=NN):
    return lax.dot_general(a, b, dims, preferred_element_type=f32)


def halves(x):
    high = x.astype(bf16)
    return high, (x - high.astype(f32)).astype(bf16)


def column(row):
    return jnp.transpose(jnp.broadcast_to(row, (HEAD_DIM, row.shape[1])))


def wide(col, width):
    return jnp.concatenate([col] * (width // HEAD_DIM), axis=1)


def cumulative(decay):
    heads, length = decay.shape
    first = decay.astype(bf16).astype(f32)
    rest = decay - first
    second = rest.astype(bf16).astype(f32)
    parts = jnp.concatenate([first, second, rest - second], axis=0).astype(bf16)
    upto = lax.broadcasted_iota(jnp.int32, (length, length), 0) <= lax.broadcasted_iota(
        jnp.int32, (length, length), 1
    )
    sums = dot(parts, jnp.where(upto, 1.0, 0.0).astype(bf16))
    return sums[:heads] + sums[heads:2 * heads] + sums[2 * heads:]


def trail_row(row):
    return jnp.exp(row[:, -1:] - row)


def outer_sum(left, scale_row, right):
    scaled = jnp.transpose(left.astype(f32)) * scale_row
    high, low = halves(scaled)
    return dot(high, right) + dot(low, right)


def cols(j):
    return slice(j * HEAD_DIM, (j + 1) * HEAD_DIM)


class Part:
    def __init__(self, first, count, slot, group_heads):
        self.first, self.count, self.slot, self.group_heads = first, count, slot, group_heads
        self.steps = 2 if count % 4 == 0 else 1
        self.per_step = count // self.steps

    def group(self, info):
        return info[0][0] if self.slot == "mine" else 1 - info[0][0]

    def head(self, info, o):
        return self.group(info) * self.group_heads + self.first + o

    def row(self, cumul_ref, info, o):
        return cumul_ref[pl.ds(self.head(info, o), 1), :]

    def wide_cols(self, info, o):
        return pl.ds(pl.multiple_of(self.head(info, o) * HEAD_DIM, HEAD_DIM), HEAD_DIM)

    def each(self, body):
        for j in range(self.per_step):
            body(pl.program_id(0) * self.per_step + j if self.steps > 1 else j, j)


def at_head(o):
    if isinstance(o, int):
        return cols(o)
    return pl.ds(pl.multiple_of(o * HEAD_DIM, HEAD_DIM), HEAD_DIM)


def chosen(part, values, o, j):
    read, refs = values
    if len(refs) == 1:
        return read(refs[0], at_head(o))
    found = read(refs[0], cols(j))
    for step in range(1, part.steps):
        found = jnp.where(pl.program_id(0) == step, read(refs[step], cols(j)), found)
    return found


def store_decay(part, info, cumul_ref, o, out_ref):
    row = part.row(cumul_ref, info, o)
    out_ref[pl.ds(part.count * HEAD_DIM + o, 1), :] = jnp.broadcast_to(
        jnp.exp(row[:, -1:]), (1, HEAD_DIM)
    )


def pieces_kernel(part, info, key_ref, value_ref, cumul_ref, out_ref):
    def head(o, j):
        at = part.wide_cols(info, o)
        out_ref[at_head(o), :] = outer_sum(
            key_ref[:, at], trail_row(part.row(cumul_ref, info, o)), value_ref[:, at]
        )
        store_decay(part, info, cumul_ref, o, out_ref)

    part.each(head)


def first_pieces_kernel(part, info, key_ref, value_ref, decay_ref, out_ref, cumul_ref):
    @pl.when(pl.program_id(0) == 0)
    def _():
        cumul_ref[...] = cumulative(decay_ref[...])

    def head(o, j):
        out_ref[at_head(o), :] = outer_sum(
            key_ref[:, cols(j)], trail_row(part.row(cumul_ref, info, o)), value_ref[:, cols(j)]
        )
        store_decay(part, info, cumul_ref, o, out_ref)

    part.each(head)


def inner_kernel(part, info, query_ref, key_ref, value_ref, cumul_ref, out_ref):
    def head(o, j):
        row = part.row(cumul_ref, info, o)
        col = column(row)
        at = part.wide_cols(info, o)
        query, key, value = query_ref[:, at], key_ref[:, at], value_ref[:, at]
        for top in range(0, BLOCK, TILE):
            end = top + TILE
            scores = dot(query[top:end], key[:end], NT)
            spread = wide(col[top:end], end) - row[:, :end]
            causal = lax.broadcasted_iota(jnp.int32, (TILE, end), 0) + top >= (
                lax.broadcasted_iota(jnp.int32, (TILE, end), 1)
            )
            weights = (scores * jnp.exp(jnp.where(causal, spread, -1e30))).astype(bf16)
            out_ref[top:end, at_head(o)] = dot(weights, value[:end])

    part.each(head)


def output_kernel(
    part, offset, info, inner_ref, query_ref, cot_ref, gain_ref, cumul_ref, state_ref, before_ref,
    out_ref, sums_ref, square_ref, product_ref,
):
    @pl.when(pl.program_id(0) == 0)
    def _():
        square_ref[...] = jnp.zeros_like(square_ref)
        product_ref[...] = jnp.zeros_like(product_ref)

    def head(o, j):
        lead = jnp.exp(column(part.row(cumul_ref, info, o)))
        high, low = halves(state_ref[at_head(o), :])
        at = part.wide_cols(info, o)
        query = query_ref[:, at]
        out = inner_ref[:, at_head(offset + o)] + lead * (dot(query, high) + dot(query, low))
        out_ref[:, at_head(o)] = out
        square_ref[...] += out * out
        product_ref[...] += cot_ref[:, at].astype(f32) * gain_ref[:, at] * out

    part.each(head)

    @pl.when(pl.program_id(0) == part.steps - 1)
    def _():
        rows = lax.broadcasted_iota(jnp.int32, (8, HEAD_DIM), 0)
        total = before_ref[...]
        for place, ref in ((0, square_ref), (1, product_ref)):
            pick = jnp.where(rows == place, 1.0, 0.0).astype(bf16)
            high, low = halves(ref[...])
            total += dot(pick, high, NT) + dot(pick, low, NT)
        sums_ref[...] = total


def grad_kernel(features, part, held, info, *refs):
    outs, (cot_ref, gain_ref, query_ref, cumul_ref, *refs) = refs[:held], refs[held:]
    shares, (attended_ref, grad_ref, piece_ref, inverse_ref, mean_ref) = refs[:-5], refs[-5:]

    @pl.when(pl.program_id(0) == 0)
    def _():
        sums = shares[0][...]
        for share in shares[1:]:
            sums = sums + share[...]
        inverse = lax.rsqrt(sums[0:1] / features + epsilon)
        inverse_ref[...] = column(inverse)
        mean_ref[...] = column(inverse * sums[1:2] / features)

    inverse_col, mean_col = inverse_ref[...], mean_ref[...]

    def head(o, j):
        at = part.wide_cols(info, o)
        gain = gain_ref[:, at]
        normed = chosen(part, (lambda ref, at: ref[:, at], outs), o, j) * inverse_col
        attended_ref[:, cols(j)] = (normed * gain).astype(bf16)
        scaled_grad = cot_ref[:, at].astype(f32) * gain
        grad = (inverse_col * (scaled_grad - normed * mean_col)).astype(bf16)
        grad_ref[:, at_head(o)] = grad
        lead = jnp.exp(part.row(cumul_ref, info, o))
        piece_ref[at_head(o), :] = outer_sum(query_ref[:, at], lead, grad)
        store_decay(part, info, cumul_ref, o, piece_ref)

    part.each(head)


def backward_kernel(part, info, query_ref, key_ref, value_ref, grad_ref, cumul_ref, *refs):
    states, (grad_query_ref, inner_key_ref, inner_value_ref) = refs[:-3], refs[-3:]

    def head(o, j):
        row = part.row(cumul_ref, info, o)
        col = column(row)
        at = part.wide_cols(info, o)
        query, key = query_ref[:, at], key_ref[:, at]
        value, grad = value_ref[:, at], grad_ref[:, at_head(o)]
        high, low = halves(chosen(part, (lambda ref, at: ref[at, :], states), o, j))
        outer = jnp.exp(col) * (dot(grad, high, NT) + dot(grad, low, NT))
        for top in range(0, BLOCK, TILE):
            end = top + TILE
            scores = dot(key[top:end], query[top:], NT)
            grad_scores = dot(value[top:end], grad[top:], NT)
            spread = row[:, top:] - wide(col[top:end], BLOCK - top)
            causal = lax.broadcasted_iota(jnp.int32, spread.shape, 0) <= (
                lax.broadcasted_iota(jnp.int32, spread.shape, 1)
            )
            decays = jnp.exp(jnp.where(causal, spread, -1e30))
            weights = (scores * decays).astype(bf16)
            grad_weights = (grad_scores * decays).astype(bf16)
            inner_value_ref[top:end, at_head(o)] = dot(weights, grad[top:])
            inner_key_ref[top:end, at_head(o)] = dot(grad_weights, query[top:])
            inner_query = dot(grad_weights, key[top:end], TN)
            outer = inner_query + outer if top == 0 else jnp.concatenate(
                [outer[:top], outer[top:] + inner_query], axis=0
            )
        grad_query_ref[:, cols(j)] = outer.astype(bf16)

    part.each(head)


def final_kernel(
    part, info, inner_key_ref, inner_value_ref, key_ref, value_ref, cumul_ref, state_ref,
    grad_key_ref, grad_value_ref,
):
    def head(o, j):
        trail = column(trail_row(part.row(cumul_ref, info, o)))
        high, low = halves(state_ref[at_head(o), :])
        at = part.wide_cols(info, o)
        key, value = key_ref[:, at], value_ref[:, at]
        grad_key_ref[:, cols(j)] = (
            inner_key_ref[:, at_head(o)] + trail * (dot(value, high, NT) + dot(value, low, NT))
        ).astype(bf16)
        grad_value_ref[:, cols(j)] = (
            inner_value_ref[:, at_head(o)] + trail * (dot(key, high) + dot(key, low))
        ).astype(bf16)

    part.each(head)


def ordered(is_first, half, j, keep_ref, got_ref):
    rows = slice(j * HEAD_DIM, (j + 1) * HEAD_DIM)
    place = slice(half * HEAD_DIM + j, half * HEAD_DIM + j + 1)
    keep, got = keep_ref[rows, :], got_ref[rows, :]
    keep_decay, got_decay = keep_ref[place, :], got_ref[place, :]
    return (
        jnp.where(is_first, keep, got),
        jnp.where(is_first, got, keep),
        jnp.where(is_first, keep_decay, got_decay),
        jnp.where(is_first, got_decay, keep_decay),
    )


def scan_position(places, forward, info):
    member, pair = info[0][0], info[1][0]
    if forward:
        return member == 0, pair
    return member == 1, places - 1 - pair


def copy_kernel(info, in_ref, out_ref):
    out_ref[...] = in_ref[...]


def hop_kernel(half, p, position, info, keep_ref, got_ref, *refs):
    arrived, out_ref = refs[:-1], refs[-1]
    is_first, place = position(info)

    @pl.when(place == p)
    def _():
        for j in range(half):
            first, second, first_decay, second_decay = ordered(is_first, half, j, keep_ref, got_ref)
            value = second_decay * first + second
            for arrived_ref in arrived:
                value += (first_decay * second_decay) * arrived_ref[cols(j), :]
            out_ref[cols(j), :] = value


def last_kernel(half, position, info, keep_ref, got_ref, *refs):
    arrived, (mine_ref, send_ref) = refs[:-2], refs[-2:]
    is_first, place = position(info)
    for p in range(len(arrived) + 1):

        @pl.when(place == p)
        def _():
            for j in range(half):
                first, _, first_decay, _ = ordered(is_first, half, j, keep_ref, got_ref)
                if p == 0:
                    before, after = jnp.zeros_like(first), first
                else:
                    before = arrived[p - 1][cols(j), :]
                    after = first_decay * before + first
                mine_ref[cols(j), :] = jnp.where(is_first, before, after)
                send_ref[cols(j), :] = jnp.where(is_first, after, before)


def on_device(queries, key_vecs, value_vecs, log_decay, norm_gain, cotangent):
    tokens, width = queries.shape
    assert tokens == BLOCK
    heads = width // HEAD_DIM
    group_heads = heads // 2
    head_count = lax.axis_size("head")
    features = width * head_count
    places = lax.axis_size("seq") // 2
    my_index = lax.axis_index("seq")
    member, pair = my_index % 2, my_index // 2
    gain = norm_gain.reshape(1, width)
    info = (member.astype(jnp.int32).reshape(1), pair.astype(jnp.int32).reshape(1))

    any_spec = pl.BlockSpec(memory_space=pl.ANY)
    whole = jax.ShapeDtypeStruct((tokens, width), bf16)
    sums_shape = jax.ShapeDtypeStruct((8, tokens), f32)

    def states_of(count, extra=0):
        return jax.ShapeDtypeStruct((count * HEAD_DIM + extra, HEAD_DIM), f32)

    def local_of(count, dtype=f32):
        return jax.ShapeDtypeStruct((tokens, count * HEAD_DIM), dtype)

    def run(kernel, grid, ins, outs, scratch=(), after=(), aliases=None, cost=1.0, limit=24):
        used = len(ins)
        after = [x for i, x in enumerate(after) if not any(x is y for y in after[:i])]

        def body(member_ref, pair_ref, *refs):
            kernel((member_ref, pair_ref), *refs[:used], *refs[used + len(after):])

        return pl.pallas_call(
            body,
            out_shape=[shape for shape, _ in outs],
            grid_spec=pltpu.PrefetchScalarGridSpec(
                num_scalar_prefetch=2,
                grid=(grid,),
                in_specs=[spec for _, spec in ins] + [any_spec] * len(after),
                out_specs=[spec for _, spec in outs],
                scratch_shapes=list(scratch),
            ),
            input_output_aliases=aliases or {},
            compiler_params=pltpu.CompilerParams(vmem_limit_bytes=limit * 1024 * 1024),
            cost_estimate=pl.CostEstimate(
                flops=int(cost * 1e9), bytes_accessed=int(cost * 2.5e6), transcendentals=0
            ),
        )(*info, *[array for array, _ in ins], *after)

    def fixed(shape):
        return pl.BlockSpec(shape, lambda i, *info: (0,) * len(shape))

    def plain(array):
        return array, fixed(array.shape)

    def give(shape):
        return shape, fixed(shape.shape)

    class Calls(Part):
        def full_spec(self):
            width = self.per_step
            return pl.BlockSpec(
                (tokens, width * HEAD_DIM),
                lambda i, *info: (
                    0, (self.group(info) * self.group_heads + self.first) // width + i
                ),
            )

        def call(self, kernel, ins, outs, **options):
            return run(functools.partial(kernel, self), self.steps, ins, outs, **options)

    def parts_of(chunks, slot):
        count = group_heads // chunks
        return [Calls(c * count, count, slot, group_heads) for c in range(chunks)]

    swap = [(2 * p + m, 2 * p + 1 - m) for p in range(places) for m in (0, 1)]

    def chain(chunks, make_piece, forward, filler, on_mine, on_theirs):
        position = functools.partial(scan_position, places, forward)
        my_parts, their_parts = parts_of(chunks, "mine"), parts_of(chunks, "theirs")
        count = group_heads // chunks
        state, wide_state = states_of(count), states_of(count, 8)

        def device(place, m):
            return 2 * (place if forward else places - 1 - place) + m

        sends, keeps, received, last = [], [], [], ()

        def exchange(last):
            c = len(received)
            if c == 0 or c >= chunks:
                if c == 0:
                    received.append(lax.ppermute(sends[0], "seq", swap))
                return last
            sent, = run(copy_kernel, 1, [plain(sends[c])], [give(wide_state)], after=last, cost=0.02)
            received.append(lax.ppermute(sent, "seq", swap))
            return (sent,)

        for part in their_parts:
            sends.append(make_piece(part, last))
            last = () if forward and len(sends) == 1 else (sends[-1],)
        last = exchange(last)
        for part in my_parts:
            keeps.append(make_piece(part, last))
            last = (keeps[-1],)
        last = exchange(last)
        arrived, mine, theirs, late = {}, [], [], []
        for step in range(chunks + places - 1):
            for p in range(places - 1):
                c = step - p
                if not 0 <= c < chunks:
                    continue
                ins = [plain(keeps[c]), plain(received[c])]
                if p > 0:
                    ins.append(plain(arrived[c, p]))
                value, = run(
                    functools.partial(hop_kernel, count, p, position), 1, ins, [give(state)],
                    after=last, cost=0.3,
                )
                pairs = [(device(p, m), device(p + 1, m)) for m in (0, 1)]
                arrived[c, p + 1] = lax.ppermute(value, "seq", pairs)
                last = (value,)
            last = exchange(last)
            c = step + 1 - places
            if c >= 0:
                ins = [plain(keeps[c]), plain(received[c])]
                ins += [plain(arrived[c, p]) for p in range(1, places)]
                own, send = run(
                    functools.partial(last_kernel, count, position), 1, ins, [give(state)] * 2,
                    after=last, cost=0.3,
                )
                theirs.append(lax.ppermute(send, "seq", swap))
                mine.append(own)
                last = (send,)
                filler.append(functools.partial(on_mine, c, own))
                late.append(functools.partial(on_theirs, c, theirs[c]))
                if c >= 2:
                    filler.append(late.pop(0))
                if forward and c >= chunks - 2 and filler:
                    last = (filler.pop(0)(last),)
            if filler:
                last = (filler.pop(0)(last),)
        for work in filler + late:
            last = (work(last),)
        return mine, theirs

    inner, outs = {}, {}
    held_cumul, held_sums = [], [jnp.zeros(sums_shape.shape, f32)]
    back_count = group_heads // BACKWARD_CHUNKS
    front_count = group_heads // FORWARD_CHUNKS
    per_back = back_count // front_count
    back_parts = {slot: parts_of(BACKWARD_CHUNKS, slot) for slot in ("mine", "theirs")}
    front_parts = {slot: parts_of(FORWARD_CHUNKS, slot) for slot in ("mine", "theirs")}

    def cumul_in():
        return plain(held_cumul[0])

    def forward_piece(part, after):
        if not held_cumul:
            piece, cumul = part.call(
                first_pieces_kernel,
                [(key_vecs, part.full_spec()), (value_vecs, part.full_spec()), plain(log_decay.T)],
                [give(states_of(part.count, 8)), give(jax.ShapeDtypeStruct((heads, tokens), f32))],
                cost=0.05, limit=60,
            )
            held_cumul.append(cumul)
            return piece
        return part.call(
            pieces_kernel, [plain(key_vecs), plain(value_vecs), cumul_in()],
            [give(states_of(part.count, 8))], after=after, cost=0.05,
        )[0]

    def inner_work(slot, c, after):
        part = back_parts[slot][c]
        inner[slot, c], = part.call(
            inner_kernel, [plain(queries), plain(key_vecs), plain(value_vecs), cumul_in()],
            [give(local_of(part.count))], after=after, cost=2.2 if inner else 0.1,
        )
        return inner[slot, c]

    def output_work(slot, c, before, after):
        part = front_parts[slot][c]
        outs[slot, c], held_sums[0] = run(
            functools.partial(output_kernel, part, c % per_back * front_count), part.steps,
            [plain(inner[slot, c // per_back]), plain(queries), plain(cotangent), plain(gain),
             cumul_in(), plain(before), plain(held_sums[0])],
            [give(local_of(part.count)), give(sums_shape)],
            scratch=[pltpu.VMEM((tokens, HEAD_DIM), f32)] * 2, after=after, cost=0.8,
        )
        return held_sums[0]

    works = [
        functools.partial(inner_work, slot, c)
        for c in range(BACKWARD_CHUNKS) for slot in ("mine", "theirs")
    ]
    mine, theirs = chain(
        FORWARD_CHUNKS, forward_piece, True, works,
        functools.partial(output_work, "mine"), functools.partial(output_work, "theirs"),
    )
    states = {"mine": mine, "theirs": theirs}

    sums = held_sums[0]
    shares = [sums] + [
        lax.ppermute(sums, "head", [(i, (i + k) % head_count) for i in range(head_count)])
        for k in range(1, head_count)
    ]

    attended, grad_queries, grad_keys, grad_values = [], [], [], []
    grads, inner_grads = {}, {}

    def target(held):
        return tuple(held[-1:])

    def covered(c):
        return range(c * per_back, (c + 1) * per_back)

    def backward_piece(part, after):
        before = target(attended)
        c = part.first // part.count
        ins = [plain(outs[part.slot, i]) for i in covered(c)]
        ins += [plain(cotangent), plain(gain), plain(queries), cumul_in()]
        ins += [plain(share) for share in shares]
        whole_out, grads[part.slot, c], piece = run(
            functools.partial(grad_kernel, features, part, per_back), part.steps, ins,
            [(whole, part.full_spec()), give(local_of(part.count, bf16)),
             give(states_of(part.count, 8))],
            scratch=[pltpu.VMEM((tokens, HEAD_DIM), f32)] * 2,
            after=before + tuple(after), aliases={2 + len(ins): 0} if before else None, cost=2.0,
        )
        attended.append(whole_out)
        return piece

    def backward_work(slot, c, after):
        part, held = back_parts[slot][c], target(grad_queries)
        ins = [plain(queries), plain(key_vecs), plain(value_vecs), plain(grads[slot, c]), cumul_in()]
        ins += [plain(states[slot][i]) for i in covered(c)]
        whole_out, *inner_grads[slot, c] = part.call(
            backward_kernel, ins,
            [(whole, part.full_spec()), give(local_of(part.count)), give(local_of(part.count))],
            after=held + tuple(after), aliases={2 + len(ins): 0} if held else None, cost=4.3,
        )
        grad_queries.append(whole_out)
        return inner_grads[slot, c][0]

    def final_work(slot, c, before, after):
        part, held = back_parts[slot][c], target(grad_keys) + target(grad_values)
        ins = [plain(array) for array in (*inner_grads[slot, c], key_vecs, value_vecs)]
        ins += [cumul_in(), plain(before)]
        whole_key, whole_value = part.call(
            final_kernel, ins, [(whole, part.full_spec())] * 2, after=held + tuple(after),
            aliases={2 + len(ins): 0, 3 + len(ins): 1} if held else None, cost=2.0,
        )
        grad_keys.append(whole_key)
        grad_values.append(whole_value)
        return whole_key

    works = [
        functools.partial(backward_work, slot, c)
        for c in range(BACKWARD_CHUNKS) for slot in ("mine", "theirs")
    ]
    chain(
        BACKWARD_CHUNKS, backward_piece, False, works,
        functools.partial(final_work, "mine"), functools.partial(final_work, "theirs"),
    )
    return attended[-1], grad_queries[-1], grad_keys[-1], grad_values[-1]


def solution(mesh):
    return jax.shard_map(
        on_device,
        mesh=mesh,
        in_specs=(
            P("seq", "head"),
            P("seq", "head"),
            P("seq", "head"),
            P("seq", "head"),
            P("head"),
            P("seq", "head"),
        ),
        out_specs=(P("seq", "head"), P("seq", "head"), P("seq", "head"), P("seq", "head")),
        check_vma=False,
    )
```

```python
import functools

import jax
import jax.numpy as jnp
from jax import lax
from jax.experimental import pallas as pl
from jax.experimental.pallas import tpu as pltpu
from jax.sharding import PartitionSpec as P

HEAD_DIM = 128
BLOCK = 512
FORWARD_CHUNKS = 2
BACKWARD_CHUNKS = 2
TILE = 256
epsilon = 1e-06
f32 = jnp.float32
bf16 = jnp.bfloat16

NN = (((1,), (0,)), ((), ()))
NT = (((1,), (1,)), ((), ()))
TN = (((0,), (0,)), ((), ()))


def dot(a, b, dims=NN):
    return lax.dot_general(a, b, dims, preferred_element_type=f32)


def halves(x):
    high = x.astype(bf16)
    return high, (x - high.astype(f32)).astype(bf16)


def column(row):
    return jnp.transpose(jnp.broadcast_to(row, (HEAD_DIM, row.shape[1])))


def wide(col, width):
    return jnp.concatenate([col] * (width // HEAD_DIM), axis=1)


def cumulative(decay):
    length = decay.shape[1]
    first = decay.astype(bf16)
    rest = decay - first.astype(f32)
    second = rest.astype(bf16)
    third = (rest - second.astype(f32)).astype(bf16)
    upto = lax.broadcasted_iota(jnp.int32, (length, length), 0) <= lax.broadcasted_iota(
        jnp.int32, (length, length), 1
    )
    upto = jnp.where(upto, 1.0, 0.0).astype(bf16)
    return dot(first, upto) + dot(second, upto) + dot(third, upto)


def trail_row(row):
    return jnp.exp(row[:, -1:] - row)


def outer_sum(left, scale_row, right):
    scaled = jnp.transpose(left.astype(f32)) * scale_row
    high, low = halves(scaled)
    return dot(high, right) + dot(low, right)


def cols(j):
    return slice(j * HEAD_DIM, (j + 1) * HEAD_DIM)


class Part:
    def __init__(self, first, count, slot, group_heads, per_step=0):
        self.first, self.count, self.slot, self.group_heads = first, count, slot, group_heads
        self.steps = count // per_step if per_step else 2 if count % 4 == 0 else 1
        self.per_step = count // self.steps

    def group(self, info):
        return info[0][0] if self.slot == "mine" else 1 - info[0][0]

    def head(self, info, o):
        return self.group(info) * self.group_heads + self.first + o

    def row(self, cumul_ref, info, o):
        return cumul_ref[pl.ds(self.head(info, o), 1), :]

    def wide_cols(self, info, o):
        return pl.ds(pl.multiple_of(self.head(info, o) * HEAD_DIM, HEAD_DIM), HEAD_DIM)

    def each(self, body):
        for j in range(self.per_step):
            body(pl.program_id(0) * self.per_step + j if self.steps > 1 else j, j)


def at_head(o):
    if isinstance(o, int):
        return cols(o)
    return pl.ds(pl.multiple_of(o * HEAD_DIM, HEAD_DIM), HEAD_DIM)


def chosen(part, values, o, j):
    read, refs = values
    if len(refs) == 1:
        return read(refs[0], at_head(o))
    found = read(refs[0], cols(j))
    for step in range(1, part.steps):
        found = jnp.where(pl.program_id(0) == step, read(refs[step], cols(j)), found)
    return found


def store_decay(part, info, cumul_ref, o, out_ref):
    row = part.row(cumul_ref, info, o)
    out_ref[pl.ds(part.count * HEAD_DIM + o, 1), :] = jnp.broadcast_to(
        jnp.exp(row[:, -1:]), (1, HEAD_DIM)
    )


def pieces_kernel(part, info, key_ref, value_ref, cumul_ref, out_ref):
    def head(o, j):
        at = part.wide_cols(info, o)
        out_ref[at_head(o), :] = outer_sum(
            key_ref[:, at], trail_row(part.row(cumul_ref, info, o)), value_ref[:, at]
        )
        store_decay(part, info, cumul_ref, o, out_ref)

    part.each(head)


def first_pieces_kernel(part, info, key_ref, value_ref, decay_ref, out_ref, cumul_ref):
    @pl.when(pl.program_id(0) == 0)
    def _():
        cumul_ref[...] = cumulative(decay_ref[...])

    def head(o, j):
        out_ref[at_head(o), :] = outer_sum(
            key_ref[:, cols(j)], trail_row(part.row(cumul_ref, info, o)), value_ref[:, cols(j)]
        )
        store_decay(part, info, cumul_ref, o, out_ref)

    part.each(head)


def inner_kernel(part, info, query_ref, key_ref, value_ref, cumul_ref, out_ref):
    def head(o, j):
        row = part.row(cumul_ref, info, o)
        col = column(row)
        at = part.wide_cols(info, o)
        query, key, value = query_ref[:, at], key_ref[:, at], value_ref[:, at]
        for top in range(0, BLOCK, TILE):
            end = top + TILE
            scores = dot(query[top:end], key[:end], NT)
            spread = wide(col[top:end], end) - row[:, :end]
            causal = lax.broadcasted_iota(jnp.int32, (TILE, end), 0) + top >= (
                lax.broadcasted_iota(jnp.int32, (TILE, end), 1)
            )
            weights = (scores * jnp.exp(jnp.where(causal, spread, -1e30))).astype(bf16)
            out_ref[top:end, at_head(o)] = dot(weights, value[:end])

    part.each(head)


def output_kernel(
    part, offset, info, inner_ref, query_ref, cot_ref, gain_ref, cumul_ref, state_ref, before_ref,
    out_ref, sums_ref, square_ref, product_ref,
):
    @pl.when(pl.program_id(0) == 0)
    def _():
        square_ref[...] = jnp.zeros_like(square_ref)
        product_ref[...] = jnp.zeros_like(product_ref)

    def head(o, j):
        lead = jnp.exp(column(part.row(cumul_ref, info, o)))
        high, low = halves(state_ref[at_head(o), :])
        at = part.wide_cols(info, o)
        query = query_ref[:, at]
        out = inner_ref[:, at_head(offset + o)] + lead * (dot(query, high) + dot(query, low))
        out_ref[:, at_head(o)] = out
        square_ref[...] += out * out
        product_ref[...] += cot_ref[:, at].astype(f32) * gain_ref[:, at] * out

    part.each(head)

    @pl.when(pl.program_id(0) == part.steps - 1)
    def _():
        rows = lax.broadcasted_iota(jnp.int32, (8, HEAD_DIM), 0)
        total = before_ref[...]
        for place, ref in ((0, square_ref), (1, product_ref)):
            pick = jnp.where(rows == place, 1.0, 0.0).astype(bf16)
            high, low = halves(ref[...])
            total += dot(pick, high, NT) + dot(pick, low, NT)
        sums_ref[...] = total


def grad_kernel(features, part, held, info, *refs):
    outs, (cot_ref, gain_ref, query_ref, cumul_ref, *refs) = refs[:held], refs[held:]
    shares, (attended_ref, grad_ref, piece_ref) = refs[:-3], refs[-3:]
    sums = shares[0][...]
    for share in shares[1:]:
        sums = sums + share[...]
    inverse = lax.rsqrt(sums[0:1] / features + epsilon)
    mean_term = inverse * sums[1:2] / features
    inverse_col, mean_col = column(inverse), column(mean_term)

    def head(o, j):
        at = part.wide_cols(info, o)
        gain = gain_ref[:, at]
        normed = chosen(part, (lambda ref, at: ref[:, at], outs), o, j) * inverse_col
        attended_ref[:, cols(j)] = (normed * gain).astype(bf16)
        scaled_grad = cot_ref[:, at].astype(f32) * gain
        grad = (inverse_col * (scaled_grad - normed * mean_col)).astype(bf16)
        grad_ref[:, at_head(o)] = grad
        lead = jnp.exp(part.row(cumul_ref, info, o))
        piece_ref[at_head(o), :] = outer_sum(query_ref[:, at], lead, grad)
        store_decay(part, info, cumul_ref, o, piece_ref)

    part.each(head)


def backward_kernel(part, info, query_ref, key_ref, value_ref, grad_ref, cumul_ref, *refs):
    states, (grad_query_ref, inner_key_ref, inner_value_ref) = refs[:-3], refs[-3:]

    def head(o, j):
        row = part.row(cumul_ref, info, o)
        col = column(row)
        at = part.wide_cols(info, o)
        query, key = query_ref[:, at], key_ref[:, at]
        value, grad = value_ref[:, at], grad_ref[:, at_head(o)]
        high, low = halves(chosen(part, (lambda ref, at: ref[at, :], states), o, j))
        outer = jnp.exp(col) * (dot(grad, high, NT) + dot(grad, low, NT))
        for top in range(0, BLOCK, TILE):
            end = top + TILE
            scores = dot(key[top:end], query[top:], NT)
            grad_scores = dot(value[top:end], grad[top:], NT)
            spread = row[:, top:] - wide(col[top:end], BLOCK - top)
            causal = lax.broadcasted_iota(jnp.int32, spread.shape, 0) <= (
                lax.broadcasted_iota(jnp.int32, spread.shape, 1)
            )
            decays = jnp.exp(jnp.where(causal, spread, -1e30))
            weights = (scores * decays).astype(bf16)
            grad_weights = (grad_scores * decays).astype(bf16)
            inner_value_ref[top:end, at_head(o)] = dot(weights, grad[top:])
            inner_key_ref[top:end, at_head(o)] = dot(grad_weights, query[top:])
            inner_query = dot(grad_weights, key[top:end], TN)
            outer = inner_query + outer if top == 0 else jnp.concatenate(
                [outer[:top], outer[top:] + inner_query], axis=0
            )
        grad_query_ref[:, cols(j)] = outer.astype(bf16)

    part.each(head)


def final_kernel(
    part, info, inner_key_ref, inner_value_ref, key_ref, value_ref, cumul_ref, state_ref,
    grad_key_ref, grad_value_ref,
):
    def head(o, j):
        trail = column(trail_row(part.row(cumul_ref, info, o)))
        high, low = halves(state_ref[at_head(o), :])
        at = part.wide_cols(info, o)
        key, value = key_ref[:, at], value_ref[:, at]
        grad_key_ref[:, cols(j)] = (
            inner_key_ref[:, at_head(o)] + trail * (dot(value, high, NT) + dot(value, low, NT))
        ).astype(bf16)
        grad_value_ref[:, cols(j)] = (
            inner_value_ref[:, at_head(o)] + trail * (dot(key, high) + dot(key, low))
        ).astype(bf16)

    part.each(head)


def ordered(is_first, half, j, keep_ref, got_ref):
    rows = slice(j * HEAD_DIM, (j + 1) * HEAD_DIM)
    place = slice(half * HEAD_DIM + j, half * HEAD_DIM + j + 1)
    keep, got = keep_ref[rows, :], got_ref[rows, :]
    keep_decay, got_decay = keep_ref[place, :], got_ref[place, :]
    return (
        jnp.where(is_first, keep, got),
        jnp.where(is_first, got, keep),
        jnp.where(is_first, keep_decay, got_decay),
        jnp.where(is_first, got_decay, keep_decay),
    )


def scan_position(places, forward, info):
    member, pair = info[0][0], info[1][0]
    if forward:
        return member == 0, pair
    return member == 1, places - 1 - pair


def copy_kernel(info, in_ref, out_ref):
    out_ref[...] = in_ref[...]


def hop_kernel(half, p, position, info, keep_ref, got_ref, *refs):
    arrived, out_ref = refs[:-1], refs[-1]
    is_first, place = position(info)

    @pl.when(place == p)
    def _():
        for j in range(half):
            first, second, first_decay, second_decay = ordered(is_first, half, j, keep_ref, got_ref)
            value = second_decay * first + second
            for arrived_ref in arrived:
                value += (first_decay * second_decay) * arrived_ref[cols(j), :]
            out_ref[cols(j), :] = value


def last_kernel(half, position, info, keep_ref, got_ref, *refs):
    arrived, (mine_ref, send_ref) = refs[:-2], refs[-2:]
    is_first, place = position(info)
    for p in range(len(arrived) + 1):

        @pl.when(place == p)
        def _():
            for j in range(half):
                first, _, first_decay, _ = ordered(is_first, half, j, keep_ref, got_ref)
                if p == 0:
                    before, after = jnp.zeros_like(first), first
                else:
                    before = arrived[p - 1][cols(j), :]
                    after = first_decay * before + first
                mine_ref[cols(j), :] = jnp.where(is_first, before, after)
                send_ref[cols(j), :] = jnp.where(is_first, after, before)


def on_device(queries, key_vecs, value_vecs, log_decay, norm_gain, cotangent):
    tokens, width = queries.shape
    assert tokens == BLOCK
    heads = width // HEAD_DIM
    group_heads = heads // 2
    head_count = lax.axis_size("head")
    features = width * head_count
    places = lax.axis_size("seq") // 2
    my_index = lax.axis_index("seq")
    member, pair = my_index % 2, my_index // 2
    gain = norm_gain.reshape(1, width)
    info = (member.astype(jnp.int32).reshape(1), pair.astype(jnp.int32).reshape(1))

    any_spec = pl.BlockSpec(memory_space=pl.ANY)
    whole = jax.ShapeDtypeStruct((tokens, width), bf16)
    sums_shape = jax.ShapeDtypeStruct((8, tokens), f32)

    def states_of(count, extra=0):
        return jax.ShapeDtypeStruct((count * HEAD_DIM + extra, HEAD_DIM), f32)

    def local_of(count, dtype=f32):
        return jax.ShapeDtypeStruct((tokens, count * HEAD_DIM), dtype)

    def run(kernel, grid, ins, outs, scratch=(), after=(), aliases=None, cost=1.0, limit=24):
        used = len(ins)
        after = [x for i, x in enumerate(after) if not any(x is y for y in after[:i])]

        def body(member_ref, pair_ref, *refs):
            kernel((member_ref, pair_ref), *refs[:used], *refs[used + len(after):])

        return pl.pallas_call(
            body,
            out_shape=[shape for shape, _ in outs],
            grid_spec=pltpu.PrefetchScalarGridSpec(
                num_scalar_prefetch=2,
                grid=(grid,),
                in_specs=[spec for _, spec in ins] + [any_spec] * len(after),
                out_specs=[spec for _, spec in outs],
                scratch_shapes=list(scratch),
            ),
            input_output_aliases=aliases or {},
            compiler_params=pltpu.CompilerParams(vmem_limit_bytes=limit * 1024 * 1024),
            cost_estimate=pl.CostEstimate(
                flops=int(cost * 1e9), bytes_accessed=int(cost * 2.5e6), transcendentals=0
            ),
        )(*info, *[array for array, _ in ins], *after)

    def fixed(shape):
        return pl.BlockSpec(shape, lambda i, *info: (0,) * len(shape))

    def plain(array):
        return array, fixed(array.shape)

    def give(shape):
        return shape, fixed(shape.shape)

    class Calls(Part):
        def full_spec(self):
            width = self.per_step
            return pl.BlockSpec(
                (tokens, width * HEAD_DIM),
                lambda i, *info: (
                    0, (self.group(info) * self.group_heads + self.first) // width + i
                ),
            )

        def call(self, kernel, ins, outs, **options):
            return run(functools.partial(kernel, self), self.steps, ins, outs, **options)

    def parts_of(chunks, slot, per_step=0):
        count = group_heads // chunks
        return [Calls(c * count, count, slot, group_heads, per_step) for c in range(chunks)]

    swap = [(2 * p + m, 2 * p + 1 - m) for p in range(places) for m in (0, 1)]

    def chain(chunks, make_piece, forward, filler, on_mine, on_theirs):
        position = functools.partial(scan_position, places, forward)
        my_parts, their_parts = parts_of(chunks, "mine"), parts_of(chunks, "theirs")
        count = group_heads // chunks
        state, wide_state = states_of(count), states_of(count, 8)

        def device(place, m):
            return 2 * (place if forward else places - 1 - place) + m

        sends, keeps, received, last = [], [], [], ()

        def exchange(last):
            c = len(received)
            if c == 0 or c >= chunks:
                if c == 0:
                    received.append(lax.ppermute(sends[0], "seq", swap))
                return last
            sent, = run(copy_kernel, 1, [plain(sends[c])], [give(wide_state)], after=last, cost=0.02)
            received.append(lax.ppermute(sent, "seq", swap))
            return (sent,)

        for part in their_parts:
            sends.append(make_piece(part, last))
            last = () if forward and len(sends) == 1 else (sends[-1],)
        last = exchange(last)
        for part in my_parts:
            keeps.append(make_piece(part, last))
            last = (keeps[-1],)
        last = exchange(last)
        arrived, mine, theirs, late = {}, [], [], []
        for step in range(chunks + places - 1):
            for p in range(places - 1):
                c = step - p
                if not 0 <= c < chunks:
                    continue
                ins = [plain(keeps[c]), plain(received[c])]
                if p > 0:
                    ins.append(plain(arrived[c, p]))
                value, = run(
                    functools.partial(hop_kernel, count, p, position), 1, ins, [give(state)],
                    after=last, cost=0.3,
                )
                pairs = [(device(p, m), device(p + 1, m)) for m in (0, 1)]
                arrived[c, p + 1] = lax.ppermute(value, "seq", pairs)
                last = (value,)
            last = exchange(last)
            c = step + 1 - places
            if c >= 0:
                ins = [plain(keeps[c]), plain(received[c])]
                ins += [plain(arrived[c, p]) for p in range(1, places)]
                own, send = run(
                    functools.partial(last_kernel, count, position), 1, ins, [give(state)] * 2,
                    after=last, cost=0.3,
                )
                theirs.append(lax.ppermute(send, "seq", swap))
                mine.append(own)
                last = (send,)
                filler.append(functools.partial(on_mine, c, own))
                late.append(functools.partial(on_theirs, c, theirs[c]))
                if c >= 2:
                    filler.append(late.pop(0))
                if forward and c >= chunks - 2 and filler:
                    last = (filler.pop(0)(last),)
            if filler:
                last = (filler.pop(0)(last),)
        for work in filler + late:
            last = (work(last),)
        return mine, theirs

    inner, outs = {}, {}
    held_cumul, held_sums = [], [jnp.zeros(sums_shape.shape, f32)]
    back_count = group_heads // BACKWARD_CHUNKS
    front_count = group_heads // FORWARD_CHUNKS
    per_back = back_count // front_count
    back_parts = {slot: parts_of(BACKWARD_CHUNKS, slot) for slot in ("mine", "theirs")}
    front_parts = {slot: parts_of(FORWARD_CHUNKS, slot, front_count) for slot in ("mine", "theirs")}

    def cumul_in():
        return plain(held_cumul[0])

    def forward_piece(part, after):
        if not held_cumul:
            piece, cumul = part.call(
                first_pieces_kernel,
                [(key_vecs, part.full_spec()), (value_vecs, part.full_spec()), plain(log_decay.T)],
                [give(states_of(part.count, 8)), give(jax.ShapeDtypeStruct((heads, tokens), f32))],
                cost=0.05, limit=60,
            )
            held_cumul.append(cumul)
            return piece
        return part.call(
            pieces_kernel, [plain(key_vecs), plain(value_vecs), cumul_in()],
            [give(states_of(part.count, 8))], after=after, cost=0.05,
        )[0]

    def inner_work(slot, c, after):
        part = back_parts[slot][c]
        inner[slot, c], = part.call(
            inner_kernel, [plain(queries), plain(key_vecs), plain(value_vecs), cumul_in()],
            [give(local_of(part.count))], after=after, cost=2.2 if inner else 0.1,
        )
        return inner[slot, c]

    def output_work(slot, c, before, after):
        part = front_parts[slot][c]
        outs[slot, c], held_sums[0] = run(
            functools.partial(output_kernel, part, c % per_back * front_count), part.steps,
            [plain(inner[slot, c // per_back]), plain(queries), plain(cotangent), plain(gain),
             cumul_in(), plain(before), plain(held_sums[0])],
            [give(local_of(part.count)), give(sums_shape)],
            scratch=[pltpu.VMEM((tokens, HEAD_DIM), f32)] * 2, after=after, cost=0.8,
        )
        return held_sums[0]

    works = [
        functools.partial(inner_work, slot, c)
        for c in range(BACKWARD_CHUNKS) for slot in ("mine", "theirs")
    ]
    mine, theirs = chain(
        FORWARD_CHUNKS, forward_piece, True, works,
        functools.partial(output_work, "mine"), functools.partial(output_work, "theirs"),
    )
    states = {"mine": mine, "theirs": theirs}

    sums = held_sums[0]
    shares = [sums] + [
        lax.ppermute(sums, "head", [(i, (i + k) % head_count) for i in range(head_count)])
        for k in range(1, head_count)
    ]

    attended, grad_queries, grad_keys, grad_values = [], [], [], []
    grads, inner_grads = {}, {}

    def target(held):
        return tuple(held[-1:])

    def covered(c):
        return range(c * per_back, (c + 1) * per_back)

    def backward_piece(part, after):
        before = target(attended)
        c = part.first // part.count
        ins = [plain(outs[part.slot, i]) for i in covered(c)]
        ins += [plain(cotangent), plain(gain), plain(queries), cumul_in()]
        ins += [plain(share) for share in shares]
        whole_out, grads[part.slot, c], piece = run(
            functools.partial(grad_kernel, features, part, per_back), part.steps, ins,
            [(whole, part.full_spec()), give(local_of(part.count, bf16)),
             give(states_of(part.count, 8))],
            after=before + tuple(after), aliases={2 + len(ins): 0} if before else None, cost=2.0,
        )
        attended.append(whole_out)
        return piece

    def backward_work(slot, c, after):
        part, held = back_parts[slot][c], target(grad_queries)
        ins = [plain(queries), plain(key_vecs), plain(value_vecs), plain(grads[slot, c]), cumul_in()]
        ins += [plain(states[slot][i]) for i in covered(c)]
        whole_out, *inner_grads[slot, c] = part.call(
            backward_kernel, ins,
            [(whole, part.full_spec()), give(local_of(part.count)), give(local_of(part.count))],
            after=held + tuple(after), aliases={2 + len(ins): 0} if held else None, cost=4.3,
        )
        grad_queries.append(whole_out)
        return inner_grads[slot, c][0]

    def final_work(slot, c, before, after):
        part, held = back_parts[slot][c], target(grad_keys) + target(grad_values)
        ins = [plain(array) for array in (*inner_grads[slot, c], key_vecs, value_vecs)]
        ins += [cumul_in(), plain(before)]
        whole_key, whole_value = part.call(
            final_kernel, ins, [(whole, part.full_spec())] * 2, after=held + tuple(after),
            aliases={2 + len(ins): 0, 3 + len(ins): 1} if held else None, cost=2.0,
        )
        grad_keys.append(whole_key)
        grad_values.append(whole_value)
        return whole_key

    works = [
        functools.partial(backward_work, slot, c)
        for c in range(BACKWARD_CHUNKS) for slot in ("mine", "theirs")
    ]
    chain(
        BACKWARD_CHUNKS, backward_piece, False, works,
        functools.partial(final_work, "mine"), functools.partial(final_work, "theirs"),
    )
    return attended[-1], grad_queries[-1], grad_keys[-1], grad_values[-1]


def solution(mesh):
    return jax.shard_map(
        on_device,
        mesh=mesh,
        in_specs=(
            P("seq", "head"),
            P("seq", "head"),
            P("seq", "head"),
            P("seq", "head"),
            P("head"),
            P("seq", "head"),
        ),
        out_specs=(P("seq", "head"), P("seq", "head"), P("seq", "head"), P("seq", "head")),
        check_vma=False,
    )
```

```python
import functools

import jax
import jax.numpy as jnp
from jax import lax
from jax.experimental import pallas as pl
from jax.experimental.pallas import tpu as pltpu
from jax.sharding import PartitionSpec as P

HEAD_DIM = 128
BLOCK = 512
FORWARD_CHUNKS = 2
BACKWARD_CHUNKS = 2
TILE = 256
epsilon = 1e-06
f32 = jnp.float32
bf16 = jnp.bfloat16

NN = (((1,), (0,)), ((), ()))
NT = (((1,), (1,)), ((), ()))
TN = (((0,), (0,)), ((), ()))


def dot(a, b, dims=NN):
    return lax.dot_general(a, b, dims, preferred_element_type=f32)


def halves(x):
    high = x.astype(bf16)
    return high, (x - high.astype(f32)).astype(bf16)


def column(row):
    return jnp.transpose(jnp.broadcast_to(row, (HEAD_DIM, row.shape[1])))


def wide(col, width):
    return jnp.concatenate([col] * (width // HEAD_DIM), axis=1)


def cumulative(decay):
    length = decay.shape[1]
    first = decay.astype(bf16)
    rest = decay - first.astype(f32)
    second = rest.astype(bf16)
    third = (rest - second.astype(f32)).astype(bf16)
    upto = lax.broadcasted_iota(jnp.int32, (length, length), 0) <= lax.broadcasted_iota(
        jnp.int32, (length, length), 1
    )
    upto = jnp.where(upto, 1.0, 0.0).astype(bf16)
    return dot(first, upto) + dot(second, upto) + dot(third, upto)


def trail_row(row):
    return jnp.exp(row[:, -1:] - row)


def outer_sum(left, scale_row, right):
    scaled = jnp.transpose(left.astype(f32)) * scale_row
    high, low = halves(scaled)
    return dot(high, right) + dot(low, right)


def cols(j):
    return slice(j * HEAD_DIM, (j + 1) * HEAD_DIM)


class Part:
    def __init__(self, first, count, slot, group_heads, per_step=0):
        self.first, self.count, self.slot, self.group_heads = first, count, slot, group_heads
        self.steps = count // per_step if per_step else 2 if count % 4 == 0 else 1
        self.per_step = count // self.steps

    def group(self, info):
        return info[0][0] if self.slot == "mine" else 1 - info[0][0]

    def head(self, info, o):
        return self.group(info) * self.group_heads + self.first + o

    def row(self, cumul_ref, info, o):
        return cumul_ref[pl.ds(self.head(info, o), 1), :]

    def wide_cols(self, info, o):
        return pl.ds(pl.multiple_of(self.head(info, o) * HEAD_DIM, HEAD_DIM), HEAD_DIM)

    def each(self, body):
        for j in range(self.per_step):
            body(pl.program_id(0) * self.per_step + j if self.steps > 1 else j, j)


def at_head(o):
    if isinstance(o, int):
        return cols(o)
    return pl.ds(pl.multiple_of(o * HEAD_DIM, HEAD_DIM), HEAD_DIM)


def chosen(part, values, o, j):
    read, refs = values
    if len(refs) == 1:
        return read(refs[0], at_head(o))
    found = read(refs[0], cols(j))
    for step in range(1, part.steps):
        found = jnp.where(pl.program_id(0) == step, read(refs[step], cols(j)), found)
    return found


def store_decay(part, info, cumul_ref, o, out_ref):
    row = part.row(cumul_ref, info, o)
    out_ref[pl.ds(part.count * HEAD_DIM + o, 1), :] = jnp.broadcast_to(
        jnp.exp(row[:, -1:]), (1, HEAD_DIM)
    )


def pieces_kernel(part, info, key_ref, value_ref, cumul_ref, out_ref):
    def head(o, j):
        at = part.wide_cols(info, o)
        out_ref[at_head(o), :] = outer_sum(
            key_ref[:, at], trail_row(part.row(cumul_ref, info, o)), value_ref[:, at]
        )
        store_decay(part, info, cumul_ref, o, out_ref)

    part.each(head)


def first_pieces_kernel(part, info, key_ref, value_ref, decay_ref, out_ref, cumul_ref):
    @pl.when(pl.program_id(0) == 0)
    def _():
        cumul_ref[...] = cumulative(decay_ref[...])

    def head(o, j):
        out_ref[at_head(o), :] = outer_sum(
            key_ref[:, cols(j)], trail_row(part.row(cumul_ref, info, o)), value_ref[:, cols(j)]
        )
        store_decay(part, info, cumul_ref, o, out_ref)

    part.each(head)


def inner_kernel(part, info, query_ref, key_ref, value_ref, cumul_ref, out_ref):
    def head(o, j):
        row = part.row(cumul_ref, info, o)
        col = column(row)
        at = part.wide_cols(info, o)
        query, key, value = query_ref[:, at], key_ref[:, at], value_ref[:, at]
        for top in range(0, BLOCK, TILE):
            end = top + TILE
            scores = dot(query[top:end], key[:end], NT)
            spread = wide(col[top:end], end) - row[:, :end]
            causal = lax.broadcasted_iota(jnp.int32, (TILE, end), 0) + top >= (
                lax.broadcasted_iota(jnp.int32, (TILE, end), 1)
            )
            weights = (scores * jnp.exp(jnp.where(causal, spread, -1e30))).astype(bf16)
            out_ref[top:end, at_head(o)] = dot(weights, value[:end])

    part.each(head)


def output_kernel(
    part, offset, info, inner_ref, query_ref, cot_ref, gain_ref, cumul_ref, state_ref, before_ref,
    out_ref, sums_ref, square_ref, product_ref,
):
    @pl.when(pl.program_id(0) == 0)
    def _():
        square_ref[...] = jnp.zeros_like(square_ref)
        product_ref[...] = jnp.zeros_like(product_ref)

    def head(o, j):
        lead = jnp.exp(column(part.row(cumul_ref, info, o)))
        high, low = halves(state_ref[at_head(o), :])
        at = part.wide_cols(info, o)
        query = query_ref[:, at]
        out = inner_ref[:, at_head(offset + o)] + lead * (dot(query, high) + dot(query, low))
        out_ref[:, at_head(o)] = out
        square_ref[...] += out * out
        product_ref[...] += cot_ref[:, at].astype(f32) * gain_ref[:, at] * out

    part.each(head)

    @pl.when(pl.program_id(0) == part.steps - 1)
    def _():
        rows = lax.broadcasted_iota(jnp.int32, (8, HEAD_DIM), 0)
        total = before_ref[...]
        for place, ref in ((0, square_ref), (1, product_ref)):
            pick = jnp.where(rows == place, 1.0, 0.0).astype(bf16)
            high, low = halves(ref[...])
            total += dot(pick, high, NT) + dot(pick, low, NT)
        sums_ref[...] = total


def grad_kernel(features, part, held, info, *refs):
    outs, (cot_ref, gain_ref, query_ref, cumul_ref, *refs) = refs[:held], refs[held:]
    shares, (attended_ref, grad_ref, piece_ref) = refs[:-3], refs[-3:]
    sums = shares[0][...]
    for share in shares[1:]:
        sums = sums + share[...]
    inverse = lax.rsqrt(sums[0:1] / features + epsilon)
    mean_term = inverse * sums[1:2] / features
    inverse_col, mean_col = column(inverse), column(mean_term)

    def head(o, j):
        at = part.wide_cols(info, o)
        gain = gain_ref[:, at]
        normed = chosen(part, (lambda ref, at: ref[:, at], outs), o, j) * inverse_col
        attended_ref[:, cols(j)] = (normed * gain).astype(bf16)
        scaled_grad = cot_ref[:, at].astype(f32) * gain
        grad = (inverse_col * (scaled_grad - normed * mean_col)).astype(bf16)
        grad_ref[:, at_head(o)] = grad
        lead = jnp.exp(part.row(cumul_ref, info, o))
        piece_ref[at_head(o), :] = outer_sum(query_ref[:, at], lead, grad)
        store_decay(part, info, cumul_ref, o, piece_ref)

    part.each(head)


def backward_kernel(part, info, query_ref, key_ref, value_ref, grad_ref, cumul_ref, *refs):
    states, (grad_query_ref, inner_key_ref, inner_value_ref) = refs[:-3], refs[-3:]

    def head(o, j):
        row = part.row(cumul_ref, info, o)
        col = column(row)
        at = part.wide_cols(info, o)
        query, key = query_ref[:, at], key_ref[:, at]
        value, grad = value_ref[:, at], grad_ref[:, at_head(o)]
        high, low = halves(chosen(part, (lambda ref, at: ref[at, :], states), o, j))
        outer = jnp.exp(col) * (dot(grad, high, NT) + dot(grad, low, NT))
        for top in range(0, BLOCK, TILE):
            end = top + TILE
            scores = dot(key[top:end], query[top:], NT)
            grad_scores = dot(value[top:end], grad[top:], NT)
            spread = row[:, top:] - wide(col[top:end], BLOCK - top)
            causal = lax.broadcasted_iota(jnp.int32, spread.shape, 0) <= (
                lax.broadcasted_iota(jnp.int32, spread.shape, 1)
            )
            decays = jnp.exp(jnp.where(causal, spread, -1e30))
            weights = (scores * decays).astype(bf16)
            grad_weights = (grad_scores * decays).astype(bf16)
            inner_value_ref[top:end, at_head(o)] = dot(weights, grad[top:])
            inner_key_ref[top:end, at_head(o)] = dot(grad_weights, query[top:])
            inner_query = dot(grad_weights, key[top:end], TN)
            outer = inner_query + outer if top == 0 else jnp.concatenate(
                [outer[:top], outer[top:] + inner_query], axis=0
            )
        grad_query_ref[:, cols(j)] = outer.astype(bf16)

    part.each(head)


def final_kernel(
    part, info, inner_key_ref, inner_value_ref, key_ref, value_ref, cumul_ref, state_ref,
    grad_key_ref, grad_value_ref,
):
    def head(o, j):
        trail = column(trail_row(part.row(cumul_ref, info, o)))
        high, low = halves(state_ref[at_head(o), :])
        at = part.wide_cols(info, o)
        key, value = key_ref[:, at], value_ref[:, at]
        grad_key_ref[:, cols(j)] = (
            inner_key_ref[:, at_head(o)] + trail * (dot(value, high, NT) + dot(value, low, NT))
        ).astype(bf16)
        grad_value_ref[:, cols(j)] = (
            inner_value_ref[:, at_head(o)] + trail * (dot(key, high) + dot(key, low))
        ).astype(bf16)

    part.each(head)


def ordered(is_first, half, j, keep_ref, got_ref):
    rows = slice(j * HEAD_DIM, (j + 1) * HEAD_DIM)
    place = slice(half * HEAD_DIM + j, half * HEAD_DIM + j + 1)
    keep, got = keep_ref[rows, :], got_ref[rows, :]
    keep_decay, got_decay = keep_ref[place, :], got_ref[place, :]
    return (
        jnp.where(is_first, keep, got),
        jnp.where(is_first, got, keep),
        jnp.where(is_first, keep_decay, got_decay),
        jnp.where(is_first, got_decay, keep_decay),
    )


def scan_position(places, forward, info):
    member, pair = info[0][0], info[1][0]
    if forward:
        return member == 0, pair
    return member == 1, places - 1 - pair


def copy_kernel(info, in_ref, out_ref):
    out_ref[...] = in_ref[...]


def hop_kernel(half, p, position, info, keep_ref, got_ref, *refs):
    arrived, out_ref = refs[:-1], refs[-1]
    is_first, place = position(info)

    @pl.when(place == p)
    def _():
        for j in range(half):
            first, second, first_decay, second_decay = ordered(is_first, half, j, keep_ref, got_ref)
            value = second_decay * first + second
            for arrived_ref in arrived:
                value += (first_decay * second_decay) * arrived_ref[cols(j), :]
            out_ref[cols(j), :] = value


def last_kernel(half, position, info, keep_ref, got_ref, *refs):
    arrived, (mine_ref, send_ref) = refs[:-2], refs[-2:]
    is_first, place = position(info)
    for p in range(len(arrived) + 1):

        @pl.when(place == p)
        def _():
            for j in range(half):
                first, _, first_decay, _ = ordered(is_first, half, j, keep_ref, got_ref)
                if p == 0:
                    before, after = jnp.zeros_like(first), first
                else:
                    before = arrived[p - 1][cols(j), :]
                    after = first_decay * before + first
                mine_ref[cols(j), :] = jnp.where(is_first, before, after)
                send_ref[cols(j), :] = jnp.where(is_first, after, before)


def on_device(queries, key_vecs, value_vecs, log_decay, norm_gain, cotangent):
    tokens, width = queries.shape
    assert tokens == BLOCK
    heads = width // HEAD_DIM
    group_heads = heads // 2
    head_count = lax.axis_size("head")
    features = width * head_count
    places = lax.axis_size("seq") // 2
    my_index = lax.axis_index("seq")
    member, pair = my_index % 2, my_index // 2
    gain = norm_gain.reshape(1, width)
    info = (member.astype(jnp.int32).reshape(1), pair.astype(jnp.int32).reshape(1))

    any_spec = pl.BlockSpec(memory_space=pl.ANY)
    whole = jax.ShapeDtypeStruct((tokens, width), bf16)
    sums_shape = jax.ShapeDtypeStruct((8, tokens), f32)

    def states_of(count, extra=0):
        return jax.ShapeDtypeStruct((count * HEAD_DIM + extra, HEAD_DIM), f32)

    def local_of(count, dtype=f32):
        return jax.ShapeDtypeStruct((tokens, count * HEAD_DIM), dtype)

    def run(kernel, grid, ins, outs, scratch=(), after=(), aliases=None, cost=1.0, limit=24):
        used = len(ins)
        after = [x for i, x in enumerate(after) if not any(x is y for y in after[:i])]

        def body(member_ref, pair_ref, *refs):
            kernel((member_ref, pair_ref), *refs[:used], *refs[used + len(after):])

        return pl.pallas_call(
            body,
            out_shape=[shape for shape, _ in outs],
            grid_spec=pltpu.PrefetchScalarGridSpec(
                num_scalar_prefetch=2,
                grid=(grid,),
                in_specs=[spec for _, spec in ins] + [any_spec] * len(after),
                out_specs=[spec for _, spec in outs],
                scratch_shapes=list(scratch),
            ),
            input_output_aliases=aliases or {},
            compiler_params=pltpu.CompilerParams(vmem_limit_bytes=limit * 1024 * 1024),
            cost_estimate=pl.CostEstimate(
                flops=int(cost * 1e9), bytes_accessed=int(cost * 2.5e6), transcendentals=0
            ),
        )(*info, *[array for array, _ in ins], *after)

    def fixed(shape):
        return pl.BlockSpec(shape, lambda i, *info: (0,) * len(shape))

    def plain(array):
        return array, fixed(array.shape)

    def give(shape):
        return shape, fixed(shape.shape)

    class Calls(Part):
        def full_spec(self):
            width = self.per_step
            return pl.BlockSpec(
                (tokens, width * HEAD_DIM),
                lambda i, *info: (
                    0, (self.group(info) * self.group_heads + self.first) // width + i
                ),
            )

        def call(self, kernel, ins, outs, **options):
            return run(functools.partial(kernel, self), self.steps, ins, outs, **options)

    def parts_of(chunks, slot, per_step=0):
        count = group_heads // chunks
        return [Calls(c * count, count, slot, group_heads, per_step) for c in range(chunks)]

    swap = [(2 * p + m, 2 * p + 1 - m) for p in range(places) for m in (0, 1)]

    def chain(chunks, make_piece, forward, filler, on_mine, on_theirs):
        position = functools.partial(scan_position, places, forward)
        my_parts, their_parts = parts_of(chunks, "mine"), parts_of(chunks, "theirs")
        count = group_heads // chunks
        state, wide_state = states_of(count), states_of(count, 8)

        def device(place, m):
            return 2 * (place if forward else places - 1 - place) + m

        sends, keeps, received, last = [], [], [], ()

        def exchange(last):
            c = len(received)
            if c == 0 or c >= chunks:
                if c == 0:
                    received.append(lax.ppermute(sends[0], "seq", swap))
                return last
            sent, = run(copy_kernel, 1, [plain(sends[c])], [give(wide_state)], after=last, cost=0.02)
            received.append(lax.ppermute(sent, "seq", swap))
            return (sent,)

        for part in their_parts:
            sends.append(make_piece(part, last))
            last = () if forward and len(sends) == 1 else (sends[-1],)
        last = exchange(last)
        for part in my_parts:
            keeps.append(make_piece(part, last))
            last = (keeps[-1],)
        last = exchange(last)
        arrived, mine, theirs, late = {}, [], [], []
        for step in range(chunks + places - 1):
            for p in range(places - 1):
                c = step - p
                if not 0 <= c < chunks:
                    continue
                ins = [plain(keeps[c]), plain(received[c])]
                if p > 0:
                    ins.append(plain(arrived[c, p]))
                value, = run(
                    functools.partial(hop_kernel, count, p, position), 1, ins, [give(state)],
                    after=last, cost=0.3,
                )
                pairs = [(device(p, m), device(p + 1, m)) for m in (0, 1)]
                arrived[c, p + 1] = lax.ppermute(value, "seq", pairs)
                last = (value,)
            last = exchange(last)
            c = step + 1 - places
            if c >= 0:
                ins = [plain(keeps[c]), plain(received[c])]
                ins += [plain(arrived[c, p]) for p in range(1, places)]
                own, send = run(
                    functools.partial(last_kernel, count, position), 1, ins, [give(state)] * 2,
                    after=last, cost=0.3,
                )
                theirs.append(lax.ppermute(send, "seq", swap))
                mine.append(own)
                last = (send,)
                filler.append(functools.partial(on_mine, c, own))
                late.append(functools.partial(on_theirs, c, theirs[c]))
                if c >= 2:
                    filler.append(late.pop(0))
                if forward and c >= chunks - 2 and filler:
                    last = (filler.pop(0)(last),)
            if filler:
                last = (filler.pop(0)(last),)
        for work in filler + late:
            last = (work(last),)
        return mine, theirs

    inner, outs = {}, {}
    held_cumul, held_sums = [], [jnp.zeros(sums_shape.shape, f32)]
    back_count = group_heads // BACKWARD_CHUNKS
    front_count = group_heads // FORWARD_CHUNKS
    per_back = back_count // front_count
    back_parts = {slot: parts_of(BACKWARD_CHUNKS, slot) for slot in ("mine", "theirs")}
    front_parts = {slot: parts_of(FORWARD_CHUNKS, slot, front_count) for slot in ("mine", "theirs")}

    def cumul_in():
        return plain(held_cumul[0])

    def forward_piece(part, after):
        if not held_cumul:
            piece, cumul = part.call(
                first_pieces_kernel,
                [(key_vecs, part.full_spec()), (value_vecs, part.full_spec()), plain(log_decay.T)],
                [give(states_of(part.count, 8)), give(jax.ShapeDtypeStruct((heads, tokens), f32))],
                cost=0.05, limit=60,
            )
            held_cumul.append(cumul)
            return piece
        part = Calls(part.first, part.count, part.slot, group_heads, part.count)
        return part.call(
            pieces_kernel, [plain(key_vecs), plain(value_vecs), cumul_in()],
            [give(states_of(part.count, 8))], after=after, cost=0.05,
        )[0]

    def inner_work(slot, c, after):
        part = back_parts[slot][c]
        inner[slot, c], = part.call(
            inner_kernel, [plain(queries), plain(key_vecs), plain(value_vecs), cumul_in()],
            [give(local_of(part.count))], after=after, cost=2.2 if inner else 0.1,
        )
        return inner[slot, c]

    def output_work(slot, c, before, after):
        part = front_parts[slot][c]
        outs[slot, c], held_sums[0] = run(
            functools.partial(output_kernel, part, c % per_back * front_count), part.steps,
            [plain(inner[slot, c // per_back]), plain(queries), plain(cotangent), plain(gain),
             cumul_in(), plain(before), plain(held_sums[0])],
            [give(local_of(part.count)), give(sums_shape)],
            scratch=[pltpu.VMEM((tokens, HEAD_DIM), f32)] * 2, after=after, cost=0.8,
        )
        return held_sums[0]

    works = [
        functools.partial(inner_work, slot, c)
        for c in range(BACKWARD_CHUNKS) for slot in ("mine", "theirs")
    ]
    mine, theirs = chain(
        FORWARD_CHUNKS, forward_piece, True, works,
        functools.partial(output_work, "mine"), functools.partial(output_work, "theirs"),
    )
    states = {"mine": mine, "theirs": theirs}

    sums = held_sums[0]
    shares = [sums] + [
        lax.ppermute(sums, "head", [(i, (i + k) % head_count) for i in range(head_count)])
        for k in range(1, head_count)
    ]

    attended, grad_queries, grad_keys, grad_values = [], [], [], []
    grads, inner_grads = {}, {}

    def target(held):
        return tuple(held[-1:])

    def covered(c):
        return range(c * per_back, (c + 1) * per_back)

    def backward_piece(part, after):
        before = target(attended)
        c = part.first // part.count
        ins = [plain(outs[part.slot, i]) for i in covered(c)]
        ins += [plain(cotangent), plain(gain), plain(queries), cumul_in()]
        ins += [plain(share) for share in shares]
        whole_out, grads[part.slot, c], piece = run(
            functools.partial(grad_kernel, features, part, per_back), part.steps, ins,
            [(whole, part.full_spec()), give(local_of(part.count, bf16)),
             give(states_of(part.count, 8))],
            after=before + tuple(after), aliases={2 + len(ins): 0} if before else None, cost=2.0,
        )
        attended.append(whole_out)
        return piece

    def backward_work(slot, c, after):
        part, held = back_parts[slot][c], target(grad_queries)
        ins = [plain(queries), plain(key_vecs), plain(value_vecs), plain(grads[slot, c]), cumul_in()]
        ins += [plain(states[slot][i]) for i in covered(c)]
        whole_out, *inner_grads[slot, c] = part.call(
            backward_kernel, ins,
            [(whole, part.full_spec()), give(local_of(part.count)), give(local_of(part.count))],
            after=held + tuple(after), aliases={2 + len(ins): 0} if held else None, cost=4.3,
        )
        grad_queries.append(whole_out)
        return inner_grads[slot, c][0]

    def final_work(slot, c, before, after):
        part, held = back_parts[slot][c], target(grad_keys) + target(grad_values)
        ins = [plain(array) for array in (*inner_grads[slot, c], key_vecs, value_vecs)]
        ins += [cumul_in(), plain(before)]
        whole_key, whole_value = part.call(
            final_kernel, ins, [(whole, part.full_spec())] * 2, after=held + tuple(after),
            aliases={2 + len(ins): 0, 3 + len(ins): 1} if held else None, cost=2.0,
        )
        grad_keys.append(whole_key)
        grad_values.append(whole_value)
        return whole_key

    works = [
        functools.partial(backward_work, slot, c)
        for c in range(BACKWARD_CHUNKS) for slot in ("mine", "theirs")
    ]
    chain(
        BACKWARD_CHUNKS, backward_piece, False, works,
        functools.partial(final_work, "mine"), functools.partial(final_work, "theirs"),
    )
    return attended[-1], grad_queries[-1], grad_keys[-1], grad_values[-1]


def solution(mesh):
    return jax.shard_map(
        on_device,
        mesh=mesh,
        in_specs=(
            P("seq", "head"),
            P("seq", "head"),
            P("seq", "head"),
            P("seq", "head"),
            P("head"),
            P("seq", "head"),
        ),
        out_specs=(P("seq", "head"), P("seq", "head"), P("seq", "head"), P("seq", "head")),
        check_vma=False,
    )
```
